128 devices in a mesh: dp: 64 (over z, y, x), mem: 2 (over core).
Axes of the slice: x: 4, y: 4, z: 4, core: 2. Of those that a mesh axis runs over, the one named last changes fastest.
Arguments:
- tokens: bfloat16 [64, 192, 1024], P('dp', 'mem'), may hold values from -16 to 16
- memory: bfloat16 [2, 64, 48, 1024], P(None, 'dp', 'mem'), may hold values from -6 to 6
- lengths: int32 [64], replicated, may hold values from 24 to 192, as said below
- segments: int32 [64, 192], P('dp'), may hold values from 0 to 2, as said below
- key_mask: int32 [64, 24], P('dp', 'mem'), may hold values from 0 to 1, as said below
- w_self_qkv: bfloat16 [1024, 3072], replicated, may hold values from -0.1875 to 0.1875
- w_self_out: bfloat16 [1024, 1024], replicated, may hold values from -1 to 1
- w_cross_q: bfloat16 [1024, 1024], replicated, may hold values from -0.1875 to 0.1875
- w_cross_kv: bfloat16 [1024, 2048], replicated, may hold values from -0.1875 to 0.1875
- w_cross_out: bfloat16 [1024, 1024], replicated, may hold values from -1 to 1
- w_up: bfloat16 [1024, 4096], replicated, may hold values from -0.1875 to 0.1875
- w_down: bfloat16 [4096, 1024], replicated, may hold values from -0.09375 to 0.09375
- norm_gains: float32 [4, 1024], replicated, may hold values from 0.5 to 1.5
- norm_biases: float32 [4, 1024], replicated, may hold values from -1.2 to 1.2
- readout: bfloat16 [1024, 25088], P(None, ('dp', 'mem')), may hold values from -0.375 to 0.375
Outputs:
- loss: float32 [64], P('dp')
- layer_out: bfloat16 [2, 64, 192, 1024], P(None, 'dp', 'mem')
- tokens_grad: float32 [64, 192, 1024], P('dp', 'mem')
- memory_grad: float32 [2, 64, 48, 1024], P(None, 'dp', 'mem')
- grad_self_qkv: float32 [1024, 3072], P(('dp', 'mem'))
- grad_self_out: float32 [1024, 1024], P(('dp', 'mem'))
- grad_cross_q: float32 [1024, 1024], P(('dp', 'mem'))
- grad_cross_kv: float32 [1024, 2048], P(('dp', 'mem'))
- grad_cross_out: float32 [1024, 1024], P(('dp', 'mem'))
- grad_up: float32 [1024, 4096], P(('dp', 'mem'))
- grad_down: float32 [4096, 1024], P(('dp', 'mem'))
- grad_gains: float32 [4, 1024], P(None, ('dp', 'mem'))
- grad_biases: float32 [4, 1024], P(None, ('dp', 'mem'))
The draws below stay inside these ranges and needn't reach their ends.
Inputs may be any that keep to these rules, and one draw needn't show every extreme that they name: `lengths`: one page has exactly 192 tokens and another exactly 24. Along each page the ids never fall; segments 0, 1 and 2 are all present, and segment 1 holds positions 95 and 96. `key_mask`: entries 0 and 12 of every page are 1, entry 1 is 0.
All inputs are finite; a program needn't handle non-finite values.
Results may differ from the reference program's by a relative error of at most 0.033.
Values may be sent and summed in bfloat16 or wider, within the bound.
No kernel may reach another device: no remote copies, remote signals or barrier semaphores. Data moves between devices by JAX's collectives and lax.ppermute only.
A program may use at most 256 MiB of HBM per device.

```python
import jax
import jax.numpy as jnp
from jax import lax

D = 1024
HEAD = 64
FF = 4096
VOCAB = 25088
PATCHES = 48
TOK_DEV = 96
PAGE_LEN = 192
PAGES = 64


def draw_lengths(key, part):
    key = jax.random.fold_in(key, 11)
    subkeys = jax.random.split(key, 3)
    shortest = PAGE_LEN // 8
    values = jax.random.randint(subkeys[0], (PAGES,), shortest, PAGE_LEN + 1)
    longest_page = jax.random.randint(subkeys[1], (), 0, PAGES)
    shortest_page = (longest_page + 1 + jax.random.randint(subkeys[2], (), 0, PAGES - 1)) % PAGES
    values = values.at[longest_page].set(PAGE_LEN).at[shortest_page].set(shortest)
    return values.astype(jnp.int32)


def draw_segments(key, part):
    key = jax.random.fold_in(key, 12)
    subkeys = jax.random.split(key, 2)
    first_bound = jax.random.randint(subkeys[0], (PAGES, 1), 1, TOK_DEV)
    second_bound = jax.random.randint(subkeys[1], (PAGES, 1), TOK_DEV + 1, PAGE_LEN)
    positions = jnp.arange(PAGE_LEN)[None, :]
    return ((positions >= first_bound).astype(jnp.int32) + (positions >= second_bound).astype(jnp.int32)).astype(jnp.int32)


def draw_key_mask(key, part):
    key = jax.random.fold_in(key, 13)
    draws = jax.random.randint(key, (PAGES, PATCHES // 2), 0, 4)
    keep = (draws >= 1).astype(jnp.int32)
    keep = keep.at[:, 0].set(1).at[:, PATCHES // 4].set(1).at[:, 1].set(0)
    return keep.astype(jnp.int32)


def with_spikes(array, rng, source, target, parts, factor):
    def block_of(dim):
        return (jnp.arange(array.shape[dim]) // (array.shape[dim] // parts)).reshape((-1,) + (1,) * (array.ndim - 1 - dim))

    near = jax.random.permutation(rng, parts)[block_of(target)]
    second = (block_of(target) + parts // 2) % parts
    return jnp.where((block_of(source) == near) | (block_of(source) == second), factor * array, array)


def shard_levels(stream_key, extent, cuts, low, largest):
    def one(axis_at, blocks):
        steps = jax.random.uniform(jax.random.fold_in(jax.random.fold_in(stream_key, 6), axis_at), (blocks,), jnp.float32, low / len(cuts), largest / len(cuts))
        return jnp.repeat(jnp.exp(steps), extent[axis_at] // blocks).reshape((-1,) + (1,) * (len(extent) - axis_at - 1))

    level = one(*cuts[0])
    for cut in cuts[1:]:
        level = level * one(*cut)
    return level


def gaussian(rng, dims, deviation, limit, shards=(), kind=jnp.bfloat16):
    values = deviation * jax.random.normal(rng, dims, jnp.float32)
    if shards:
        values = values * shard_levels(rng, dims, shards, -0.22, 0.18)
    return jnp.clip(values, -limit, limit).astype(kind)


def gaussian_with(stream_key, dims, scale, reach, cuts, heavy, dtype=jnp.bfloat16):
    entries = scale * jax.random.normal(stream_key, dims, jnp.float32)
    if cuts:
        entries = entries * shard_levels(stream_key, dims, cuts, -0.22, 0.18)
    return jnp.clip(with_spikes(entries, jax.random.fold_in(stream_key, 3), *heavy), -reach, reach).astype(dtype)


def setup_inputs(seed: int = 0) -> dict:
    key_of = jax.random.split(jax.random.key(seed), 16)
    return {
        "tokens": gaussian_with(key_of[0], (PAGES, PAGE_LEN, D), 1.0, 16.0, ((0, 64), (1, 2)), (0, 2, 64, 4.0)),
        "memory": gaussian(key_of[1], (2, PAGES, PATCHES, D), 1.0, 6.0, ((1, 64), (2, 2))),
        "lengths": draw_lengths(jax.random.fold_in(key_of[15], 71), 0),
        "segments": draw_segments(jax.random.fold_in(key_of[15], 71), 0),
        "key_mask": draw_key_mask(jax.random.fold_in(key_of[15], 71), 0),
        "w_self_qkv": gaussian(key_of[5], (D, 3 * D), D ** -0.5, 0.1875),
        "w_self_out": gaussian(key_of[6], (D, D), (max(6 * D // PAGE_LEN, 1)) ** -0.5, 1.0),
        "w_cross_q": gaussian(key_of[7], (D, D), D ** -0.5, 0.1875),
        "w_cross_kv": gaussian(key_of[8], (D, 2 * D), D ** -0.5, 0.1875),
        "w_cross_out": gaussian(key_of[9], (D, D), (max(4 * D // (3 * PATCHES), 1)) ** -0.5, 1.0),
        "w_up": gaussian(key_of[10], (D, FF), D ** -0.5, 0.1875),
        "w_down": gaussian(key_of[11], (FF, D), FF ** -0.5, 0.09375),
        "norm_gains": jnp.clip(1.0 + 0.1 * jax.random.normal(key_of[12], (4, D), jnp.float32), 0.5, 1.5),
        "norm_biases": gaussian(key_of[13], (4, D), 0.2, 1.2, (), jnp.float32),
        "readout": gaussian(key_of[14], (D, VOCAB), (D // 4) ** -0.5, 0.375, ((1, 128),)),
    }


@jax.custom_vjp
def low(v):
    return lax.optimization_barrier(v.astype(jnp.bfloat16)).astype(jnp.float32)

@jax.custom_vjp
def low_back(v):
    return v

def low_keep(v):
    return (low(v), None)

def low_pass(kept, grad):
    return (grad,)

def back_keep(v):
    return (v, None)

def back_low(kept, grad):
    return (low(grad),)
low.defvjp(low_keep, low_pass)
low_back.defvjp(back_keep, back_low)
epsilon = 1e-05
masked_score = -1e+30
highest = lax.Precision.HIGHEST

def both_ways(value):
    return low(low_back(value))

def product(left, right):
    return jnp.dot(left, right, precision=highest, preferred_element_type=jnp.float32)

def layer_norm(values, gain, bias):
    centre = values - lax.optimization_barrier(jnp.mean(values, -1, keepdims=True))
    inverse = lax.rsqrt(lax.optimization_barrier(jnp.mean(centre * centre, -1, keepdims=True)) + epsilon)
    return centre * inverse * gain + bias

def attend(queries, keys, values, allowed):
    query_count = queries.shape[0]
    key_count = keys.shape[0]
    query_heads = queries.reshape(query_count, -1, HEAD)
    key_heads = keys.reshape(key_count, -1, HEAD)
    value_heads = values.reshape(key_count, -1, HEAD)
    raw_scores = jnp.einsum('qhd,khd->hqk', query_heads, key_heads, precision=highest) * HEAD ** (-0.5)
    scores = jnp.where(allowed[None], low_back(raw_scores), masked_score)
    probs = low(jax.nn.softmax(scores, axis=-1))
    mixed = jnp.einsum('hqk,khd->qhd', probs, value_heads, precision=highest)
    return both_ways(mixed.reshape(query_count, -1))

def page_forward(weight_set, page_tokens, page_memory, page_segments, page_keep, page_length, readout_wide):
    w_self_qkv, w_self_out, w_cross_q, w_cross_kv, w_cross_out, w_up, w_down, norm_gains, norm_biases = weight_set
    width = page_tokens.shape[1]
    slot_count = page_tokens.shape[0]
    positions = jnp.arange(slot_count)
    self_allowed = (positions[None, :] <= positions[:, None]) & (page_segments[None, :] == page_segments[:, None])
    normed_one = low(layer_norm(page_tokens, norm_gains[0], norm_biases[0]))
    joined = both_ways(product(normed_one, w_self_qkv))
    attended = attend(joined[:, :width], joined[:, width:2 * width], joined[:, 2 * width:], self_allowed)
    hidden_one = page_tokens + low_back(product(attended, w_self_out))
    normed_two = low(layer_norm(hidden_one, norm_gains[1], norm_biases[1]))
    query_cross = both_ways(product(normed_two, w_cross_q))
    keep_keys = jnp.repeat(page_keep, 2) == 1
    cross_allowed = jnp.broadcast_to(keep_keys[None, :], (slot_count, keep_keys.shape[0]))
    outputs = []
    logit_views = []
    for view_index in range(2):
        memory_kv = both_ways(product(page_memory[view_index], w_cross_kv))
        attended_cross = attend(query_cross, memory_kv[:, :width], memory_kv[:, width:], cross_allowed)
        hidden_two = hidden_one + low_back(product(attended_cross, w_cross_out))
        normed_three = low(layer_norm(hidden_two, norm_gains[2], norm_biases[2]))
        up_values = low_back(product(normed_three, w_up))
        active = low(jax.nn.gelu(up_values, approximate=False))
        hidden_three = hidden_two + low_back(product(active, w_down))
        final_rows = low(layer_norm(hidden_three, norm_gains[3], norm_biases[3]))
        logit_views.append(low_back(product(final_rows, readout_wide)))
        outputs.append(hidden_three)
    first_log = jax.nn.log_softmax(logit_views[0], axis=-1)
    second_log = jax.nn.log_softmax(logit_views[1], axis=-1)
    divergence = lax.optimization_barrier(jnp.sum(jnp.exp(first_log) * (first_log - second_log), -1))
    kept_sum = jnp.sum(jnp.where(positions < page_length, divergence, 0.0))
    return (kept_sum, jnp.stack(outputs))

def reference(tokens, memory, lengths, segments, key_mask, w_self_qkv, w_self_out, w_cross_q, w_cross_kv, w_cross_out, w_up, w_down, norm_gains, norm_biases, readout):
    weight_set = (w_self_qkv.astype(jnp.float32), w_self_out.astype(jnp.float32), w_cross_q.astype(jnp.float32), w_cross_kv.astype(jnp.float32), w_cross_out.astype(jnp.float32), w_up.astype(jnp.float32), w_down.astype(jnp.float32), norm_gains.astype(jnp.float32), norm_biases.astype(jnp.float32))
    readout_wide = readout.astype(jnp.float32)
    count = jnp.sum(lengths).astype(jnp.float32)

    def total(weights_now, token_values, memory_values):

        def one_page(pieces):
            return page_forward(weights_now, pieces[0], pieces[1], pieces[2], pieces[3], pieces[4], readout_wide)
        page_sums, stacked = lax.map(jax.checkpoint(one_page), (token_values, jnp.swapaxes(memory_values, 0, 1), segments, key_mask, lengths))
        return (page_sums / count, stacked)
    primal, pullback = jax.vjp(total, weight_set, tokens.astype(jnp.float32), memory.astype(jnp.float32))
    loss, stacked = primal
    weight_grads, token_grad, memory_grad = pullback((jnp.ones_like(loss), jnp.zeros_like(stacked)))
    layer_out = jnp.swapaxes(stacked, 0, 1).astype(jnp.bfloat16)
    return (loss, layer_out, token_grad, memory_grad, weight_grads[0], weight_grads[1], weight_grads[2], weight_grads[3], weight_grads[4], weight_grads[5], weight_grads[6], weight_grads[7], weight_grads[8])
```

```python
from functools import partial

import jax
import jax.numpy as jnp
from jax import lax
from jax.experimental import pallas as pl
from jax.experimental.pallas import tpu as pltpu
from jax.sharding import PartitionSpec as P

HEAD = 64
SIDE = 4
CHIPS = SIDE * SIDE * SIDE
TILE = 256
ROWS = 16
LANES = 208


epsilon = 1e-05
masked_score = -1e30
bf16 = jnp.bfloat16
f32 = jnp.float32


def swapped(block):
    return lax.ppermute(block, "mem", [(0, 1), (1, 0)])


def product(left, right):
    return jnp.dot(left, right, preferred_element_type=f32)


def product_right(left, right):
    return lax.dot_general(left, right, (((1,), (1,)), ((), ())), preferred_element_type=f32)


def norm_forward(values, gain, bias):
    centre = values - jnp.mean(values, -1, keepdims=True)
    inverse = lax.rsqrt(jnp.mean(centre * centre, -1, keepdims=True) + epsilon)
    normed = centre * inverse
    return (normed * gain + bias, normed, inverse)


def norm_backward(upstream, normed, inverse, gain):
    scaled = upstream * gain
    back = inverse * (
        scaled
        - jnp.mean(scaled, -1, keepdims=True)
        - normed * jnp.mean(scaled * normed, -1, keepdims=True)
    )
    return (back, jnp.sum(upstream * normed, 0), jnp.sum(upstream, 0))


def combine_views(earlier, later):
    top_first = jnp.maximum(earlier[0], later[0])
    early_first = jnp.exp(earlier[0] - top_first)
    late_first = jnp.exp(later[0] - top_first)
    top_second = jnp.maximum(earlier[3], later[3])
    early_second = jnp.exp(earlier[3] - top_second)
    late_second = jnp.exp(later[3] - top_second)
    return (
        top_first,
        earlier[1] * early_first + later[1] * late_first,
        earlier[2] * early_first + later[2] * late_first,
        top_second,
        earlier[4] * early_second + later[4] * late_second,
    )


def lines(stride, core):
    starts = [d for d in range(CHIPS) if (d // stride) % SIDE == 0]
    return [[2 * (start + stride * k) + core for k in range(SIDE)] for start in starts]


def exchange(block, strides):
    groups = lines(strides[0], 0) + lines(strides[1], 1)
    return lax.all_to_all(block, ("dp", "mem"), 0, 0, axis_index_groups=groups, tiled=True)


def reduced(bucket):
    for strides in ((1, 4), (4, 16), (16, 1)):
        bucket = bucket.reshape((SIDE, -1) + bucket.shape[1:])
        bucket = exchange(bucket, strides)
        total = bucket.astype(f32).sum(0)
        bucket = total.astype(bf16)
    return total[0]


def outer_kernel(shapes, core_ref, *refs):
    n_in = 4 * len(shapes) + 1
    inputs, out_ref, turned = refs[:n_in], refs[n_in], refs[n_in + 1 :]
    extra = inputs[-1]
    step = pl.program_id(0)
    core = core_ref[0]

    def place(chip):
        z, y, x = chip // 16, (chip // 4) % 4, chip % 4
        return jnp.where(core == 0, x * 16 + y * 4 + z, y * 16 + z * 4 + x)

    first = 0
    for i, (groups, columns) in enumerate(shapes):
        left_a, left_b, right_a, right_b = inputs[4 * i : 4 * i + 4]
        tiles = columns // TILE
        depth = left_a.shape[0]
        low, high = first, first + groups * tiles
        first = high

        @pl.when(step == low)
        def _(left_a=left_a, left_b=left_b, to=turned[i], groups=groups, depth=depth):
            wide = left_a.shape[1]
            for start in range(0, wide, 1024):
                both = jnp.concatenate(
                    [left_a[:, start : start + 1024], left_b[:, start : start + 1024]], 0
                )
                flat = both.T
                if groups == 1:
                    to[0, start : start + 1024] = flat
                else:
                    per = ROWS * groups
                    for c in range(1024 // per):
                        chip = start // per + c
                        for g in range(groups):
                            at = c * per + g * ROWS
                            to[g, chip * ROWS : (chip + 1) * ROWS] = flat[at : at + ROWS]

        @pl.when((step >= low) & (step < high))
        def _(right_a=right_a, right_b=right_b, to=turned[i], tiles=tiles, low=low):
            at = step - low
            group = at // tiles
            tile = at - group * tiles
            column = pl.multiple_of(tile * TILE, TILE)
            both = jnp.concatenate(
                [right_a[:, pl.ds(column, TILE)], right_b[:, pl.ds(column, TILE)]], 0
            )
            result = jnp.dot(to[group], both, preferred_element_type=f32).astype(bf16)
            for chip in range(CHIPS):
                out_ref[place(chip)] = result[chip * ROWS : (chip + 1) * ROWS]

    @pl.when(step == first)
    def _():
        for chip in range(CHIPS):
            out_ref[place(chip)] = extra[chip]


def outer_products(core, items, extra):
    shapes, operands, scratch = [], [], []
    total = 0
    for left, left_other, right, right_other in items:
        groups = left.shape[1] // (ROWS * CHIPS)
        shapes.append((groups, right.shape[1]))
        operands += [left, left_other, right, right_other]
        depth = left.shape[0] + left_other.shape[0]
        scratch.append(pltpu.VMEM((groups, ROWS * CHIPS, depth), bf16))
        total += groups * right.shape[1]
    operands.append(extra)
    width = total + TILE
    flops = sum(2 * s[0] * ROWS * CHIPS * s[1] * 384 for s in shapes)
    return pl.pallas_call(
        partial(outer_kernel, tuple(shapes)),
        out_shape=jax.ShapeDtypeStruct((CHIPS, ROWS, width), bf16),
        grid_spec=pltpu.PrefetchScalarGridSpec(
            num_scalar_prefetch=1,
            grid=(width // TILE,),
            in_specs=[pl.BlockSpec(memory_space=pltpu.VMEM) for _ in operands],
            out_specs=pl.BlockSpec((CHIPS, ROWS, TILE), lambda i, core: (0, 0, i)),
            scratch_shapes=scratch,
        ),
        compiler_params=pltpu.CompilerParams(vmem_limit_bytes=40 * 1024 * 1024),
        cost_estimate=pl.CostEstimate(
            flops=flops, bytes_accessed=CHIPS * ROWS * width * 2, transcendentals=0
        ),
    )(core.reshape(1), *operands)


def norm_vectors(vectors):
    spread = vectors.reshape(8, CHIPS, ROWS).transpose(1, 0, 2).reshape(CHIPS, 1, 128)
    return jnp.pad(spread.astype(bf16), ((0, 0), (0, ROWS - 1), (0, TILE - 128)))


def on_device(
    tokens,
    memory,
    lengths,
    segments,
    key_mask,
    w_self_qkv,
    w_self_out,
    w_cross_q,
    w_cross_kv,
    w_cross_out,
    w_up,
    w_down,
    norm_gains,
    norm_biases,
    readout,
):
    tok_rows = tokens.shape[1]
    width = tokens.shape[2]
    heads = width // HEAD
    scale = HEAD ** (-0.5)
    page_len = 2 * tok_rows
    half = lax.axis_index("mem")
    page_index = lax.axis_index("dp")
    patches = 2 * memory.shape[2]

    vocab_dev = readout.shape[1]
    readout_turned = jnp.pad(readout.T, ((0, LANES - vocab_dev), (0, 0)))
    readout_half = lax.all_gather(readout_turned, "dp", axis=0, tiled=True)

    tokens_page = lax.all_gather(tokens[0], "mem", axis=0, tiled=True)
    memory_page = lax.all_gather(memory[:, 0], "mem", axis=1, tiled=True)
    memory_rows = memory_page.reshape(2 * patches, width)
    mask_page = lax.all_gather(
        key_mask[0].astype(f32), "mem", axis=0, tiled=True
    )
    keep_keys = jnp.repeat(mask_page, 2) == 1

    def own_half(full, axis):
        size = full.shape[axis] // 2
        return lax.dynamic_slice_in_dim(full, half * size, size, axis)

    def other_half(full, axis):
        size = full.shape[axis] // 2
        return lax.dynamic_slice_in_dim(full, (1 - half) * size, size, axis)

    inputs = tokens[0].astype(f32)
    page_segments = segments[0]
    positions = jnp.arange(tok_rows) + half * tok_rows
    key_positions = jnp.arange(page_len)
    query_segments = own_half(page_segments, 0)
    self_allowed = (key_positions[None, :] <= positions[:, None]) & (
        page_segments[None, :] == query_segments[:, None]
    )
    unused, norm_one, inverse_one = norm_forward(inputs, norm_gains[0], norm_biases[0])
    normed_page = norm_forward(tokens_page.astype(f32), norm_gains[0], norm_biases[0])[0]
    normed_page_low = normed_page.astype(bf16)
    normed_one_low = own_half(normed_page_low, 0)
    query_self = product(normed_one_low, w_self_qkv[:, :width]).astype(bf16)
    query_self = query_self.reshape(tok_rows, heads, HEAD)
    pairs_self = product(normed_page_low, w_self_qkv[:, width:]).astype(bf16)
    key_self = pairs_self[:, :width].reshape(page_len, heads, HEAD)
    value_self = pairs_self[:, width:].reshape(page_len, heads, HEAD)
    scores = jnp.einsum("qhd,khd->hqk", query_self, key_self, preferred_element_type=f32) * scale
    scores = jnp.where(self_allowed[None], scores, masked_score)
    score_top = jnp.max(scores, -1, keepdims=True)
    score_exp = jnp.exp(scores - score_top)
    self_probs = score_exp / jnp.sum(score_exp, -1, keepdims=True)
    self_probs_low = self_probs.astype(bf16)
    attn_self = (
        jnp.einsum("hqk,khd->qhd", self_probs_low, value_self, preferred_element_type=f32)
        .reshape(tok_rows, width)
        .astype(bf16)
    )
    attn_self_other = swapped(attn_self)
    hidden_one = inputs + product(attn_self, w_self_out)

    normed_two, norm_two, inverse_two = norm_forward(hidden_one, norm_gains[1], norm_biases[1])
    normed_two_low = normed_two.astype(bf16)
    normed_two_other = swapped(normed_two_low)
    query_cross = product(normed_two_low, w_cross_q).astype(bf16).reshape(tok_rows, heads, HEAD)
    pairs_cross = product(memory_rows, w_cross_kv).astype(bf16).reshape(2, patches, 2 * width)
    key_cross = pairs_cross[:, :, :width].reshape(2, patches, heads, HEAD)
    value_cross = pairs_cross[:, :, width:].reshape(2, patches, heads, HEAD)
    cross_scores = (
        jnp.einsum("qhd,vkhd->vhqk", query_cross, key_cross, preferred_element_type=f32) * scale
    )
    cross_scores = jnp.where(keep_keys, cross_scores, masked_score)
    cross_exp = jnp.exp(cross_scores - jnp.max(cross_scores, -1, keepdims=True))
    cross_probs = cross_exp / jnp.sum(cross_exp, -1, keepdims=True)
    cross_probs_low = cross_probs.astype(bf16)
    attn_cross = (
        jnp.einsum("vhqk,vkhd->vqhd", cross_probs_low, value_cross, preferred_element_type=f32)
        .reshape(2 * tok_rows, width)
        .astype(bf16)
    )
    attn_cross_other = swapped(attn_cross)
    hidden_two = jnp.concatenate([hidden_one, hidden_one], 0) + product(attn_cross, w_cross_out)

    normed_three, norm_three, inverse_three = norm_forward(
        hidden_two, norm_gains[2], norm_biases[2]
    )
    normed_three_low = normed_three.astype(bf16)
    normed_three_other = swapped(normed_three_low)
    up_values = product(normed_three_low, w_up)
    active_low = jax.nn.gelu(up_values, approximate=False).astype(bf16)
    active_other = swapped(active_low)
    hidden_three = hidden_two + product(active_low, w_down)
    layer_out = hidden_three.reshape(2, 1, tok_rows, width).astype(bf16)

    final_norm, norm_four, inverse_four = norm_forward(hidden_three, norm_gains[3], norm_biases[3])
    final_low = final_norm.astype(bf16).reshape(2, tok_rows, width)
    count = jnp.sum(lengths).astype(f32)
    page_length = lengths[page_index]
    final_page = lax.all_gather(final_low, "mem", axis=1, tiled=True)
    logits = product_right(final_page.reshape(2 * page_len, width), readout_half)
    logits = logits.reshape(2, page_len, -1)
    is_entry = jnp.arange(logits.shape[-1]) % LANES < vocab_dev
    logits = jnp.where(is_entry, logits, masked_score)
    first = logits[0]
    second = logits[1]
    first_top = jnp.max(first, -1)
    first_exp = jnp.exp(first - first_top[:, None])
    second_top = jnp.max(second, -1)
    partial_stats = jnp.stack(
        [
            first_top,
            jnp.sum(first_exp, -1),
            jnp.sum(first_exp * (first - second), -1),
            second_top,
            jnp.sum(jnp.exp(second - second_top[:, None]), -1),
        ]
    )
    all_stats = lax.all_gather(partial_stats, "mem")
    merged = combine_views(tuple(all_stats[0]), tuple(all_stats[1]))
    first_lse = merged[0] + jnp.log(merged[1])
    second_lse = merged[3] + jnp.log(merged[4])
    cross_mean = merged[2] / merged[1]
    divergence = cross_mean - first_lse + second_lse
    valid_rows = jnp.arange(page_len) < page_length
    row_weight = valid_rows.astype(f32) / count
    loss = (jnp.sum(jnp.where(valid_rows, divergence, 0.0)) / count).reshape(1)
    first_prob = jnp.exp(first - first_lse[:, None])
    second_prob = jnp.exp(second - second_lse[:, None])
    grad_first = row_weight[:, None] * first_prob * (first - second - cross_mean[:, None])
    grad_second = row_weight[:, None] * (second_prob - first_prob)
    grad_logits = jnp.stack([grad_first, grad_second], 0).astype(bf16)
    grad_part = product(grad_logits.reshape(2 * page_len, -1), readout_half)
    grad_part = grad_part.reshape(2, page_len, width)
    grad_final = own_half(grad_part, 1) + swapped(other_half(grad_part, 1))

    grad_three, gain_four, bias_four = norm_backward(
        grad_final.reshape(2 * tok_rows, width), norm_four, inverse_four, norm_gains[3]
    )
    grad_three_low = grad_three.astype(bf16)
    grad_three_other = swapped(other_half(grad_three_low, 1))
    grad_active = product_right(grad_three_low, w_down)
    unused_value, gelu_back = jax.vjp(partial(jax.nn.gelu, approximate=False), up_values)
    grad_up_low = gelu_back(grad_active)[0].astype(bf16)
    grad_up_other = swapped(other_half(grad_up_low, 1))
    first_bucket = outer_products(
        half,
        [
            (active_low, active_other, own_half(grad_three_low, 1), grad_three_other),
            (normed_three_low, normed_three_other, own_half(grad_up_low, 1), grad_up_other),
        ],
        jnp.zeros((CHIPS, ROWS, TILE), bf16),
    )
    first_sum = reduced(first_bucket)
    grad_norm_three, gain_three, bias_three = norm_backward(
        product_right(grad_up_low, w_up), norm_three, inverse_three, norm_gains[2]
    )
    grad_two = grad_three + grad_norm_three

    grad_branch_low = grad_two.astype(bf16)
    grad_branch_other = swapped(other_half(grad_branch_low, 1))
    grad_heads = product_right(grad_branch_low, w_cross_out).astype(bf16)
    grad_heads = grad_heads.reshape(2, tok_rows, heads, HEAD)
    grad_probs = jnp.einsum(
        "vqhd,vkhd->vhqk", grad_heads, value_cross, preferred_element_type=f32
    )
    delta = jnp.sum(cross_probs * grad_probs, -1, keepdims=True)
    grad_scores = (cross_probs * (grad_probs - delta)).astype(bf16)
    grad_query = (
        jnp.einsum("vhqk,vkhd->qhd", grad_scores, key_cross, preferred_element_type=f32) * scale
    )
    grad_query = grad_query.reshape(tok_rows, width).astype(bf16)
    grad_query_other = swapped(other_half(grad_query, 1))
    grad_key = (
        jnp.einsum("vhqk,qhd->vkhd", grad_scores, query_cross, preferred_element_type=f32) * scale
    )
    grad_value = jnp.einsum(
        "vhqk,vqhd->vkhd", cross_probs_low, grad_heads, preferred_element_type=f32
    )
    grad_pairs = jnp.concatenate(
        [
            grad_key.reshape(2 * patches, width),
            grad_value.reshape(2 * patches, width),
        ],
        -1,
    )
    grad_pairs_low = (grad_pairs + swapped(grad_pairs)).astype(bf16)
    own_pairs_low = own_half(grad_pairs_low.reshape(2, patches, 2 * width), 1)
    memory_grad = product_right(own_pairs_low.reshape(patches, 2 * width), w_cross_kv)
    memory_grad = memory_grad.reshape(2, 1, patches // 2, width)
    grad_norm_two, gain_two, bias_two = norm_backward(
        product_right(grad_query, w_cross_q), norm_two, inverse_two, norm_gains[1]
    )
    grad_one = grad_two[:tok_rows] + grad_two[tok_rows:] + grad_norm_two

    grad_self_low = grad_one.astype(bf16)
    grad_self_other = swapped(other_half(grad_self_low, 1))
    grad_self_heads = product_right(grad_self_low, w_self_out).astype(bf16)
    grad_self_heads = grad_self_heads.reshape(tok_rows, heads, HEAD)
    grad_probs_self = jnp.einsum(
        "qhd,khd->hqk", grad_self_heads, value_self, preferred_element_type=f32
    )
    delta_self = jnp.sum(self_probs * grad_probs_self, -1, keepdims=True)
    grad_scores_self = (self_probs * (grad_probs_self - delta_self)).astype(bf16)
    grad_query_self = (
        jnp.einsum("hqk,khd->qhd", grad_scores_self, key_self, preferred_element_type=f32) * scale
    )
    grad_query_self = grad_query_self.reshape(tok_rows, width).astype(bf16)
    grad_query_self_other = swapped(other_half(grad_query_self, 1))
    grad_key_self = (
        jnp.einsum("hqk,qhd->khd", grad_scores_self, query_self, preferred_element_type=f32)
        * scale
    )
    grad_value_self = jnp.einsum(
        "hqk,qhd->khd", self_probs_low, grad_self_heads, preferred_element_type=f32
    )
    grad_pairs_self = jnp.concatenate(
        [grad_key_self.reshape(page_len, width), grad_value_self.reshape(page_len, width)], -1
    )
    grad_pairs_self_low = (grad_pairs_self + swapped(grad_pairs_self)).astype(bf16)
    grad_joined_low = jnp.concatenate([grad_query_self, own_half(grad_pairs_self_low, 0)], -1)
    grad_norm_one, gain_one, bias_one = norm_backward(
        product_right(grad_joined_low, w_self_qkv), norm_one, inverse_one, norm_gains[0]
    )
    tokens_grad = (grad_one + grad_norm_one)[None]

    vectors = jnp.stack(
        [gain_one, gain_two, gain_three, gain_four, bias_one, bias_two, bias_three, bias_four]
    )
    normed_one_other = other_half(normed_page_low, 0)
    pairs_here = grad_pairs_self_low.reshape(page_len, 2, width)
    pairs_here = own_half(pairs_here, 2).reshape(page_len, width)
    memory_low = grad_pairs_low.reshape(2 * patches, 2, width)
    memory_low = own_half(memory_low, 2).reshape(2 * patches, width)
    second_bucket = outer_products(
        half,
        [
            (
                normed_one_low,
                normed_one_other,
                jnp.concatenate([own_half(grad_query_self, 1), own_half(pairs_here, 0)], -1),
                jnp.concatenate([grad_query_self_other, other_half(pairs_here, 0)], -1),
            ),
            (attn_self, attn_self_other, own_half(grad_self_low, 1), grad_self_other),
            (normed_two_low, normed_two_other, own_half(grad_query, 1), grad_query_other),
            (memory_rows[:patches], memory_rows[patches:], memory_low[:patches], memory_low[patches:]),
            (attn_cross, attn_cross_other, own_half(grad_branch_low, 1), grad_branch_other),
        ],
        norm_vectors(vectors),
    )
    second_sum = reduced(second_bucket)

    down_width = width // 2 * 4
    down = first_sum[:, :down_width].reshape(ROWS, 2, 2, width // 2)
    down = down.transpose(1, 2, 0, 3).reshape(2, -1)
    up_width = first_sum.shape[1] - down_width - TILE
    up = first_sum[:, down_width : down_width + up_width].reshape(2, -1)
    rest_width = second_sum.shape[1] - TILE
    rest = second_sum[:, :rest_width].reshape(2, -1)
    vector_sum = second_sum[0, rest_width : rest_width + 128]
    mine = jnp.concatenate([down, up, rest], 1)
    keep = lax.dynamic_index_in_dim(mine, half, 0, False)
    give = lax.dynamic_index_in_dim(mine, 1 - half, 0, False)
    come = swapped(jnp.concatenate([give, vector_sum]))
    vector_sum = vector_sum + come[-128:]
    vector_sum = own_half(vector_sum.reshape(8, ROWS), 1)
    come = come[:-128]
    left = jnp.where(half == 0, keep, come)
    right = jnp.where(half == 0, come, keep)

    def sides(at, rows, columns):
        size = rows * columns
        return left[at : at + size].reshape(rows, columns), right[at : at + size].reshape(
            rows, columns
        )

    weight_down = jnp.concatenate(sides(0, 2 * ROWS, width // 2), 1)
    at = down.shape[1]
    weight_up = jnp.concatenate(sides(at, ROWS // 2, up_width), 1)
    at += up.shape[1]
    rest_left, rest_right = sides(at, ROWS // 2, rest_width)

    def columns(start, size):
        return jnp.concatenate(
            [rest_left[:, start : start + size], rest_right[:, start : start + size]], 1
        )

    part = width // 2
    weight_self_qkv = jnp.concatenate([columns(k * part, part) for k in range(3)], 1)
    weight_self_out = columns(3 * part, part)
    weight_cross_q = columns(4 * part, part)
    weight_cross_kv = jnp.concatenate([columns((5 + k) * part, part) for k in range(2)], 1)
    weight_cross_out = columns(7 * part, part)
    return (
        loss,
        layer_out,
        tokens_grad,
        memory_grad,
        weight_self_qkv,
        weight_self_out,
        weight_cross_q,
        weight_cross_kv,
        weight_cross_out,
        weight_up,
        weight_down,
        vector_sum[:4],
        vector_sum[4:],
    )
def solution(mesh):
    in_specs = (
        P("dp", "mem", None),
        P(None, "dp", "mem", None),
        P(),
        P("dp", None),
        P("dp", "mem"),
        P(),
        P(),
        P(),
        P(),
        P(),
        P(),
        P(),
        P(),
        P(),
        P(None, ("dp", "mem")),
    )
    out_specs = (
        P("dp"),
        P(None, "dp", "mem", None),
        P("dp", "mem", None),
        P(None, "dp", "mem", None),
        P(("dp", "mem"), None),
        P(("dp", "mem"), None),
        P(("dp", "mem"), None),
        P(("dp", "mem"), None),
        P(("dp", "mem"), None),
        P(("dp", "mem"), None),
        P(("dp", "mem"), None),
        P(None, ("dp", "mem")),
        P(None, ("dp", "mem")),
    )
    return jax.shard_map(
        on_device, mesh=mesh, in_specs=in_specs, out_specs=out_specs, check_vma=False
    )
```

```python
from functools import partial

import jax
import jax.numpy as jnp
from jax import lax
from jax.experimental import pallas as pl
from jax.experimental.pallas import tpu as pltpu
from jax.sharding import PartitionSpec as P

HEAD = 64
PAIR = 2 * HEAD
SIDE = 4
CHIPS = SIDE * SIDE * SIDE
ROWS = 16
TILE = 256
FF_TILE = 512
BLOCK = 1280
CHUNK = 16
ENTRIES = 200
MIB = 1024 * 1024
epsilon = 1e-05
masked_score = -1e30
bf16 = jnp.bfloat16
f32 = jnp.float32


def dot(left, right):
    return jnp.dot(left, right, preferred_element_type=f32)


def dot_nt(left, right):
    return lax.dot_general(left, right, (((1,), (1,)), ((), ())), preferred_element_type=f32)


def dot_tn(left, right):
    return lax.dot_general(left, right, (((0,), (0,)), ((), ())), preferred_element_type=f32)


def normalized(values):
    centre = values - jnp.mean(values, -1, keepdims=True)
    inverse = lax.rsqrt(jnp.mean(centre * centre, -1, keepdims=True) + epsilon)
    return centre * inverse, inverse


def norm_back(upstream, normed, inverse, gain):
    scaled = upstream * gain
    back = inverse * (
        scaled
        - jnp.mean(scaled, -1, keepdims=True)
        - normed * jnp.mean(scaled * normed, -1, keepdims=True)
    )
    return back, jnp.sum(upstream * normed, 0, keepdims=True), jnp.sum(upstream, 0, keepdims=True)


def lower_lanes(shape):
    return lax.broadcasted_iota(jnp.int32, shape, 1) < HEAD


def parted(block):
    low = lower_lanes(block.shape)
    none = jnp.zeros_like(block)
    return jnp.concatenate([jnp.where(low, block, none), jnp.where(low, none, block)], 0)


def merged(block):
    rows = block.shape[0] // 2
    return jnp.where(lower_lanes((rows, PAIR)), block[:rows], block[rows:])


def self_softmax(queries, keys, allowed):
    scores = dot_nt(queries, keys) * HEAD ** (-0.5)
    scores = jnp.where(allowed, scores, masked_score)
    weights = jnp.exp(scores - jnp.max(scores, -1, keepdims=True))
    return weights * (1.0 / jnp.sum(weights, -1, keepdims=True))


def by_view(values, is_first, combine, neutral):
    first = combine(jnp.where(is_first, values, neutral), -1, keepdims=True)
    second = combine(jnp.where(is_first, neutral, values), -1, keepdims=True)
    return jnp.where(is_first, first, second)


def cross_softmax(queries, keys, kept, is_first):
    scores = dot_nt(queries, keys) * HEAD ** (-0.5)
    scores = jnp.where(kept, scores, masked_score)
    weights = jnp.exp(scores - by_view(scores, is_first, jnp.max, masked_score))
    return weights * (1.0 / by_view(weights, is_first, jnp.sum, 0.0))


def each_view(block, is_first):
    none = jnp.zeros_like(block)
    return jnp.concatenate([jnp.where(is_first, block, none), jnp.where(is_first, none, block)], 0)


def allowed_of(allowed_ref):
    allowed = allowed_ref[...] > 0.5
    return jnp.concatenate([allowed, allowed], 0)


def attention_kernel(
    tokens_ref, allowed_ref, memory_ref, keep_ref, w_qkv, w_out, w_q, w_kv, w_cross_out, gains,
    biases, a1_ref, q_ref, kv_ref, o_ref, h1_ref, a2_ref, qc_ref, kvc_ref, oc_ref, h2_ref, a3_ref,
):
    rows = q_ref.shape[0]
    width = tokens_ref.shape[1]
    values = tokens_ref[...].astype(f32)
    normed, _ = normalized(values)
    a1_ref[...] = (normed * gains[0:1] + biases[0:1]).astype(bf16)
    q_ref[...] = dot(a1_ref[:rows], w_qkv[:, :width]).astype(bf16)
    kv_ref[...] = dot(a1_ref[...], w_qkv[:, width:]).astype(bf16)
    allowed = allowed_of(allowed_ref)
    for at in range(0, width, PAIR):
        queries = parted(q_ref[:, at : at + PAIR])
        probs = self_softmax(queries, kv_ref[:, at : at + PAIR], allowed)
        mixed = dot(probs.astype(bf16), kv_ref[:, width + at : width + at + PAIR])
        o_ref[:, at : at + PAIR] = merged(mixed).astype(bf16)
    h1 = values[:rows] + dot(o_ref[...], w_out[...])
    h1_ref[...] = h1
    normed, _ = normalized(h1)
    a2_ref[...] = (normed * gains[1:2] + biases[1:2]).astype(bf16)
    qc_ref[...] = dot(a2_ref[...], w_q[...]).astype(bf16)
    kvc_ref[...] = dot(memory_ref[...], w_kv[...]).astype(bf16)
    shape = (2 * rows, memory_ref.shape[0])
    kept = jnp.broadcast_to(keep_ref[...], shape) > 0.5
    is_first = lax.broadcasted_iota(jnp.int32, shape, 1) < shape[1] // 2
    for at in range(0, width, PAIR):
        queries = parted(qc_ref[:, at : at + PAIR])
        probs = cross_softmax(queries, kvc_ref[:, at : at + PAIR], kept, is_first)
        mixed = dot(
            each_view(probs.astype(bf16), is_first), kvc_ref[:, width + at : width + at + PAIR]
        )
        oc_ref[:rows, at : at + PAIR] = merged(mixed[: 2 * rows]).astype(bf16)
        oc_ref[rows:, at : at + PAIR] = merged(mixed[2 * rows :]).astype(bf16)
    h2 = jnp.concatenate([h1, h1], 0) + dot(oc_ref[...], w_cross_out[...])
    h2_ref[...] = h2
    normed, _ = normalized(h2)
    a3_ref[...] = (normed * gains[2:3] + biases[2:3]).astype(bf16)


def attention(tokens_page, allowed, memory_rows, keep, weights, gains, biases):
    rows, width = allowed.shape[0], tokens_page.shape[1]
    shape = jax.ShapeDtypeStruct
    return pl.pallas_call(
        attention_kernel,
        out_shape=(
            shape((2 * rows, width), bf16),
            shape((rows, width), bf16),
            shape((2 * rows, 2 * width), bf16),
            shape((rows, width), bf16),
            shape((rows, width), f32),
            shape((rows, width), bf16),
            shape((rows, width), bf16),
            shape((memory_rows.shape[0], 2 * width), bf16),
            shape((2 * rows, width), bf16),
            shape((2 * rows, width), f32),
            shape((2 * rows, width), bf16),
        ),
        compiler_params=pltpu.CompilerParams(vmem_limit_bytes=56 * MIB),
        cost_estimate=pl.CostEstimate(
            flops=20 * 10**9 // 10, bytes_accessed=24 * MIB, transcendentals=10**6
        ),
    )(tokens_page, allowed, memory_rows, keep, *weights, gains, biases)


def erf_parts(values):
    return 0.5 + 0.5 * lax.erf(values * (0.5**0.5))


def feed_forward_kernel(
    h2_ref, a3_ref, w_up, w_down, gains, biases, up_ref, act_ref, h3_ref, out_ref, fin_ref, total
):
    step = pl.program_id(0)

    @pl.when(step == 0)
    def _():
        total[...] = jnp.zeros_like(total)

    up = dot(a3_ref[...], w_up[...])
    up_ref[...] = up
    act = (up * erf_parts(up)).astype(bf16)
    act_ref[...] = act
    total[...] += dot(act, w_down[...])

    @pl.when(step == pl.num_programs(0) - 1)
    def _():
        h3 = h2_ref[...] + total[...]
        h3_ref[...] = h3
        out_ref[...] = h3.astype(bf16)
        normed, _ = normalized(h3)
        fin_ref[...] = (normed * gains[3:4] + biases[3:4]).astype(bf16)


def whole(*shape):
    return pl.BlockSpec(shape, lambda i: (0,) * len(shape))


def feed_forward(h2, a3, w_up, w_down, gains, biases):
    rows, width = h2.shape
    hidden = w_up.shape[1]
    shape = jax.ShapeDtypeStruct
    return pl.pallas_call(
        feed_forward_kernel,
        grid=(hidden // FF_TILE,),
        in_specs=[
            whole(rows, width),
            whole(rows, width),
            pl.BlockSpec((width, FF_TILE), lambda i: (0, i)),
            pl.BlockSpec((FF_TILE, width), lambda i: (i, 0)),
            whole(4, width),
            whole(4, width),
        ],
        out_specs=(
            pl.BlockSpec((rows, FF_TILE), lambda i: (0, i)),
            pl.BlockSpec((rows, FF_TILE), lambda i: (0, i)),
            whole(rows, width),
            whole(rows, width),
            whole(rows, width),
        ),
        out_shape=(
            shape((rows, hidden), f32),
            shape((rows, hidden), bf16),
            shape((rows, width), f32),
            shape((rows, width), bf16),
            shape((rows, width), bf16),
        ),
        scratch_shapes=[pltpu.VMEM((rows, width), f32)],
        compiler_params=pltpu.CompilerParams(vmem_limit_bytes=56 * MIB),
        cost_estimate=pl.CostEstimate(
            flops=4 * rows * width * hidden, bytes_accessed=24 * MIB, transcendentals=rows * hidden
        ),
    )(h2, a3, w_up, w_down, gains, biases)


def halves(block):
    middle = block.shape[1] // 2
    return block[:, :middle], block[:, middle:]


def feed_forward_back_kernel(
    core_ref, own_ref, other_ref, h3_ref, h2_ref, up_ref, w_up, w_down, gains, gh3_half_ref,
    gup_ref, gh2_ref, gh2_half_ref, vector_ref, gh3, gh3_low_ref, total,
):
    step = pl.program_id(0)
    core = core_ref[0]

    @pl.when(step == 0)
    def _():
        upstream = own_ref[...] + other_ref[...].astype(f32)
        normed, inverse = normalized(h3_ref[...])
        back, gain, bias = norm_back(upstream, normed, inverse, gains[3:4])
        gh3[...] = back
        gh3_low_ref[...] = back.astype(bf16)
        for side, part in enumerate(halves(gh3_low_ref[...])):
            gh3_half_ref[side ^ core] = part
        vector_ref[...] = jnp.zeros_like(vector_ref)
        vector_ref[3:4] = gain
        vector_ref[7:8] = bias
        total[...] = jnp.zeros_like(total)

    grad = dot_nt(gh3_low_ref[...], w_down[...])
    up = up_ref[...]
    slope = erf_parts(up) + up * jnp.exp(-0.5 * up * up) * (0.5 / jnp.pi) ** 0.5
    gup = (grad * slope).astype(bf16)
    gup_ref[0] = gup
    total[...] += dot_nt(gup, w_up[...])

    @pl.when(step == pl.num_programs(0) - 1)
    def _():
        normed, inverse = normalized(h2_ref[...])
        back, gain, bias = norm_back(total[...], normed, inverse, gains[2:3])
        gh2 = gh3[...] + back
        gh2_ref[...] = gh2
        for side, part in enumerate(halves(gh2.astype(bf16))):
            gh2_half_ref[side ^ core] = part
        vector_ref[2:3] = gain
        vector_ref[6:7] = bias


def feed_forward_back(core, own, other, h3, h2, up, w_up, w_down, gains):
    rows, width = h2.shape
    hidden = w_up.shape[1]
    tiles = hidden // FF_TILE
    shape = jax.ShapeDtypeStruct

    def all_of(*dims):
        return pl.BlockSpec(dims, lambda i, core: (0,) * len(dims))

    def half_tile(i, core):
        return ((i // (tiles // 2)) ^ core[0], 0, i % (tiles // 2))

    return pl.pallas_call(
        feed_forward_back_kernel,
        grid_spec=pltpu.PrefetchScalarGridSpec(
            num_scalar_prefetch=1,
            grid=(tiles,),
            in_specs=[
                all_of(rows, width),
                all_of(rows, width),
                all_of(rows, width),
                all_of(rows, width),
                pl.BlockSpec((rows, FF_TILE), lambda i, core: (0, i)),
                pl.BlockSpec((width, FF_TILE), lambda i, core: (0, i)),
                pl.BlockSpec((FF_TILE, width), lambda i, core: (i, 0)),
                all_of(4, width),
            ],
            out_specs=(
                all_of(2, rows, width // 2),
                pl.BlockSpec((1, rows, FF_TILE), half_tile),
                all_of(rows, width),
                all_of(2, rows, width // 2),
                all_of(8, width),
            ),
            scratch_shapes=[
                pltpu.VMEM((rows, width), f32),
                pltpu.VMEM((rows, width), bf16),
                pltpu.VMEM((rows, width), f32),
            ],
        ),
        out_shape=(
            shape((2, rows, width // 2), bf16),
            shape((2, rows, hidden // 2), bf16),
            shape((rows, width), f32),
            shape((2, rows, width // 2), bf16),
            shape((8, width), f32),
        ),
        compiler_params=pltpu.CompilerParams(vmem_limit_bytes=56 * MIB),
        cost_estimate=pl.CostEstimate(
            flops=4 * rows * width * hidden,
            bytes_accessed=24 * MIB,
            transcendentals=2 * rows * hidden,
        ),
    )(core, own, other, h3, h2, up, w_up, w_down, gains)


def attention_back_kernel(
    core_ref, gh2_ref, allowed_ref, keep_ref, kvc_ref, qc_ref, h1_ref, kv_ref, q_ref, w_cross_out, w_q,
    w_out, gains, gqc_ref, gkvc_ref, gh1_ref, gh1_half_ref, gq_ref, gkv_ref, vector_ref, goc, go, gqc,
    gh1_low,
):
    rows, width = q_ref.shape
    half = width // 2
    core = core_ref[0]
    scale = HEAD ** (-0.5)
    goc[...] = dot_nt(gh2_ref[...].astype(bf16), w_cross_out[...]).astype(bf16)
    shape = (2 * rows, kvc_ref.shape[0])
    kept = jnp.broadcast_to(keep_ref[...], shape) > 0.5
    is_first = lax.broadcasted_iota(jnp.int32, shape, 1) < shape[1] // 2
    for at in range(0, width, PAIR):
        here, there = slice(at, at + PAIR), slice(width + at, width + at + PAIR)
        slot = (at // half) ^ core
        low, high = slice(at % half, at % half + PAIR), slice(half + at % half, half + at % half + PAIR)
        queries = parted(qc_ref[:, here])
        probs = cross_softmax(queries, kvc_ref[:, here], kept, is_first)
        upstream = jnp.concatenate([parted(goc[:rows, here]), parted(goc[rows:, here])], 0)
        grad = dot_nt(upstream, kvc_ref[:, there])
        grad = jnp.where(is_first, grad[: 2 * rows], grad[2 * rows :])
        slope = probs * (grad - by_view(probs * grad, is_first, jnp.sum, 0.0))
        slope = slope.astype(bf16)
        change = (merged(dot(slope, kvc_ref[:, here])) * scale).astype(bf16)
        gqc[:, here] = change
        gqc_ref[slot, :, low] = change
        gkvc_ref[slot, :, low] = (dot_tn(slope, queries) * scale).astype(bf16)
        change = dot_tn(each_view(probs.astype(bf16), is_first), upstream)
        gkvc_ref[slot, :, high] = change.astype(bf16)
    normed, inverse = normalized(h1_ref[...])
    back, gain, bias = norm_back(dot_nt(gqc[...], w_q[...]), normed, inverse, gains[1:2])
    vector_ref[...] = jnp.zeros_like(vector_ref)
    vector_ref[1:2] = gain
    vector_ref[5:6] = bias
    gh1 = gh2_ref[:rows] + gh2_ref[rows:] + back
    gh1_ref[...] = gh1
    gh1_low[...] = gh1.astype(bf16)
    for side, part in enumerate(halves(gh1_low[...])):
        gh1_half_ref[side ^ core] = part
    go[...] = dot_nt(gh1_low[...], w_out[...]).astype(bf16)
    allowed = allowed_of(allowed_ref)
    for at in range(0, width, PAIR):
        here, there = slice(at, at + PAIR), slice(width + at, width + at + PAIR)
        slot = (at // half) ^ core
        low, high = slice(at % half, at % half + PAIR), slice(half + at % half, half + at % half + PAIR)
        queries = parted(q_ref[:, here])
        probs = self_softmax(queries, kv_ref[:, here], allowed)
        upstream = parted(go[:, here])
        grad = dot_nt(upstream, kv_ref[:, there])
        slope = probs * (grad - jnp.sum(probs * grad, -1, keepdims=True))
        slope = slope.astype(bf16)
        gq_ref[slot, :, low] = (merged(dot(slope, kv_ref[:, here])) * scale).astype(bf16)
        gkv_ref[slot, :, low] = (dot_tn(slope, queries) * scale).astype(bf16)
        gkv_ref[slot, :, high] = dot_tn(probs.astype(bf16), upstream).astype(bf16)


def scalar_first(count):
    return [pl.BlockSpec(memory_space=pltpu.SMEM)] + [
        pl.BlockSpec(memory_space=pltpu.VMEM) for _ in range(count)
    ]


def attention_back(core, *operands):
    rows, width = operands[7].shape
    shape = jax.ShapeDtypeStruct
    return pl.pallas_call(
        attention_back_kernel,
        in_specs=scalar_first(len(operands)),
        out_shape=(
            shape((2, rows, width // 2), bf16),
            shape((2, rows, width), bf16),
            shape((rows, width), f32),
            shape((2, rows, width // 2), bf16),
            shape((2, rows, width // 2), bf16),
            shape((2, 2 * rows, width), bf16),
            shape((8, width), f32),
        ),
        scratch_shapes=[
            pltpu.VMEM((2 * rows, width), bf16),
            pltpu.VMEM((rows, width), bf16),
            pltpu.VMEM((rows, width), bf16),
            pltpu.VMEM((rows, width), bf16),
        ],
        compiler_params=pltpu.CompilerParams(vmem_limit_bytes=56 * MIB),
        cost_estimate=pl.CostEstimate(
            flops=2 * 10**9, bytes_accessed=12 * MIB, transcendentals=10**6
        ),
    )(core, *operands)


def inputs_back_kernel(
    core_ref, tokens_ref, gh1_ref, gq_ref, gkv_ref, come_ref, gkvc_ref, come_cross_ref, w_qkv, w_kv,
    gains, tokens_grad_ref, memory_grad_ref, vector_ref, grads,
):
    core = core_ref[0]
    rows, width = gh1_ref.shape
    half = width // 2
    total = jnp.zeros((rows, width), f32)
    for side in range(2):
        slot, away = side ^ core, 1 - (side ^ core)
        pairs = gkv_ref[slot, :rows].astype(f32) + come_ref[away, rows:].astype(f32)
        pairs = pairs.astype(bf16)
        at = side * half
        total += dot_nt(gq_ref[slot], w_qkv[:, at : at + half])
        total += dot_nt(pairs[:, :half], w_qkv[:, width + at : width + at + half])
        total += dot_nt(pairs[:, half:], w_qkv[:, 2 * width + at : 2 * width + at + half])
    normed, inverse = normalized(tokens_ref[...].astype(f32))
    back, gain, bias = norm_back(total, normed, inverse, gains[0:1])
    tokens_grad_ref[...] = gh1_ref[...] + back
    vector_ref[...] = jnp.zeros_like(vector_ref)
    vector_ref[0:1] = gain
    vector_ref[4:5] = bias
    patches = gkvc_ref.shape[1]
    total = jnp.zeros((patches, width), f32)
    for side in range(2):
        slot, away = side ^ core, 1 - (side ^ core)
        pairs = gkvc_ref[slot].astype(f32) + come_cross_ref[away].astype(f32)
        pairs = pairs.astype(bf16)
        at = side * half
        total += dot_nt(pairs[:, :half], w_kv[:, at : at + half])
        total += dot_nt(pairs[:, half:], w_kv[:, width + at : width + at + half])
    grads[...] = total
    own = memory_grad_ref.shape[1]
    for view in range(2):
        start = pl.multiple_of(view * 2 * own + core * own, 8)
        memory_grad_ref[view] = grads[pl.ds(start, own)]


def inputs_back(core, *operands):
    rows, width = operands[1].shape
    patches = operands[5].shape[1]
    shape = jax.ShapeDtypeStruct
    return pl.pallas_call(
        inputs_back_kernel,
        in_specs=scalar_first(len(operands)),
        out_shape=(
            shape((rows, width), f32),
            shape((2, patches // 4, width), f32),
            shape((8, width), f32),
        ),
        scratch_shapes=[pltpu.VMEM((patches, width), f32)],
        compiler_params=pltpu.CompilerParams(vmem_limit_bytes=56 * MIB),
        cost_estimate=pl.CostEstimate(flops=10**9, bytes_accessed=14 * MIB, transcendentals=0),
    )(core, *operands)


def logits_kernel(rows_ref, readout_ref, bias_ref, logits_ref, stats_ref, kept):
    step = pl.program_id(0)
    tokens = rows_ref.shape[1]
    block = readout_ref.shape[0]

    @pl.when(step == 0)
    def _():
        for k in range(5):
            kept[k] = jnp.full(kept.shape[1:], masked_score if k in (0, 3) else 0.0, f32)

    rows = rows_ref[...].reshape(2 * tokens, rows_ref.shape[2])
    values = lax.dot_general(
        rows, readout_ref[...], (((1,), (1,)), ((), ())), preferred_element_type=f32
    )
    logits_ref[...] = (values + bias_ref[...]).reshape(2, tokens, block)

    def chunk(i, carry):
        at = pl.ds(pl.multiple_of(i * CHUNK, CHUNK), CHUNK)
        first = [logits_ref[0, at, c : c + 128] for c in range(0, block, 128)]
        second = [logits_ref[1, at, c : c + 128] for c in range(0, block, 128)]
        top_first, top_second = kept[0, at], kept[3, at]
        new_first, new_second = top_first, top_second
        for a, b in zip(first, second):
            new_first = jnp.maximum(new_first, a)
            new_second = jnp.maximum(new_second, b)
        fade_first = jnp.exp(top_first - new_first)
        fade_second = jnp.exp(top_second - new_second)
        total_first = kept[1, at] * fade_first
        total_apart = kept[2, at] * fade_first
        total_second = kept[4, at] * fade_second
        for a, b in zip(first, second):
            weight = jnp.exp(a - new_first)
            total_first += weight
            total_apart += weight * (a - b)
            total_second += jnp.exp(b - new_second)
        kept[0, at], kept[1, at], kept[2, at] = new_first, total_first, total_apart
        kept[3, at], kept[4, at] = new_second, total_second
        return carry

    lax.fori_loop(0, tokens // CHUNK, chunk, 0)

    @pl.when(step == pl.num_programs(0) - 1)
    def _():
        top_first = jnp.max(kept[0], -1, keepdims=True)
        top_second = jnp.max(kept[3], -1, keepdims=True)
        fade_first = jnp.exp(kept[0] - top_first)
        fade_second = jnp.exp(kept[3] - top_second)
        stats = (
            top_first,
            jnp.sum(kept[1] * fade_first, -1, keepdims=True),
            jnp.sum(kept[2] * fade_first, -1, keepdims=True),
            top_second,
            jnp.sum(kept[4] * fade_second, -1, keepdims=True),
        )
        lane = lax.broadcasted_iota(jnp.int32, stats_ref.shape, 1)
        result = jnp.zeros(stats_ref.shape, f32)
        for k, stat in enumerate(stats):
            result = jnp.where(lane == k, stat, result)
        stats_ref[...] = result


def logits_and_stats(rows, readout_rows, bias):
    views, tokens, width = rows.shape
    entries = readout_rows.shape[0]
    return pl.pallas_call(
        logits_kernel,
        out_shape=(
            jax.ShapeDtypeStruct((2, tokens, entries), f32),
            jax.ShapeDtypeStruct((tokens, 128), f32),
        ),
        grid=(entries // BLOCK,),
        in_specs=[
            pl.BlockSpec((2, tokens, width), lambda i: (0, 0, 0)),
            pl.BlockSpec((BLOCK, width), lambda i: (i, 0)),
            pl.BlockSpec((1, BLOCK), lambda i: (0, i)),
        ],
        out_specs=(
            pl.BlockSpec((2, tokens, BLOCK), lambda i: (0, 0, i)),
            pl.BlockSpec((tokens, 128), lambda i: (0, 0)),
        ),
        scratch_shapes=[pltpu.VMEM((5, tokens, 128), f32)],
        compiler_params=pltpu.CompilerParams(vmem_limit_bytes=58 * 1024 * 1024),
        cost_estimate=pl.CostEstimate(
            flops=4 * tokens * entries * width,
            bytes_accessed=2 * entries * width + 8 * tokens * entries,
            transcendentals=2 * tokens * entries,
        ),
    )(rows, readout_rows, bias)


def readout_back_kernel(
    stats_a, stats_b, weight_ref, logits_ref, readout_ref, grad_ref, part_ref, kept, slopes
):
    step = pl.program_id(0)
    tokens = logits_ref.shape[1]
    block = readout_ref.shape[0]

    @pl.when(step == 0)
    def _():
        a, b = stats_a[...], stats_b[...]
        weight = weight_ref[...]
        top_first = jnp.maximum(a[:, 0:1], b[:, 0:1])
        fade_a, fade_b = jnp.exp(a[:, 0:1] - top_first), jnp.exp(b[:, 0:1] - top_first)
        total_first = a[:, 1:2] * fade_a + b[:, 1:2] * fade_b
        total_apart = a[:, 2:3] * fade_a + b[:, 2:3] * fade_b
        top_second = jnp.maximum(a[:, 3:4], b[:, 3:4])
        total_second = a[:, 4:5] * jnp.exp(a[:, 3:4] - top_second) + b[:, 4:5] * jnp.exp(
            b[:, 3:4] - top_second
        )
        first_lse = top_first + jnp.log(total_first)
        second_lse = top_second + jnp.log(total_second)
        apart = total_apart / total_first
        shape = (tokens, 128)
        kept[0] = jnp.broadcast_to(first_lse, shape)
        kept[1] = jnp.broadcast_to(second_lse, shape)
        kept[2] = jnp.broadcast_to(apart, shape)
        kept[3] = weight
        part_ref[...] = weight * (apart - first_lse + second_lse)
        grad_ref[...] = jnp.zeros_like(grad_ref)

    def chunk(i, carry):
        at = pl.ds(pl.multiple_of(i * CHUNK, CHUNK), CHUNK)
        first_lse, second_lse, apart, weight = (kept[k, at] for k in range(4))
        for c in range(0, block, 128):
            first = logits_ref[0, at, c : c + 128]
            second = logits_ref[1, at, c : c + 128]
            first_prob = jnp.exp(first - first_lse) * weight
            second_prob = jnp.exp(second - second_lse) * weight
            slopes[0, at, c : c + 128] = (first_prob * (first - second - apart)).astype(bf16)
            slopes[1, at, c : c + 128] = (second_prob - first_prob).astype(bf16)
        return carry

    lax.fori_loop(0, tokens // CHUNK, chunk, 0)
    result = jnp.dot(
        slopes[...].reshape(2 * tokens, block), readout_ref[...], preferred_element_type=f32
    )
    grad_ref[...] += result.reshape(grad_ref.shape)


def readout_back(stats_a, stats_b, weight, logits, readout_rows):
    views, tokens, entries = logits.shape
    width = readout_rows.shape[1]
    whole = lambda *shape: pl.BlockSpec(shape, lambda i: (0,) * len(shape))
    return pl.pallas_call(
        readout_back_kernel,
        out_shape=(
            jax.ShapeDtypeStruct((2, tokens, width), f32),
            jax.ShapeDtypeStruct((tokens, 128), f32),
        ),
        grid=(entries // BLOCK,),
        in_specs=[
            whole(tokens, 128),
            whole(tokens, 128),
            whole(tokens, 128),
            pl.BlockSpec((2, tokens, BLOCK), lambda i: (0, 0, i)),
            pl.BlockSpec((BLOCK, width), lambda i: (i, 0)),
        ],
        out_specs=(whole(2, tokens, width), whole(tokens, 128)),
        scratch_shapes=[
            pltpu.VMEM((4, tokens, 128), f32),
            pltpu.VMEM((2, tokens, BLOCK), bf16),
        ],
        compiler_params=pltpu.CompilerParams(vmem_limit_bytes=58 * 1024 * 1024),
        cost_estimate=pl.CostEstimate(
            flops=4 * tokens * entries * width,
            bytes_accessed=2 * entries * width + 8 * tokens * entries,
            transcendentals=2 * tokens * entries,
        ),
    )(stats_a, stats_b, weight, logits, readout_rows)


def swapped(block):
    return lax.ppermute(block, "mem", [(0, 1), (1, 0)])


def lines(stride, core):
    starts = [d for d in range(CHIPS) if (d // stride) % SIDE == 0]
    return [[2 * (start + stride * k) + core for k in range(SIDE)] for start in starts]


def groups_of(strides):
    return lines(strides[0], 0) + lines(strides[1], 1)


def summed(bucket, strides):
    parts = bucket.reshape(SIDE, -1, bucket.shape[-1])
    parts = lax.all_to_all(
        parts, ("dp", "mem"), 0, 0, axis_index_groups=groups_of(strides), tiled=True
    )
    return parts.astype(f32).sum(0)


def reduced(bucket):
    flat = bucket.reshape(CHIPS * ROWS, bucket.shape[-1])
    flat = lax.psum_scatter(
        flat, ("dp", "mem"), axis_index_groups=groups_of((1, 4)), scatter_dimension=0, tiled=True
    )
    flat = summed(flat, (4, 16)).astype(bf16)
    return summed(flat, (16, 1))


def outer_kernel(shapes, core_ref, *refs):
    n_in = 4 * len(shapes)
    inputs, out_ref, turned = refs[:n_in], refs[n_in], refs[n_in + 1 :]
    step = pl.program_id(0)
    core = core_ref[0]

    def place(chip):
        z, y, x = chip // 16, (chip // 4) % 4, chip % 4
        return jnp.where(core == 0, x * 16 + y * 4 + z, y * 16 + z * 4 + x)

    first = 0
    for i, (groups, columns, shared) in enumerate(shapes):
        left_a, left_b, right_a, right_b = inputs[4 * i : 4 * i + 4]
        tiles = columns // TILE
        low, high = first, first + groups * tiles
        first = high

        @pl.when(step == low)
        def _(left_a=left_a, left_b=left_b, to=turned[i], groups=groups):
            wide = left_a.shape[1]
            for start in range(0, wide, 1024):
                both = jnp.concatenate(
                    [left_a[:, start : start + 1024], left_b[:, start : start + 1024]], 0
                )
                flat = both.T
                if groups == 1:
                    to[0, start : start + 1024] = flat
                else:
                    per = ROWS * groups
                    for c in range(1024 // per):
                        chip = start // per + c
                        for g in range(groups):
                            at = c * per + g * ROWS
                            to[g, chip * ROWS : (chip + 1) * ROWS] = flat[at : at + ROWS]

        @pl.when((step >= low) & (step < high))
        def _(right_a=right_a, right_b=right_b, to=turned[i], tiles=tiles, low=low, shared=shared):
            at = step - low
            group = at // tiles
            tile = at - group * tiles
            column = pl.ds(pl.multiple_of(tile * TILE, TILE), TILE)
            if shared == 0:
                both = jnp.concatenate([right_a[0, :, column], right_b[:, column]], 0)
            else:
                here, there = right_a[0, :, column], right_b[1, :, column]
                if shared == 2:
                    middle = there.shape[0] // 2
                    there = jnp.concatenate([there[middle:], there[:middle]], 0)
                both = (here.astype(f32) + there.astype(f32)).astype(bf16)
            result = dot(to[group], both).astype(bf16)
            for chip in range(CHIPS):
                out_ref[place(chip)] = result[chip * ROWS : (chip + 1) * ROWS]


def outer_products(core, items):
    shapes, operands, scratch = [], [], []
    total = flops = 0
    for left, left_other, right, right_other, shared in items:
        groups = left.shape[1] // (ROWS * CHIPS)
        columns = right.shape[2]
        shapes.append((groups, columns, shared))
        operands += [left, left_other, right, right_other]
        depth = left.shape[0] + left_other.shape[0]
        scratch.append(pltpu.VMEM((groups, ROWS * CHIPS, depth), bf16))
        total += groups * columns
        flops += 2 * left.shape[1] * columns * depth
    return pl.pallas_call(
        partial(outer_kernel, tuple(shapes)),
        out_shape=jax.ShapeDtypeStruct((CHIPS, ROWS, total), bf16),
        grid_spec=pltpu.PrefetchScalarGridSpec(
            num_scalar_prefetch=1,
            grid=(total // TILE,),
            in_specs=[pl.BlockSpec(memory_space=pltpu.VMEM) for _ in operands],
            out_specs=pl.BlockSpec((CHIPS, ROWS, TILE), lambda i, core: (0, 0, i)),
            scratch_shapes=scratch,
        ),
        compiler_params=pltpu.CompilerParams(vmem_limit_bytes=56 * MIB),
        cost_estimate=pl.CostEstimate(
            flops=flops, bytes_accessed=CHIPS * ROWS * total * 2, transcendentals=0
        ),
    )(core, *operands)


def divide_kernel(grouped, core_ref, sums_ref, keep_ref, give_ref):
    core = core_ref[0]
    half = grouped // 2
    columns = sums_ref.shape[1]
    for ref, side in ((keep_ref, core), (give_ref, 1 - core)):
        if grouped:
            start = pl.ds(pl.multiple_of(side * half, 128), half)
            block = sums_ref[:, start]
            ref[:, :half] = block[: ROWS // 2]
            ref[:, half:grouped] = block[ROWS // 2 :]
        rows = pl.ds(pl.multiple_of(side * (ROWS // 2), 8), ROWS // 2)
        if columns > grouped:
            ref[:, grouped:] = sums_ref[rows, grouped:]


def divided(core, sums, grouped):
    shape = jax.ShapeDtypeStruct((ROWS // 2, sums.shape[1]), f32)
    return pl.pallas_call(
        partial(divide_kernel, grouped),
        in_specs=scalar_first(1),
        out_shape=(shape, shape),
    )(core, sums)


def assemble_kernel(layout, core_ref, keep_ref, come_ref, *outs):
    core = core_ref[0]
    for ref, side in ((keep_ref, core), (come_ref, 1 - core)):
        at = 0
        for out, (grouped, columns, span) in zip(outs, layout):
            part = span // 2
            if grouped:
                for g in range(2):
                    for h in range(2):
                        rows = slice(g * ROWS + h * ROWS // 2, g * ROWS + (h + 1) * ROWS // 2)
                        start = at + h * 2 * part + g * part
                        column = pl.ds(pl.multiple_of(side * part, 128), part)
                        out[rows, column] = ref[:, start : start + part]
                at += 4 * part
                continue
            for k in range(0, columns, span):
                column = pl.ds(pl.multiple_of(k + side * part, 128), part)
                out[:, column] = ref[:, at : at + part]
                at += part


def assembled(core, keep, come, layout):
    return pl.pallas_call(
        partial(assemble_kernel, tuple(layout)),
        in_specs=scalar_first(2),
        out_shape=tuple(
            jax.ShapeDtypeStruct((2 * ROWS if grouped else ROWS // 2, columns), f32)
            for grouped, columns, span in layout
        ),
    )(core, keep, come)


def on_device(
    tokens,
    memory,
    lengths,
    segments,
    key_mask,
    w_self_qkv,
    w_self_out,
    w_cross_q,
    w_cross_kv,
    w_cross_out,
    w_up,
    w_down,
    norm_gains,
    norm_biases,
    readout,
):
    tok_rows = tokens.shape[1]
    width = tokens.shape[2]
    half = lax.axis_index("mem")
    core = half.astype(jnp.int32).reshape(1)
    page_index = lax.axis_index("dp")
    patches = 2 * memory.shape[2]

    vocab_dev = readout.shape[1]
    readout_turned = jnp.pad(readout.T, ((0, ENTRIES - vocab_dev), (0, 0)))
    readout_half = lax.all_gather(readout_turned, "dp", axis=0, tiled=True)
    is_entry = jnp.arange(readout_half.shape[0]) % ENTRIES < vocab_dev
    entry_bias = jnp.where(is_entry, 0.0, masked_score).astype(f32)[None]

    tokens_own = tokens[0]
    tokens_page = jnp.concatenate([tokens_own, swapped(tokens_own)], 0)
    memory_own = memory[:, 0]
    memory_come = swapped(memory_own)
    memory_rows = jnp.where(
        half == 0,
        jnp.concatenate([memory_own, memory_come], 1),
        jnp.concatenate([memory_come, memory_own], 1),
    ).reshape(2 * patches, width)
    mask_own = key_mask[0].astype(f32)
    mask_come = swapped(mask_own)
    mask_page = jnp.where(
        half == 0,
        jnp.concatenate([mask_own, mask_come]),
        jnp.concatenate([mask_come, mask_own]),
    )
    keep = jnp.tile(jnp.repeat(mask_page, 2), 2)[None]
    own_positions = jnp.arange(tok_rows) + half * tok_rows
    other_positions = jnp.arange(tok_rows) + (1 - half) * tok_rows
    key_positions = jnp.concatenate([own_positions, other_positions])
    cut = segments[0].reshape(2, tok_rows)
    own_segments = lax.dynamic_index_in_dim(cut, half, 0, False)
    other_segments = lax.dynamic_index_in_dim(cut, 1 - half, 0, False)
    key_segments = jnp.concatenate([own_segments, other_segments])
    allowed = (key_positions[None, :] <= own_positions[:, None]) & (
        key_segments[None, :] == own_segments[:, None]
    )
    allowed = allowed.astype(f32)
    count = jnp.sum(lengths).astype(f32)
    valid = key_positions < lengths[page_index]
    row_weight = jnp.broadcast_to((valid.astype(f32) / count)[:, None], (2 * tok_rows, 128))

    weights = (w_self_qkv, w_self_out, w_cross_q, w_cross_kv, w_cross_out)
    a1, q, kv, o_self, h1, a2, qc, kvc, oc, h2, a3 = attention(
        tokens_page, allowed, memory_rows, keep, weights, norm_gains, norm_biases
    )
    up, act, h3, layer_out, final = feed_forward(h2, a3, w_up, w_down, norm_gains, norm_biases)
    final = final.reshape(2, tok_rows, width)
    final_page = jnp.concatenate([final, swapped(final)], 1)
    o_self_other, a2_other, oc_other, a3_other, act_other = map(
        swapped, (o_self, a2, oc, a3, act)
    )

    logits, stats = logits_and_stats(final_page, readout_half, entry_bias)
    stats_come = swapped(stats)
    stats_come = jnp.concatenate([stats_come[tok_rows:], stats_come[:tok_rows]], 0)
    grad_page, terms = readout_back(stats, stats_come, row_weight, logits, readout_half)
    terms = terms[:, 0].reshape(2, tok_rows).sum(1)
    loss = (terms[0] + terms[1]).reshape(1)
    grad_own = grad_page[:, :tok_rows].reshape(2 * tok_rows, width)
    grad_come = swapped(grad_page[:, tok_rows:]).reshape(2 * tok_rows, width)

    gh3_half, gup_half, gh2, gh2_half, vectors_ff = feed_forward_back(
        core, grad_own, grad_come, h3, h2, up, w_up, w_down, norm_gains
    )
    first_bucket = outer_products(
        core,
        [
            (act, act_other, gh3_half, swapped(gh3_half[1]), 0),
            (a3, a3_other, gup_half, swapped(gup_half[1]), 0),
        ],
    )
    gh2, first_bucket = lax.optimization_barrier((gh2, first_bucket))
    first_sums = reduced(first_bucket)

    gqc_half, gkvc_half, gh1, gh1_half, gq_half, gkv_half, vectors_att = attention_back(
        core, gh2, allowed, keep, kvc, qc, h1, kv, q, w_cross_out, w_cross_q, w_self_out, norm_gains
    )
    gkv_come, gkvc_come = swapped(gkv_half), swapped(gkvc_half)
    middle = tok_rows
    second_bucket = outer_products(
        core,
        [
            (a1[:middle], a1[middle:], gq_half, swapped(gq_half[1]), 0),
            (a1[:middle], a1[middle:], gkv_half, gkv_come, 2),
            (o_self, o_self_other, gh1_half, swapped(gh1_half[1]), 0),
            (a2, a2_other, gqc_half, swapped(gqc_half[1]), 0),
            (memory_rows[:patches], memory_rows[patches:], gkvc_half, gkvc_come, 1),
            (oc, oc_other, gh2_half, swapped(gh2_half[1]), 0),
        ],
    )
    second_sums = reduced(second_bucket)
    tokens_grad, memory_grad, vectors_in = inputs_back(
        core, tokens_own, gh1, gq_half, gkv_half, gkv_come, gkvc_half, gkvc_come, w_self_qkv,
        w_cross_kv, norm_gains,
    )

    vectors = vectors_ff + vectors_att + vectors_in
    vectors = vectors.reshape(8, CHIPS, ROWS).transpose(1, 0, 2).reshape(CHIPS, 8 * ROWS)
    vectors = lax.all_to_all(vectors, "dp", 0, 0, tiled=True).sum(0)
    vectors = (vectors + swapped(vectors)).reshape(8, 2, ROWS // 2)
    vectors = lax.dynamic_index_in_dim(vectors, half, 1, False)

    grouped = 2 * width
    first_keep, first_give = divided(core, first_sums, grouped)
    weight_down, weight_up = assembled(
        core, first_keep, swapped(first_give), [(True, width, width), (False, 4 * width, 4 * width)]
    )
    second_keep, second_give = divided(core, second_sums, 0)
    weight_qkv, weight_out, weight_q, weight_kv, weight_cross_out = assembled(
        core,
        second_keep,
        swapped(second_give),
        [(False, n * width, width) for n in (3, 1, 1, 2, 1)],
    )
    return (
        loss,
        layer_out.reshape(2, 1, tok_rows, width),
        tokens_grad[None],
        memory_grad[:, None],
        weight_qkv,
        weight_out,
        weight_q,
        weight_kv,
        weight_cross_out,
        weight_up,
        weight_down,
        vectors[:4],
        vectors[4:],
    )


def solution(mesh):
    in_specs = (
        P("dp", "mem", None),
        P(None, "dp", "mem", None),
        P(),
        P("dp", None),
        P("dp", "mem"),
        P(),
        P(),
        P(),
        P(),
        P(),
        P(),
        P(),
        P(),
        P(),
        P(None, ("dp", "mem")),
    )
    out_specs = (
        P("dp"),
        P(None, "dp", "mem", None),
        P("dp", "mem", None),
        P(None, "dp", "mem", None),
        P(("dp", "mem"), None),
        P(("dp", "mem"), None),
        P(("dp", "mem"), None),
        P(("dp", "mem"), None),
        P(("dp", "mem"), None),
        P(("dp", "mem"), None),
        P(("dp", "mem"), None),
        P(None, ("dp", "mem")),
        P(None, ("dp", "mem")),
    )
    return jax.shard_map(
        on_device, mesh=mesh, in_specs=in_specs, out_specs=out_specs, check_vma=False
    )
```

```python
from functools import partial

import jax
import jax.numpy as jnp
from jax import lax
from jax.experimental import pallas as pl
from jax.experimental.pallas import tpu as pltpu
from jax.sharding import PartitionSpec as P

HEAD = 64
PAIR = 2 * HEAD
SIDE = 4
CHIPS = SIDE * SIDE * SIDE
ROWS = 16
TILE = 256
FF_TILE = 512
BLOCK = 640
CHUNK = 16
ENTRIES = 200
MIB = 1024 * 1024
epsilon = 1e-05
masked_score = -1e30
bf16 = jnp.bfloat16
f32 = jnp.float32


def dot(left, right):
    return jnp.dot(left, right, preferred_element_type=f32)


def dot_nt(left, right):
    return lax.dot_general(left, right, (((1,), (1,)), ((), ())), preferred_element_type=f32)


def dot_tn(left, right):
    return lax.dot_general(left, right, (((0,), (0,)), ((), ())), preferred_element_type=f32)


def normalized(values):
    centre = values - jnp.mean(values, -1, keepdims=True)
    inverse = lax.rsqrt(jnp.mean(centre * centre, -1, keepdims=True) + epsilon)
    return centre * inverse, inverse


def norm_back(upstream, normed, inverse, gain):
    scaled = upstream * gain
    back = inverse * (
        scaled
        - jnp.mean(scaled, -1, keepdims=True)
        - normed * jnp.mean(scaled * normed, -1, keepdims=True)
    )
    return back, jnp.sum(upstream * normed, 0, keepdims=True), jnp.sum(upstream, 0, keepdims=True)


def lower_lanes(shape):
    return lax.broadcasted_iota(jnp.int32, shape, 1) < HEAD


def parted(block):
    low = lower_lanes(block.shape)
    none = jnp.zeros_like(block)
    return jnp.concatenate([jnp.where(low, block, none), jnp.where(low, none, block)], 0)


def merged(block):
    rows = block.shape[0] // 2
    return jnp.where(lower_lanes((rows, PAIR)), block[:rows], block[rows:])


def self_softmax(queries, keys, allowed):
    scores = dot_nt(queries, keys) * HEAD ** (-0.5)
    scores = jnp.where(allowed, scores, masked_score)
    weights = jnp.exp(scores - jnp.max(scores, -1, keepdims=True))
    return weights * (1.0 / jnp.sum(weights, -1, keepdims=True))


def by_view(values, is_first, combine, neutral):
    first = combine(jnp.where(is_first, values, neutral), -1, keepdims=True)
    second = combine(jnp.where(is_first, neutral, values), -1, keepdims=True)
    return jnp.where(is_first, first, second)


def cross_softmax(queries, keys, kept, is_first):
    scores = dot_nt(queries, keys) * HEAD ** (-0.5)
    scores = jnp.where(kept, scores, masked_score)
    weights = jnp.exp(scores - by_view(scores, is_first, jnp.max, masked_score))
    return weights * (1.0 / by_view(weights, is_first, jnp.sum, 0.0))


def each_view(block, is_first):
    none = jnp.zeros_like(block)
    return jnp.concatenate([jnp.where(is_first, block, none), jnp.where(is_first, none, block)], 0)


def allowed_of(allowed_ref):
    allowed = allowed_ref[...] > 0.5
    return jnp.concatenate([allowed, allowed], 0)


def attention_kernel(
    tokens_ref, allowed_ref, memory_ref, keep_ref, w_qkv, w_out, w_q, w_kv, w_cross_out, gains,
    biases, a1_ref, q_ref, kv_ref, o_ref, h1_ref, a2_ref, qc_ref, kvc_ref, oc_ref, h2_ref, a3_ref,
):
    rows = q_ref.shape[0]
    width = tokens_ref.shape[1]
    values = tokens_ref[...].astype(f32)
    normed, _ = normalized(values)
    a1_ref[...] = (normed * gains[0:1] + biases[0:1]).astype(bf16)
    q_ref[...] = dot(a1_ref[:rows], w_qkv[:, :width]).astype(bf16)
    kv_ref[...] = dot(a1_ref[...], w_qkv[:, width:]).astype(bf16)
    allowed = allowed_of(allowed_ref)
    for at in range(0, width, PAIR):
        queries = parted(q_ref[:, at : at + PAIR])
        probs = self_softmax(queries, kv_ref[:, at : at + PAIR], allowed)
        mixed = dot(probs.astype(bf16), kv_ref[:, width + at : width + at + PAIR])
        o_ref[:, at : at + PAIR] = merged(mixed).astype(bf16)
    h1 = values[:rows] + dot(o_ref[...], w_out[...])
    h1_ref[...] = h1
    normed, _ = normalized(h1)
    a2_ref[...] = (normed * gains[1:2] + biases[1:2]).astype(bf16)
    qc_ref[...] = dot(a2_ref[...], w_q[...]).astype(bf16)
    kvc_ref[...] = dot(memory_ref[...], w_kv[...]).astype(bf16)
    shape = (2 * rows, memory_ref.shape[0])
    kept = jnp.broadcast_to(keep_ref[...], shape) > 0.5
    is_first = lax.broadcasted_iota(jnp.int32, shape, 1) < shape[1] // 2
    for at in range(0, width, PAIR):
        queries = parted(qc_ref[:, at : at + PAIR])
        probs = cross_softmax(queries, kvc_ref[:, at : at + PAIR], kept, is_first)
        mixed = dot(
            each_view(probs.astype(bf16), is_first), kvc_ref[:, width + at : width + at + PAIR]
        )
        oc_ref[:rows, at : at + PAIR] = merged(mixed[: 2 * rows]).astype(bf16)
        oc_ref[rows:, at : at + PAIR] = merged(mixed[2 * rows :]).astype(bf16)
    h2 = jnp.concatenate([h1, h1], 0) + dot(oc_ref[...], w_cross_out[...])
    h2_ref[...] = h2
    normed, _ = normalized(h2)
    a3_ref[...] = (normed * gains[2:3] + biases[2:3]).astype(bf16)


def attention(tokens_page, allowed, memory_rows, keep, weights, gains, biases):
    rows, width = allowed.shape[0], tokens_page.shape[1]
    shape = jax.ShapeDtypeStruct
    return pl.pallas_call(
        attention_kernel,
        out_shape=(
            shape((2 * rows, width), bf16),
            shape((rows, width), bf16),
            shape((2 * rows, 2 * width), bf16),
            shape((rows, width), bf16),
            shape((rows, width), f32),
            shape((rows, width), bf16),
            shape((rows, width), bf16),
            shape((memory_rows.shape[0], 2 * width), bf16),
            shape((2 * rows, width), bf16),
            shape((2 * rows, width), f32),
            shape((2 * rows, width), bf16),
        ),
        compiler_params=pltpu.CompilerParams(vmem_limit_bytes=56 * MIB),
        cost_estimate=pl.CostEstimate(
            flops=20 * 10**9 // 10, bytes_accessed=24 * MIB, transcendentals=10**6
        ),
    )(tokens_page, allowed, memory_rows, keep, *weights, gains, biases)


def erf_parts(values):
    return 0.5 + 0.5 * lax.erf(values * (0.5**0.5))


def feed_forward_kernel(
    h2_ref, a3_ref, w_up, w_down, gains, biases, up_ref, act_ref, h3_ref, out_ref, fin_ref, total
):
    step = pl.program_id(0)

    @pl.when(step == 0)
    def _():
        total[...] = jnp.zeros_like(total)

    up = dot(a3_ref[...], w_up[...])
    up_ref[...] = up
    act = (up * erf_parts(up)).astype(bf16)
    act_ref[...] = act
    total[...] += dot(act, w_down[...])

    @pl.when(step == pl.num_programs(0) - 1)
    def _():
        h3 = h2_ref[...] + total[...]
        h3_ref[...] = h3
        out_ref[...] = h3.astype(bf16)
        normed, _ = normalized(h3)
        fin_ref[...] = (normed * gains[3:4] + biases[3:4]).astype(bf16)


def whole(*shape):
    return pl.BlockSpec(shape, lambda i: (0,) * len(shape))


def feed_forward(h2, a3, w_up, w_down, gains, biases):
    rows, width = h2.shape
    hidden = w_up.shape[1]
    shape = jax.ShapeDtypeStruct
    return pl.pallas_call(
        feed_forward_kernel,
        grid=(hidden // FF_TILE,),
        in_specs=[
            whole(rows, width),
            whole(rows, width),
            pl.BlockSpec((width, FF_TILE), lambda i: (0, i)),
            pl.BlockSpec((FF_TILE, width), lambda i: (i, 0)),
            whole(4, width),
            whole(4, width),
        ],
        out_specs=(
            pl.BlockSpec((rows, FF_TILE), lambda i: (0, i)),
            pl.BlockSpec((rows, FF_TILE), lambda i: (0, i)),
            whole(rows, width),
            whole(rows, width),
            whole(rows, width),
        ),
        out_shape=(
            shape((rows, hidden), f32),
            shape((rows, hidden), bf16),
            shape((rows, width), f32),
            shape((rows, width), bf16),
            shape((rows, width), bf16),
        ),
        scratch_shapes=[pltpu.VMEM((rows, width), f32)],
        compiler_params=pltpu.CompilerParams(vmem_limit_bytes=56 * MIB),
        cost_estimate=pl.CostEstimate(
            flops=4 * rows * width * hidden, bytes_accessed=24 * MIB, transcendentals=rows * hidden
        ),
    )(h2, a3, w_up, w_down, gains, biases)


def halves(block):
    middle = block.shape[1] // 2
    return block[:, :middle], block[:, middle:]


def feed_forward_back_kernel(
    core_ref, own_ref, other_ref, far_a, far_b, far_c, h3_ref, h2_ref, up_ref, w_up, w_down, gains, gh3_half_ref,
    gup_ref, gh2_ref, gh2_half_ref, vector_ref, gh3, gh3_low_ref, total,
):
    step = pl.program_id(0)
    core = core_ref[0]

    @pl.when(step == 0)
    def _():
        upstream = own_ref[...]
        for ref in (other_ref, far_a, far_b, far_c):
            upstream += ref[...].astype(f32)
        normed, inverse = normalized(h3_ref[...])
        back, gain, bias = norm_back(upstream, normed, inverse, gains[3:4])
        gh3[...] = back
        gh3_low_ref[...] = back.astype(bf16)
        for side, part in enumerate(halves(gh3_low_ref[...])):
            gh3_half_ref[side ^ core] = part
        vector_ref[...] = jnp.zeros_like(vector_ref)
        vector_ref[3:4] = gain
        vector_ref[7:8] = bias
        total[...] = jnp.zeros_like(total)

    grad = dot_nt(gh3_low_ref[...], w_down[...])
    up = up_ref[...]
    slope = erf_parts(up) + up * jnp.exp(-0.5 * up * up) * (0.5 / jnp.pi) ** 0.5
    gup = (grad * slope).astype(bf16)
    gup_ref[0] = gup
    total[...] += dot_nt(gup, w_up[...])

    @pl.when(step == pl.num_programs(0) - 1)
    def _():
        normed, inverse = normalized(h2_ref[...])
        back, gain, bias = norm_back(total[...], normed, inverse, gains[2:3])
        gh2 = gh3[...] + back
        gh2_ref[...] = gh2
        for side, part in enumerate(halves(gh2.astype(bf16))):
            gh2_half_ref[side ^ core] = part
        vector_ref[2:3] = gain
        vector_ref[6:7] = bias


def feed_forward_back(core, parts, h3, h2, up, w_up, w_down, gains):
    rows, width = h2.shape
    hidden = w_up.shape[1]
    tiles = hidden // FF_TILE
    shape = jax.ShapeDtypeStruct

    def all_of(*dims):
        return pl.BlockSpec(dims, lambda i, core: (0,) * len(dims))

    def half_tile(i, core):
        return ((i // (tiles // 2)) ^ core[0], 0, i % (tiles // 2))

    return pl.pallas_call(
        feed_forward_back_kernel,
        grid_spec=pltpu.PrefetchScalarGridSpec(
            num_scalar_prefetch=1,
            grid=(tiles,),
            in_specs=[
                *(all_of(rows, width) for _ in range(7)),
                pl.BlockSpec((rows, FF_TILE), lambda i, core: (0, i)),
                pl.BlockSpec((width, FF_TILE), lambda i, core: (0, i)),
                pl.BlockSpec((FF_TILE, width), lambda i, core: (i, 0)),
                all_of(4, width),
            ],
            out_specs=(
                all_of(2, rows, width // 2),
                pl.BlockSpec((1, rows, FF_TILE), half_tile),
                all_of(rows, width),
                all_of(2, rows, width // 2),
                all_of(8, width),
            ),
            scratch_shapes=[
                pltpu.VMEM((rows, width), f32),
                pltpu.VMEM((rows, width), bf16),
                pltpu.VMEM((rows, width), f32),
            ],
        ),
        out_shape=(
            shape((2, rows, width // 2), bf16),
            shape((2, rows, hidden // 2), bf16),
            shape((rows, width), f32),
            shape((2, rows, width // 2), bf16),
            shape((8, width), f32),
        ),
        compiler_params=pltpu.CompilerParams(vmem_limit_bytes=56 * MIB),
        cost_estimate=pl.CostEstimate(
            flops=4 * rows * width * hidden,
            bytes_accessed=24 * MIB,
            transcendentals=2 * rows * hidden,
        ),
    )(core, *parts, h3, h2, up, w_up, w_down, gains)


def attention_back_kernel(
    core_ref, gh2_ref, allowed_ref, keep_ref, kvc_ref, qc_ref, h1_ref, kv_ref, q_ref, w_cross_out, w_q,
    w_out, gains, gqc_ref, gkvc_ref, gh1_ref, gh1_half_ref, gq_ref, gkv_ref, vector_ref, goc, go, gqc,
    gh1_low,
):
    rows, width = q_ref.shape
    half = width // 2
    core = core_ref[0]
    scale = HEAD ** (-0.5)
    goc[...] = dot_nt(gh2_ref[...].astype(bf16), w_cross_out[...]).astype(bf16)
    shape = (2 * rows, kvc_ref.shape[0])
    kept = jnp.broadcast_to(keep_ref[...], shape) > 0.5
    is_first = lax.broadcasted_iota(jnp.int32, shape, 1) < shape[1] // 2
    for at in range(0, width, PAIR):
        here, there = slice(at, at + PAIR), slice(width + at, width + at + PAIR)
        slot = (at // half) ^ core
        low, high = slice(at % half, at % half + PAIR), slice(half + at % half, half + at % half + PAIR)
        queries = parted(qc_ref[:, here])
        probs = cross_softmax(queries, kvc_ref[:, here], kept, is_first)
        upstream = jnp.concatenate([parted(goc[:rows, here]), parted(goc[rows:, here])], 0)
        grad = dot_nt(upstream, kvc_ref[:, there])
        grad = jnp.where(is_first, grad[: 2 * rows], grad[2 * rows :])
        slope = probs * (grad - by_view(probs * grad, is_first, jnp.sum, 0.0))
        slope = slope.astype(bf16)
        change = (merged(dot(slope, kvc_ref[:, here])) * scale).astype(bf16)
        gqc[:, here] = change
        gqc_ref[slot, :, low] = change
        gkvc_ref[slot, :, low] = (dot_tn(slope, queries) * scale).astype(bf16)
        change = dot_tn(each_view(probs.astype(bf16), is_first), upstream)
        gkvc_ref[slot, :, high] = change.astype(bf16)
    normed, inverse = normalized(h1_ref[...])
    back, gain, bias = norm_back(dot_nt(gqc[...], w_q[...]), normed, inverse, gains[1:2])
    vector_ref[...] = jnp.zeros_like(vector_ref)
    vector_ref[1:2] = gain
    vector_ref[5:6] = bias
    gh1 = gh2_ref[:rows] + gh2_ref[rows:] + back
    gh1_ref[...] = gh1
    gh1_low[...] = gh1.astype(bf16)
    for side, part in enumerate(halves(gh1_low[...])):
        gh1_half_ref[side ^ core] = part
    go[...] = dot_nt(gh1_low[...], w_out[...]).astype(bf16)
    allowed = allowed_of(allowed_ref)
    for at in range(0, width, PAIR):
        here, there = slice(at, at + PAIR), slice(width + at, width + at + PAIR)
        slot = (at // half) ^ core
        low, high = slice(at % half, at % half + PAIR), slice(half + at % half, half + at % half + PAIR)
        queries = parted(q_ref[:, here])
        probs = self_softmax(queries, kv_ref[:, here], allowed)
        upstream = parted(go[:, here])
        grad = dot_nt(upstream, kv_ref[:, there])
        slope = probs * (grad - jnp.sum(probs * grad, -1, keepdims=True))
        slope = slope.astype(bf16)
        gq_ref[slot, :, low] = (merged(dot(slope, kv_ref[:, here])) * scale).astype(bf16)
        gkv_ref[slot, :, low] = (dot_tn(slope, queries) * scale).astype(bf16)
        gkv_ref[slot, :, high] = dot_tn(probs.astype(bf16), upstream).astype(bf16)


def scalar_first(count):
    return [pl.BlockSpec(memory_space=pltpu.SMEM)] + [
        pl.BlockSpec(memory_space=pltpu.VMEM) for _ in range(count)
    ]


def attention_back(core, *operands):
    rows, width = operands[7].shape
    shape = jax.ShapeDtypeStruct
    return pl.pallas_call(
        attention_back_kernel,
        in_specs=scalar_first(len(operands)),
        out_shape=(
            shape((2, rows, width // 2), bf16),
            shape((2, rows, width), bf16),
            shape((rows, width), f32),
            shape((2, rows, width // 2), bf16),
            shape((2, rows, width // 2), bf16),
            shape((2, 2 * rows, width), bf16),
            shape((8, width), f32),
        ),
        scratch_shapes=[
            pltpu.VMEM((2 * rows, width), bf16),
            pltpu.VMEM((rows, width), bf16),
            pltpu.VMEM((rows, width), bf16),
            pltpu.VMEM((rows, width), bf16),
        ],
        compiler_params=pltpu.CompilerParams(vmem_limit_bytes=56 * MIB),
        cost_estimate=pl.CostEstimate(
            flops=2 * 10**9, bytes_accessed=12 * MIB, transcendentals=10**6
        ),
    )(core, *operands)


def inputs_back_kernel(
    core_ref, tokens_ref, gh1_ref, gq_ref, gkv_ref, come_ref, gkvc_ref, come_cross_ref, w_qkv, w_kv,
    gains, tokens_grad_ref, memory_grad_ref, vector_ref, grads,
):
    core = core_ref[0]
    rows, width = gh1_ref.shape
    half = width // 2
    total = jnp.zeros((rows, width), f32)
    for side in range(2):
        slot, away = side ^ core, 1 - (side ^ core)
        pairs = gkv_ref[slot, :rows].astype(f32) + come_ref[away, rows:].astype(f32)
        pairs = pairs.astype(bf16)
        at = side * half
        total += dot_nt(gq_ref[slot], w_qkv[:, at : at + half])
        total += dot_nt(pairs[:, :half], w_qkv[:, width + at : width + at + half])
        total += dot_nt(pairs[:, half:], w_qkv[:, 2 * width + at : 2 * width + at + half])
    normed, inverse = normalized(tokens_ref[...].astype(f32))
    back, gain, bias = norm_back(total, normed, inverse, gains[0:1])
    tokens_grad_ref[...] = gh1_ref[...] + back
    vector_ref[...] = jnp.zeros_like(vector_ref)
    vector_ref[0:1] = gain
    vector_ref[4:5] = bias
    patches = gkvc_ref.shape[1]
    total = jnp.zeros((patches, width), f32)
    for side in range(2):
        slot, away = side ^ core, 1 - (side ^ core)
        pairs = gkvc_ref[slot].astype(f32) + come_cross_ref[away].astype(f32)
        pairs = pairs.astype(bf16)
        at = side * half
        total += dot_nt(pairs[:, :half], w_kv[:, at : at + half])
        total += dot_nt(pairs[:, half:], w_kv[:, width + at : width + at + half])
    grads[...] = total
    own = memory_grad_ref.shape[1]
    for view in range(2):
        start = pl.multiple_of(view * 2 * own + core * own, 8)
        memory_grad_ref[view] = grads[pl.ds(start, own)]


def inputs_back(core, *operands):
    rows, width = operands[1].shape
    patches = operands[5].shape[1]
    shape = jax.ShapeDtypeStruct
    return pl.pallas_call(
        inputs_back_kernel,
        in_specs=scalar_first(len(operands)),
        out_shape=(
            shape((rows, width), f32),
            shape((2, patches // 4, width), f32),
            shape((8, width), f32),
        ),
        scratch_shapes=[pltpu.VMEM((patches, width), f32)],
        compiler_params=pltpu.CompilerParams(vmem_limit_bytes=56 * MIB),
        cost_estimate=pl.CostEstimate(flops=10**9, bytes_accessed=14 * MIB, transcendentals=0),
    )(core, *operands)


def logits_kernel(rows_ref, readout_ref, bias_ref, own_ref, far_ref, stats_ref, kept):
    step = pl.program_id(0)
    width = rows_ref.shape[2]
    block = readout_ref.shape[0]
    near = own_ref.shape[1]

    @pl.when(step == 0)
    def _():
        for k in range(5):
            kept[k] = jnp.full(kept.shape[1:], masked_score if k in (0, 3) else 0.0, f32)

    for ref, begin in ((own_ref, 0), (far_ref, near)):
        tokens = ref.shape[1]
        rows = rows_ref[:, begin : begin + tokens].reshape(2 * tokens, width)
        values = dot_nt(rows, readout_ref[...]) + bias_ref[...]
        ref[...] = values.reshape(2, tokens, block)

        def chunk(i, carry, ref=ref, begin=begin):
            at = pl.ds(pl.multiple_of(i * CHUNK, CHUNK), CHUNK)
            to = pl.ds(pl.multiple_of(begin + i * CHUNK, CHUNK), CHUNK)
            first = [ref[0, at, c : c + 128] for c in range(0, block, 128)]
            second = [ref[1, at, c : c + 128] for c in range(0, block, 128)]
            top_first, top_second = kept[0, to], kept[3, to]
            new_first, new_second = top_first, top_second
            for a, b in zip(first, second):
                new_first = jnp.maximum(new_first, a)
                new_second = jnp.maximum(new_second, b)
            fade_first = jnp.exp(top_first - new_first)
            fade_second = jnp.exp(top_second - new_second)
            total_first = kept[1, to] * fade_first
            total_apart = kept[2, to] * fade_first
            total_second = kept[4, to] * fade_second
            for a, b in zip(first, second):
                weight = jnp.exp(a - new_first)
                total_first += weight
                total_apart += weight * (a - b)
                total_second += jnp.exp(b - new_second)
            kept[0, to], kept[1, to], kept[2, to] = new_first, total_first, total_apart
            kept[3, to], kept[4, to] = new_second, total_second
            return carry

        lax.fori_loop(0, tokens // CHUNK, chunk, 0)

    @pl.when(step == pl.num_programs(0) - 1)
    def _():
        top_first = jnp.max(kept[0], -1, keepdims=True)
        top_second = jnp.max(kept[3], -1, keepdims=True)
        fade_first = jnp.exp(kept[0] - top_first)
        fade_second = jnp.exp(kept[3] - top_second)
        stats = (
            top_first,
            jnp.sum(kept[1] * fade_first, -1, keepdims=True),
            jnp.sum(kept[2] * fade_first, -1, keepdims=True),
            top_second,
            jnp.sum(kept[4] * fade_second, -1, keepdims=True),
        )
        lane = lax.broadcasted_iota(jnp.int32, kept.shape[1:], 1)
        result = jnp.zeros(kept.shape[1:], f32)
        for k, stat in enumerate(stats):
            result = jnp.where(lane == k, stat, result)
        stats_ref[...] = result.T[:8]


def logits_and_stats(rows, readout_rows, bias):
    views, tokens, width = rows.shape
    entries = readout_rows.shape[0]
    near = tokens // SIDE
    shape = jax.ShapeDtypeStruct
    return pl.pallas_call(
        logits_kernel,
        out_shape=(
            shape((2, near, entries), f32),
            shape((2, tokens - near, entries), f32),
            shape((8, tokens), f32),
        ),
        grid=(entries // BLOCK,),
        in_specs=[
            whole(2, tokens, width),
            pl.BlockSpec((BLOCK, width), lambda i: (i, 0)),
            pl.BlockSpec((1, BLOCK), lambda i: (0, i)),
        ],
        out_specs=(
            pl.BlockSpec((2, near, BLOCK), lambda i: (0, 0, i)),
            pl.BlockSpec((2, tokens - near, BLOCK), lambda i: (0, 0, i)),
            whole(8, tokens),
        ),
        scratch_shapes=[pltpu.VMEM((5, tokens, 128), f32)],
        compiler_params=pltpu.CompilerParams(vmem_limit_bytes=58 * MIB),
        cost_estimate=pl.CostEstimate(
            flops=4 * tokens * entries * width,
            bytes_accessed=2 * entries * width + 8 * tokens * entries,
            transcendentals=2 * tokens * entries,
        ),
    )(rows, readout_rows, bias)


def merged_stats(near_ref, come_ref):
    tokens = near_ref.shape[2]
    page = tokens // SIDE
    is_first = lax.broadcasted_iota(jnp.int32, (8, tokens), 1) % page < page // 2
    parts = []
    for ref, flipped in ((near_ref, False), (come_ref, True)):
        for r in range(SIDE):
            part = ref[r]
            if r:
                part = pltpu.roll(part, r * page, 1)
            if flipped:
                part = jnp.where(
                    is_first,
                    pltpu.roll(part, tokens - page // 2, 1),
                    pltpu.roll(part, page // 2, 1),
                )
            parts.append(part)
    top_first = parts[0][0:1]
    top_second = parts[0][3:4]
    for part in parts[1:]:
        top_first = jnp.maximum(top_first, part[0:1])
        top_second = jnp.maximum(top_second, part[3:4])
    total_first = total_apart = total_second = jnp.zeros((1, tokens), f32)
    for part in parts:
        fade = jnp.exp(part[0:1] - top_first)
        total_first += part[1:2] * fade
        total_apart += part[2:3] * fade
        total_second += part[4:5] * jnp.exp(part[3:4] - top_second)
    first_lse = top_first + jnp.log(total_first)
    second_lse = top_second + jnp.log(total_second)
    return first_lse, second_lse, total_apart / total_first


def readout_back_kernel(
    begin, near_ref, come_ref, weight_ref, logits_ref, readout_ref, *refs
):
    stay_ref, give_ref, *term_ref, kept, slopes, total = refs
    step = pl.program_id(0)
    tokens = logits_ref.shape[1]
    block = readout_ref.shape[0]
    end = begin + tokens

    @pl.when(step == 0)
    def _():
        for k, row in enumerate(merged_stats(near_ref, come_ref)):
            kept[k] = jnp.broadcast_to(row, (128, row.shape[1])).T[begin:end]
        kept[3] = weight_ref[...]
        if term_ref:
            term_ref[0][...] = kept[3] * (kept[2] - kept[0] + kept[1])
        total[...] = jnp.zeros_like(total)

    def chunk(i, carry):
        at = pl.ds(pl.multiple_of(i * CHUNK, CHUNK), CHUNK)
        first_lse, second_lse, apart, weight = (kept[k, at] for k in range(4))
        for c in range(0, block, 128):
            first = logits_ref[0, at, c : c + 128]
            second = logits_ref[1, at, c : c + 128]
            first_prob = jnp.exp(first - first_lse) * weight
            second_prob = jnp.exp(second - second_lse) * weight
            slopes[0, at, c : c + 128] = (first_prob * (first - second - apart)).astype(bf16)
            slopes[1, at, c : c + 128] = (second_prob - first_prob).astype(bf16)
        return carry

    lax.fori_loop(0, tokens // CHUNK, chunk, 0)
    total[...] += dot(slopes[...].reshape(2 * tokens, block), readout_ref[...])

    @pl.when(step == pl.num_programs(0) - 1)
    def _():
        pages, views, rows, width = stay_ref.shape
        for p in range(pages):
            for v in range(views):
                at = v * tokens + p * 2 * rows
                stay_ref[p, v] = total[at : at + rows]
                give_ref[p, v] = total[at + rows : at + 2 * rows].astype(bf16)


def readout_back(stats_near, stats_come, weight, logits, readout_rows, begin):
    views, tokens, entries = logits.shape
    all_tokens = stats_near.shape[2]
    width = readout_rows.shape[1]
    rows = all_tokens // SIDE // 2
    pages = tokens // rows // 2
    shape = jax.ShapeDtypeStruct
    out_shape = [
        shape((pages, 2, rows, width), f32),
        shape((pages, 2, rows, width), bf16),
    ]
    out_specs = [whole(pages, 2, rows, width), whole(pages, 2, rows, width)]
    if begin == 0:
        out_shape.append(shape((tokens, 128), f32))
        out_specs.append(whole(tokens, 128))
    return pl.pallas_call(
        partial(readout_back_kernel, begin),
        out_shape=tuple(out_shape),
        grid=(entries // BLOCK,),
        in_specs=[
            whole(SIDE, 8, all_tokens),
            whole(SIDE, 8, all_tokens),
            whole(tokens, 128),
            pl.BlockSpec((2, tokens, BLOCK), lambda i: (0, 0, i)),
            pl.BlockSpec((BLOCK, width), lambda i: (i, 0)),
        ],
        out_specs=tuple(out_specs),
        scratch_shapes=[
            pltpu.VMEM((4, tokens, 128), f32),
            pltpu.VMEM((2, tokens, BLOCK), bf16),
            pltpu.VMEM((2 * tokens, width), f32),
        ],
        compiler_params=pltpu.CompilerParams(vmem_limit_bytes=58 * MIB),
        cost_estimate=pl.CostEstimate(
            flops=4 * tokens * entries * width,
            bytes_accessed=2 * entries * width + 8 * tokens * entries,
            transcendentals=2 * tokens * entries,
        ),
    )(stats_near, stats_come, weight, logits, readout_rows)


def swapped(block):
    return lax.ppermute(block, "mem", [(0, 1), (1, 0)])


def along_line(block, distance):
    route = [(d, d // SIDE * SIDE + (d - distance) % SIDE) for d in range(CHIPS)]
    return lax.ppermute(block, "dp", route)


def lines(stride, core):
    starts = [d for d in range(CHIPS) if (d // stride) % SIDE == 0]
    return [[2 * (start + stride * k) + core for k in range(SIDE)] for start in starts]


def groups_of(strides):
    return lines(strides[0], 0) + lines(strides[1], 1)


def summed(bucket, strides):
    parts = bucket.reshape(SIDE, -1, bucket.shape[-1])
    parts = lax.all_to_all(
        parts, ("dp", "mem"), 0, 0, axis_index_groups=groups_of(strides), tiled=True
    )
    return parts.astype(f32).sum(0)


def first_sum(bucket):
    flat = bucket.reshape(CHIPS * ROWS, bucket.shape[-1])
    return lax.psum_scatter(
        flat, ("dp", "mem"), axis_index_groups=groups_of((1, 4)), scatter_dimension=0, tiled=True
    )


def last_sums(part):
    return summed(summed(part, (4, 16)).astype(bf16), (16, 1))


def outer_kernel(shapes, core_ref, *refs):
    n_in = 4 * len(shapes)
    inputs, out_ref, turned = refs[:n_in], refs[n_in], refs[n_in + 1 :]
    step = pl.program_id(0)
    core = core_ref[0]

    def place(chip):
        z, y, x = chip // 16, (chip // 4) % 4, chip % 4
        return jnp.where(core == 0, x * 16 + y * 4 + z, y * 16 + z * 4 + x)

    first = 0
    for i, (groups, columns, shared) in enumerate(shapes):
        left_a, left_b, right_a, right_b = inputs[4 * i : 4 * i + 4]
        tiles = columns // TILE
        low, high = first, first + groups * tiles
        first = high

        @pl.when(step == low)
        def _(left_a=left_a, left_b=left_b, to=turned[i], groups=groups):
            wide = left_a.shape[1]
            for start in range(0, wide, 1024):
                both = jnp.concatenate(
                    [left_a[:, start : start + 1024], left_b[:, start : start + 1024]], 0
                )
                flat = both.T
                if groups == 1:
                    to[0, start : start + 1024] = flat
                else:
                    per = ROWS * groups
                    for c in range(1024 // per):
                        chip = start // per + c
                        for g in range(groups):
                            at = c * per + g * ROWS
                            to[g, chip * ROWS : (chip + 1) * ROWS] = flat[at : at + ROWS]

        @pl.when((step >= low) & (step < high))
        def _(right_a=right_a, right_b=right_b, to=turned[i], tiles=tiles, low=low, shared=shared):
            at = step - low
            group = at // tiles
            tile = at - group * tiles
            column = pl.ds(pl.multiple_of(tile * TILE, TILE), TILE)
            if shared == 0:
                both = jnp.concatenate([right_a[0, :, column], right_b[:, column]], 0)
            else:
                here, there = right_a[0, :, column], right_b[1, :, column]
                if shared == 2:
                    middle = there.shape[0] // 2
                    there = jnp.concatenate([there[middle:], there[:middle]], 0)
                both = (here.astype(f32) + there.astype(f32)).astype(bf16)
            result = dot(to[group], both).astype(bf16)
            for chip in range(CHIPS):
                out_ref[place(chip)] = result[chip * ROWS : (chip + 1) * ROWS]


def outer_products(core, items):
    shapes, operands, scratch = [], [], []
    total = flops = 0
    for left, left_other, right, right_other, shared in items:
        groups = left.shape[1] // (ROWS * CHIPS)
        columns = right.shape[2]
        shapes.append((groups, columns, shared))
        operands += [left, left_other, right, right_other]
        depth = left.shape[0] + left_other.shape[0]
        scratch.append(pltpu.VMEM((groups, ROWS * CHIPS, depth), bf16))
        total += groups * columns
        flops += 2 * left.shape[1] * columns * depth
    return pl.pallas_call(
        partial(outer_kernel, tuple(shapes)),
        out_shape=jax.ShapeDtypeStruct((CHIPS, ROWS, total), bf16),
        grid_spec=pltpu.PrefetchScalarGridSpec(
            num_scalar_prefetch=1,
            grid=(total // TILE,),
            in_specs=[pl.BlockSpec(memory_space=pltpu.VMEM) for _ in operands],
            out_specs=pl.BlockSpec((CHIPS, ROWS, TILE), lambda i, core: (0, 0, i)),
            scratch_shapes=scratch,
        ),
        compiler_params=pltpu.CompilerParams(vmem_limit_bytes=56 * MIB),
        cost_estimate=pl.CostEstimate(
            flops=flops, bytes_accessed=CHIPS * ROWS * total * 2, transcendentals=0
        ),
    )(core, *operands)


def divide_kernel(grouped, core_ref, sums_ref, keep_ref, give_ref):
    core = core_ref[0]
    half = grouped // 2
    columns = sums_ref.shape[1]
    for ref, side in ((keep_ref, core), (give_ref, 1 - core)):
        if grouped:
            start = pl.ds(pl.multiple_of(side * half, 128), half)
            block = sums_ref[:, start]
            ref[:, :half] = block[: ROWS // 2]
            ref[:, half:grouped] = block[ROWS // 2 :]
        rows = pl.ds(pl.multiple_of(side * (ROWS // 2), 8), ROWS // 2)
        if columns > grouped:
            ref[:, grouped:] = sums_ref[rows, grouped:]


def divided(core, sums, grouped):
    shape = jax.ShapeDtypeStruct((ROWS // 2, sums.shape[1]), f32)
    return pl.pallas_call(
        partial(divide_kernel, grouped),
        in_specs=scalar_first(1),
        out_shape=(shape, shape),
    )(core, sums)


def assemble_kernel(layout, core_ref, keep_ref, come_ref, *outs):
    core = core_ref[0]
    for ref, side in ((keep_ref, core), (come_ref, 1 - core)):
        at = 0
        for out, (grouped, columns, span) in zip(outs, layout):
            part = span // 2
            if grouped:
                for g in range(2):
                    for h in range(2):
                        rows = slice(g * ROWS + h * ROWS // 2, g * ROWS + (h + 1) * ROWS // 2)
                        start = at + h * 2 * part + g * part
                        column = pl.ds(pl.multiple_of(side * part, 128), part)
                        out[rows, column] = ref[:, start : start + part]
                at += 4 * part
                continue
            for k in range(0, columns, span):
                column = pl.ds(pl.multiple_of(k + side * part, 128), part)
                out[:, column] = ref[:, at : at + part]
                at += part


def assembled(core, keep, come, layout):
    return pl.pallas_call(
        partial(assemble_kernel, tuple(layout)),
        in_specs=scalar_first(2),
        out_shape=tuple(
            jax.ShapeDtypeStruct((2 * ROWS if grouped else ROWS // 2, columns), f32)
            for grouped, columns, span in layout
        ),
    )(core, keep, come)


def on_device(
    tokens,
    memory,
    lengths,
    segments,
    key_mask,
    w_self_qkv,
    w_self_out,
    w_cross_q,
    w_cross_kv,
    w_cross_out,
    w_up,
    w_down,
    norm_gains,
    norm_biases,
    readout,
):
    tok_rows = tokens.shape[1]
    width = tokens.shape[2]
    half = lax.axis_index("mem")
    core = half.astype(jnp.int32).reshape(1)
    page_index = lax.axis_index("dp")
    patches = 2 * memory.shape[2]

    vocab_dev = readout.shape[1]
    readout_turned = jnp.pad(readout.T, ((0, ENTRIES - vocab_dev), (0, 0)))
    planes = [[d for d in range(CHIPS) if d % SIDE == x] for x in range(SIDE)]
    readout_part = lax.all_gather(
        readout_turned, "dp", axis=0, tiled=True, axis_index_groups=planes
    )
    is_entry = jnp.arange(readout_part.shape[0]) % ENTRIES < vocab_dev
    entry_bias = jnp.where(is_entry, 0.0, masked_score).astype(f32)[None]

    tokens_own = tokens[0]
    tokens_page = jnp.concatenate([tokens_own, swapped(tokens_own)], 0)
    memory_own = memory[:, 0]
    memory_come = swapped(memory_own)
    memory_rows = jnp.where(
        half == 0,
        jnp.concatenate([memory_own, memory_come], 1),
        jnp.concatenate([memory_come, memory_own], 1),
    ).reshape(2 * patches, width)
    mask_own = key_mask[0].astype(f32)
    mask_come = swapped(mask_own)
    mask_page = jnp.where(
        half == 0,
        jnp.concatenate([mask_own, mask_come]),
        jnp.concatenate([mask_come, mask_own]),
    )
    keep = jnp.tile(jnp.repeat(mask_page, 2), 2)[None]
    own_positions = jnp.arange(tok_rows) + half * tok_rows
    other_positions = jnp.arange(tok_rows) + (1 - half) * tok_rows
    key_positions = jnp.concatenate([own_positions, other_positions])
    cut = segments[0].reshape(2, tok_rows)
    own_segments = lax.dynamic_index_in_dim(cut, half, 0, False)
    other_segments = lax.dynamic_index_in_dim(cut, 1 - half, 0, False)
    key_segments = jnp.concatenate([own_segments, other_segments])
    allowed = (key_positions[None, :] <= own_positions[:, None]) & (
        key_segments[None, :] == own_segments[:, None]
    )
    allowed = allowed.astype(f32)
    count = jnp.sum(lengths).astype(f32)
    line = page_index // SIDE * SIDE + (page_index + jnp.arange(SIDE)) % SIDE
    valid = key_positions[None] < lengths[line][:, None]
    row_weight = (valid.astype(f32) / count).reshape(-1, 1)
    row_weight = jnp.broadcast_to(row_weight, (row_weight.shape[0], 128))

    weights = (w_self_qkv, w_self_out, w_cross_q, w_cross_kv, w_cross_out)
    a1, q, kv, o_self, h1, a2, qc, kvc, oc, h2, a3 = attention(
        tokens_page, allowed, memory_rows, keep, weights, norm_gains, norm_biases
    )
    up, act, h3, layer_out, final = feed_forward(h2, a3, w_up, w_down, norm_gains, norm_biases)
    final = final.reshape(2, tok_rows, width)
    near = jnp.stack([final] + [along_line(final, r) for r in range(1, SIDE)])
    final_line = jnp.stack([near, swapped(near)], 1).transpose(2, 0, 1, 3, 4)
    final_line = final_line.reshape(2, 2 * SIDE * tok_rows, width)
    o_self_other, a2_other, oc_other, a3_other, act_other = map(
        swapped, (o_self, a2, oc, a3, act)
    )

    own_logits, far_logits, stats = logits_and_stats(final_line, readout_part, entry_bias)
    stats = jnp.stack([stats] + [along_line(stats, r) for r in range(1, SIDE)])
    stats_come = swapped(stats)
    page = 2 * tok_rows
    far_stay, far_give = readout_back(
        stats, stats_come, row_weight[page:], far_logits, readout_part, page
    )
    far = (far_stay + swapped(far_give).astype(f32)).astype(bf16)
    far = [along_line(far[r - 1], -r) for r in range(1, SIDE)]
    own_stay, own_give, terms = readout_back(
        stats, stats_come, row_weight[:page], own_logits, readout_part, 0
    )
    terms = terms[:, 0].reshape(2, tok_rows).sum(1)
    loss = (terms[0] + terms[1]).reshape(1)
    grad_parts = [own_stay[0], swapped(own_give[0])] + far
    grad_parts = [part.reshape(2 * tok_rows, width) for part in grad_parts]

    gh3_half, gup_half, gh2, gh2_half, vectors_ff = feed_forward_back(
        core, grad_parts, h3, h2, up, w_up, w_down, norm_gains
    )
    first_bucket = outer_products(
        core,
        [
            (act, act_other, gh3_half, swapped(gh3_half[1]), 0),
            (a3, a3_other, gup_half, swapped(gup_half[1]), 0),
        ],
    )
    gh2, first_bucket = lax.optimization_barrier((gh2, first_bucket))
    first_part = first_sum(first_bucket)

    gqc_half, gkvc_half, gh1, gh1_half, gq_half, gkv_half, vectors_att = attention_back(
        core, gh2, allowed, keep, kvc, qc, h1, kv, q, w_cross_out, w_cross_q, w_self_out, norm_gains
    )
    gkv_come, gkvc_come = swapped(gkv_half), swapped(gkvc_half)
    middle = tok_rows
    second_bucket = outer_products(
        core,
        [
            (a1[:middle], a1[middle:], gq_half, swapped(gq_half[1]), 0),
            (a1[:middle], a1[middle:], gkv_half, gkv_come, 2),
            (o_self, o_self_other, gh1_half, swapped(gh1_half[1]), 0),
            (a2, a2_other, gqc_half, swapped(gqc_half[1]), 0),
            (memory_rows[:patches], memory_rows[patches:], gkvc_half, gkvc_come, 1),
            (oc, oc_other, gh2_half, swapped(gh2_half[1]), 0),
        ],
    )
    second_part = first_sum(second_bucket)
    tokens_grad, memory_grad, vectors_in = inputs_back(
        core, tokens_own, gh1, gq_half, gkv_half, gkv_come, gkvc_half, gkvc_come, w_self_qkv,
        w_cross_kv, norm_gains,
    )

    vectors = vectors_ff + vectors_att + vectors_in
    vectors = vectors.reshape(8, CHIPS, ROWS).transpose(1, 0, 2).reshape(CHIPS, 8 * ROWS)
    vectors = lax.all_to_all(vectors, "dp", 0, 0, tiled=True)
    first_part, vectors = lax.optimization_barrier((first_part, vectors))
    vectors = vectors.sum(0)
    vectors = (vectors + swapped(vectors)).reshape(8, 2, ROWS // 2)
    vectors = lax.dynamic_index_in_dim(vectors, half, 1, False)

    first_sums = last_sums(first_part)
    first_keep, first_give = divided(core, first_sums, 2 * width)
    weight_down, weight_up = assembled(
        core,
        first_keep,
        swapped(first_give),
        [(True, width, width), (False, 4 * width, 4 * width)],
    )
    second_part, first_sums = lax.optimization_barrier((second_part, first_sums))
    second_sums = last_sums(second_part)
    second_keep, second_give = divided(core, second_sums, 0)
    weight_qkv, weight_out, weight_q, weight_kv, weight_cross_out = assembled(
        core,
        second_keep,
        swapped(second_give),
        [(False, n * width, width) for n in (3, 1, 1, 2, 1)],
    )
    return (
        loss,
        layer_out.reshape(2, 1, tok_rows, width),
        tokens_grad[None],
        memory_grad[:, None],
        weight_qkv,
        weight_out,
        weight_q,
        weight_kv,
        weight_cross_out,
        weight_up,
        weight_down,
        vectors[:4],
        vectors[4:],
    )


def solution(mesh):
    in_specs = (
        P("dp", "mem", None),
        P(None, "dp", "mem", None),
        P(),
        P("dp", None),
        P("dp", "mem"),
        P(),
        P(),
        P(),
        P(),
        P(),
        P(),
        P(),
        P(),
        P(),
        P(None, ("dp", "mem")),
    )
    out_specs = (
        P("dp"),
        P(None, "dp", "mem", None),
        P("dp", "mem", None),
        P(None, "dp", "mem", None),
        P(("dp", "mem"), None),
        P(("dp", "mem"), None),
        P(("dp", "mem"), None),
        P(("dp", "mem"), None),
        P(("dp", "mem"), None),
        P(("dp", "mem"), None),
        P(("dp", "mem"), None),
        P(None, ("dp", "mem")),
        P(None, ("dp", "mem")),
    )
    return jax.shard_map(
        on_device, mesh=mesh, in_specs=in_specs, out_specs=out_specs, check_vma=False
    )
```

```python
from functools import partial

import jax
import jax.numpy as jnp
from jax import lax
from jax.experimental import pallas as pl
from jax.experimental.pallas import tpu as pltpu
from jax.sharding import PartitionSpec as P

HEAD = 64
PAIR = 2 * HEAD
SIDE = 4
CHIPS = SIDE * SIDE * SIDE
ROWS = 16
TILE = 512
FF_TILE = 512
BLOCK = 640
CHUNK = 16
PART = 192
ENTRIES = 200
MIB = 1024 * 1024
epsilon = 1e-05
masked_score = -1e30
bf16 = jnp.bfloat16
f32 = jnp.float32


def dot(left, right):
    return jnp.dot(left, right, preferred_element_type=f32)


def dot_nt(left, right):
    return lax.dot_general(left, right, (((1,), (1,)), ((), ())), preferred_element_type=f32)


def dot_tn(left, right):
    return lax.dot_general(left, right, (((0,), (0,)), ((), ())), preferred_element_type=f32)


def normalized(values):
    centre = values - jnp.mean(values, -1, keepdims=True)
    inverse = lax.rsqrt(jnp.mean(centre * centre, -1, keepdims=True) + epsilon)
    return centre * inverse, inverse


def norm_back(upstream, normed, inverse, gain):
    scaled = upstream * gain
    back = inverse * (
        scaled
        - jnp.mean(scaled, -1, keepdims=True)
        - normed * jnp.mean(scaled * normed, -1, keepdims=True)
    )
    return back, jnp.sum(upstream * normed, 0, keepdims=True), jnp.sum(upstream, 0, keepdims=True)


def lower_lanes(shape):
    return lax.broadcasted_iota(jnp.int32, shape, 1) < HEAD


def parted(block):
    low = lower_lanes(block.shape)
    none = jnp.zeros_like(block)
    return jnp.concatenate([jnp.where(low, block, none), jnp.where(low, none, block)], 0)


def merged(block):
    rows = block.shape[0] // 2
    return jnp.where(lower_lanes((rows, PAIR)), block[:rows], block[rows:])


def self_softmax(queries, keys, allowed):
    scores = dot_nt(queries, keys) * HEAD ** (-0.5)
    scores = jnp.where(allowed, scores, masked_score)
    weights = jnp.exp(scores - jnp.max(scores, -1, keepdims=True))
    return weights * (1.0 / jnp.sum(weights, -1, keepdims=True))


def by_view(values, is_first, combine, neutral):
    first = combine(jnp.where(is_first, values, neutral), -1, keepdims=True)
    second = combine(jnp.where(is_first, neutral, values), -1, keepdims=True)
    return jnp.where(is_first, first, second)


def cross_softmax(queries, keys, kept, is_first):
    scores = dot_nt(queries, keys) * HEAD ** (-0.5)
    scores = jnp.where(kept, scores, masked_score)
    weights = jnp.exp(scores - by_view(scores, is_first, jnp.max, masked_score))
    return weights * (1.0 / by_view(weights, is_first, jnp.sum, 0.0))


def each_view(block, is_first):
    none = jnp.zeros_like(block)
    return jnp.concatenate([jnp.where(is_first, block, none), jnp.where(is_first, none, block)], 0)


def allowed_of(allowed_ref):
    allowed = allowed_ref[...] > 0.5
    return jnp.concatenate([allowed, allowed], 0)


def attention_kernel(
    tokens_ref, allowed_ref, memory_ref, keep_ref, w_qkv, w_out, w_q, w_kv, w_cross_out, gains,
    biases, a1_ref, q_ref, kv_ref, o_ref, h1_ref, a2_ref, qc_ref, kvc_ref, oc_ref, h2_ref, a3_ref,
):
    rows = q_ref.shape[0]
    width = tokens_ref.shape[1]
    values = tokens_ref[...].astype(f32)
    normed, _ = normalized(values)
    a1_ref[...] = (normed * gains[0:1] + biases[0:1]).astype(bf16)
    q_ref[...] = dot(a1_ref[:rows], w_qkv[:, :width]).astype(bf16)
    kv_ref[...] = dot(a1_ref[...], w_qkv[:, width:]).astype(bf16)
    allowed = allowed_of(allowed_ref)
    for at in range(0, width, PAIR):
        queries = parted(q_ref[:, at : at + PAIR])
        probs = self_softmax(queries, kv_ref[:, at : at + PAIR], allowed)
        mixed = dot(probs.astype(bf16), kv_ref[:, width + at : width + at + PAIR])
        o_ref[:, at : at + PAIR] = merged(mixed).astype(bf16)
    h1 = values[:rows] + dot(o_ref[...], w_out[...])
    h1_ref[...] = h1
    normed, _ = normalized(h1)
    a2_ref[...] = (normed * gains[1:2] + biases[1:2]).astype(bf16)
    qc_ref[...] = dot(a2_ref[...], w_q[...]).astype(bf16)
    kvc_ref[...] = dot(memory_ref[...], w_kv[...]).astype(bf16)
    shape = (2 * rows, memory_ref.shape[0])
    kept = jnp.broadcast_to(keep_ref[...], shape) > 0.5
    is_first = lax.broadcasted_iota(jnp.int32, shape, 1) < shape[1] // 2
    for at in range(0, width, PAIR):
        queries = parted(qc_ref[:, at : at + PAIR])
        probs = cross_softmax(queries, kvc_ref[:, at : at + PAIR], kept, is_first)
        mixed = dot(
            each_view(probs.astype(bf16), is_first), kvc_ref[:, width + at : width + at + PAIR]
        )
        oc_ref[:rows, at : at + PAIR] = merged(mixed[: 2 * rows]).astype(bf16)
        oc_ref[rows:, at : at + PAIR] = merged(mixed[2 * rows :]).astype(bf16)
    h2 = jnp.concatenate([h1, h1], 0) + dot(oc_ref[...], w_cross_out[...])
    h2_ref[...] = h2
    normed, _ = normalized(h2)
    a3_ref[...] = (normed * gains[2:3] + biases[2:3]).astype(bf16)


def attention(tokens_page, allowed, memory_rows, keep, weights, gains, biases):
    rows, width = allowed.shape[0], tokens_page.shape[1]
    shape = jax.ShapeDtypeStruct
    return pl.pallas_call(
        attention_kernel,
        out_shape=(
            shape((2 * rows, width), bf16),
            shape((rows, width), bf16),
            shape((2 * rows, 2 * width), bf16),
            shape((rows, width), bf16),
            shape((rows, width), f32),
            shape((rows, width), bf16),
            shape((rows, width), bf16),
            shape((memory_rows.shape[0], 2 * width), bf16),
            shape((2 * rows, width), bf16),
            shape((2 * rows, width), f32),
            shape((2 * rows, width), bf16),
        ),
        compiler_params=pltpu.CompilerParams(vmem_limit_bytes=56 * MIB),
        cost_estimate=pl.CostEstimate(
            flops=20 * 10**9 // 10, bytes_accessed=24 * MIB, transcendentals=10**6
        ),
    )(tokens_page, allowed, memory_rows, keep, *weights, gains, biases)


def erf_parts(values):
    return 0.5 + 0.5 * lax.erf(values * (0.5**0.5))


def feed_forward_kernel(
    h2_ref, a3_ref, w_up, w_down, gains, biases, up_ref, act_ref, h3_ref, out_ref, fin_ref, total
):
    step = pl.program_id(0)

    @pl.when(step == 0)
    def _():
        total[...] = jnp.zeros_like(total)

    up = dot(a3_ref[...], w_up[...])
    up_ref[...] = up
    act = (up * erf_parts(up)).astype(bf16)
    act_ref[...] = act
    total[...] += dot(act, w_down[...])

    @pl.when(step == pl.num_programs(0) - 1)
    def _():
        h3 = h2_ref[...] + total[...]
        h3_ref[...] = h3
        out_ref[...] = h3.astype(bf16)
        normed, _ = normalized(h3)
        fin_ref[...] = (normed * gains[3:4] + biases[3:4]).astype(bf16)


def whole(*shape):
    return pl.BlockSpec(shape, lambda i: (0,) * len(shape))


def feed_forward(h2, a3, w_up, w_down, gains, biases):
    rows, width = h2.shape
    hidden = w_up.shape[1]
    shape = jax.ShapeDtypeStruct
    return pl.pallas_call(
        feed_forward_kernel,
        grid=(hidden // FF_TILE,),
        in_specs=[
            whole(rows, width),
            whole(rows, width),
            pl.BlockSpec((width, FF_TILE), lambda i: (0, i)),
            pl.BlockSpec((FF_TILE, width), lambda i: (i, 0)),
            whole(4, width),
            whole(4, width),
        ],
        out_specs=(
            pl.BlockSpec((rows, FF_TILE), lambda i: (0, i)),
            pl.BlockSpec((rows, FF_TILE), lambda i: (0, i)),
            whole(rows, width),
            whole(rows, width),
            whole(rows, width),
        ),
        out_shape=(
            shape((rows, hidden), f32),
            shape((rows, hidden), bf16),
            shape((rows, width), f32),
            shape((rows, width), bf16),
            shape((rows, width), bf16),
        ),
        scratch_shapes=[pltpu.VMEM((rows, width), f32)],
        compiler_params=pltpu.CompilerParams(vmem_limit_bytes=56 * MIB),
        cost_estimate=pl.CostEstimate(
            flops=4 * rows * width * hidden, bytes_accessed=24 * MIB, transcendentals=rows * hidden
        ),
    )(h2, a3, w_up, w_down, gains, biases)


def halves(block):
    middle = block.shape[1] // 2
    return block[:, :middle], block[:, middle:]


def feed_forward_back_kernel(
    core_ref, own_ref, other_ref, far_a, far_b, far_c, h3_ref, h2_ref, up_ref, w_up, w_down, gains, gh3_half_ref,
    gup_ref, gh2_ref, gh2_half_ref, vector_ref, gh3, gh3_low_ref, total,
):
    step = pl.program_id(0)
    core = core_ref[0]

    @pl.when(step == 0)
    def _():
        upstream = own_ref[...]
        for ref in (other_ref, far_a, far_b, far_c):
            upstream += ref[...].astype(f32)
        normed, inverse = normalized(h3_ref[...])
        back, gain, bias = norm_back(upstream, normed, inverse, gains[3:4])
        gh3[...] = back
        gh3_low_ref[...] = back.astype(bf16)
        for side, part in enumerate(halves(gh3_low_ref[...])):
            gh3_half_ref[side ^ core] = part
        vector_ref[...] = jnp.zeros_like(vector_ref)
        vector_ref[3:4] = gain
        vector_ref[7:8] = bias
        total[...] = jnp.zeros_like(total)

    grad = dot_nt(gh3_low_ref[...], w_down[...])
    up = up_ref[...]
    slope = erf_parts(up) + up * jnp.exp(-0.5 * up * up) * (0.5 / jnp.pi) ** 0.5
    gup = (grad * slope).astype(bf16)
    gup_ref[0] = gup
    total[...] += dot_nt(gup, w_up[...])

    @pl.when(step == pl.num_programs(0) - 1)
    def _():
        normed, inverse = normalized(h2_ref[...])
        back, gain, bias = norm_back(total[...], normed, inverse, gains[2:3])
        gh2 = gh3[...] + back
        gh2_ref[...] = gh2
        for side, part in enumerate(halves(gh2.astype(bf16))):
            gh2_half_ref[side ^ core] = part
        vector_ref[2:3] = gain
        vector_ref[6:7] = bias


def feed_forward_back(core, parts, h3, h2, up, w_up, w_down, gains):
    rows, width = h2.shape
    hidden = w_up.shape[1]
    tiles = hidden // FF_TILE
    shape = jax.ShapeDtypeStruct

    def all_of(*dims):
        return pl.BlockSpec(dims, lambda i, core: (0,) * len(dims))

    def half_tile(i, core):
        return ((i // (tiles // 2)) ^ core[0], 0, i % (tiles // 2))

    return pl.pallas_call(
        feed_forward_back_kernel,
        grid_spec=pltpu.PrefetchScalarGridSpec(
            num_scalar_prefetch=1,
            grid=(tiles,),
            in_specs=[
                *(all_of(rows, width) for _ in range(7)),
                pl.BlockSpec((rows, FF_TILE), lambda i, core: (0, i)),
                pl.BlockSpec((width, FF_TILE), lambda i, core: (0, i)),
                pl.BlockSpec((FF_TILE, width), lambda i, core: (i, 0)),
                all_of(4, width),
            ],
            out_specs=(
                all_of(2, rows, width // 2),
                pl.BlockSpec((1, rows, FF_TILE), half_tile),
                all_of(rows, width),
                all_of(2, rows, width // 2),
                all_of(8, width),
            ),
            scratch_shapes=[
                pltpu.VMEM((rows, width), f32),
                pltpu.VMEM((rows, width), bf16),
                pltpu.VMEM((rows, width), f32),
            ],
        ),
        out_shape=(
            shape((2, rows, width // 2), bf16),
            shape((2, rows, hidden // 2), bf16),
            shape((rows, width), f32),
            shape((2, rows, width // 2), bf16),
            shape((8, width), f32),
        ),
        compiler_params=pltpu.CompilerParams(vmem_limit_bytes=56 * MIB),
        cost_estimate=pl.CostEstimate(
            flops=4 * rows * width * hidden,
            bytes_accessed=24 * MIB,
            transcendentals=2 * rows * hidden,
        ),
    )(core, *parts, h3, h2, up, w_up, w_down, gains)


def attention_back_kernel(
    core_ref, gh2_ref, allowed_ref, keep_ref, kvc_ref, qc_ref, h1_ref, kv_ref, q_ref, w_cross_out, w_q,
    w_out, gains, gqc_ref, gkvc_ref, gh1_ref, gh1_half_ref, gq_ref, gkv_ref, vector_ref, goc, go, gqc,
    gh1_low,
):
    rows, width = q_ref.shape
    half = width // 2
    core = core_ref[0]
    scale = HEAD ** (-0.5)
    goc[...] = dot_nt(gh2_ref[...].astype(bf16), w_cross_out[...]).astype(bf16)
    shape = (2 * rows, kvc_ref.shape[0])
    kept = jnp.broadcast_to(keep_ref[...], shape) > 0.5
    is_first = lax.broadcasted_iota(jnp.int32, shape, 1) < shape[1] // 2
    for at in range(0, width, PAIR):
        here, there = slice(at, at + PAIR), slice(width + at, width + at + PAIR)
        slot = (at // half) ^ core
        low, high = slice(at % half, at % half + PAIR), slice(half + at % half, half + at % half + PAIR)
        queries = parted(qc_ref[:, here])
        probs = cross_softmax(queries, kvc_ref[:, here], kept, is_first)
        upstream = jnp.concatenate([parted(goc[:rows, here]), parted(goc[rows:, here])], 0)
        grad = dot_nt(upstream, kvc_ref[:, there])
        grad = jnp.where(is_first, grad[: 2 * rows], grad[2 * rows :])
        slope = probs * (grad - by_view(probs * grad, is_first, jnp.sum, 0.0))
        slope = slope.astype(bf16)
        change = (merged(dot(slope, kvc_ref[:, here])) * scale).astype(bf16)
        gqc[:, here] = change
        gqc_ref[slot, :, low] = change
        gkvc_ref[slot, :, low] = (dot_tn(slope, queries) * scale).astype(bf16)
        change = dot_tn(each_view(probs.astype(bf16), is_first), upstream)
        gkvc_ref[slot, :, high] = change.astype(bf16)
    normed, inverse = normalized(h1_ref[...])
    back, gain, bias = norm_back(dot_nt(gqc[...], w_q[...]), normed, inverse, gains[1:2])
    vector_ref[...] = jnp.zeros_like(vector_ref)
    vector_ref[1:2] = gain
    vector_ref[5:6] = bias
    gh1 = gh2_ref[:rows] + gh2_ref[rows:] + back
    gh1_ref[...] = gh1
    gh1_low[...] = gh1.astype(bf16)
    for side, part in enumerate(halves(gh1_low[...])):
        gh1_half_ref[side ^ core] = part
    go[...] = dot_nt(gh1_low[...], w_out[...]).astype(bf16)
    allowed = allowed_of(allowed_ref)
    for at in range(0, width, PAIR):
        here, there = slice(at, at + PAIR), slice(width + at, width + at + PAIR)
        slot = (at // half) ^ core
        low, high = slice(at % half, at % half + PAIR), slice(half + at % half, half + at % half + PAIR)
        queries = parted(q_ref[:, here])
        probs = self_softmax(queries, kv_ref[:, here], allowed)
        upstream = parted(go[:, here])
        grad = dot_nt(upstream, kv_ref[:, there])
        slope = probs * (grad - jnp.sum(probs * grad, -1, keepdims=True))
        slope = slope.astype(bf16)
        gq_ref[slot, :, low] = (merged(dot(slope, kv_ref[:, here])) * scale).astype(bf16)
        gkv_ref[slot, :, low] = (dot_tn(slope, queries) * scale).astype(bf16)
        gkv_ref[slot, :, high] = dot_tn(probs.astype(bf16), upstream).astype(bf16)


def scalar_first(count):
    return [pl.BlockSpec(memory_space=pltpu.SMEM)] + [
        pl.BlockSpec(memory_space=pltpu.VMEM) for _ in range(count)
    ]


def attention_back(core, *operands):
    rows, width = operands[7].shape
    shape = jax.ShapeDtypeStruct
    return pl.pallas_call(
        attention_back_kernel,
        in_specs=scalar_first(len(operands)),
        out_shape=(
            shape((2, rows, width // 2), bf16),
            shape((2, rows, width), bf16),
            shape((rows, width), f32),
            shape((2, rows, width // 2), bf16),
            shape((2, rows, width // 2), bf16),
            shape((2, 2 * rows, width), bf16),
            shape((8, width), f32),
        ),
        scratch_shapes=[
            pltpu.VMEM((2 * rows, width), bf16),
            pltpu.VMEM((rows, width), bf16),
            pltpu.VMEM((rows, width), bf16),
            pltpu.VMEM((rows, width), bf16),
        ],
        compiler_params=pltpu.CompilerParams(vmem_limit_bytes=56 * MIB),
        cost_estimate=pl.CostEstimate(
            flops=2 * 10**9, bytes_accessed=12 * MIB, transcendentals=10**6
        ),
    )(core, *operands)


def inputs_back_kernel(
    core_ref, tokens_ref, gh1_ref, gq_ref, gkv_ref, come_ref, gkvc_ref, come_cross_ref, w_qkv, w_kv,
    gains, tokens_grad_ref, memory_grad_ref, vector_ref, grads,
):
    core = core_ref[0]
    rows, width = gh1_ref.shape
    half = width // 2
    total = jnp.zeros((rows, width), f32)
    for side in range(2):
        slot, away = side ^ core, 1 - (side ^ core)
        pairs = gkv_ref[slot, :rows].astype(f32) + come_ref[away, rows:].astype(f32)
        pairs = pairs.astype(bf16)
        at = side * half
        total += dot_nt(gq_ref[slot], w_qkv[:, at : at + half])
        total += dot_nt(pairs[:, :half], w_qkv[:, width + at : width + at + half])
        total += dot_nt(pairs[:, half:], w_qkv[:, 2 * width + at : 2 * width + at + half])
    normed, inverse = normalized(tokens_ref[...].astype(f32))
    back, gain, bias = norm_back(total, normed, inverse, gains[0:1])
    tokens_grad_ref[...] = gh1_ref[...] + back
    vector_ref[...] = jnp.zeros_like(vector_ref)
    vector_ref[0:1] = gain
    vector_ref[4:5] = bias
    patches = gkvc_ref.shape[1]
    total = jnp.zeros((patches, width), f32)
    for side in range(2):
        slot, away = side ^ core, 1 - (side ^ core)
        pairs = gkvc_ref[slot].astype(f32) + come_cross_ref[away].astype(f32)
        pairs = pairs.astype(bf16)
        at = side * half
        total += dot_nt(pairs[:, :half], w_kv[:, at : at + half])
        total += dot_nt(pairs[:, half:], w_kv[:, width + at : width + at + half])
    grads[...] = total
    own = memory_grad_ref.shape[1]
    for view in range(2):
        start = pl.multiple_of(view * 2 * own + core * own, 8)
        memory_grad_ref[view] = grads[pl.ds(start, own)]


def inputs_back(core, *operands):
    rows, width = operands[1].shape
    patches = operands[5].shape[1]
    shape = jax.ShapeDtypeStruct
    return pl.pallas_call(
        inputs_back_kernel,
        in_specs=scalar_first(len(operands)),
        out_shape=(
            shape((rows, width), f32),
            shape((2, patches // 4, width), f32),
            shape((8, width), f32),
        ),
        scratch_shapes=[pltpu.VMEM((patches, width), f32)],
        compiler_params=pltpu.CompilerParams(vmem_limit_bytes=56 * MIB),
        cost_estimate=pl.CostEstimate(flops=10**9, bytes_accessed=14 * MIB, transcendentals=0),
    )(core, *operands)


def logits_kernel(rows_ref, readout_ref, bias_ref, own_ref, far_ref, stats_ref, kept):
    step = pl.program_id(0)
    width = rows_ref.shape[2]
    block = readout_ref.shape[0]
    near = own_ref.shape[1]

    @pl.when(step == 0)
    def _():
        for k in range(5):
            kept[k] = jnp.full(kept.shape[1:], masked_score if k in (0, 3) else 0.0, f32)

    def statistics(ref, start, begin):
        for at in range(0, near, CHUNK):
            here = slice(start + at, start + at + CHUNK)
            to = slice(begin + at, begin + at + CHUNK)
            first = [ref[0, here, c : c + 128] for c in range(0, block, 128)]
            second = [ref[1, here, c : c + 128] for c in range(0, block, 128)]
            top_first, top_second = kept[0, to], kept[3, to]
            new_first, new_second = top_first, top_second
            for a, b in zip(first, second):
                new_first = jnp.maximum(new_first, a)
                new_second = jnp.maximum(new_second, b)
            fade_first = jnp.exp(top_first - new_first)
            fade_second = jnp.exp(top_second - new_second)
            total_first = kept[1, to] * fade_first
            total_apart = kept[2, to] * fade_first
            total_second = kept[4, to] * fade_second
            for a, b in zip(first, second):
                weight = jnp.exp(a - new_first)
                total_first += weight
                total_apart += weight * (a - b)
                total_second += jnp.exp(b - new_second)
            kept[0, to], kept[1, to], kept[2, to] = new_first, total_first, total_apart
            kept[3, to], kept[4, to] = new_second, total_second

    pages = [(own_ref, 0)] + [(far_ref, at) for at in range(0, far_ref.shape[1], near)]
    for page, (ref, start) in enumerate(pages):
        begin = page * near
        rows = jnp.concatenate([rows_ref[v, begin : begin + near] for v in range(2)], 0)
        values = dot_nt(rows, readout_ref[...]) + bias_ref[...]
        for v in range(2):
            ref[v, start : start + near] = values[v * near : (v + 1) * near]
        if page:
            statistics(*pages[page - 1], begin - near)
    statistics(*pages[-1], begin)

    @pl.when(step == pl.num_programs(0) - 1)
    def _():
        top_first = jnp.max(kept[0], -1, keepdims=True)
        top_second = jnp.max(kept[3], -1, keepdims=True)
        fade_first = jnp.exp(kept[0] - top_first)
        fade_second = jnp.exp(kept[3] - top_second)
        stats = (
            top_first,
            jnp.sum(kept[1] * fade_first, -1, keepdims=True),
            jnp.sum(kept[2] * fade_first, -1, keepdims=True),
            top_second,
            jnp.sum(kept[4] * fade_second, -1, keepdims=True),
        )
        lane = lax.broadcasted_iota(jnp.int32, kept.shape[1:], 1)
        result = jnp.zeros(kept.shape[1:], f32)
        for k, stat in enumerate(stats):
            result = jnp.where(lane == k, stat, result)
        stats_ref[...] = result.T[:8]


def logits_and_stats(rows, readout_rows, bias):
    views, tokens, width = rows.shape
    entries = readout_rows.shape[0]
    near = tokens // SIDE
    shape = jax.ShapeDtypeStruct
    return pl.pallas_call(
        logits_kernel,
        out_shape=(
            shape((2, near, entries), f32),
            shape((2, tokens - near, entries), f32),
            shape((8, tokens), f32),
        ),
        grid=(entries // BLOCK,),
        in_specs=[
            whole(2, tokens, width),
            pl.BlockSpec((BLOCK, width), lambda i: (i, 0)),
            pl.BlockSpec((1, BLOCK), lambda i: (0, i)),
        ],
        out_specs=(
            pl.BlockSpec((2, near, BLOCK), lambda i: (0, 0, i)),
            pl.BlockSpec((2, tokens - near, BLOCK), lambda i: (0, 0, i)),
            whole(8, tokens),
        ),
        scratch_shapes=[pltpu.VMEM((5, tokens, 128), f32)],
        compiler_params=pltpu.CompilerParams(vmem_limit_bytes=58 * MIB),
        cost_estimate=pl.CostEstimate(
            flops=4 * tokens * entries * width,
            bytes_accessed=2 * entries * width + 8 * tokens * entries,
            transcendentals=2 * tokens * entries,
        ),
    )(rows, readout_rows, bias)


def merged_stats(near_ref, come_ref):
    tokens = near_ref.shape[2]
    page = tokens // SIDE
    is_first = lax.broadcasted_iota(jnp.int32, (8, tokens), 1) % page < page // 2
    parts = []
    for ref, flipped in ((near_ref, False), (come_ref, True)):
        for r in range(SIDE):
            part = ref[r]
            if r:
                part = pltpu.roll(part, r * page, 1)
            if flipped:
                part = jnp.where(
                    is_first,
                    pltpu.roll(part, tokens - page // 2, 1),
                    pltpu.roll(part, page // 2, 1),
                )
            parts.append(part)
    top_first = parts[0][0:1]
    top_second = parts[0][3:4]
    for part in parts[1:]:
        top_first = jnp.maximum(top_first, part[0:1])
        top_second = jnp.maximum(top_second, part[3:4])
    total_first = total_apart = total_second = jnp.zeros((1, tokens), f32)
    for part in parts:
        fade = jnp.exp(part[0:1] - top_first)
        total_first += part[1:2] * fade
        total_apart += part[2:3] * fade
        total_second += part[4:5] * jnp.exp(part[3:4] - top_second)
    first_lse = top_first + jnp.log(total_first)
    second_lse = top_second + jnp.log(total_second)
    return first_lse, second_lse, total_apart / total_first


def readout_back_kernel(
    begin, near_ref, come_ref, weight_ref, logits_ref, readout_ref, *refs
):
    stay_ref, give_ref, *term_ref, kept, slopes, total = refs
    step = pl.program_id(0)
    tokens = logits_ref.shape[1]
    block = readout_ref.shape[0]
    end = begin + tokens

    @pl.when(step == 0)
    def _():
        for k, row in enumerate(merged_stats(near_ref, come_ref)):
            kept[k] = jnp.broadcast_to(row, (128, row.shape[1])).T[begin:end]
        kept[3] = weight_ref[...]
        if term_ref:
            term_ref[0][...] = kept[3] * (kept[2] - kept[0] + kept[1])
        total[...] = jnp.zeros_like(total)

    def derivatives(start, size):
        for at in range(start, start + size, CHUNK):
            here = slice(at, at + CHUNK)
            first_lse, second_lse, apart, weight = (kept[k, here] for k in range(4))
            for c in range(0, block, 128):
                first = logits_ref[0, here, c : c + 128]
                second = logits_ref[1, here, c : c + 128]
                first_prob = jnp.exp(first - first_lse) * weight
                second_prob = jnp.exp(second - second_lse) * weight
                slopes[0, here, c : c + 128] = (first_prob * (first - second - apart)).astype(bf16)
                slopes[1, here, c : c + 128] = (second_prob - first_prob).astype(bf16)

    part = PART
    derivatives(0, part)
    for at in range(0, tokens, part):
        rows = jnp.concatenate([slopes[v, at : at + part] for v in range(2)], 0)
        result = dot(rows, readout_ref[...])
        if at + part < tokens:
            derivatives(at + part, part)
        for v in range(2):
            total[v * tokens + at : v * tokens + at + part] += result[v * part : (v + 1) * part]

    @pl.when(step == pl.num_programs(0) - 1)
    def _():
        pages, views, rows, width = stay_ref.shape
        for p in range(pages):
            for v in range(views):
                at = v * tokens + p * 2 * rows
                stay_ref[p, v] = total[at : at + rows]
                give_ref[p, v] = total[at + rows : at + 2 * rows].astype(bf16)


def readout_back(stats_near, stats_come, weight, logits, readout_rows, begin):
    views, tokens, entries = logits.shape
    all_tokens = stats_near.shape[2]
    width = readout_rows.shape[1]
    rows = all_tokens // SIDE // 2
    pages = tokens // rows // 2
    shape = jax.ShapeDtypeStruct
    out_shape = [
        shape((pages, 2, rows, width), f32),
        shape((pages, 2, rows, width), bf16),
    ]
    out_specs = [whole(pages, 2, rows, width), whole(pages, 2, rows, width)]
    if begin == 0:
        out_shape.append(shape((tokens, 128), f32))
        out_specs.append(whole(tokens, 128))
    return pl.pallas_call(
        partial(readout_back_kernel, begin),
        out_shape=tuple(out_shape),
        grid=(entries // BLOCK,),
        in_specs=[
            whole(SIDE, 8, all_tokens),
            whole(SIDE, 8, all_tokens),
            whole(tokens, 128),
            pl.BlockSpec((2, tokens, BLOCK), lambda i: (0, 0, i)),
            pl.BlockSpec((BLOCK, width), lambda i: (i, 0)),
        ],
        out_specs=tuple(out_specs),
        scratch_shapes=[
            pltpu.VMEM((4, tokens, 128), f32),
            pltpu.VMEM((2, tokens, BLOCK), bf16),
            pltpu.VMEM((2 * tokens, width), f32),
        ],
        compiler_params=pltpu.CompilerParams(vmem_limit_bytes=58 * MIB),
        cost_estimate=pl.CostEstimate(
            flops=4 * tokens * entries * width,
            bytes_accessed=2 * entries * width + 8 * tokens * entries,
            transcendentals=2 * tokens * entries,
        ),
    )(stats_near, stats_come, weight, logits, readout_rows)


def swapped(block):
    return lax.ppermute(block, "mem", [(0, 1), (1, 0)])


def along_line(block, distance):
    route = [(d, d // SIDE * SIDE + (d - distance) % SIDE) for d in range(CHIPS)]
    return lax.ppermute(block, "dp", route)


def lines(stride, core):
    starts = [d for d in range(CHIPS) if (d // stride) % SIDE == 0]
    return [[2 * (start + stride * k) + core for k in range(SIDE)] for start in starts]


def groups_of(strides):
    return lines(strides[0], 0) + lines(strides[1], 1)


def line_sum(part, strides):
    parts = part.reshape(SIDE, -1, part.shape[-1])
    chip, core = lax.axis_index("dp"), lax.axis_index("mem")
    digit = jnp.where(core == 0, chip // strides[0], chip // strides[1]) % SIDE
    come = []
    for r in range(1, SIDE):
        route = []
        for d in range(CHIPS):
            for m, stride in enumerate(strides):
                own = d // stride % SIDE
                to = d + ((own + r) % SIDE - own) * stride
                route.append((2 * d + m, 2 * to + m))
        give = lax.dynamic_index_in_dim(parts, (digit + r) % SIDE, 0, False)
        come.append(lax.ppermute(give, ("dp", "mem"), route))
    total = lax.dynamic_index_in_dim(parts, digit, 0, False).astype(f32)
    for block in come:
        total += block.astype(f32)
    return total


def first_sum(bucket):
    flat = bucket.reshape(CHIPS * ROWS, bucket.shape[-1])
    return lax.psum_scatter(
        flat, ("dp", "mem"), axis_index_groups=groups_of((1, 4)), scatter_dimension=0, tiled=True
    )


def last_sums(part):
    return line_sum(line_sum(part, (4, 16)).astype(bf16), (16, 1))


def outer_kernel(shapes, core_ref, *refs):
    n_in = 4 * len(shapes)
    inputs, out_ref, turned = refs[:n_in], refs[n_in], refs[n_in + 1 :]
    step = pl.program_id(0)
    core = core_ref[0]

    def place(chip):
        z, y, x = chip // 16, (chip // 4) % 4, chip % 4
        return jnp.where(core == 0, x * 16 + y * 4 + z, y * 16 + z * 4 + x)

    first = 0
    for i, (groups, columns, shared) in enumerate(shapes):
        left_a, left_b, right_a, right_b = inputs[4 * i : 4 * i + 4]
        tiles = columns // TILE
        low, high = first, first + groups * tiles
        first = high

        @pl.when(step == low)
        def _(left_a=left_a, left_b=left_b, to=turned[i], groups=groups):
            wide = left_a.shape[1]
            for start in range(0, wide, 1024):
                both = jnp.concatenate(
                    [left_a[:, start : start + 1024], left_b[:, start : start + 1024]], 0
                )
                flat = both.T
                if groups == 1:
                    to[0, start : start + 1024] = flat
                else:
                    per = ROWS * groups
                    for c in range(1024 // per):
                        chip = start // per + c
                        for g in range(groups):
                            at = c * per + g * ROWS
                            to[g, chip * ROWS : (chip + 1) * ROWS] = flat[at : at + ROWS]

        @pl.when((step >= low) & (step < high))
        def _(right_a=right_a, right_b=right_b, to=turned[i], tiles=tiles, low=low, shared=shared):
            at = step - low
            group = at // tiles
            tile = at - group * tiles
            column = pl.ds(pl.multiple_of(tile * TILE, TILE), TILE)
            if shared == 0:
                both = jnp.concatenate([right_a[0, :, column], right_b[:, column]], 0)
            else:
                here, there = right_a[0, :, column], right_b[1, :, column]
                if shared == 2:
                    middle = there.shape[0] // 2
                    there = jnp.concatenate([there[middle:], there[:middle]], 0)
                both = (here.astype(f32) + there.astype(f32)).astype(bf16)
            result = dot(to[group], both).astype(bf16)
            for chip in range(CHIPS):
                out_ref[place(chip)] = result[chip * ROWS : (chip + 1) * ROWS]


def outer_products(core, items):
    shapes, operands, scratch = [], [], []
    total = flops = 0
    for left, left_other, right, right_other, shared in items:
        groups = left.shape[1] // (ROWS * CHIPS)
        columns = right.shape[2]
        shapes.append((groups, columns, shared))
        operands += [left, left_other, right, right_other]
        depth = left.shape[0] + left_other.shape[0]
        scratch.append(pltpu.VMEM((groups, ROWS * CHIPS, depth), bf16))
        total += groups * columns
        flops += 2 * left.shape[1] * columns * depth
    return pl.pallas_call(
        partial(outer_kernel, tuple(shapes)),
        out_shape=jax.ShapeDtypeStruct((CHIPS, ROWS, total), bf16),
        grid_spec=pltpu.PrefetchScalarGridSpec(
            num_scalar_prefetch=1,
            grid=(total // TILE,),
            in_specs=[pl.BlockSpec(memory_space=pltpu.VMEM) for _ in operands],
            out_specs=pl.BlockSpec((CHIPS, ROWS, TILE), lambda i, core: (0, 0, i)),
            scratch_shapes=scratch,
        ),
        compiler_params=pltpu.CompilerParams(vmem_limit_bytes=56 * MIB),
        cost_estimate=pl.CostEstimate(
            flops=flops, bytes_accessed=CHIPS * ROWS * total * 2, transcendentals=0
        ),
    )(core, *operands)


def divide_kernel(grouped, core_ref, sums_ref, keep_ref, give_ref):
    core = core_ref[0]
    half = grouped // 2
    columns = sums_ref.shape[1]
    for ref, side in ((keep_ref, core), (give_ref, 1 - core)):
        if grouped:
            start = pl.ds(pl.multiple_of(side * half, 128), half)
            block = sums_ref[:, start]
            ref[:, :half] = block[: ROWS // 2]
            ref[:, half:grouped] = block[ROWS // 2 :]
        rows = pl.ds(pl.multiple_of(side * (ROWS // 2), 8), ROWS // 2)
        if columns > grouped:
            ref[:, grouped:] = sums_ref[rows, grouped:]


def divided(core, sums, grouped):
    shape = jax.ShapeDtypeStruct((ROWS // 2, sums.shape[1]), f32)
    return pl.pallas_call(
        partial(divide_kernel, grouped),
        in_specs=scalar_first(1),
        out_shape=(shape, shape),
    )(core, sums)


def assemble_kernel(layout, core_ref, keep_ref, come_ref, *outs):
    core = core_ref[0]
    for ref, side in ((keep_ref, core), (come_ref, 1 - core)):
        at = 0
        for out, (grouped, columns, span) in zip(outs, layout):
            part = span // 2
            if grouped:
                for g in range(2):
                    for h in range(2):
                        rows = slice(g * ROWS + h * ROWS // 2, g * ROWS + (h + 1) * ROWS // 2)
                        start = at + h * 2 * part + g * part
                        column = pl.ds(pl.multiple_of(side * part, 128), part)
                        out[rows, column] = ref[:, start : start + part]
                at += 4 * part
                continue
            for k in range(0, columns, span):
                column = pl.ds(pl.multiple_of(k + side * part, 128), part)
                out[:, column] = ref[:, at : at + part]
                at += part


def assembled(core, keep, come, layout):
    return pl.pallas_call(
        partial(assemble_kernel, tuple(layout)),
        in_specs=scalar_first(2),
        out_shape=tuple(
            jax.ShapeDtypeStruct((2 * ROWS if grouped else ROWS // 2, columns), f32)
            for grouped, columns, span in layout
        ),
    )(core, keep, come)


def on_device(
    tokens,
    memory,
    lengths,
    segments,
    key_mask,
    w_self_qkv,
    w_self_out,
    w_cross_q,
    w_cross_kv,
    w_cross_out,
    w_up,
    w_down,
    norm_gains,
    norm_biases,
    readout,
):
    tok_rows = tokens.shape[1]
    width = tokens.shape[2]
    half = lax.axis_index("mem")
    core = half.astype(jnp.int32).reshape(1)
    page_index = lax.axis_index("dp")
    patches = 2 * memory.shape[2]

    vocab_dev = readout.shape[1]
    readout_turned = jnp.pad(readout.T, ((0, ENTRIES - vocab_dev), (0, 0)))
    planes = [[d for d in range(CHIPS) if d % SIDE == x] for x in range(SIDE)]
    readout_part = lax.all_gather(
        readout_turned, "dp", axis=0, tiled=True, axis_index_groups=planes
    )
    is_entry = jnp.arange(readout_part.shape[0]) % ENTRIES < vocab_dev
    entry_bias = jnp.where(is_entry, 0.0, masked_score).astype(f32)[None]

    tokens_own = tokens[0]
    tokens_page = jnp.concatenate([tokens_own, swapped(tokens_own)], 0)
    memory_own = memory[:, 0]
    memory_come = swapped(memory_own)
    memory_rows = jnp.where(
        half == 0,
        jnp.concatenate([memory_own, memory_come], 1),
        jnp.concatenate([memory_come, memory_own], 1),
    ).reshape(2 * patches, width)
    mask_own = key_mask[0].astype(f32)
    mask_come = swapped(mask_own)
    mask_page = jnp.where(
        half == 0,
        jnp.concatenate([mask_own, mask_come]),
        jnp.concatenate([mask_come, mask_own]),
    )
    keep = jnp.tile(jnp.repeat(mask_page, 2), 2)[None]
    own_positions = jnp.arange(tok_rows) + half * tok_rows
    other_positions = jnp.arange(tok_rows) + (1 - half) * tok_rows
    key_positions = jnp.concatenate([own_positions, other_positions])
    cut = segments[0].reshape(2, tok_rows)
    own_segments = lax.dynamic_index_in_dim(cut, half, 0, False)
    other_segments = lax.dynamic_index_in_dim(cut, 1 - half, 0, False)
    key_segments = jnp.concatenate([own_segments, other_segments])
    allowed = (key_positions[None, :] <= own_positions[:, None]) & (
        key_segments[None, :] == own_segments[:, None]
    )
    allowed = allowed.astype(f32)
    count = jnp.sum(lengths).astype(f32)
    line = page_index // SIDE * SIDE + (page_index + jnp.arange(SIDE)) % SIDE
    valid = key_positions[None] < lengths[line][:, None]
    row_weight = (valid.astype(f32) / count).reshape(-1, 1)
    row_weight = jnp.broadcast_to(row_weight, (row_weight.shape[0], 128))

    weights = (w_self_qkv, w_self_out, w_cross_q, w_cross_kv, w_cross_out)
    a1, q, kv, o_self, h1, a2, qc, kvc, oc, h2, a3 = attention(
        tokens_page, allowed, memory_rows, keep, weights, norm_gains, norm_biases
    )
    up, act, h3, layer_out, final = feed_forward(h2, a3, w_up, w_down, norm_gains, norm_biases)
    final = final.reshape(2, tok_rows, width)
    near = jnp.stack([final] + [along_line(final, r) for r in range(1, SIDE)])
    final_line = jnp.stack([near, swapped(near)], 1).transpose(2, 0, 1, 3, 4)
    final_line = final_line.reshape(2, 2 * SIDE * tok_rows, width)
    o_self_other, a2_other, oc_other, a3_other, act_other = map(
        swapped, (o_self, a2, oc, a3, act)
    )

    own_logits, far_logits, stats = logits_and_stats(final_line, readout_part, entry_bias)
    stats = jnp.stack([stats] + [along_line(stats, r) for r in range(1, SIDE)])
    stats_come = swapped(stats)
    page = 2 * tok_rows
    far_stay, far_give = readout_back(
        stats, stats_come, row_weight[page:], far_logits, readout_part, page
    )
    far = (far_stay + swapped(far_give).astype(f32)).astype(bf16)
    own_logits, far = lax.optimization_barrier((own_logits, far))
    far = [along_line(far[r - 1], -r) for r in range(1, SIDE)]
    own_stay, own_give, terms = readout_back(
        stats, stats_come, row_weight[:page], own_logits, readout_part, 0
    )
    terms = terms[:, 0].reshape(2, tok_rows).sum(1)
    loss = (terms[0] + terms[1]).reshape(1)
    grad_parts = [own_stay[0], swapped(own_give[0])] + far
    grad_parts = [part.reshape(2 * tok_rows, width) for part in grad_parts]

    gh3_half, gup_half, gh2, gh2_half, vectors_ff = feed_forward_back(
        core, grad_parts, h3, h2, up, w_up, w_down, norm_gains
    )
    first_bucket = outer_products(
        core,
        [
            (act, act_other, gh3_half, swapped(gh3_half[1]), 0),
            (a3, a3_other, gup_half, swapped(gup_half[1]), 0),
        ],
    )
    gh2, first_bucket = lax.optimization_barrier((gh2, first_bucket))
    first_part = first_sum(first_bucket)

    gqc_half, gkvc_half, gh1, gh1_half, gq_half, gkv_half, vectors_att = attention_back(
        core, gh2, allowed, keep, kvc, qc, h1, kv, q, w_cross_out, w_cross_q, w_self_out, norm_gains
    )
    gkv_come, gkvc_come = swapped(gkv_half), swapped(gkvc_half)
    middle = tok_rows
    second_bucket = outer_products(
        core,
        [
            (a1[:middle], a1[middle:], gq_half, swapped(gq_half[1]), 0),
            (a1[:middle], a1[middle:], gkv_half, gkv_come, 2),
            (o_self, o_self_other, gh1_half, swapped(gh1_half[1]), 0),
            (a2, a2_other, gqc_half, swapped(gqc_half[1]), 0),
            (memory_rows[:patches], memory_rows[patches:], gkvc_half, gkvc_come, 1),
            (oc, oc_other, gh2_half, swapped(gh2_half[1]), 0),
        ],
    )
    second_part = first_sum(second_bucket)
    tokens_grad, memory_grad, vectors_in = inputs_back(
        core, tokens_own, gh1, gq_half, gkv_half, gkv_come, gkvc_half, gkvc_come, w_self_qkv,
        w_cross_kv, norm_gains,
    )

    vectors = vectors_ff + vectors_att + vectors_in
    vectors = vectors.reshape(8, CHIPS, ROWS).transpose(1, 0, 2).reshape(CHIPS, 8 * ROWS)
    vectors = lax.all_to_all(vectors, "dp", 0, 0, tiled=True)
    first_part, vectors = lax.optimization_barrier((first_part, vectors))
    vectors = vectors.sum(0)
    vectors = (vectors + swapped(vectors)).reshape(8, 2, ROWS // 2)
    vectors = lax.dynamic_index_in_dim(vectors, half, 1, False)

    first_sums = last_sums(first_part)
    first_keep, first_give = divided(core, first_sums, 2 * width)
    weight_down, weight_up = assembled(
        core,
        first_keep,
        swapped(first_give),
        [(True, width, width), (False, 4 * width, 4 * width)],
    )
    second_part, first_sums = lax.optimization_barrier((second_part, first_sums))
    second_sums = last_sums(second_part)
    second_keep, second_give = divided(core, second_sums, 0)
    weight_qkv, weight_out, weight_q, weight_kv, weight_cross_out = assembled(
        core,
        second_keep,
        swapped(second_give),
        [(False, n * width, width) for n in (3, 1, 1, 2, 1)],
    )
    return (
        loss,
        layer_out.reshape(2, 1, tok_rows, width),
        tokens_grad[None],
        memory_grad[:, None],
        weight_qkv,
        weight_out,
        weight_q,
        weight_kv,
        weight_cross_out,
        weight_up,
        weight_down,
        vectors[:4],
        vectors[4:],
    )


def solution(mesh):
    in_specs = (
        P("dp", "mem", None),
        P(None, "dp", "mem", None),
        P(),
        P("dp", None),
        P("dp", "mem"),
        P(),
        P(),
        P(),
        P(),
        P(),
        P(),
        P(),
        P(),
        P(),
        P(None, ("dp", "mem")),
    )
    out_specs = (
        P("dp"),
        P(None, "dp", "mem", None),
        P("dp", "mem", None),
        P(None, "dp", "mem", None),
        P(("dp", "mem"), None),
        P(("dp", "mem"), None),
        P(("dp", "mem"), None),
        P(("dp", "mem"), None),
        P(("dp", "mem"), None),
        P(("dp", "mem"), None),
        P(("dp", "mem"), None),
        P(None, ("dp", "mem")),
        P(None, ("dp", "mem")),
    )
    return jax.shard_map(
        on_device, mesh=mesh, in_specs=in_specs, out_specs=out_specs, check_vma=False
    )
```

```python
from functools import partial

import jax
import jax.numpy as jnp
from jax import lax
from jax.experimental import pallas as pl
from jax.experimental.pallas import tpu as pltpu
from jax.sharding import PartitionSpec as P

HEAD = 64
PAIR = 2 * HEAD
SIDE = 4
CHIPS = SIDE * SIDE * SIDE
ROWS = 16
TILE = 512
FF_TILE = 512
BLOCK = 640
CHUNK = 16
PARTS = ((0, 1024), (1024, 2048), (2048, 3200))
ENTRIES = 200
MIB = 1024 * 1024
epsilon = 1e-05
masked_score = -1e30
bf16 = jnp.bfloat16
f32 = jnp.float32


def dot(left, right):
    return jnp.dot(left, right, preferred_element_type=f32)


def dot_nt(left, right):
    return lax.dot_general(left, right, (((1,), (1,)), ((), ())), preferred_element_type=f32)


def dot_tn(left, right):
    return lax.dot_general(left, right, (((0,), (0,)), ((), ())), preferred_element_type=f32)


def normalized(values):
    centre = values - jnp.mean(values, -1, keepdims=True)
    inverse = lax.rsqrt(jnp.mean(centre * centre, -1, keepdims=True) + epsilon)
    return centre * inverse, inverse


def norm_back(upstream, normed, inverse, gain):
    scaled = upstream * gain
    back = inverse * (
        scaled
        - jnp.mean(scaled, -1, keepdims=True)
        - normed * jnp.mean(scaled * normed, -1, keepdims=True)
    )
    return back, jnp.sum(upstream * normed, 0, keepdims=True), jnp.sum(upstream, 0, keepdims=True)


def lower_lanes(shape):
    return lax.broadcasted_iota(jnp.int32, shape, 1) < HEAD


def parted(block):
    low = lower_lanes(block.shape)
    none = jnp.zeros_like(block)
    return jnp.concatenate([jnp.where(low, block, none), jnp.where(low, none, block)], 0)


def merged(block):
    rows = block.shape[0] // 2
    return jnp.where(lower_lanes((rows, PAIR)), block[:rows], block[rows:])


def self_softmax(queries, keys, allowed):
    scores = dot_nt(queries, keys) * HEAD ** (-0.5)
    scores = jnp.where(allowed, scores, masked_score)
    weights = jnp.exp(scores - jnp.max(scores, -1, keepdims=True))
    return weights * (1.0 / jnp.sum(weights, -1, keepdims=True))


def by_view(values, is_first, combine, neutral):
    first = combine(jnp.where(is_first, values, neutral), -1, keepdims=True)
    second = combine(jnp.where(is_first, neutral, values), -1, keepdims=True)
    return jnp.where(is_first, first, second)


def cross_softmax(queries, keys, kept, is_first):
    scores = dot_nt(queries, keys) * HEAD ** (-0.5)
    scores = jnp.where(kept, scores, masked_score)
    weights = jnp.exp(scores - by_view(scores, is_first, jnp.max, masked_score))
    return weights * (1.0 / by_view(weights, is_first, jnp.sum, 0.0))


def each_view(block, is_first):
    none = jnp.zeros_like(block)
    return jnp.concatenate([jnp.where(is_first, block, none), jnp.where(is_first, none, block)], 0)


def allowed_of(allowed_ref):
    allowed = allowed_ref[...] > 0.5
    return jnp.concatenate([allowed, allowed], 0)


def attention_kernel(
    tokens_ref, allowed_ref, memory_ref, keep_ref, w_qkv, w_out, w_q, w_kv, w_cross_out, gains,
    biases, a1_ref, q_ref, kv_ref, o_ref, h1_ref, a2_ref, qc_ref, kvc_ref, oc_ref, h2_ref, a3_ref,
):
    rows = q_ref.shape[0]
    width = tokens_ref.shape[1]
    values = tokens_ref[...].astype(f32)
    normed, _ = normalized(values)
    a1_ref[...] = (normed * gains[0:1] + biases[0:1]).astype(bf16)
    q_ref[...] = dot(a1_ref[:rows], w_qkv[:, :width]).astype(bf16)
    kv_ref[...] = dot(a1_ref[...], w_qkv[:, width:]).astype(bf16)
    allowed = allowed_of(allowed_ref)
    for at in range(0, width, PAIR):
        queries = parted(q_ref[:, at : at + PAIR])
        probs = self_softmax(queries, kv_ref[:, at : at + PAIR], allowed)
        mixed = dot(probs.astype(bf16), kv_ref[:, width + at : width + at + PAIR])
        o_ref[:, at : at + PAIR] = merged(mixed).astype(bf16)
    h1 = values[:rows] + dot(o_ref[...], w_out[...])
    h1_ref[...] = h1
    normed, _ = normalized(h1)
    a2_ref[...] = (normed * gains[1:2] + biases[1:2]).astype(bf16)
    qc_ref[...] = dot(a2_ref[...], w_q[...]).astype(bf16)
    kvc_ref[...] = dot(memory_ref[...], w_kv[...]).astype(bf16)
    shape = (2 * rows, memory_ref.shape[0])
    kept = jnp.broadcast_to(keep_ref[...], shape) > 0.5
    is_first = lax.broadcasted_iota(jnp.int32, shape, 1) < shape[1] // 2
    for at in range(0, width, PAIR):
        queries = parted(qc_ref[:, at : at + PAIR])
        probs = cross_softmax(queries, kvc_ref[:, at : at + PAIR], kept, is_first)
        mixed = dot(
            each_view(probs.astype(bf16), is_first), kvc_ref[:, width + at : width + at + PAIR]
        )
        oc_ref[:rows, at : at + PAIR] = merged(mixed[: 2 * rows]).astype(bf16)
        oc_ref[rows:, at : at + PAIR] = merged(mixed[2 * rows :]).astype(bf16)
    h2 = jnp.concatenate([h1, h1], 0) + dot(oc_ref[...], w_cross_out[...])
    h2_ref[...] = h2
    normed, _ = normalized(h2)
    a3_ref[...] = (normed * gains[2:3] + biases[2:3]).astype(bf16)


def attention(tokens_page, allowed, memory_rows, keep, weights, gains, biases):
    rows, width = allowed.shape[0], tokens_page.shape[1]
    shape = jax.ShapeDtypeStruct
    return pl.pallas_call(
        attention_kernel,
        out_shape=(
            shape((2 * rows, width), bf16),
            shape((rows, width), bf16),
            shape((2 * rows, 2 * width), bf16),
            shape((rows, width), bf16),
            shape((rows, width), f32),
            shape((rows, width), bf16),
            shape((rows, width), bf16),
            shape((memory_rows.shape[0], 2 * width), bf16),
            shape((2 * rows, width), bf16),
            shape((2 * rows, width), f32),
            shape((2 * rows, width), bf16),
        ),
        compiler_params=pltpu.CompilerParams(vmem_limit_bytes=58 * MIB),
        cost_estimate=pl.CostEstimate(
            flops=20 * 10**9 // 10, bytes_accessed=24 * MIB, transcendentals=10**6
        ),
    )(tokens_page, allowed, memory_rows, keep, *weights, gains, biases)


def erf_parts(values):
    return 0.5 + 0.5 * lax.erf(values * (0.5**0.5))


def feed_forward_kernel(
    h2_ref, a3_ref, w_up, w_down, gains, biases, slope_ref, act_ref, h3_ref, out_ref, fin_ref, total
):
    step = pl.program_id(0)

    @pl.when(step == 0)
    def _():
        total[...] = jnp.zeros_like(total)

    up = dot(a3_ref[...], w_up[...])
    below = erf_parts(up)
    slope_ref[...] = below + up * jnp.exp(-0.5 * up * up) * (0.5 / jnp.pi) ** 0.5
    act = (up * below).astype(bf16)
    act_ref[...] = act
    total[...] += dot(act, w_down[...])

    @pl.when(step == pl.num_programs(0) - 1)
    def _():
        h3 = h2_ref[...] + total[...]
        h3_ref[...] = h3
        out_ref[...] = h3.astype(bf16)
        normed, _ = normalized(h3)
        fin_ref[...] = (normed * gains[3:4] + biases[3:4]).astype(bf16)


def whole(*shape):
    return pl.BlockSpec(shape, lambda i: (0,) * len(shape))


def feed_forward(h2, a3, w_up, w_down, gains, biases):
    rows, width = h2.shape
    hidden = w_up.shape[1]
    shape = jax.ShapeDtypeStruct
    return pl.pallas_call(
        feed_forward_kernel,
        grid=(hidden // FF_TILE,),
        in_specs=[
            whole(rows, width),
            whole(rows, width),
            pl.BlockSpec((width, FF_TILE), lambda i: (0, i)),
            pl.BlockSpec((FF_TILE, width), lambda i: (i, 0)),
            whole(4, width),
            whole(4, width),
        ],
        out_specs=(
            pl.BlockSpec((rows, FF_TILE), lambda i: (0, i)),
            pl.BlockSpec((rows, FF_TILE), lambda i: (0, i)),
            whole(rows, width),
            whole(rows, width),
            whole(rows, width),
        ),
        out_shape=(
            shape((rows, hidden), f32),
            shape((rows, hidden), bf16),
            shape((rows, width), f32),
            shape((rows, width), bf16),
            shape((rows, width), bf16),
        ),
        scratch_shapes=[pltpu.VMEM((rows, width), f32)],
        compiler_params=pltpu.CompilerParams(vmem_limit_bytes=58 * MIB),
        cost_estimate=pl.CostEstimate(
            flops=4 * rows * width * hidden, bytes_accessed=24 * MIB, transcendentals=rows * hidden
        ),
    )(h2, a3, w_up, w_down, gains, biases)


def halves(block):
    middle = block.shape[1] // 2
    return block[:, :middle], block[:, middle:]


def divide(core, block, keep_ref, give_ref):
    for side in range(2):

        @pl.when(core == side)
        def _(side=side):
            keep_ref[...] = halves(block)[side]
            give_ref[...] = halves(block)[1 - side]


def feed_forward_back_kernel(
    core_ref, own_ref, other_ref, far_a, far_b, far_c, h3_ref, h2_ref, slope_ref, w_up, w_down,
    gains, gh3_keep, gh3_give, gup_keep, gup_give, gh2_ref, gh2_keep, gh2_give, vector_ref, gh3, gh3_low_ref, total,
):
    step = pl.program_id(0)
    core = core_ref[0]

    @pl.when(step == 0)
    def _():
        upstream = own_ref[...]
        for ref in (other_ref, far_a, far_b, far_c):
            upstream += ref[...].astype(f32)
        normed, inverse = normalized(h3_ref[...])
        back, gain, bias = norm_back(upstream, normed, inverse, gains[3:4])
        gh3[...] = back
        gh3_low_ref[...] = back.astype(bf16)
        divide(core, gh3_low_ref[...], gh3_keep, gh3_give)
        vector_ref[...] = jnp.zeros_like(vector_ref)
        vector_ref[3:4] = gain
        vector_ref[7:8] = bias
        total[...] = jnp.zeros_like(total)

    grad = dot_nt(gh3_low_ref[...], w_down[...])
    gup = (grad * slope_ref[...]).astype(bf16)
    side = step // (pl.num_programs(0) // 2)

    @pl.when(side == core)
    def _():
        gup_keep[...] = gup

    @pl.when(side != core)
    def _():
        gup_give[...] = gup

    total[...] += dot_nt(gup, w_up[...])

    @pl.when(step == pl.num_programs(0) - 1)
    def _():
        normed, inverse = normalized(h2_ref[...])
        back, gain, bias = norm_back(total[...], normed, inverse, gains[2:3])
        gh2 = gh3[...] + back
        gh2_ref[...] = gh2
        divide(core, gh2.astype(bf16), gh2_keep, gh2_give)
        vector_ref[2:3] = gain
        vector_ref[6:7] = bias


def feed_forward_back(core, parts, h3, h2, slope, w_up, w_down, gains):
    rows, width = h2.shape
    hidden = w_up.shape[1]
    tiles = hidden // FF_TILE
    shape = jax.ShapeDtypeStruct

    def all_of(*dims):
        return pl.BlockSpec(dims, lambda i, core: (0,) * len(dims))

    middle = tiles // 2

    def half_tile(kept):
        def index(i, core):
            side = core[0] if kept else 1 - core[0]
            return (0, jnp.clip(i - side * middle, 0, middle - 1))

        return pl.BlockSpec((rows, FF_TILE), index)

    return pl.pallas_call(
        feed_forward_back_kernel,
        grid_spec=pltpu.PrefetchScalarGridSpec(
            num_scalar_prefetch=1,
            grid=(tiles,),
            in_specs=[
                *(all_of(rows, width) for _ in range(7)),
                pl.BlockSpec((rows, FF_TILE), lambda i, core: (0, i)),
                pl.BlockSpec((width, FF_TILE), lambda i, core: (0, i)),
                pl.BlockSpec((FF_TILE, width), lambda i, core: (i, 0)),
                all_of(4, width),
            ],
            out_specs=(
                all_of(rows, width // 2),
                all_of(rows, width // 2),
                half_tile(True),
                half_tile(False),
                all_of(rows, width),
                all_of(rows, width // 2),
                all_of(rows, width // 2),
                all_of(8, width),
            ),
            scratch_shapes=[
                pltpu.VMEM((rows, width), f32),
                pltpu.VMEM((rows, width), bf16),
                pltpu.VMEM((rows, width), f32),
            ],
        ),
        out_shape=(
            shape((rows, width // 2), bf16),
            shape((rows, width // 2), bf16),
            shape((rows, hidden // 2), bf16),
            shape((rows, hidden // 2), bf16),
            shape((rows, width), f32),
            shape((rows, width // 2), bf16),
            shape((rows, width // 2), bf16),
            shape((8, width), f32),
        ),
        compiler_params=pltpu.CompilerParams(vmem_limit_bytes=58 * MIB),
        cost_estimate=pl.CostEstimate(
            flops=4 * rows * width * hidden,
            bytes_accessed=24 * MIB,
            transcendentals=2 * rows * hidden,
        ),
    )(core, *parts, h3, h2, slope, w_up, w_down, gains)


def attention_back_kernel(
    core_ref, gh2_ref, allowed_ref, keep_ref, kvc_ref, qc_ref, h1_ref, kv_ref, q_ref, w_cross_out, w_q,
    w_out, gains, gh1_ref, mix_ref, pairs_ref, vector_ref, goc, go, gqc, gh1_low,
):
    rows, width = q_ref.shape
    half = width // 2
    core = core_ref[0]
    scale = HEAD ** (-0.5)
    goc[...] = dot_nt(gh2_ref[...].astype(bf16), w_cross_out[...]).astype(bf16)
    shape = (2 * rows, kvc_ref.shape[0])
    kept = jnp.broadcast_to(keep_ref[...], shape) > 0.5
    is_first = lax.broadcasted_iota(jnp.int32, shape, 1) < shape[1] // 2
    for at in range(0, width, PAIR):
        here, there = slice(at, at + PAIR), slice(width + at, width + at + PAIR)
        slot = (at // half) ^ core
        low, high = slice(at % half, at % half + PAIR), slice(half + at % half, half + at % half + PAIR)
        queries = parted(qc_ref[:, here])
        probs = cross_softmax(queries, kvc_ref[:, here], kept, is_first)
        upstream = jnp.concatenate([parted(goc[:rows, here]), parted(goc[rows:, here])], 0)
        grad = dot_nt(upstream, kvc_ref[:, there])
        grad = jnp.where(is_first, grad[: 2 * rows], grad[2 * rows :])
        slope = probs * (grad - by_view(probs * grad, is_first, jnp.sum, 0.0))
        slope = slope.astype(bf16)
        change = (merged(dot(slope, kvc_ref[:, here])) * scale).astype(bf16)
        gqc[:, here] = change
        mix_ref[slot, 2 * rows :, low] = change
        pairs_ref[slot, 2 * rows :, low] = (dot_tn(slope, queries) * scale).astype(bf16)
        change = dot_tn(each_view(probs.astype(bf16), is_first), upstream)
        pairs_ref[slot, 2 * rows :, high] = change.astype(bf16)
    normed, inverse = normalized(h1_ref[...])
    back, gain, bias = norm_back(dot_nt(gqc[...], w_q[...]), normed, inverse, gains[1:2])
    vector_ref[...] = jnp.zeros_like(vector_ref)
    vector_ref[1:2] = gain
    vector_ref[5:6] = bias
    gh1 = gh2_ref[:rows] + gh2_ref[rows:] + back
    gh1_ref[...] = gh1
    gh1_low[...] = gh1.astype(bf16)
    for side, part in enumerate(halves(gh1_low[...])):
        mix_ref[side ^ core, rows : 2 * rows] = part
    go[...] = dot_nt(gh1_low[...], w_out[...]).astype(bf16)
    allowed = allowed_of(allowed_ref)
    for at in range(0, width, PAIR):
        here, there = slice(at, at + PAIR), slice(width + at, width + at + PAIR)
        slot = (at // half) ^ core
        low, high = slice(at % half, at % half + PAIR), slice(half + at % half, half + at % half + PAIR)
        queries = parted(q_ref[:, here])
        probs = self_softmax(queries, kv_ref[:, here], allowed)
        upstream = parted(go[:, here])
        grad = dot_nt(upstream, kv_ref[:, there])
        slope = probs * (grad - jnp.sum(probs * grad, -1, keepdims=True))
        slope = slope.astype(bf16)
        mix_ref[slot, :rows, low] = (merged(dot(slope, kv_ref[:, here])) * scale).astype(bf16)
        pairs_ref[slot, : 2 * rows, low] = (dot_tn(slope, queries) * scale).astype(bf16)
        pairs_ref[slot, : 2 * rows, high] = dot_tn(probs.astype(bf16), upstream).astype(bf16)


def scalar_first(count):
    return [pl.BlockSpec(memory_space=pltpu.SMEM)] + [
        pl.BlockSpec(memory_space=pltpu.VMEM) for _ in range(count)
    ]


def attention_back(core, *operands):
    kvc, kv, q = operands[3], operands[6], operands[7]
    rows, width = q.shape
    shape = jax.ShapeDtypeStruct
    return pl.pallas_call(
        attention_back_kernel,
        in_specs=scalar_first(len(operands)),
        out_shape=(
            shape((rows, width), f32),
            shape((2, 3 * rows, width // 2), bf16),
            shape((2, kv.shape[0] + kvc.shape[0], width), bf16),
            shape((8, width), f32),
        ),
        scratch_shapes=[
            pltpu.VMEM((2 * rows, width), bf16),
            pltpu.VMEM((rows, width), bf16),
            pltpu.VMEM((rows, width), bf16),
            pltpu.VMEM((rows, width), bf16),
        ],
        compiler_params=pltpu.CompilerParams(vmem_limit_bytes=58 * MIB),
        cost_estimate=pl.CostEstimate(
            flops=2 * 10**9, bytes_accessed=12 * MIB, transcendentals=10**6
        ),
    )(core, *operands)


def inputs_back_kernel(
    core_ref, tokens_ref, gh1_ref, mix_ref, pairs_ref, come_ref, w_qkv, w_kv, gains,
    tokens_grad_ref, memory_grad_ref, vector_ref, grads,
):
    core = core_ref[0]
    rows, width = gh1_ref.shape
    half = width // 2
    total = jnp.zeros((rows, width), f32)
    for side in range(2):
        slot, away = side ^ core, 1 - (side ^ core)
        pairs = pairs_ref[slot, :rows].astype(f32) + come_ref[away, rows : 2 * rows].astype(f32)
        pairs = pairs.astype(bf16)
        at = side * half
        total += dot_nt(mix_ref[slot, :rows], w_qkv[:, at : at + half])
        total += dot_nt(pairs[:, :half], w_qkv[:, width + at : width + at + half])
        total += dot_nt(pairs[:, half:], w_qkv[:, 2 * width + at : 2 * width + at + half])
    normed, inverse = normalized(tokens_ref[...].astype(f32))
    back, gain, bias = norm_back(total, normed, inverse, gains[0:1])
    tokens_grad_ref[...] = gh1_ref[...] + back
    vector_ref[...] = jnp.zeros_like(vector_ref)
    vector_ref[0:1] = gain
    vector_ref[4:5] = bias
    patches = pairs_ref.shape[1] - 2 * rows
    total = jnp.zeros((patches, width), f32)
    for side in range(2):
        slot, away = side ^ core, 1 - (side ^ core)
        pairs = pairs_ref[slot, 2 * rows :].astype(f32) + come_ref[away, 2 * rows :].astype(f32)
        pairs = pairs.astype(bf16)
        at = side * half
        total += dot_nt(pairs[:, :half], w_kv[:, at : at + half])
        total += dot_nt(pairs[:, half:], w_kv[:, width + at : width + at + half])
    grads[...] = total
    own = memory_grad_ref.shape[1]
    for view in range(2):
        start = pl.multiple_of(view * 2 * own + core * own, 8)
        memory_grad_ref[view] = grads[pl.ds(start, own)]


def inputs_back(core, *operands):
    rows, width = operands[1].shape
    patches = operands[3].shape[1] - 2 * rows
    shape = jax.ShapeDtypeStruct
    return pl.pallas_call(
        inputs_back_kernel,
        in_specs=scalar_first(len(operands)),
        out_shape=(
            shape((rows, width), f32),
            shape((2, patches // 4, width), f32),
            shape((8, width), f32),
        ),
        scratch_shapes=[pltpu.VMEM((patches, width), f32)],
        compiler_params=pltpu.CompilerParams(vmem_limit_bytes=58 * MIB),
        cost_estimate=pl.CostEstimate(flops=10**9, bytes_accessed=14 * MIB, transcendentals=0),
    )(core, *operands)


def logits_kernel(rows_ref, readout_ref, bias_ref, logits_ref, stats_ref, kept):
    tokens = rows_ref.shape[1]
    rows = jnp.concatenate([rows_ref[0], rows_ref[1]], 0)

    def statistics(begin, end):
        spans = range(begin, end, 128)
        for at in range(0, tokens, CHUNK):
            here = slice(at, at + CHUNK)
            first = [logits_ref[0, 0, here, c : c + 128] for c in spans]
            second = [logits_ref[0, 1, here, c : c + 128] for c in spans]
            new_first, new_second = first[0], second[0]
            for a, b in zip(first[1:], second[1:]):
                new_first = jnp.maximum(new_first, a)
                new_second = jnp.maximum(new_second, b)
            total_first = total_apart = total_second = jnp.zeros((CHUNK, 128), f32)
            if begin:
                top_first, top_second = kept[0, here], kept[3, here]
                new_first = jnp.maximum(new_first, top_first)
                new_second = jnp.maximum(new_second, top_second)
                fade_first = jnp.exp(top_first - new_first)
                total_first = kept[1, here] * fade_first
                total_apart = kept[2, here] * fade_first
                total_second = kept[4, here] * jnp.exp(top_second - new_second)
            for a, b in zip(first, second):
                weight = jnp.exp(a - new_first)
                total_first += weight
                total_apart += weight * (a - b)
                total_second += jnp.exp(b - new_second)
            kept[0, here], kept[1, here], kept[2, here] = new_first, total_first, total_apart
            kept[3, here], kept[4, here] = new_second, total_second

    before = None
    for begin, end in PARTS:
        values = dot_nt(rows, readout_ref[begin:end]) + bias_ref[:, begin:end]
        for v in range(2):
            logits_ref[0, v, :, begin:end] = values[v * tokens : (v + 1) * tokens]
        if before:
            statistics(*before)
        before = begin, end
    statistics(*before)

    top_first = jnp.max(kept[0], -1, keepdims=True)
    top_second = jnp.max(kept[3], -1, keepdims=True)
    fade_first = jnp.exp(kept[0] - top_first)
    fade_second = jnp.exp(kept[3] - top_second)
    stats = (
        top_first,
        jnp.sum(kept[1] * fade_first, -1, keepdims=True),
        jnp.sum(kept[2] * fade_first, -1, keepdims=True),
        top_second,
        jnp.sum(kept[4] * fade_second, -1, keepdims=True),
    )
    lane = lax.broadcasted_iota(jnp.int32, kept.shape[1:], 1)
    result = jnp.zeros(kept.shape[1:], f32)
    for k, stat in enumerate(stats):
        result = jnp.where(lane == k, stat, result)
    stats_ref[0] = result.T[:8]


def once(*shape):
    return pl.BlockSpec(shape, lambda i: (0,) * len(shape), pipeline_mode=pl.Buffered(1))


def logits_and_stats(rows, readout_rows, bias):
    views, tokens, width = rows.shape
    entries = readout_rows.shape[0]
    page = tokens // SIDE
    shape = jax.ShapeDtypeStruct
    return pl.pallas_call(
        logits_kernel,
        out_shape=(
            shape((SIDE, 2, page, entries), f32),
            shape((SIDE, 8, page), f32),
        ),
        grid=(SIDE,),
        in_specs=[
            pl.BlockSpec((2, page, width), lambda i: (0, i, 0)),
            once(entries, width),
            once(1, entries),
        ],
        out_specs=(
            pl.BlockSpec((1, 2, page, entries), lambda i: (i, 0, 0, 0)),
            pl.BlockSpec((1, 8, page), lambda i: (i, 0, 0)),
        ),
        scratch_shapes=[pltpu.VMEM((5, page, 128), f32)],
        compiler_params=pltpu.CompilerParams(vmem_limit_bytes=58 * MIB),
        cost_estimate=pl.CostEstimate(
            flops=4 * tokens * entries * width,
            bytes_accessed=2 * entries * width + 8 * tokens * entries,
            transcendentals=2 * tokens * entries,
        ),
    )(rows, readout_rows, bias)


def merged_stats(near_ref, come_ref, slot):
    tokens = near_ref.shape[3]
    middle = tokens // 2
    parts = []
    for ref, flipped in ((near_ref, False), (come_ref, True)):
        for r in range(SIDE):
            part = ref[r, lax.rem(slot + SIDE - r, SIDE)]
            if flipped:
                part = jnp.concatenate([part[:, middle:], part[:, :middle]], 1)
            parts.append(part)
    top_first = parts[0][0:1]
    top_second = parts[0][3:4]
    for part in parts[1:]:
        top_first = jnp.maximum(top_first, part[0:1])
        top_second = jnp.maximum(top_second, part[3:4])
    total_first = total_apart = total_second = jnp.zeros((1, tokens), f32)
    for part in parts:
        fade = jnp.exp(part[0:1] - top_first)
        total_first += part[1:2] * fade
        total_apart += part[2:3] * fade
        total_second += part[4:5] * jnp.exp(part[3:4] - top_second)
    first_lse = top_first + jnp.log(total_first)
    second_lse = top_second + jnp.log(total_second)
    return first_lse, second_lse, total_apart / total_first


def readout_back_kernel(
    far, near_ref, come_ref, weight_ref, logits_ref, readout_ref, stay_ref, other_ref, kept, slopes
):
    step = pl.program_id(0)
    tokens = weight_ref.shape[1]
    rows = tokens // 2
    slot = lax.rem(step + 1, SIDE) if far else 0
    for k, row in enumerate(merged_stats(near_ref, come_ref, slot)):
        kept[k] = jnp.broadcast_to(row, (128, row.shape[1])).T
    kept[3] = weight_ref[0]

    def gradient(start, count):
        def derivatives(begin, end):
            for at in range(start, start + count, CHUNK):
                here = slice(at, at + CHUNK)
                first_lse, second_lse, apart, weight = (kept[k, here] for k in range(4))
                for c in range(begin, end, 128):
                    first = logits_ref[0, 0, here, c : c + 128]
                    second = logits_ref[0, 1, here, c : c + 128]
                    first_prob = jnp.exp(first - first_lse) * weight
                    second_prob = jnp.exp(second - second_lse) * weight
                    change = first_prob * (first - second - apart)
                    slopes[0, here, c : c + 128] = change.astype(bf16)
                    slopes[1, here, c : c + 128] = (second_prob - first_prob).astype(bf16)

        derivatives(*PARTS[0])
        total = None
        for i, (begin, end) in enumerate(PARTS):
            block = [slopes[v, start : start + count, begin:end] for v in range(2)]
            result = dot(jnp.concatenate(block, 0), readout_ref[begin:end])
            if i + 1 < len(PARTS):
                derivatives(*PARTS[i + 1])
            total = result if total is None else total + result
        return total

    if not far:
        total = gradient(0, rows)
        for v in range(2):
            stay_ref[0, v] = total[v * rows : (v + 1) * rows]
        other_ref[...] = kept[3] * (kept[2] - kept[0] + kept[1])
        return

    @pl.when(step < SIDE - 1)
    def _():
        total = gradient(0, tokens)
        for v in range(2):
            stay_ref[0, v] = total[v * tokens : v * tokens + rows]
            other_ref[0, v] = total[v * tokens + rows : (v + 1) * tokens].astype(bf16)

    @pl.when(step == SIDE - 1)
    def _():
        total = gradient(rows, rows)
        for v in range(2):
            other_ref[0, v] = total[v * rows : (v + 1) * rows].astype(bf16)


def readout_back(stats_near, stats_come, weight, logits, readout_rows, far):
    tokens, entries = logits.shape[2:]
    width = readout_rows.shape[1]
    rows = tokens // 2
    pages = SIDE if far else 1
    shape = jax.ShapeDtypeStruct
    block = (1, 2, rows, width)
    if far:
        out_shape = (
            shape((SIDE - 1, 2, rows, width), f32),
            shape((SIDE, 2, rows, width), bf16),
        )
        out_specs = (
            pl.BlockSpec(block, lambda i: (jnp.minimum(i, SIDE - 2), 0, 0, 0)),
            pl.BlockSpec(block, lambda i: (i, 0, 0, 0)),
        )
    else:
        out_shape = (shape(block, f32), shape((tokens, 128), f32))
        out_specs = (whole(*block), whole(tokens, 128))

    def page(i):
        return lax.rem(i + 1, SIDE) if far else i

    here = tokens if far else rows
    return pl.pallas_call(
        partial(readout_back_kernel, far),
        out_shape=out_shape,
        grid=(pages,),
        in_specs=[
            once(SIDE, SIDE, 8, tokens),
            once(SIDE, SIDE, 8, tokens),
            pl.BlockSpec((1, tokens, 128), lambda i: (page(i), 0, 0)),
            pl.BlockSpec((1, 2, here, entries), lambda i: (page(i), 0, 0, 0)),
            once(entries, width),
        ],
        out_specs=out_specs,
        scratch_shapes=[
            pltpu.VMEM((4, tokens, 128), f32),
            pltpu.VMEM((2, here, entries), bf16),
        ],
        compiler_params=pltpu.CompilerParams(vmem_limit_bytes=58 * MIB),
        cost_estimate=pl.CostEstimate(
            flops=4 * pages * here * entries * width,
            bytes_accessed=2 * entries * width + 8 * pages * here * entries,
            transcendentals=2 * pages * here * entries,
        ),
    )(stats_near, stats_come, weight, logits, readout_rows)


FIRST_AXES = ((1, 4), (4, 16), (16, 1))
SECOND_AXES = ((16, 1), (1, 4), (4, 16))


def swapped(block):
    return lax.ppermute(block, "mem", [(0, 1), (1, 0)])


def along_line(block, distance):
    route = [(d, d // SIDE * SIDE + (d - distance) % SIDE) for d in range(CHIPS)]
    return lax.ppermute(block, "dp", route)


def lines(stride, core):
    starts = [d for d in range(CHIPS) if (d // stride) % SIDE == 0]
    return [[2 * (start + stride * k) + core for k in range(SIDE)] for start in starts]


def line_sum(part, strides):
    parts = part.reshape(SIDE, -1, part.shape[-1])
    chip, core = lax.axis_index("dp"), lax.axis_index("mem")
    digit = jnp.where(core == 0, chip // strides[0], chip // strides[1]) % SIDE
    come = []
    for r in range(1, SIDE):
        route = []
        for d in range(CHIPS):
            for m, stride in enumerate(strides):
                own = d // stride % SIDE
                to = d + ((own + r) % SIDE - own) * stride
                route.append((2 * d + m, 2 * to + m))
        give = lax.dynamic_index_in_dim(parts, (digit + r) % SIDE, 0, False)
        come.append(lax.ppermute(give, ("dp", "mem"), route))
    total = lax.dynamic_index_in_dim(parts, digit, 0, False).astype(f32)
    for block in come:
        total += block.astype(f32)
    return total


def scattered_sum(bucket, strides):
    flat = bucket.reshape(CHIPS * ROWS, bucket.shape[-1])
    groups = lines(strides[0], 0) + lines(strides[1], 1)
    return lax.psum_scatter(
        flat, ("dp", "mem"), axis_index_groups=groups, scatter_dimension=0, tiled=True
    )


def last_sums(part, axes):
    return line_sum(line_sum(part, axes[1]).astype(bf16), axes[2])


def outer_kernel(items, orders, core_ref, *refs):
    n_in = 1 + max(max(item["left"] + item["right"]) for item in items)
    inputs, out_ref, turned = refs[:n_in], refs[n_in], refs[n_in + 1 :]
    step = pl.program_id(0)
    core = core_ref[0]

    def place(chip):
        at = [0, 0]
        for m in range(2):
            for stride in orders[m]:
                at[m] = at[m] * SIDE + chip // stride % SIDE
        return jnp.where(core == 0, at[0], at[1])

    def turn(item):
        to, groups = turned[item["turned"]], item["groups"]
        lefts = [inputs[k] for k in item["left"]]
        for start in range(0, lefts[0].shape[1], 1024):
            flat = jnp.concatenate([left[:, start : start + 1024] for left in lefts], 0).T
            if groups == 1:
                to[0, start : start + 1024] = flat
                continue
            per = ROWS * groups
            for c in range(1024 // per):
                chip = start // per + c
                for g in range(groups):
                    at = c * per + g * ROWS
                    to[g, chip * ROWS : (chip + 1) * ROWS] = flat[at : at + ROWS]

    def multiply(item):
        at = step - item["begin"]
        group = at // item["tiles"]
        column = pl.ds(pl.multiple_of((at - group * item["tiles"]) * TILE, TILE), TILE)
        mine, come = (inputs[k] for k in item["right"])
        rows = slice(item["row"], item["row"] + item["rows"])
        if item["shared"] == 0:
            here = mine[0, rows, column] if len(mine.shape) == 3 else mine[rows, column]
            both = jnp.concatenate([here, come[rows, column]], 0)
        else:
            here, there = mine[0, rows, column], come[1, rows, column]
            if item["shared"] == 2:
                middle = item["rows"] // 2
                there = jnp.concatenate([there[middle:], there[:middle]], 0)
            both = (here.astype(f32) + there.astype(f32)).astype(bf16)
        result = dot(turned[item["turned"]][group], both).astype(bf16)
        for chip in range(CHIPS):
            out_ref[place(chip)] = result[chip * ROWS : (chip + 1) * ROWS]

    for item in items:
        if item["first"]:
            pl.when(step == item["begin"])(partial(turn, item))
        pl.when((step >= item["begin"]) & (step < item["end"]))(partial(multiply, item))


def outer_products(core, products, axes):
    items, operands, scratch, known = [], [], [], {}
    total = flops = 0

    def operand(array):
        for k, other in enumerate(operands):
            if other is array:
                return k
        operands.append(array)
        return len(operands) - 1

    for lefts, right, come, row, rows, shared in products:
        left = tuple(operand(array) for array in lefts)
        groups = lefts[0].shape[1] // (ROWS * CHIPS)
        depth = sum(array.shape[0] for array in lefts)
        columns = right.shape[-1]
        first = left not in known
        if first:
            known[left] = len(scratch)
            scratch.append(pltpu.VMEM((groups, ROWS * CHIPS, depth), bf16))
        begin = total // TILE
        total += groups * columns
        flops += 2 * groups * ROWS * CHIPS * columns * depth
        items.append(
            {
                "left": left,
                "right": (operand(right), operand(come)),
                "turned": known[left],
                "first": first,
                "groups": groups,
                "tiles": columns // TILE,
                "begin": begin,
                "end": total // TILE,
                "row": row,
                "rows": rows,
                "shared": shared,
            }
        )
    return pl.pallas_call(
        partial(outer_kernel, items, tuple(zip(*axes))),
        out_shape=jax.ShapeDtypeStruct((CHIPS, ROWS, total), bf16),
        grid_spec=pltpu.PrefetchScalarGridSpec(
            num_scalar_prefetch=1,
            grid=(total // TILE,),
            in_specs=[pl.BlockSpec(memory_space=pltpu.VMEM) for _ in operands],
            out_specs=pl.BlockSpec((CHIPS, ROWS, TILE), lambda i, core: (0, 0, i)),
            scratch_shapes=scratch,
        ),
        compiler_params=pltpu.CompilerParams(vmem_limit_bytes=58 * MIB),
        cost_estimate=pl.CostEstimate(
            flops=flops, bytes_accessed=CHIPS * ROWS * total * 2, transcendentals=0
        ),
    )(core, *operands)


def divide_kernel(grouped, core_ref, sums_ref, keep_ref, give_ref):
    core = core_ref[0]
    half = grouped // 2
    columns = sums_ref.shape[1]
    for ref, side in ((keep_ref, core), (give_ref, 1 - core)):
        if grouped:
            start = pl.ds(pl.multiple_of(side * half, 128), half)
            block = sums_ref[:, start]
            ref[:, :half] = block[: ROWS // 2]
            ref[:, half:grouped] = block[ROWS // 2 :]
        rows = pl.ds(pl.multiple_of(side * (ROWS // 2), 8), ROWS // 2)
        if columns > grouped:
            ref[:, grouped:] = sums_ref[rows, grouped:]


def divided(core, sums, grouped):
    shape = jax.ShapeDtypeStruct((ROWS // 2, sums.shape[1]), f32)
    return pl.pallas_call(
        partial(divide_kernel, grouped),
        in_specs=scalar_first(1),
        out_shape=(shape, shape),
    )(core, sums)


def assemble_kernel(layout, core_ref, keep_ref, come_ref, *outs):
    core = core_ref[0]
    for ref, side in ((keep_ref, core), (come_ref, 1 - core)):
        at = 0
        for out, (grouped, columns, span) in zip(outs, layout):
            part = span // 2
            if grouped:
                for g in range(2):
                    for h in range(2):
                        rows = slice(g * ROWS + h * ROWS // 2, g * ROWS + (h + 1) * ROWS // 2)
                        start = at + h * 2 * part + g * part
                        column = pl.ds(pl.multiple_of(side * part, 128), part)
                        out[rows, column] = ref[:, start : start + part]
                at += 4 * part
                continue
            for k in range(0, columns, span):
                column = pl.ds(pl.multiple_of(k + side * part, 128), part)
                out[:, column] = ref[:, at : at + part]
                at += part


def assembled(core, keep, come, layout):
    return pl.pallas_call(
        partial(assemble_kernel, tuple(layout)),
        in_specs=scalar_first(2),
        out_shape=tuple(
            jax.ShapeDtypeStruct((2 * ROWS if grouped else ROWS // 2, columns), f32)
            for grouped, columns, span in layout
        ),
    )(core, keep, come)


def on_device(
    tokens,
    memory,
    lengths,
    segments,
    key_mask,
    w_self_qkv,
    w_self_out,
    w_cross_q,
    w_cross_kv,
    w_cross_out,
    w_up,
    w_down,
    norm_gains,
    norm_biases,
    readout,
):
    tok_rows = tokens.shape[1]
    width = tokens.shape[2]
    half = lax.axis_index("mem")
    core = half.astype(jnp.int32).reshape(1)
    page_index = lax.axis_index("dp")
    patches = 2 * memory.shape[2]

    vocab_dev = readout.shape[1]
    readout_turned = jnp.pad(readout.T, ((0, ENTRIES - vocab_dev), (0, 0)))
    planes = [[d for d in range(CHIPS) if d % SIDE == x] for x in range(SIDE)]
    readout_part = lax.all_gather(
        readout_turned, "dp", axis=0, tiled=True, axis_index_groups=planes
    )
    is_entry = jnp.arange(readout_part.shape[0]) % ENTRIES < vocab_dev
    entry_bias = jnp.where(is_entry, 0.0, masked_score).astype(f32)[None]

    tokens_own = tokens[0]
    tokens_page = jnp.concatenate([tokens_own, swapped(tokens_own)], 0)
    memory_own = memory[:, 0]
    memory_come = swapped(memory_own)
    memory_rows = jnp.where(
        half == 0,
        jnp.concatenate([memory_own, memory_come], 1),
        jnp.concatenate([memory_come, memory_own], 1),
    ).reshape(2 * patches, width)
    mask_own = key_mask[0].astype(f32)
    mask_come = swapped(mask_own)
    mask_page = jnp.where(
        half == 0,
        jnp.concatenate([mask_own, mask_come]),
        jnp.concatenate([mask_come, mask_own]),
    )
    keep = jnp.tile(jnp.repeat(mask_page, 2), 2)[None]
    own_positions = jnp.arange(tok_rows) + half * tok_rows
    other_positions = jnp.arange(tok_rows) + (1 - half) * tok_rows
    key_positions = jnp.concatenate([own_positions, other_positions])
    cut = segments[0].reshape(2, tok_rows)
    own_segments = lax.dynamic_index_in_dim(cut, half, 0, False)
    other_segments = lax.dynamic_index_in_dim(cut, 1 - half, 0, False)
    key_segments = jnp.concatenate([own_segments, other_segments])
    allowed = (key_positions[None, :] <= own_positions[:, None]) & (
        key_segments[None, :] == own_segments[:, None]
    )
    allowed = allowed.astype(f32)
    count = jnp.sum(lengths).astype(f32)
    line = page_index // SIDE * SIDE + (page_index + jnp.arange(SIDE)) % SIDE
    valid = key_positions[None] < lengths[line][:, None]
    row_weight = (valid.astype(f32) / count)[:, :, None]
    row_weight = jnp.broadcast_to(row_weight, row_weight.shape[:2] + (128,))

    weights = (w_self_qkv, w_self_out, w_cross_q, w_cross_kv, w_cross_out)
    a1, q, kv, o_self, h1, a2, qc, kvc, oc, h2, a3 = attention(
        tokens_page, allowed, memory_rows, keep, weights, norm_gains, norm_biases
    )
    slope, act, h3, layer_out, final = feed_forward(h2, a3, w_up, w_down, norm_gains, norm_biases)
    final = final.reshape(2, tok_rows, width)
    near = jnp.stack([final] + [along_line(final, r) for r in range(1, SIDE)])
    final_line = jnp.stack([near, swapped(near)], 1).transpose(2, 0, 1, 3, 4)
    final_line = final_line.reshape(2, 2 * SIDE * tok_rows, width)
    o_self_other, a2_other, oc_other, a3_other, act_other = map(
        swapped, (o_self, a2, oc, a3, act)
    )

    logits, stats = logits_and_stats(final_line, readout_part, entry_bias)
    stats = jnp.stack([stats] + [along_line(stats, r) for r in range(1, SIDE)])
    stats_come = swapped(stats)
    far_stay, give = readout_back(stats, stats_come, row_weight, logits, readout_part, True)
    come = swapped(give)
    far = (far_stay + come[: SIDE - 1].astype(f32)).astype(bf16)
    logits, far = lax.optimization_barrier((logits, far))
    far = [along_line(far[r - 1], -r) for r in range(1, SIDE)]
    own, terms = readout_back(stats, stats_come, row_weight, logits, readout_part, False)
    terms = terms[:, 0].reshape(2, tok_rows).sum(1)
    loss = (terms[0] + terms[1]).reshape(1)
    grad_parts = [part.reshape(2 * tok_rows, width) for part in [own[0], come[SIDE - 1]] + far]

    gh3_keep, gh3_give, gup_keep, gup_give, gh2, gh2_keep, gh2_give, vectors_ff = (
        feed_forward_back(core, grad_parts, h3, h2, slope, w_up, w_down, norm_gains)
    )
    both = 2 * tok_rows
    first_bucket = outer_products(
        core,
        [
            ((act, act_other), gh3_keep, swapped(gh3_give), 0, both, 0),
            ((a3, a3_other), gup_keep, swapped(gup_give), 0, both, 0),
        ],
        FIRST_AXES,
    )
    gh2, first_bucket = lax.optimization_barrier((gh2, first_bucket))
    first_part = scattered_sum(first_bucket, FIRST_AXES[0])

    gh1, mix, pairs, vectors_att = attention_back(
        core, gh2, allowed, keep, kvc, qc, h1, kv, q, w_cross_out, w_cross_q, w_self_out, norm_gains
    )
    mix_come, pairs_come = swapped(mix[1]), swapped(pairs)
    second_bucket = outer_products(
        core,
        [
            ((a1,), mix, mix_come, 0, tok_rows, 0),
            ((a1,), pairs, pairs_come, 0, both, 2),
            ((o_self, o_self_other), mix, mix_come, tok_rows, tok_rows, 0),
            ((a2, a2_other), mix, mix_come, both, tok_rows, 0),
            ((memory_rows,), pairs, pairs_come, both, 2 * patches, 1),
            ((oc, oc_other), gh2_keep, swapped(gh2_give), 0, both, 0),
        ],
        SECOND_AXES,
    )
    gh1, second_bucket = lax.optimization_barrier((gh1, second_bucket))
    second_part = scattered_sum(second_bucket, SECOND_AXES[0])
    tokens_grad, memory_grad, vectors_in = inputs_back(
        core, tokens_own, gh1, mix, pairs, pairs_come, w_self_qkv, w_cross_kv, norm_gains
    )

    vectors = vectors_ff + vectors_att + vectors_in
    vectors = vectors.reshape(8, CHIPS, ROWS).transpose(1, 0, 2).reshape(CHIPS, 8 * ROWS)
    for stride in (16, 4, 1):
        vectors = line_sum(vectors, (stride, stride))
    vectors = (vectors + swapped(vectors)).reshape(8, 2, ROWS // 2)
    vectors = lax.dynamic_index_in_dim(vectors, half, 1, False)

    first_sums = last_sums(first_part, FIRST_AXES)
    first_keep, first_give = divided(core, first_sums, 2 * width)
    weight_down, weight_up = assembled(
        core,
        first_keep,
        swapped(first_give),
        [(True, width, width), (False, 4 * width, 4 * width)],
    )
    second_part, first_sums = lax.optimization_barrier((second_part, first_sums))
    second_sums = last_sums(second_part, SECOND_AXES)
    second_keep, second_give = divided(core, second_sums, 0)
    weight_qkv, weight_out, weight_q, weight_kv, weight_cross_out = assembled(
        core,
        second_keep,
        swapped(second_give),
        [(False, n * width, width) for n in (3, 1, 1, 2, 1)],
    )
    return (
        loss,
        layer_out.reshape(2, 1, tok_rows, width),
        tokens_grad[None],
        memory_grad[:, None],
        weight_qkv,
        weight_out,
        weight_q,
        weight_kv,
        weight_cross_out,
        weight_up,
        weight_down,
        vectors[:4],
        vectors[4:],
    )


def solution(mesh):
    in_specs = (
        P("dp", "mem", None),
        P(None, "dp", "mem", None),
        P(),
        P("dp", None),
        P("dp", "mem"),
        P(),
        P(),
        P(),
        P(),
        P(),
        P(),
        P(),
        P(),
        P(),
        P(None, ("dp", "mem")),
    )
    out_specs = (
        P("dp"),
        P(None, "dp", "mem", None),
        P("dp", "mem", None),
        P(None, "dp", "mem", None),
        P(("dp", "mem"), None),
        P(("dp", "mem"), None),
        P(("dp", "mem"), None),
        P(("dp", "mem"), None),
        P(("dp", "mem"), None),
        P(("dp", "mem"), None),
        P(("dp", "mem"), None),
        P(None, ("dp", "mem")),
        P(None, ("dp", "mem")),
    )
    return jax.shard_map(
        on_device, mesh=mesh, in_specs=in_specs, out_specs=out_specs, check_vma=False
    )
```

```python
from functools import partial

import jax
import jax.numpy as jnp
from jax import lax
from jax.experimental import pallas as pl
from jax.experimental.pallas import tpu as pltpu
from jax.sharding import PartitionSpec as P

HEAD = 64
PAIR = 2 * HEAD
SIDE = 4
CHIPS = SIDE * SIDE * SIDE
ROWS = 16
TILE = 512
FF_TILE = 1024
BLOCK = 640
CHUNK = 16
PARTS = ((0, 1024), (1024, 2048), (2048, 3200))
ENTRIES = 200
MIB = 1024 * 1024
epsilon = 1e-05
masked_score = -1e30
bf16 = jnp.bfloat16
f32 = jnp.float32


def dot(left, right):
    return jnp.dot(left, right, preferred_element_type=f32)


def dot_nt(left, right):
    return lax.dot_general(left, right, (((1,), (1,)), ((), ())), preferred_element_type=f32)


def dot_tn(left, right):
    return lax.dot_general(left, right, (((0,), (0,)), ((), ())), preferred_element_type=f32)


def normalized(values):
    centre = values - jnp.mean(values, -1, keepdims=True)
    inverse = lax.rsqrt(jnp.mean(centre * centre, -1, keepdims=True) + epsilon)
    return centre * inverse, inverse


def norm_back(upstream, normed, inverse, gain):
    scaled = upstream * gain
    back = inverse * (
        scaled
        - jnp.mean(scaled, -1, keepdims=True)
        - normed * jnp.mean(scaled * normed, -1, keepdims=True)
    )
    return back, jnp.sum(upstream * normed, 0, keepdims=True), jnp.sum(upstream, 0, keepdims=True)


def lower_lanes(shape):
    return lax.broadcasted_iota(jnp.int32, shape, 1) < HEAD


def parted(block):
    low = lower_lanes(block.shape)
    none = jnp.zeros_like(block)
    return jnp.concatenate([jnp.where(low, block, none), jnp.where(low, none, block)], 0)


def merged(block):
    rows = block.shape[0] // 2
    return jnp.where(lower_lanes((rows, PAIR)), block[:rows], block[rows:])


def self_softmax(queries, keys, allowed):
    scores = dot_nt(queries, keys) * HEAD ** (-0.5)
    scores = jnp.where(allowed, scores, masked_score)
    weights = jnp.exp(scores - jnp.max(scores, -1, keepdims=True))
    return weights * (1.0 / jnp.sum(weights, -1, keepdims=True))


def by_view(values, is_first, combine, neutral):
    first = combine(jnp.where(is_first, values, neutral), -1, keepdims=True)
    second = combine(jnp.where(is_first, neutral, values), -1, keepdims=True)
    return jnp.where(is_first, first, second)


def cross_softmax(queries, keys, kept, is_first):
    scores = dot_nt(queries, keys) * HEAD ** (-0.5)
    scores = jnp.where(kept, scores, masked_score)
    weights = jnp.exp(scores - by_view(scores, is_first, jnp.max, masked_score))
    return weights * (1.0 / by_view(weights, is_first, jnp.sum, 0.0))


def each_view(block, is_first):
    none = jnp.zeros_like(block)
    return jnp.concatenate([jnp.where(is_first, block, none), jnp.where(is_first, none, block)], 0)


def allowed_of(allowed_ref):
    allowed = allowed_ref[...] > 0.5
    return jnp.concatenate([allowed, allowed], 0)


PACK = (0, 96, 192, 288, 480, 576)
SENT = (0, 96, 192, 288, 480, 672, 864, 960, 1056)


def attention_kernel(
    tokens_ref, allowed_ref, memory_ref, keep_ref, w_qkv, w_out, w_q, w_kv, w_cross_out, gains,
    biases, q_ref, kv_ref, h1_ref, qc_ref, kvc_ref, h2_ref, a3_ref, pack_ref, a1,
):
    rows = q_ref.shape[0]
    width = tokens_ref.shape[1]
    a1_rows, o_rows, a2_rows, oc_rows, memory_rows = map(slice, PACK[:-1], PACK[1:])
    first_rows, second_rows = slice(PACK[3], PACK[3] + rows), slice(PACK[3] + rows, PACK[4])
    values = tokens_ref[...].astype(f32)
    normed, _ = normalized(values)
    a1[...] = (normed * gains[0:1] + biases[0:1]).astype(bf16)
    pack_ref[a1_rows] = a1[:rows]
    pack_ref[memory_rows] = memory_ref[...]
    q_ref[...] = dot(a1[:rows], w_qkv[:, :width]).astype(bf16)
    kv_ref[...] = dot(a1[...], w_qkv[:, width:]).astype(bf16)
    allowed = allowed_of(allowed_ref)
    for at in range(0, width, PAIR):
        queries = parted(q_ref[:, at : at + PAIR])
        probs = self_softmax(queries, kv_ref[:, at : at + PAIR], allowed)
        mixed = dot(probs.astype(bf16), kv_ref[:, width + at : width + at + PAIR])
        pack_ref[o_rows, at : at + PAIR] = merged(mixed).astype(bf16)
    h1 = values[:rows] + dot(pack_ref[o_rows], w_out[...])
    h1_ref[...] = h1
    normed, _ = normalized(h1)
    pack_ref[a2_rows] = (normed * gains[1:2] + biases[1:2]).astype(bf16)
    qc_ref[...] = dot(pack_ref[a2_rows], w_q[...]).astype(bf16)
    kvc_ref[...] = dot(memory_ref[...], w_kv[...]).astype(bf16)
    shape = (2 * rows, memory_ref.shape[0])
    kept = jnp.broadcast_to(keep_ref[...], shape) > 0.5
    is_first = lax.broadcasted_iota(jnp.int32, shape, 1) < shape[1] // 2
    for at in range(0, width, PAIR):
        queries = parted(qc_ref[:, at : at + PAIR])
        probs = cross_softmax(queries, kvc_ref[:, at : at + PAIR], kept, is_first)
        mixed = dot(
            each_view(probs.astype(bf16), is_first), kvc_ref[:, width + at : width + at + PAIR]
        )
        pack_ref[first_rows, at : at + PAIR] = merged(mixed[: 2 * rows]).astype(bf16)
        pack_ref[second_rows, at : at + PAIR] = merged(mixed[2 * rows :]).astype(bf16)
    h2 = jnp.concatenate([h1, h1], 0) + dot(pack_ref[oc_rows], w_cross_out[...])
    h2_ref[...] = h2
    normed, _ = normalized(h2)
    a3_ref[...] = (normed * gains[2:3] + biases[2:3]).astype(bf16)


def attention(tokens_page, allowed, memory_rows, keep, weights, gains, biases):
    rows, width = allowed.shape[0], tokens_page.shape[1]
    shape = jax.ShapeDtypeStruct
    return pl.pallas_call(
        attention_kernel,
        out_shape=(
            shape((rows, width), bf16),
            shape((2 * rows, 2 * width), bf16),
            shape((rows, width), f32),
            shape((rows, width), bf16),
            shape((memory_rows.shape[0], 2 * width), bf16),
            shape((2 * rows, width), f32),
            shape((2 * rows, width), bf16),
            shape((PACK[-1], width), bf16),
        ),
        scratch_shapes=[pltpu.VMEM((2 * rows, width), bf16)],
        compiler_params=pltpu.CompilerParams(vmem_limit_bytes=58 * MIB),
        cost_estimate=pl.CostEstimate(
            flops=2 * 10**9, bytes_accessed=24 * MIB, transcendentals=10**6
        ),
    )(tokens_page, allowed, memory_rows, keep, *weights, gains, biases)


def erf_parts(values):
    return 0.5 + 0.5 * lax.erf(values * (0.5**0.5))


def feed_forward_kernel(
    h2_ref, a3_ref, w_up, w_down, gains, biases, slope_ref, act_ref, h3_ref, out_ref, fin_ref, total
):
    step = pl.program_id(0)

    @pl.when(step == 0)
    def _():
        total[...] = jnp.zeros_like(total)

    up = dot(a3_ref[...], w_up[...])
    below = erf_parts(up)
    slope_ref[...] = below + up * jnp.exp(-0.5 * up * up) * (0.5 / jnp.pi) ** 0.5
    act = (up * below).astype(bf16)
    act_ref[...] = act
    total[...] += dot(act, w_down[...])

    @pl.when(step == pl.num_programs(0) - 1)
    def _():
        h3 = h2_ref[...] + total[...]
        h3_ref[...] = h3
        out_ref[...] = h3.astype(bf16)
        normed, _ = normalized(h3)
        fin_ref[...] = (normed * gains[3:4] + biases[3:4]).astype(bf16)


def whole(*shape):
    return pl.BlockSpec(shape, lambda i: (0,) * len(shape))


def feed_forward(h2, a3, w_up, w_down, gains, biases):
    rows, width = h2.shape
    hidden = w_up.shape[1]
    shape = jax.ShapeDtypeStruct
    return pl.pallas_call(
        feed_forward_kernel,
        grid=(hidden // FF_TILE,),
        in_specs=[
            whole(rows, width),
            whole(rows, width),
            pl.BlockSpec((width, FF_TILE), lambda i: (0, i)),
            pl.BlockSpec((FF_TILE, width), lambda i: (i, 0)),
            whole(4, width),
            whole(4, width),
        ],
        out_specs=(
            pl.BlockSpec((rows, FF_TILE), lambda i: (0, i)),
            pl.BlockSpec((rows, FF_TILE), lambda i: (0, i)),
            whole(rows, width),
            whole(rows, width),
            whole(rows, width),
        ),
        out_shape=(
            shape((rows, hidden), f32),
            shape((rows, hidden), bf16),
            shape((rows, width), f32),
            shape((rows, width), bf16),
            shape((rows, width), bf16),
        ),
        scratch_shapes=[pltpu.VMEM((rows, width), f32)],
        compiler_params=pltpu.CompilerParams(vmem_limit_bytes=58 * MIB),
        cost_estimate=pl.CostEstimate(
            flops=4 * rows * width * hidden, bytes_accessed=24 * MIB, transcendentals=rows * hidden
        ),
    )(h2, a3, w_up, w_down, gains, biases)


def halves(block):
    middle = block.shape[1] // 2
    return block[:, :middle], block[:, middle:]


def divide(core, block, keep_ref, give_ref):
    for side in range(2):

        @pl.when(core == side)
        def _(side=side):
            keep_ref[...] = halves(block)[side]
            give_ref[...] = halves(block)[1 - side]


def feed_forward_back_kernel(
    core_ref, own_ref, other_ref, far_a, far_b, far_c, h3_ref, h2_ref, slope_ref, w_up, w_down,
    gains, gh3_keep, gh3_give, gup_keep, gup_give, gh2_ref, vector_ref, gh3, gh3_low_ref, total,
):
    step = pl.program_id(0)
    core = core_ref[0]

    @pl.when(step == 0)
    def _():
        upstream = own_ref[...]
        for ref in (other_ref, far_a, far_b, far_c):
            upstream += ref[...].astype(f32)
        normed, inverse = normalized(h3_ref[...])
        back, gain, bias = norm_back(upstream, normed, inverse, gains[3:4])
        gh3[...] = back
        gh3_low_ref[...] = back.astype(bf16)
        divide(core, gh3_low_ref[...], gh3_keep, gh3_give)
        vector_ref[...] = jnp.zeros_like(vector_ref)
        vector_ref[3:4] = gain
        vector_ref[7:8] = bias
        total[...] = jnp.zeros_like(total)

    grad = dot_nt(gh3_low_ref[...], w_down[...])
    gup = (grad * slope_ref[...]).astype(bf16)
    side = step // (pl.num_programs(0) // 2)

    @pl.when(side == core)
    def _():
        gup_keep[...] = gup

    @pl.when(side != core)
    def _():
        gup_give[...] = gup

    total[...] += dot_nt(gup, w_up[...])

    @pl.when(step == pl.num_programs(0) - 1)
    def _():
        normed, inverse = normalized(h2_ref[...])
        back, gain, bias = norm_back(total[...], normed, inverse, gains[2:3])
        gh2 = gh3[...] + back
        gh2_ref[...] = gh2
        vector_ref[2:3] = gain
        vector_ref[6:7] = bias


def feed_forward_back(core, parts, h3, h2, slope, w_up, w_down, gains):
    rows, width = h2.shape
    hidden = w_up.shape[1]
    tiles = hidden // FF_TILE
    shape = jax.ShapeDtypeStruct

    def all_of(*dims):
        return pl.BlockSpec(dims, lambda i, core: (0,) * len(dims))

    middle = tiles // 2

    def half_tile(kept):
        def index(i, core):
            side = core[0] if kept else 1 - core[0]
            return (0, jnp.clip(i - side * middle, 0, middle - 1))

        return pl.BlockSpec((rows, FF_TILE), index)

    return pl.pallas_call(
        feed_forward_back_kernel,
        grid_spec=pltpu.PrefetchScalarGridSpec(
            num_scalar_prefetch=1,
            grid=(tiles,),
            in_specs=[
                *(all_of(rows, width) for _ in range(7)),
                pl.BlockSpec((rows, FF_TILE), lambda i, core: (0, i)),
                pl.BlockSpec((width, FF_TILE), lambda i, core: (0, i)),
                pl.BlockSpec((FF_TILE, width), lambda i, core: (i, 0)),
                all_of(4, width),
            ],
            out_specs=(
                all_of(rows, width // 2),
                all_of(rows, width // 2),
                half_tile(True),
                half_tile(False),
                all_of(rows, width),
                all_of(8, width),
            ),
            scratch_shapes=[
                pltpu.VMEM((rows, width), f32),
                pltpu.VMEM((rows, width), bf16),
                pltpu.VMEM((rows, width), f32),
            ],
        ),
        out_shape=(
            shape((rows, width // 2), bf16),
            shape((rows, width // 2), bf16),
            shape((rows, hidden // 2), bf16),
            shape((rows, hidden // 2), bf16),
            shape((rows, width), f32),
            shape((8, width), f32),
        ),
        compiler_params=pltpu.CompilerParams(vmem_limit_bytes=58 * MIB),
        cost_estimate=pl.CostEstimate(
            flops=4 * rows * width * hidden,
            bytes_accessed=24 * MIB,
            transcendentals=2 * rows * hidden,
        ),
    )(core, *parts, h3, h2, slope, w_up, w_down, gains)


def attention_back_kernel(
    gh2_ref, allowed_ref, keep_ref, kvc_ref, qc_ref, h1_ref, kv_ref, q_ref, w_cross_out, w_q, w_out,
    gains, gh1_ref, gq_ref, gkv_ref, give_ref, gkvc_ref, vector_ref, sent_ref, goc, go, gqc,
    gh1_low,
):
    rows, width = q_ref.shape
    scale = HEAD ** (-0.5)
    sent_rows = list(map(slice, SENT[:-1], SENT[1:]))

    def pairs_of_heads():
        for number in range(2 * SIDE):
            at = number * PAIR
            yield sent_ref.at[number], slice(at, at + PAIR), slice(width + at, width + at + PAIR)

    gh2_low = gh2_ref[...].astype(bf16)
    goc[...] = dot_nt(gh2_low, w_cross_out[...]).astype(bf16)
    shape = (2 * rows, kvc_ref.shape[0])
    kept = jnp.broadcast_to(keep_ref[...], shape) > 0.5
    is_first = lax.broadcasted_iota(jnp.int32, shape, 1) < shape[1] // 2
    for to, here, there in pairs_of_heads():
        queries = parted(qc_ref[:, here])
        probs = cross_softmax(queries, kvc_ref[:, here], kept, is_first)
        upstream = jnp.concatenate([parted(goc[:rows, here]), parted(goc[rows:, here])], 0)
        grad = dot_nt(upstream, kvc_ref[:, there])
        grad = jnp.where(is_first, grad[: 2 * rows], grad[2 * rows :])
        slope = probs * (grad - by_view(probs * grad, is_first, jnp.sum, 0.0))
        slope = slope.astype(bf16)
        change = (merged(dot(slope, kvc_ref[:, here])) * scale).astype(bf16)
        gqc[:, here] = change
        to[sent_rows[2]] = change
        to[sent_rows[3]] = gh2_ref[:, here].astype(bf16)
        change = (dot_tn(slope, queries) * scale).astype(bf16)
        gkvc_ref[:, here] = change
        to[sent_rows[6]] = change
        change = dot_tn(each_view(probs.astype(bf16), is_first), upstream).astype(bf16)
        gkvc_ref[:, there] = change
        to[sent_rows[7]] = change
    normed, inverse = normalized(h1_ref[...])
    back, gain, bias = norm_back(dot_nt(gqc[...], w_q[...]), normed, inverse, gains[1:2])
    vector_ref[...] = jnp.zeros_like(vector_ref)
    vector_ref[1:2] = gain
    vector_ref[5:6] = bias
    gh1 = gh2_ref[:rows] + gh2_ref[rows:] + back
    gh1_ref[...] = gh1
    gh1_low[...] = gh1.astype(bf16)
    go[...] = dot_nt(gh1_low[...], w_out[...]).astype(bf16)
    allowed = allowed_of(allowed_ref)
    for to, here, there in pairs_of_heads():
        queries = parted(q_ref[:, here])
        probs = self_softmax(queries, kv_ref[:, here], allowed)
        upstream = parted(go[:, here])
        grad = dot_nt(upstream, kv_ref[:, there])
        slope = probs * (grad - jnp.sum(probs * grad, -1, keepdims=True))
        slope = slope.astype(bf16)
        change = (merged(dot(slope, kv_ref[:, here])) * scale).astype(bf16)
        gq_ref[:, here] = change
        to[sent_rows[0]] = change
        to[sent_rows[1]] = gh1_low[:, here]
        change = (dot_tn(slope, queries) * scale).astype(bf16)
        gkv_ref[:, here] = change[:rows]
        give_ref[:, here] = change[rows:]
        to[sent_rows[4]] = change
        change = dot_tn(probs.astype(bf16), upstream).astype(bf16)
        gkv_ref[:, there] = change[:rows]
        give_ref[:, there] = change[rows:]
        to[sent_rows[5]] = change


def scalar_first(count):
    return [pl.BlockSpec(memory_space=pltpu.SMEM)] + [
        pl.BlockSpec(memory_space=pltpu.VMEM) for _ in range(count)
    ]


def attention_back(*operands):
    kvc, kv, q = operands[3], operands[6], operands[7]
    rows, width = q.shape
    shape = jax.ShapeDtypeStruct
    return pl.pallas_call(
        attention_back_kernel,
        out_shape=(
            shape((rows, width), f32),
            shape((rows, width), bf16),
            shape((rows, 2 * width), bf16),
            shape((rows, 2 * width), bf16),
            shape(kvc.shape, bf16),
            shape((8, width), f32),
            shape((2 * SIDE, SENT[-1], PAIR), bf16),
        ),
        scratch_shapes=[
            pltpu.VMEM((2 * rows, width), bf16),
            pltpu.VMEM((rows, width), bf16),
            pltpu.VMEM((rows, width), bf16),
            pltpu.VMEM((rows, width), bf16),
        ],
        compiler_params=pltpu.CompilerParams(vmem_limit_bytes=58 * MIB),
        cost_estimate=pl.CostEstimate(
            flops=2 * 10**9, bytes_accessed=14 * MIB, transcendentals=10**6
        ),
    )(*operands)


def inputs_back_kernel(
    core_ref, tokens_ref, gh1_ref, gq_ref, gkv_ref, come_ref, gkvc_ref, come_cross_ref, w_qkv,
    w_kv, gains, tokens_grad_ref, memory_grad_ref, vector_ref, grads,
):
    core = core_ref[0]
    width = gh1_ref.shape[1]
    pairs = (gkv_ref[...].astype(f32) + come_ref[...].astype(f32)).astype(bf16)
    total = dot_nt(gq_ref[...], w_qkv[:, :width]) + dot_nt(pairs, w_qkv[:, width:])
    normed, inverse = normalized(tokens_ref[...].astype(f32))
    back, gain, bias = norm_back(total, normed, inverse, gains[0:1])
    tokens_grad_ref[...] = gh1_ref[...] + back
    vector_ref[...] = jnp.zeros_like(vector_ref)
    vector_ref[0:1] = gain
    vector_ref[4:5] = bias
    pairs = (gkvc_ref[...].astype(f32) + come_cross_ref[...].astype(f32)).astype(bf16)
    grads[...] = dot_nt(pairs, w_kv[...])
    own = memory_grad_ref.shape[1]
    for view in range(2):
        start = pl.multiple_of(view * 2 * own + core * own, 8)
        memory_grad_ref[view] = grads[pl.ds(start, own)]


def inputs_back(core, *operands):
    rows, width = operands[1].shape
    patches = operands[5].shape[0]
    shape = jax.ShapeDtypeStruct
    return pl.pallas_call(
        inputs_back_kernel,
        in_specs=scalar_first(len(operands)),
        out_shape=(
            shape((rows, width), f32),
            shape((2, patches // 4, width), f32),
            shape((8, width), f32),
        ),
        scratch_shapes=[pltpu.VMEM((patches, width), f32)],
        compiler_params=pltpu.CompilerParams(vmem_limit_bytes=58 * MIB),
        cost_estimate=pl.CostEstimate(flops=10**9, bytes_accessed=14 * MIB, transcendentals=0),
    )(core, *operands)


def logits_kernel(rows_ref, readout_ref, bias_ref, logits_ref, stats_ref, kept):
    tokens = rows_ref.shape[1]
    rows = jnp.concatenate([rows_ref[0], rows_ref[1]], 0)

    def statistics(begin, end):
        spans = range(begin, end, 128)
        for at in range(0, tokens, CHUNK):
            here = slice(at, at + CHUNK)
            first = [logits_ref[0, 0, here, c : c + 128] for c in spans]
            second = [logits_ref[0, 1, here, c : c + 128] for c in spans]
            new_first, new_second = first[0], second[0]
            for a, b in zip(first[1:], second[1:]):
                new_first = jnp.maximum(new_first, a)
                new_second = jnp.maximum(new_second, b)
            total_first = total_apart = total_second = jnp.zeros((CHUNK, 128), f32)
            if begin:
                top_first, top_second = kept[0, here], kept[3, here]
                new_first = jnp.maximum(new_first, top_first)
                new_second = jnp.maximum(new_second, top_second)
                fade_first = jnp.exp(top_first - new_first)
                total_first = kept[1, here] * fade_first
                total_apart = kept[2, here] * fade_first
                total_second = kept[4, here] * jnp.exp(top_second - new_second)
            for a, b in zip(first, second):
                weight = jnp.exp(a - new_first)
                total_first += weight
                total_apart += weight * (a - b)
                total_second += jnp.exp(b - new_second)
            kept[0, here], kept[1, here], kept[2, here] = new_first, total_first, total_apart
            kept[3, here], kept[4, here] = new_second, total_second

    before = None
    for begin, end in PARTS:
        values = dot_nt(rows, readout_ref[begin:end]) + bias_ref[:, begin:end]
        for v in range(2):
            logits_ref[0, v, :, begin:end] = values[v * tokens : (v + 1) * tokens]
        if before:
            statistics(*before)
        before = begin, end
    statistics(*before)

    top_first = jnp.max(kept[0], -1, keepdims=True)
    top_second = jnp.max(kept[3], -1, keepdims=True)
    fade_first = jnp.exp(kept[0] - top_first)
    fade_second = jnp.exp(kept[3] - top_second)
    stats = (
        top_first,
        jnp.sum(kept[1] * fade_first, -1, keepdims=True),
        jnp.sum(kept[2] * fade_first, -1, keepdims=True),
        top_second,
        jnp.sum(kept[4] * fade_second, -1, keepdims=True),
    )
    lane = lax.broadcasted_iota(jnp.int32, kept.shape[1:], 1)
    result = jnp.zeros(kept.shape[1:], f32)
    for k, stat in enumerate(stats):
        result = jnp.where(lane == k, stat, result)
    stats_ref[0] = result.T[:8]


def once(*shape):
    return pl.BlockSpec(shape, lambda i: (0,) * len(shape), pipeline_mode=pl.Buffered(1))


def logits_and_stats(rows, readout_rows, bias):
    views, tokens, width = rows.shape
    entries = readout_rows.shape[0]
    page = tokens // SIDE
    shape = jax.ShapeDtypeStruct
    return pl.pallas_call(
        logits_kernel,
        out_shape=(
            shape((SIDE, 2, page, entries), f32),
            shape((SIDE, 8, page), f32),
        ),
        grid=(SIDE,),
        in_specs=[
            pl.BlockSpec((2, page, width), lambda i: (0, i, 0)),
            once(entries, width),
            once(1, entries),
        ],
        out_specs=(
            pl.BlockSpec((1, 2, page, entries), lambda i: (i, 0, 0, 0)),
            pl.BlockSpec((1, 8, page), lambda i: (i, 0, 0)),
        ),
        scratch_shapes=[pltpu.VMEM((5, page, 128), f32)],
        compiler_params=pltpu.CompilerParams(vmem_limit_bytes=58 * MIB),
        cost_estimate=pl.CostEstimate(
            flops=4 * tokens * entries * width,
            bytes_accessed=2 * entries * width + 8 * tokens * entries,
            transcendentals=2 * tokens * entries,
        ),
    )(rows, readout_rows, bias)


def merged_stats(near_ref, come_ref, slot):
    tokens = near_ref.shape[3]
    middle = tokens // 2
    parts = []
    for ref, flipped in ((near_ref, False), (come_ref, True)):
        for r in range(SIDE):
            part = ref[r, lax.rem(slot + SIDE - r, SIDE)]
            if flipped:
                part = jnp.concatenate([part[:, middle:], part[:, :middle]], 1)
            parts.append(part)
    top_first = parts[0][0:1]
    top_second = parts[0][3:4]
    for part in parts[1:]:
        top_first = jnp.maximum(top_first, part[0:1])
        top_second = jnp.maximum(top_second, part[3:4])
    total_first = total_apart = total_second = jnp.zeros((1, tokens), f32)
    for part in parts:
        fade = jnp.exp(part[0:1] - top_first)
        total_first += part[1:2] * fade
        total_apart += part[2:3] * fade
        total_second += part[4:5] * jnp.exp(part[3:4] - top_second)
    first_lse = top_first + jnp.log(total_first)
    second_lse = top_second + jnp.log(total_second)
    return first_lse, second_lse, total_apart / total_first


def readout_back_kernel(
    far, near_ref, come_ref, weight_ref, logits_ref, readout_ref, stay_ref, other_ref, kept, slopes
):
    step = pl.program_id(0)
    tokens = weight_ref.shape[1]
    rows = tokens // 2
    slot = lax.rem(step + 1, SIDE) if far else 0
    for k, row in enumerate(merged_stats(near_ref, come_ref, slot)):
        kept[k] = jnp.broadcast_to(row, (128, row.shape[1])).T
    kept[3] = weight_ref[0]

    def gradient(start, count):
        def derivatives(begin, end):
            for at in range(start, start + count, CHUNK):
                here = slice(at, at + CHUNK)
                first_lse, second_lse, apart, weight = (kept[k, here] for k in range(4))
                for c in range(begin, end, 128):
                    first = logits_ref[0, 0, here, c : c + 128]
                    second = logits_ref[0, 1, here, c : c + 128]
                    first_prob = jnp.exp(first - first_lse) * weight
                    second_prob = jnp.exp(second - second_lse) * weight
                    change = first_prob * (first - second - apart)
                    slopes[0, here, c : c + 128] = change.astype(bf16)
                    slopes[1, here, c : c + 128] = (second_prob - first_prob).astype(bf16)

        derivatives(*PARTS[0])
        total = None
        for i, (begin, end) in enumerate(PARTS):
            block = [slopes[v, start : start + count, begin:end] for v in range(2)]
            result = dot(jnp.concatenate(block, 0), readout_ref[begin:end])
            if i + 1 < len(PARTS):
                derivatives(*PARTS[i + 1])
            total = result if total is None else total + result
        return total

    if not far:
        total = gradient(0, rows)
        for v in range(2):
            stay_ref[0, v] = total[v * rows : (v + 1) * rows]
        other_ref[...] = kept[3] * (kept[2] - kept[0] + kept[1])
        return

    @pl.when(step < SIDE - 1)
    def _():
        total = gradient(0, tokens)
        for v in range(2):
            stay_ref[0, v] = total[v * tokens : v * tokens + rows]
            other_ref[0, v] = total[v * tokens + rows : (v + 1) * tokens].astype(bf16)

    @pl.when(step == SIDE - 1)
    def _():
        total = gradient(rows, rows)
        for v in range(2):
            other_ref[0, v] = total[v * rows : (v + 1) * rows].astype(bf16)


def readout_back(stats_near, stats_come, weight, logits, readout_rows, far):
    tokens, entries = logits.shape[2:]
    width = readout_rows.shape[1]
    rows = tokens // 2
    pages = SIDE if far else 1
    shape = jax.ShapeDtypeStruct
    block = (1, 2, rows, width)
    if far:
        out_shape = (
            shape((SIDE - 1, 2, rows, width), f32),
            shape((SIDE, 2, rows, width), bf16),
        )
        out_specs = (
            pl.BlockSpec(block, lambda i: (jnp.minimum(i, SIDE - 2), 0, 0, 0)),
            pl.BlockSpec(block, lambda i: (i, 0, 0, 0)),
        )
    else:
        out_shape = (shape(block, f32), shape((tokens, 128), f32))
        out_specs = (whole(*block), whole(tokens, 128))

    def page(i):
        return lax.rem(i + 1, SIDE) if far else i

    here = tokens if far else rows
    return pl.pallas_call(
        partial(readout_back_kernel, far),
        out_shape=out_shape,
        grid=(pages,),
        in_specs=[
            once(SIDE, SIDE, 8, tokens),
            once(SIDE, SIDE, 8, tokens),
            pl.BlockSpec((1, tokens, 128), lambda i: (page(i), 0, 0)),
            pl.BlockSpec((1, 2, here, entries), lambda i: (page(i), 0, 0, 0)),
            once(entries, width),
        ],
        out_specs=out_specs,
        scratch_shapes=[
            pltpu.VMEM((4, tokens, 128), f32),
            pltpu.VMEM((2, here, entries), bf16),
        ],
        compiler_params=pltpu.CompilerParams(vmem_limit_bytes=58 * MIB),
        cost_estimate=pl.CostEstimate(
            flops=4 * pages * here * entries * width,
            bytes_accessed=2 * entries * width + 8 * pages * here * entries,
            transcendentals=2 * pages * here * entries,
        ),
    )(stats_near, stats_come, weight, logits, readout_rows)


FIRST_AXES = ((4, 16), (1, 1), (16, 4))
SECOND_AXES = ((4, 16), (16, 4))


def swapped(block):
    return lax.ppermute(block, "mem", [(0, 1), (1, 0)])


def along_line(block, distance):
    route = [(d, d // SIDE * SIDE + (d - distance) % SIDE) for d in range(CHIPS)]
    return lax.ppermute(block, "dp", route)


def lines(stride, core):
    starts = [d for d in range(CHIPS) if (d // stride) % SIDE == 0]
    return [[2 * (start + stride * k) + core for k in range(SIDE)] for start in starts]


def line_sum(part, strides):
    parts = part.reshape(SIDE, -1, part.shape[-1])
    chip, core = lax.axis_index("dp"), lax.axis_index("mem")
    digit = jnp.where(core == 0, chip // strides[0], chip // strides[1]) % SIDE
    come = []
    for r in range(1, SIDE):
        route = []
        for d in range(CHIPS):
            for m, stride in enumerate(strides):
                own = d // stride % SIDE
                to = d + ((own + r) % SIDE - own) * stride
                route.append((2 * d + m, 2 * to + m))
        give = lax.dynamic_index_in_dim(parts, (digit + r) % SIDE, 0, False)
        come.append(lax.ppermute(give, ("dp", "mem"), route))
    total = lax.dynamic_index_in_dim(parts, digit, 0, False).astype(f32)
    for block in come:
        total += block.astype(f32)
    return total


def scattered_sum(bucket, strides):
    flat = bucket.reshape(CHIPS * ROWS, bucket.shape[-1])
    groups = lines(strides[0], 0) + lines(strides[1], 1)
    return lax.psum_scatter(
        flat, ("dp", "mem"), axis_index_groups=groups, scatter_dimension=0, tiled=True
    )


def outer_kernel(items, orders, core_ref, *refs):
    inputs, out_ref, turned = refs[: 4 * len(items)], refs[4 * len(items)], refs[-len(items) :]
    step = pl.program_id(0)
    core = core_ref[0]

    def place(chip):
        at = [0, 0]
        for m in range(2):
            for stride in orders[m]:
                at[m] = at[m] * SIDE + chip // stride % SIDE
        return jnp.where(core == 0, at[0], at[1])

    def turn(lefts, to, groups):
        for start in range(0, lefts[0].shape[1], 1024):
            flat = jnp.concatenate([left[:, start : start + 1024] for left in lefts], 0).T
            if groups == 1:
                to[0, start : start + 1024] = flat
                continue
            per = ROWS * groups
            for c in range(1024 // per):
                chip = start // per + c
                for g in range(groups):
                    at = c * per + g * ROWS
                    to[g, chip * ROWS : (chip + 1) * ROWS] = flat[at : at + ROWS]

    def multiply(rights, to, begin, tiles):
        at = step - begin
        group = at // tiles
        column = pl.ds(pl.multiple_of((at - group * tiles) * TILE, TILE), TILE)
        both = jnp.concatenate([right[:, column] for right in rights], 0)
        result = dot(to[group], both).astype(bf16)
        for chip in range(CHIPS):
            out_ref[place(chip)] = result[chip * ROWS : (chip + 1) * ROWS]

    for k, (groups, tiles, begin, end) in enumerate(items):
        lefts, rights, to = inputs[4 * k : 4 * k + 2], inputs[4 * k + 2 : 4 * k + 4], turned[k]
        pl.when(step == begin)(partial(turn, lefts, to, groups))
        pl.when((step >= begin) & (step < end))(partial(multiply, rights, to, begin, tiles))


def outer_products(core, products, axes):
    items, scratch = [], []
    total = flops = 0
    for left, left_come, right, _ in products:
        groups = left.shape[1] // (ROWS * CHIPS)
        depth = left.shape[0] + left_come.shape[0]
        columns = right.shape[1]
        scratch.append(pltpu.VMEM((groups, ROWS * CHIPS, depth), bf16))
        begin = total // TILE
        total += groups * columns
        flops += 2 * groups * ROWS * CHIPS * columns * depth
        items.append((groups, columns // TILE, begin, total // TILE))
    operands = [array for product in products for array in product]
    return pl.pallas_call(
        partial(outer_kernel, tuple(items), tuple(zip(*axes))),
        out_shape=jax.ShapeDtypeStruct((CHIPS, ROWS, total), bf16),
        grid_spec=pltpu.PrefetchScalarGridSpec(
            num_scalar_prefetch=1,
            grid=(total // TILE,),
            in_specs=[pl.BlockSpec(memory_space=pltpu.VMEM) for _ in operands],
            out_specs=pl.BlockSpec((CHIPS, ROWS, TILE), lambda i, core: (0, 0, i)),
            scratch_shapes=scratch,
        ),
        compiler_params=pltpu.CompilerParams(vmem_limit_bytes=58 * MIB),
        cost_estimate=pl.CostEstimate(
            flops=flops, bytes_accessed=CHIPS * ROWS * total * 2, transcendentals=0
        ),
    )(core, *operands)


LINE = ROWS * SIDE
DEPTHS = tuple(
    2 * SIDE * (PACK[k + 1] - PACK[k]) // (2 if k == 4 else 1) for k in range(len(PACK) - 1)
)


def turn_kernel(orders, core_ref, packs_ref, out_ref):
    core = core_ref[0]
    start = 0
    for k, depth in enumerate(DEPTHS):
        numbers = range(0, 2 * SIDE, 2 if k == 4 else 1)
        blocks = [packs_ref[number, PACK[k] : PACK[k + 1]] for number in numbers]
        flat = jnp.concatenate(blocks, 0).T
        for line in range(SIDE * SIDE):
            z, y = line // SIDE, line % SIDE
            digit = {4: y, 16: z}
            at = [SIDE * digit[first] + digit[second] for first, second in orders]
            at = pl.multiple_of(jnp.where(core == 0, at[0], at[1]) * LINE, LINE)
            out_ref[pl.ds(at, LINE), start : start + depth] = flat[line * LINE : (line + 1) * LINE]
        start += depth


def turned_packs(core, packs, axes):
    width = packs.shape[2]
    return pl.pallas_call(
        partial(turn_kernel, tuple(zip(*axes))),
        in_specs=scalar_first(1),
        out_shape=jax.ShapeDtypeStruct((width, sum(DEPTHS)), bf16),
        compiler_params=pltpu.CompilerParams(vmem_limit_bytes=58 * MIB),
        cost_estimate=pl.CostEstimate(flops=0, bytes_accessed=20 * MIB, transcendentals=0),
    )(core, packs)


def line_products_kernel(turned_ref, come_ref, vectors_ref, out_ref, joint, plain, cross, wide):
    rows = SENT[1]

    @pl.when(pl.program_id(0) == 0)
    def _():
        def part(number, k):
            return come_ref[number, SENT[k] : SENT[k + 1]]

        def added(first, second):
            return (first.astype(f32) + second.astype(f32)).astype(bf16)

        for number in range(2 * SIDE):
            at = number * rows
            here = slice(at, at + rows)
            joint[here, :PAIR] = part(number, 0)
            for k in (4, 5):
                share = added(part(number, k)[:rows], part(number ^ 1, k)[rows:])
                joint[here, (k - 3) * PAIR : (k - 2) * PAIR] = share
            plain[here, :PAIR] = part(number, 1)
            plain[here, PAIR:] = part(number, 2)
            wide[2 * at : 2 * (at + rows)] = part(number, 3)
        for chip in range(SIDE):
            here = slice(chip * rows, (chip + 1) * rows)
            for k in (6, 7):
                column = slice((k - 6) * PAIR, (k - 5) * PAIR)
                cross[here, column] = added(part(2 * chip, k), part(2 * chip + 1, k))

    ends = [sum(DEPTHS[: k + 1]) for k in range(len(DEPTHS))]
    a1, o, a2, oc, memory = (
        turned_ref[:, end - depth : end] for end, depth in zip(ends, DEPTHS)
    )
    out_ref[:, : 3 * PAIR] = dot(a1, joint[...]).astype(bf16)
    out_ref[:, 3 * PAIR : 4 * PAIR] = dot(o, plain[:, :PAIR]).astype(bf16)
    out_ref[:, 4 * PAIR : 5 * PAIR] = dot(a2, plain[:, PAIR:]).astype(bf16)
    out_ref[:, 5 * PAIR : 7 * PAIR] = dot(memory, cross[...]).astype(bf16)
    out_ref[:, 7 * PAIR : 8 * PAIR] = dot(oc, wide[...]).astype(bf16)
    out_ref[:, 8 * PAIR :] = vectors_ref[...]


def line_products(turned, come, vectors):
    width, depth = turned.shape
    block = 256
    columns = 9 * PAIR
    return pl.pallas_call(
        line_products_kernel,
        grid=(width // block,),
        in_specs=[
            pl.BlockSpec((block, depth), lambda i: (i, 0)),
            once(2 * SIDE, SENT[-1], PAIR),
            pl.BlockSpec((block, PAIR), lambda i: (i, 0)),
        ],
        out_specs=pl.BlockSpec((block, columns), lambda i: (i, 0)),
        out_shape=jax.ShapeDtypeStruct((width, columns), bf16),
        scratch_shapes=[
            pltpu.VMEM((DEPTHS[0], 3 * PAIR), bf16),
            pltpu.VMEM((DEPTHS[1], 2 * PAIR), bf16),
            pltpu.VMEM((DEPTHS[4], 2 * PAIR), bf16),
            pltpu.VMEM((DEPTHS[3], PAIR), bf16),
        ],
        compiler_params=pltpu.CompilerParams(vmem_limit_bytes=58 * MIB),
        cost_estimate=pl.CostEstimate(
            flops=2 * 10**9, bytes_accessed=14 * MIB, transcendentals=0
        ),
    )(turned, come, vectors)


def collect_kernel(come_ref, *outs):
    qkv, out, q, kv, cross_out, vectors = outs
    targets = [(qkv, 0), (qkv, 1), (qkv, 2), (out, 0), (q, 0), (kv, 0), (kv, 1), (cross_out, 0)]
    for number in range(2 * SIDE):
        for k, (target, block) in enumerate(targets):
            start = (block * 2 * SIDE + number) * PAIR
            target[:, start : start + PAIR] = come_ref[number, :, k * PAIR : (k + 1) * PAIR]
    total = come_ref[0, :, 8 * PAIR :]
    for number in range(1, 2 * SIDE):
        total += come_ref[number, :, 8 * PAIR :]
    vectors[...] = total


def collected(come):
    return pl.pallas_call(
        collect_kernel,
        out_shape=tuple(
            jax.ShapeDtypeStruct((ROWS // 2, columns), f32)
            for columns in (24 * PAIR, 8 * PAIR, 8 * PAIR, 16 * PAIR, 8 * PAIR, PAIR)
        ),
    )(come)


def divide_kernel(grouped, core_ref, sums_ref, keep_ref, give_ref):
    core = core_ref[0]
    half = grouped // 2
    columns = sums_ref.shape[1]
    for ref, side in ((keep_ref, core), (give_ref, 1 - core)):
        if grouped:
            start = pl.ds(pl.multiple_of(side * half, 128), half)
            block = sums_ref[:, start]
            ref[:, :half] = block[: ROWS // 2]
            ref[:, half:grouped] = block[ROWS // 2 :]
        rows = pl.ds(pl.multiple_of(side * (ROWS // 2), 8), ROWS // 2)
        if columns > grouped:
            ref[:, grouped:] = sums_ref[rows, grouped:]


def divided(core, sums, grouped):
    shape = jax.ShapeDtypeStruct((ROWS // 2, sums.shape[1]), f32)
    return pl.pallas_call(
        partial(divide_kernel, grouped),
        in_specs=scalar_first(1),
        out_shape=(shape, shape),
    )(core, sums)


def assemble_kernel(layout, core_ref, keep_ref, come_ref, *outs):
    core = core_ref[0]
    for ref, side in ((keep_ref, core), (come_ref, 1 - core)):
        at = 0
        for out, (grouped, columns, span) in zip(outs, layout):
            part = span // 2
            if grouped:
                for g in range(2):
                    for h in range(2):
                        rows = slice(g * ROWS + h * ROWS // 2, g * ROWS + (h + 1) * ROWS // 2)
                        start = at + h * 2 * part + g * part
                        column = pl.ds(pl.multiple_of(side * part, 128), part)
                        out[rows, column] = ref[:, start : start + part]
                at += 4 * part
                continue
            for k in range(0, columns, span):
                column = pl.ds(pl.multiple_of(k + side * part, 128), part)
                out[:, column] = ref[:, at : at + part]
                at += part


def assembled(core, keep, come, layout):
    return pl.pallas_call(
        partial(assemble_kernel, tuple(layout)),
        in_specs=scalar_first(2),
        out_shape=tuple(
            jax.ShapeDtypeStruct((2 * ROWS if grouped else ROWS // 2, columns), f32)
            for grouped, columns, span in layout
        ),
    )(core, keep, come)


def on_device(
    tokens,
    memory,
    lengths,
    segments,
    key_mask,
    w_self_qkv,
    w_self_out,
    w_cross_q,
    w_cross_kv,
    w_cross_out,
    w_up,
    w_down,
    norm_gains,
    norm_biases,
    readout,
):
    tok_rows = tokens.shape[1]
    width = tokens.shape[2]
    half = lax.axis_index("mem")
    core = half.astype(jnp.int32).reshape(1)
    page_index = lax.axis_index("dp")
    patches = 2 * memory.shape[2]

    vocab_dev = readout.shape[1]
    readout_turned = jnp.pad(readout.T, ((0, ENTRIES - vocab_dev), (0, 0)))
    planes = [[d for d in range(CHIPS) if d % SIDE == x] for x in range(SIDE)]
    readout_part = lax.all_gather(
        readout_turned, "dp", axis=0, tiled=True, axis_index_groups=planes
    )
    is_entry = jnp.arange(readout_part.shape[0]) % ENTRIES < vocab_dev
    entry_bias = jnp.where(is_entry, 0.0, masked_score).astype(f32)[None]

    tokens_own = tokens[0]
    tokens_page = jnp.concatenate([tokens_own, swapped(tokens_own)], 0)
    memory_own = memory[:, 0]
    memory_come = swapped(memory_own)
    memory_rows = jnp.where(
        half == 0,
        jnp.concatenate([memory_own, memory_come], 1),
        jnp.concatenate([memory_come, memory_own], 1),
    ).reshape(2 * patches, width)
    mask_own = key_mask[0].astype(f32)
    mask_come = swapped(mask_own)
    mask_page = jnp.where(
        half == 0,
        jnp.concatenate([mask_own, mask_come]),
        jnp.concatenate([mask_come, mask_own]),
    )
    keep = jnp.tile(jnp.repeat(mask_page, 2), 2)[None]
    own_positions = jnp.arange(tok_rows) + half * tok_rows
    other_positions = jnp.arange(tok_rows) + (1 - half) * tok_rows
    key_positions = jnp.concatenate([own_positions, other_positions])
    cut = segments[0].reshape(2, tok_rows)
    own_segments = lax.dynamic_index_in_dim(cut, half, 0, False)
    other_segments = lax.dynamic_index_in_dim(cut, 1 - half, 0, False)
    key_segments = jnp.concatenate([own_segments, other_segments])
    allowed = (key_positions[None, :] <= own_positions[:, None]) & (
        key_segments[None, :] == own_segments[:, None]
    )
    allowed = allowed.astype(f32)
    count = jnp.sum(lengths).astype(f32)
    line = page_index // SIDE * SIDE + (page_index + jnp.arange(SIDE)) % SIDE
    valid = key_positions[None] < lengths[line][:, None]
    row_weight = (valid.astype(f32) / count)[:, :, None]
    row_weight = jnp.broadcast_to(row_weight, row_weight.shape[:2] + (128,))

    weights = (w_self_qkv, w_self_out, w_cross_q, w_cross_kv, w_cross_out)
    q, kv, h1, qc, kvc, h2, a3, pack = attention(
        tokens_page, allowed, memory_rows, keep, weights, norm_gains, norm_biases
    )
    slope, act, h3, layer_out, final = feed_forward(h2, a3, w_up, w_down, norm_gains, norm_biases)
    final = final.reshape(2, tok_rows, width)
    near = jnp.stack([final] + [along_line(final, r) for r in range(1, SIDE)])
    final_line = jnp.stack([near, swapped(near)], 1).transpose(2, 0, 1, 3, 4)
    final_line = final_line.reshape(2, 2 * SIDE * tok_rows, width)
    a3_other, act_other = swapped(a3), swapped(act)

    final_line, row_weight = lax.optimization_barrier((final_line, row_weight))

    line_groups = [
        [2 * (start + k) + m for k in range(SIDE) for m in range(2)]
        for start in range(0, CHIPS, SIDE)
    ]
    packs = lax.all_gather(pack, ("dp", "mem"), axis_index_groups=line_groups)

    def exchanged(block):
        return lax.all_to_all(
            block, ("dp", "mem"), 0, 0, axis_index_groups=line_groups, tiled=True
        )

    logits, stats = logits_and_stats(final_line, readout_part, entry_bias)
    stats = jnp.stack([stats] + [along_line(stats, r) for r in range(1, SIDE)])
    stats_come = swapped(stats)
    far_stay, give = readout_back(stats, stats_come, row_weight, logits, readout_part, True)
    come = swapped(give)
    far = (far_stay + come[: SIDE - 1].astype(f32)).astype(bf16)
    logits, far, core_late = lax.optimization_barrier((logits, far, core))
    far = [along_line(far[r - 1], -r) for r in range(1, SIDE)]
    own, terms = readout_back(stats, stats_come, row_weight, logits, readout_part, False)
    terms = terms[:, 0].reshape(2, tok_rows).sum(1)
    loss = (terms[0] + terms[1]).reshape(1)
    turned = turned_packs(core_late, packs, SECOND_AXES)
    own, turned = lax.optimization_barrier((own, turned))
    grad_parts = [part.reshape(2 * tok_rows, width) for part in [own[0], come[SIDE - 1]] + far]

    gh3_keep, gh3_give, gup_keep, gup_give, gh2, vectors_ff = feed_forward_back(
        core, grad_parts, h3, h2, slope, w_up, w_down, norm_gains
    )
    first_bucket = outer_products(
        core,
        [
            (act, act_other, gh3_keep, swapped(gh3_give)),
            (a3, a3_other, gup_keep, swapped(gup_give)),
        ],
        FIRST_AXES,
    )
    gh2, first_bucket = lax.optimization_barrier((gh2, first_bucket))
    first_part = scattered_sum(first_bucket, FIRST_AXES[0])

    gh1, gq, gkv, gkv_give, gkvc, vectors_att, sent = attention_back(
        gh2, allowed, keep, kvc, qc, h1, kv, q, w_cross_out, w_cross_q, w_self_out, norm_gains
    )
    sent = exchanged(sent)
    tokens_grad, memory_grad, vectors_in = inputs_back(
        core, tokens_own, gh1, gq, gkv, swapped(gkv_give), gkvc, swapped(gkvc), w_self_qkv,
        w_cross_kv, norm_gains,
    )
    vectors = (vectors_ff + vectors_att + vectors_in).astype(bf16)
    vectors = jnp.pad(vectors.T, ((0, 0), (0, PAIR - 8))).reshape(SIDE, SIDE, LINE, PAIR)
    vectors = jnp.where(half == 0, vectors.transpose(1, 0, 2, 3), vectors).reshape(width, PAIR)
    second_bucket = line_products(turned, sent, vectors)
    second_sums = line_sum(second_bucket, SECOND_AXES[0]).astype(bf16)
    first_sums = line_sum(first_part, FIRST_AXES[1]).astype(bf16)
    first_sums, second_sums = lax.optimization_barrier((first_sums, second_sums))
    second_sums = line_sum(second_sums, SECOND_AXES[1])
    first_sums = line_sum(first_sums, FIRST_AXES[2])
    first_sums, second_sums = lax.optimization_barrier((first_sums, second_sums))

    first_keep, first_give = divided(core, first_sums, 2 * width)
    weight_down, weight_up = assembled(
        core,
        first_keep,
        swapped(first_give),
        [(True, width, width), (False, 4 * width, 4 * width)],
    )
    weight_qkv, weight_out, weight_q, weight_kv, weight_cross_out, vectors = collected(
        exchanged(second_sums.reshape(2 * SIDE, ROWS // 2, -1))
    )
    vectors = vectors[:, :8].T
    return (
        loss,
        layer_out.reshape(2, 1, tok_rows, width),
        tokens_grad[None],
        memory_grad[:, None],
        weight_qkv,
        weight_out,
        weight_q,
        weight_kv,
        weight_cross_out,
        weight_up,
        weight_down,
        vectors[:4],
        vectors[4:],
    )


def solution(mesh):
    in_specs = (
        P("dp", "mem", None),
        P(None, "dp", "mem", None),
        P(),
        P("dp", None),
        P("dp", "mem"),
        P(),
        P(),
        P(),
        P(),
        P(),
        P(),
        P(),
        P(),
        P(),
        P(None, ("dp", "mem")),
    )
    out_specs = (
        P("dp"),
        P(None, "dp", "mem", None),
        P("dp", "mem", None),
        P(None, "dp", "mem", None),
        P(("dp", "mem"), None),
        P(("dp", "mem"), None),
        P(("dp", "mem"), None),
        P(("dp", "mem"), None),
        P(("dp", "mem"), None),
        P(("dp", "mem"), None),
        P(("dp", "mem"), None),
        P(None, ("dp", "mem")),
        P(None, ("dp", "mem")),
    )
    return jax.shard_map(
        on_device, mesh=mesh, in_specs=in_specs, out_specs=out_specs, check_vma=False
    )
```

```python
from functools import partial

import jax
import jax.numpy as jnp
from jax import lax
from jax.experimental import pallas as pl
from jax.experimental.pallas import tpu as pltpu
from jax.sharding import PartitionSpec as P

HEAD = 64
PAIR = 2 * HEAD
SIDE = 4
CHIPS = SIDE * SIDE * SIDE
ROWS = 16
TILE = 512
FF_TILE = 1024
BLOCK = 640
CHUNK = 16
PARTS = ((0, 1024), (1024, 2048), (2048, 3200))
ENTRIES = 200
MIB = 1024 * 1024
epsilon = 1e-05
masked_score = -1e30
bf16 = jnp.bfloat16
f32 = jnp.float32


def dot(left, right):
    return jnp.dot(left, right, preferred_element_type=f32)


def dot_nt(left, right):
    return lax.dot_general(left, right, (((1,), (1,)), ((), ())), preferred_element_type=f32)


def dot_tn(left, right):
    return lax.dot_general(left, right, (((0,), (0,)), ((), ())), preferred_element_type=f32)


def normalized(values):
    centre = values - jnp.mean(values, -1, keepdims=True)
    inverse = lax.rsqrt(jnp.mean(centre * centre, -1, keepdims=True) + epsilon)
    return centre * inverse, inverse


def norm_back(upstream, normed, inverse, gain):
    scaled = upstream * gain
    back = inverse * (
        scaled
        - jnp.mean(scaled, -1, keepdims=True)
        - normed * jnp.mean(scaled * normed, -1, keepdims=True)
    )
    return back, jnp.sum(upstream * normed, 0, keepdims=True), jnp.sum(upstream, 0, keepdims=True)


def lower_lanes(shape):
    return lax.broadcasted_iota(jnp.int32, shape, 1) < HEAD


def parted(block):
    low = lower_lanes(block.shape)
    none = jnp.zeros_like(block)
    return jnp.concatenate([jnp.where(low, block, none), jnp.where(low, none, block)], 0)


def merged(block):
    rows = block.shape[0] // 2
    return jnp.where(lower_lanes((rows, PAIR)), block[:rows], block[rows:])


def self_softmax(queries, keys, allowed):
    scores = dot_nt(queries, keys) * HEAD ** (-0.5)
    scores = jnp.where(allowed, scores, masked_score)
    weights = jnp.exp(scores - jnp.max(scores, -1, keepdims=True))
    return weights * (1.0 / jnp.sum(weights, -1, keepdims=True))


def by_view(values, is_first, combine, neutral):
    first = combine(jnp.where(is_first, values, neutral), -1, keepdims=True)
    second = combine(jnp.where(is_first, neutral, values), -1, keepdims=True)
    return jnp.where(is_first, first, second)


def cross_softmax(queries, keys, kept, is_first):
    scores = dot_nt(queries, keys) * HEAD ** (-0.5)
    scores = jnp.where(kept, scores, masked_score)
    weights = jnp.exp(scores - by_view(scores, is_first, jnp.max, masked_score))
    return weights * (1.0 / by_view(weights, is_first, jnp.sum, 0.0))


def each_view(block, is_first):
    none = jnp.zeros_like(block)
    return jnp.concatenate([jnp.where(is_first, block, none), jnp.where(is_first, none, block)], 0)


def allowed_of(allowed_ref):
    allowed = allowed_ref[...] > 0.5
    return jnp.concatenate([allowed, allowed], 0)


PACK = (0, 96, 192, 288, 480, 576)
SENT = (0, 96, 192, 288, 480, 672, 864, 960, 1056)


def attention_kernel(
    tokens_ref, allowed_ref, memory_ref, keep_ref, w_qkv, w_out, w_q, w_kv, w_cross_out, gains,
    biases, q_ref, kv_ref, h1_ref, qc_ref, kvc_ref, h2_ref, a3_ref, pack_ref, a1,
):
    rows = q_ref.shape[0]
    width = tokens_ref.shape[1]
    a1_rows, o_rows, a2_rows, oc_rows, memory_rows = map(slice, PACK[:-1], PACK[1:])
    first_rows, second_rows = slice(PACK[3], PACK[3] + rows), slice(PACK[3] + rows, PACK[4])
    values = tokens_ref[...].astype(f32)
    normed, _ = normalized(values)
    a1[...] = (normed * gains[0:1] + biases[0:1]).astype(bf16)
    pack_ref[a1_rows] = a1[:rows]
    pack_ref[memory_rows] = memory_ref[...]
    q_ref[...] = dot(a1[:rows], w_qkv[:, :width]).astype(bf16)
    kv_ref[...] = dot(a1[...], w_qkv[:, width:]).astype(bf16)
    allowed = allowed_of(allowed_ref)
    for at in range(0, width, PAIR):
        queries = parted(q_ref[:, at : at + PAIR])
        probs = self_softmax(queries, kv_ref[:, at : at + PAIR], allowed)
        mixed = dot(probs.astype(bf16), kv_ref[:, width + at : width + at + PAIR])
        pack_ref[o_rows, at : at + PAIR] = merged(mixed).astype(bf16)
    h1 = values[:rows] + dot(pack_ref[o_rows], w_out[...])
    h1_ref[...] = h1
    normed, _ = normalized(h1)
    pack_ref[a2_rows] = (normed * gains[1:2] + biases[1:2]).astype(bf16)
    qc_ref[...] = dot(pack_ref[a2_rows], w_q[...]).astype(bf16)
    kvc_ref[...] = dot(memory_ref[...], w_kv[...]).astype(bf16)
    shape = (2 * rows, memory_ref.shape[0])
    kept = jnp.broadcast_to(keep_ref[...], shape) > 0.5
    is_first = lax.broadcasted_iota(jnp.int32, shape, 1) < shape[1] // 2
    for at in range(0, width, PAIR):
        queries = parted(qc_ref[:, at : at + PAIR])
        probs = cross_softmax(queries, kvc_ref[:, at : at + PAIR], kept, is_first)
        mixed = dot(
            each_view(probs.astype(bf16), is_first), kvc_ref[:, width + at : width + at + PAIR]
        )
        pack_ref[first_rows, at : at + PAIR] = merged(mixed[: 2 * rows]).astype(bf16)
        pack_ref[second_rows, at : at + PAIR] = merged(mixed[2 * rows :]).astype(bf16)
    h2 = jnp.concatenate([h1, h1], 0) + dot(pack_ref[oc_rows], w_cross_out[...])
    h2_ref[...] = h2
    normed, _ = normalized(h2)
    a3_ref[...] = (normed * gains[2:3] + biases[2:3]).astype(bf16)


def attention(tokens_page, allowed, memory_rows, keep, weights, gains, biases):
    rows, width = allowed.shape[0], tokens_page.shape[1]
    shape = jax.ShapeDtypeStruct
    return pl.pallas_call(
        attention_kernel,
        out_shape=(
            shape((rows, width), bf16),
            shape((2 * rows, 2 * width), bf16),
            shape((rows, width), f32),
            shape((rows, width), bf16),
            shape((memory_rows.shape[0], 2 * width), bf16),
            shape((2 * rows, width), f32),
            shape((2 * rows, width), bf16),
            shape((PACK[-1], width), bf16),
        ),
        scratch_shapes=[pltpu.VMEM((2 * rows, width), bf16)],
        compiler_params=pltpu.CompilerParams(vmem_limit_bytes=58 * MIB),
        cost_estimate=pl.CostEstimate(
            flops=2 * 10**9, bytes_accessed=24 * MIB, transcendentals=10**6
        ),
    )(tokens_page, allowed, memory_rows, keep, *weights, gains, biases)


def erf_parts(values):
    return 0.5 + 0.5 * lax.erf(values * (0.5**0.5))


def feed_forward_kernel(
    h2_ref, a3_ref, w_up, w_down, gains, biases, slope_ref, act_ref, h3_ref, out_ref, fin_ref, total
):
    step = pl.program_id(0)

    @pl.when(step == 0)
    def _():
        total[...] = jnp.zeros_like(total)

    up = dot(a3_ref[...], w_up[...])
    below = erf_parts(up)
    slope_ref[...] = below + up * jnp.exp(-0.5 * up * up) * (0.5 / jnp.pi) ** 0.5
    act = (up * below).astype(bf16)
    act_ref[...] = act
    total[...] += dot(act, w_down[...])

    @pl.when(step == pl.num_programs(0) - 1)
    def _():
        h3 = h2_ref[...] + total[...]
        h3_ref[...] = h3
        out_ref[...] = h3.astype(bf16)
        normed, _ = normalized(h3)
        fin_ref[...] = (normed * gains[3:4] + biases[3:4]).astype(bf16)


def whole(*shape):
    return pl.BlockSpec(shape, lambda i: (0,) * len(shape))


def feed_forward(h2, a3, w_up, w_down, gains, biases):
    rows, width = h2.shape
    hidden = w_up.shape[1]
    shape = jax.ShapeDtypeStruct
    return pl.pallas_call(
        feed_forward_kernel,
        grid=(hidden // FF_TILE,),
        in_specs=[
            whole(rows, width),
            whole(rows, width),
            pl.BlockSpec((width, FF_TILE), lambda i: (0, i)),
            pl.BlockSpec((FF_TILE, width), lambda i: (i, 0)),
            whole(4, width),
            whole(4, width),
        ],
        out_specs=(
            pl.BlockSpec((rows, FF_TILE), lambda i: (0, i)),
            pl.BlockSpec((rows, FF_TILE), lambda i: (0, i)),
            whole(rows, width),
            whole(rows, width),
            whole(rows, width),
        ),
        out_shape=(
            shape((rows, hidden), f32),
            shape((rows, hidden), bf16),
            shape((rows, width), f32),
            shape((rows, width), bf16),
            shape((rows, width), bf16),
        ),
        scratch_shapes=[pltpu.VMEM((rows, width), f32)],
        compiler_params=pltpu.CompilerParams(vmem_limit_bytes=58 * MIB),
        cost_estimate=pl.CostEstimate(
            flops=4 * rows * width * hidden, bytes_accessed=24 * MIB, transcendentals=rows * hidden
        ),
    )(h2, a3, w_up, w_down, gains, biases)


def halves(block):
    middle = block.shape[1] // 2
    return block[:, :middle], block[:, middle:]


def divide(core, block, keep_ref, give_ref):
    for side in range(2):

        @pl.when(core == side)
        def _(side=side):
            keep_ref[...] = halves(block)[side]
            give_ref[...] = halves(block)[1 - side]


def feed_forward_back_kernel(
    core_ref, own_ref, other_ref, far_a, far_b, far_c, h3_ref, h2_ref, slope_ref, w_up, w_down,
    gains, gh3_keep, gh3_give, gup_keep, gup_give, gh2_ref, vector_ref, gh3, gh3_low_ref, total,
):
    step = pl.program_id(0)
    core = core_ref[0]

    @pl.when(step == 0)
    def _():
        upstream = own_ref[...]
        for ref in (other_ref, far_a, far_b, far_c):
            upstream += ref[...].astype(f32)
        normed, inverse = normalized(h3_ref[...])
        back, gain, bias = norm_back(upstream, normed, inverse, gains[3:4])
        gh3[...] = back
        gh3_low_ref[...] = back.astype(bf16)
        divide(core, gh3_low_ref[...], gh3_keep, gh3_give)
        vector_ref[...] = jnp.zeros_like(vector_ref)
        vector_ref[3:4] = gain
        vector_ref[7:8] = bias
        total[...] = jnp.zeros_like(total)

    grad = dot_nt(gh3_low_ref[...], w_down[...])
    gup = (grad * slope_ref[...]).astype(bf16)
    side = step // (pl.num_programs(0) // 2)

    @pl.when(side == core)
    def _():
        gup_keep[...] = gup

    @pl.when(side != core)
    def _():
        gup_give[...] = gup

    total[...] += dot_nt(gup, w_up[...])

    @pl.when(step == pl.num_programs(0) - 1)
    def _():
        normed, inverse = normalized(h2_ref[...])
        back, gain, bias = norm_back(total[...], normed, inverse, gains[2:3])
        gh2 = gh3[...] + back
        gh2_ref[...] = gh2
        vector_ref[2:3] = gain
        vector_ref[6:7] = bias


def feed_forward_back(core, parts, h3, h2, slope, w_up, w_down, gains):
    rows, width = h2.shape
    hidden = w_up.shape[1]
    tiles = hidden // FF_TILE
    shape = jax.ShapeDtypeStruct

    def all_of(*dims):
        return pl.BlockSpec(dims, lambda i, core: (0,) * len(dims))

    middle = tiles // 2

    def half_tile(kept):
        def index(i, core):
            side = core[0] if kept else 1 - core[0]
            return (0, jnp.clip(i - side * middle, 0, middle - 1))

        return pl.BlockSpec((rows, FF_TILE), index)

    return pl.pallas_call(
        feed_forward_back_kernel,
        grid_spec=pltpu.PrefetchScalarGridSpec(
            num_scalar_prefetch=1,
            grid=(tiles,),
            in_specs=[
                *(all_of(rows, width) for _ in range(7)),
                pl.BlockSpec((rows, FF_TILE), lambda i, core: (0, i)),
                pl.BlockSpec((width, FF_TILE), lambda i, core: (0, i)),
                pl.BlockSpec((FF_TILE, width), lambda i, core: (i, 0)),
                all_of(4, width),
            ],
            out_specs=(
                all_of(rows, width // 2),
                all_of(rows, width // 2),
                half_tile(True),
                half_tile(False),
                all_of(rows, width),
                all_of(8, width),
            ),
            scratch_shapes=[
                pltpu.VMEM((rows, width), f32),
                pltpu.VMEM((rows, width), bf16),
                pltpu.VMEM((rows, width), f32),
            ],
        ),
        out_shape=(
            shape((rows, width // 2), bf16),
            shape((rows, width // 2), bf16),
            shape((rows, hidden // 2), bf16),
            shape((rows, hidden // 2), bf16),
            shape((rows, width), f32),
            shape((8, width), f32),
        ),
        compiler_params=pltpu.CompilerParams(vmem_limit_bytes=58 * MIB),
        cost_estimate=pl.CostEstimate(
            flops=4 * rows * width * hidden,
            bytes_accessed=24 * MIB,
            transcendentals=2 * rows * hidden,
        ),
    )(core, *parts, h3, h2, slope, w_up, w_down, gains)


def attention_back_kernel(
    gh2_ref, allowed_ref, keep_ref, kvc_ref, qc_ref, h1_ref, kv_ref, q_ref, w_cross_out, w_q, w_out,
    gains, gh1_ref, gq_ref, gkv_ref, give_ref, gkvc_ref, vector_ref, sent_ref, goc, go, gqc,
    gh1_low,
):
    rows, width = q_ref.shape
    scale = HEAD ** (-0.5)
    sent_rows = list(map(slice, SENT[:-1], SENT[1:]))

    def pairs_of_heads():
        for number in range(2 * SIDE):
            at = number * PAIR
            yield sent_ref.at[number], slice(at, at + PAIR), slice(width + at, width + at + PAIR)

    gh2_low = gh2_ref[...].astype(bf16)
    goc[...] = dot_nt(gh2_low, w_cross_out[...]).astype(bf16)
    shape = (2 * rows, kvc_ref.shape[0])
    kept = jnp.broadcast_to(keep_ref[...], shape) > 0.5
    is_first = lax.broadcasted_iota(jnp.int32, shape, 1) < shape[1] // 2
    for to, here, there in pairs_of_heads():
        queries = parted(qc_ref[:, here])
        probs = cross_softmax(queries, kvc_ref[:, here], kept, is_first)
        upstream = jnp.concatenate([parted(goc[:rows, here]), parted(goc[rows:, here])], 0)
        grad = dot_nt(upstream, kvc_ref[:, there])
        grad = jnp.where(is_first, grad[: 2 * rows], grad[2 * rows :])
        slope = probs * (grad - by_view(probs * grad, is_first, jnp.sum, 0.0))
        slope = slope.astype(bf16)
        change = (merged(dot(slope, kvc_ref[:, here])) * scale).astype(bf16)
        gqc[:, here] = change
        to[sent_rows[2]] = change
        to[sent_rows[3]] = gh2_ref[:, here].astype(bf16)
        change = (dot_tn(slope, queries) * scale).astype(bf16)
        gkvc_ref[:, here] = change
        to[sent_rows[6]] = change
        change = dot_tn(each_view(probs.astype(bf16), is_first), upstream).astype(bf16)
        gkvc_ref[:, there] = change
        to[sent_rows[7]] = change
    normed, inverse = normalized(h1_ref[...])
    back, gain, bias = norm_back(dot_nt(gqc[...], w_q[...]), normed, inverse, gains[1:2])
    vector_ref[...] = jnp.zeros_like(vector_ref)
    vector_ref[1:2] = gain
    vector_ref[5:6] = bias
    gh1 = gh2_ref[:rows] + gh2_ref[rows:] + back
    gh1_ref[...] = gh1
    gh1_low[...] = gh1.astype(bf16)
    go[...] = dot_nt(gh1_low[...], w_out[...]).astype(bf16)
    allowed = allowed_of(allowed_ref)
    for to, here, there in pairs_of_heads():
        queries = parted(q_ref[:, here])
        probs = self_softmax(queries, kv_ref[:, here], allowed)
        upstream = parted(go[:, here])
        grad = dot_nt(upstream, kv_ref[:, there])
        slope = probs * (grad - jnp.sum(probs * grad, -1, keepdims=True))
        slope = slope.astype(bf16)
        change = (merged(dot(slope, kv_ref[:, here])) * scale).astype(bf16)
        gq_ref[:, here] = change
        to[sent_rows[0]] = change
        to[sent_rows[1]] = gh1_low[:, here]
        change = (dot_tn(slope, queries) * scale).astype(bf16)
        gkv_ref[:, here] = change[:rows]
        give_ref[:, here] = change[rows:]
        to[sent_rows[4]] = change
        change = dot_tn(probs.astype(bf16), upstream).astype(bf16)
        gkv_ref[:, there] = change[:rows]
        give_ref[:, there] = change[rows:]
        to[sent_rows[5]] = change


def scalar_first(count):
    return [pl.BlockSpec(memory_space=pltpu.SMEM)] + [
        pl.BlockSpec(memory_space=pltpu.VMEM) for _ in range(count)
    ]


def attention_back(*operands):
    kvc, kv, q = operands[3], operands[6], operands[7]
    rows, width = q.shape
    shape = jax.ShapeDtypeStruct
    return pl.pallas_call(
        attention_back_kernel,
        out_shape=(
            shape((rows, width), f32),
            shape((rows, width), bf16),
            shape((rows, 2 * width), bf16),
            shape((rows, 2 * width), bf16),
            shape(kvc.shape, bf16),
            shape((8, width), f32),
            shape((2 * SIDE, SENT[-1], PAIR), bf16),
        ),
        scratch_shapes=[
            pltpu.VMEM((2 * rows, width), bf16),
            pltpu.VMEM((rows, width), bf16),
            pltpu.VMEM((rows, width), bf16),
            pltpu.VMEM((rows, width), bf16),
        ],
        compiler_params=pltpu.CompilerParams(vmem_limit_bytes=58 * MIB),
        cost_estimate=pl.CostEstimate(
            flops=2 * 10**9, bytes_accessed=14 * MIB, transcendentals=10**6
        ),
    )(*operands)


def inputs_back_kernel(
    core_ref, tokens_ref, gh1_ref, gq_ref, gkv_ref, come_ref, gkvc_ref, come_cross_ref, w_qkv,
    w_kv, gains, tokens_grad_ref, memory_grad_ref, vector_ref, grads,
):
    core = core_ref[0]
    width = gh1_ref.shape[1]
    pairs = (gkv_ref[...].astype(f32) + come_ref[...].astype(f32)).astype(bf16)
    total = dot_nt(gq_ref[...], w_qkv[:, :width]) + dot_nt(pairs, w_qkv[:, width:])
    normed, inverse = normalized(tokens_ref[...].astype(f32))
    back, gain, bias = norm_back(total, normed, inverse, gains[0:1])
    tokens_grad_ref[...] = gh1_ref[...] + back
    vector_ref[...] = jnp.zeros_like(vector_ref)
    vector_ref[0:1] = gain
    vector_ref[4:5] = bias
    pairs = (gkvc_ref[...].astype(f32) + come_cross_ref[...].astype(f32)).astype(bf16)
    grads[...] = dot_nt(pairs, w_kv[...])
    own = memory_grad_ref.shape[1]
    for view in range(2):
        start = pl.multiple_of(view * 2 * own + core * own, 8)
        memory_grad_ref[view] = grads[pl.ds(start, own)]


def inputs_back(core, *operands):
    rows, width = operands[1].shape
    patches = operands[5].shape[0]
    shape = jax.ShapeDtypeStruct
    return pl.pallas_call(
        inputs_back_kernel,
        in_specs=scalar_first(len(operands)),
        out_shape=(
            shape((rows, width), f32),
            shape((2, patches // 4, width), f32),
            shape((8, width), f32),
        ),
        scratch_shapes=[pltpu.VMEM((patches, width), f32)],
        compiler_params=pltpu.CompilerParams(vmem_limit_bytes=58 * MIB),
        cost_estimate=pl.CostEstimate(flops=10**9, bytes_accessed=14 * MIB, transcendentals=0),
    )(core, *operands)


def logits_kernel(rows_ref, readout_ref, bias_ref, logits_ref, stats_ref, kept):
    tokens = rows_ref.shape[1]
    rows = jnp.concatenate([rows_ref[0], rows_ref[1]], 0)

    def statistics(begin, end):
        spans = range(begin, end, 128)
        for at in range(0, tokens, CHUNK):
            here = slice(at, at + CHUNK)
            first = [logits_ref[0, 0, here, c : c + 128] for c in spans]
            second = [logits_ref[0, 1, here, c : c + 128] for c in spans]
            new_first, new_second = first[0], second[0]
            for a, b in zip(first[1:], second[1:]):
                new_first = jnp.maximum(new_first, a)
                new_second = jnp.maximum(new_second, b)
            total_first = total_apart = total_second = jnp.zeros((CHUNK, 128), f32)
            if begin:
                top_first, top_second = kept[0, here], kept[3, here]
                new_first = jnp.maximum(new_first, top_first)
                new_second = jnp.maximum(new_second, top_second)
                fade_first = jnp.exp(top_first - new_first)
                total_first = kept[1, here] * fade_first
                total_apart = kept[2, here] * fade_first
                total_second = kept[4, here] * jnp.exp(top_second - new_second)
            for a, b in zip(first, second):
                weight = jnp.exp(a - new_first)
                total_first += weight
                total_apart += weight * (a - b)
                total_second += jnp.exp(b - new_second)
            kept[0, here], kept[1, here], kept[2, here] = new_first, total_first, total_apart
            kept[3, here], kept[4, here] = new_second, total_second

    before = None
    for begin, end in PARTS:
        values = dot_nt(rows, readout_ref[begin:end]) + bias_ref[:, begin:end]
        for v in range(2):
            logits_ref[0, v, :, begin:end] = values[v * tokens : (v + 1) * tokens]
        if before:
            statistics(*before)
        before = begin, end
    statistics(*before)

    top_first = jnp.max(kept[0], -1, keepdims=True)
    top_second = jnp.max(kept[3], -1, keepdims=True)
    fade_first = jnp.exp(kept[0] - top_first)
    fade_second = jnp.exp(kept[3] - top_second)
    stats = (
        top_first,
        jnp.sum(kept[1] * fade_first, -1, keepdims=True),
        jnp.sum(kept[2] * fade_first, -1, keepdims=True),
        top_second,
        jnp.sum(kept[4] * fade_second, -1, keepdims=True),
    )
    lane = lax.broadcasted_iota(jnp.int32, kept.shape[1:], 1)
    result = jnp.zeros(kept.shape[1:], f32)
    for k, stat in enumerate(stats):
        result = jnp.where(lane == k, stat, result)
    stats_ref[0] = result.T[:8]


def once(*shape):
    return pl.BlockSpec(shape, lambda i: (0,) * len(shape), pipeline_mode=pl.Buffered(1))


def logits_and_stats(rows, readout_rows, bias):
    views, tokens, width = rows.shape
    entries = readout_rows.shape[0]
    page = tokens // SIDE
    shape = jax.ShapeDtypeStruct
    return pl.pallas_call(
        logits_kernel,
        out_shape=(
            shape((SIDE, 2, page, entries), f32),
            shape((SIDE, 8, page), f32),
        ),
        grid=(SIDE,),
        in_specs=[
            pl.BlockSpec((2, page, width), lambda i: (0, i, 0)),
            once(entries, width),
            once(1, entries),
        ],
        out_specs=(
            pl.BlockSpec((1, 2, page, entries), lambda i: (i, 0, 0, 0)),
            pl.BlockSpec((1, 8, page), lambda i: (i, 0, 0)),
        ),
        scratch_shapes=[pltpu.VMEM((5, page, 128), f32)],
        compiler_params=pltpu.CompilerParams(vmem_limit_bytes=58 * MIB),
        cost_estimate=pl.CostEstimate(
            flops=4 * tokens * entries * width,
            bytes_accessed=2 * entries * width + 8 * tokens * entries,
            transcendentals=2 * tokens * entries,
        ),
    )(rows, readout_rows, bias)


def merged_stats(near_ref, come_ref, slot):
    tokens = near_ref.shape[3]
    middle = tokens // 2
    parts = []
    for ref, flipped in ((near_ref, False), (come_ref, True)):
        for r in range(SIDE):
            part = ref[r, lax.rem(slot + SIDE - r, SIDE)]
            if flipped:
                part = jnp.concatenate([part[:, middle:], part[:, :middle]], 1)
            parts.append(part)
    top_first = parts[0][0:1]
    top_second = parts[0][3:4]
    for part in parts[1:]:
        top_first = jnp.maximum(top_first, part[0:1])
        top_second = jnp.maximum(top_second, part[3:4])
    total_first = total_apart = total_second = jnp.zeros((1, tokens), f32)
    for part in parts:
        fade = jnp.exp(part[0:1] - top_first)
        total_first += part[1:2] * fade
        total_apart += part[2:3] * fade
        total_second += part[4:5] * jnp.exp(part[3:4] - top_second)
    first_lse = top_first + jnp.log(total_first)
    second_lse = top_second + jnp.log(total_second)
    return first_lse, second_lse, total_apart / total_first


def readout_back_kernel(
    far, near_ref, come_ref, weight_ref, logits_ref, readout_ref, stay_ref, other_ref, kept, slopes
):
    step = pl.program_id(0)
    tokens = weight_ref.shape[1]
    rows = tokens // 2
    slot = lax.rem(step + 1, SIDE) if far else 0
    for k, row in enumerate(merged_stats(near_ref, come_ref, slot)):
        kept[k] = jnp.broadcast_to(row, (128, row.shape[1])).T
    kept[3] = weight_ref[0]

    def gradient(start, count):
        def derivatives(begin, end):
            for at in range(start, start + count, CHUNK):
                here = slice(at, at + CHUNK)
                first_lse, second_lse, apart, weight = (kept[k, here] for k in range(4))
                for c in range(begin, end, 128):
                    first = logits_ref[0, 0, here, c : c + 128]
                    second = logits_ref[0, 1, here, c : c + 128]
                    first_prob = jnp.exp(first - first_lse) * weight
                    second_prob = jnp.exp(second - second_lse) * weight
                    change = first_prob * (first - second - apart)
                    slopes[0, here, c : c + 128] = change.astype(bf16)
                    slopes[1, here, c : c + 128] = (second_prob - first_prob).astype(bf16)

        derivatives(*PARTS[0])
        total = None
        for i, (begin, end) in enumerate(PARTS):
            block = [slopes[v, start : start + count, begin:end] for v in range(2)]
            result = dot(jnp.concatenate(block, 0), readout_ref[begin:end])
            if i + 1 < len(PARTS):
                derivatives(*PARTS[i + 1])
            total = result if total is None else total + result
        return total

    if not far:
        total = gradient(0, rows)
        for v in range(2):
            stay_ref[0, v] = total[v * rows : (v + 1) * rows]
        other_ref[...] = kept[3] * (kept[2] - kept[0] + kept[1])
        return

    @pl.when(step < SIDE - 1)
    def _():
        total = gradient(0, tokens)
        for v in range(2):
            stay_ref[0, v] = total[v * tokens : v * tokens + rows]
            other_ref[0, v] = total[v * tokens + rows : (v + 1) * tokens].astype(bf16)

    @pl.when(step == SIDE - 1)
    def _():
        total = gradient(rows, rows)
        for v in range(2):
            other_ref[0, v] = total[v * rows : (v + 1) * rows].astype(bf16)


def readout_back(stats_near, stats_come, weight, logits, readout_rows, far):
    tokens, entries = logits.shape[2:]
    width = readout_rows.shape[1]
    rows = tokens // 2
    pages = SIDE if far else 1
    shape = jax.ShapeDtypeStruct
    block = (1, 2, rows, width)
    if far:
        out_shape = (
            shape((SIDE - 1, 2, rows, width), f32),
            shape((SIDE, 2, rows, width), bf16),
        )
        out_specs = (
            pl.BlockSpec(block, lambda i: (jnp.minimum(i, SIDE - 2), 0, 0, 0)),
            pl.BlockSpec(block, lambda i: (i, 0, 0, 0)),
        )
    else:
        out_shape = (shape(block, f32), shape((tokens, 128), f32))
        out_specs = (whole(*block), whole(tokens, 128))

    def page(i):
        return lax.rem(i + 1, SIDE) if far else i

    here = tokens if far else rows
    return pl.pallas_call(
        partial(readout_back_kernel, far),
        out_shape=out_shape,
        grid=(pages,),
        in_specs=[
            once(SIDE, SIDE, 8, tokens),
            once(SIDE, SIDE, 8, tokens),
            pl.BlockSpec((1, tokens, 128), lambda i: (page(i), 0, 0)),
            pl.BlockSpec((1, 2, here, entries), lambda i: (page(i), 0, 0, 0)),
            once(entries, width),
        ],
        out_specs=out_specs,
        scratch_shapes=[
            pltpu.VMEM((4, tokens, 128), f32),
            pltpu.VMEM((2, here, entries), bf16),
        ],
        compiler_params=pltpu.CompilerParams(vmem_limit_bytes=58 * MIB),
        cost_estimate=pl.CostEstimate(
            flops=4 * pages * here * entries * width,
            bytes_accessed=2 * entries * width + 8 * pages * here * entries,
            transcendentals=2 * pages * here * entries,
        ),
    )(stats_near, stats_come, weight, logits, readout_rows)


FIRST_AXES = ((4, 16), (16, 1), (1, 4))
SECOND_AXES = ((4, 16), (16, 4))


def swapped(block):
    return lax.ppermute(block, "mem", [(0, 1), (1, 0)])


def along_line(block, distance):
    route = [(d, d // SIDE * SIDE + (d - distance) % SIDE) for d in range(CHIPS)]
    return lax.ppermute(block, "dp", route)


def lines(stride, core):
    starts = [d for d in range(CHIPS) if (d // stride) % SIDE == 0]
    return [[2 * (start + stride * k) + core for k in range(SIDE)] for start in starts]


def digit_of(strides):
    chip, core = lax.axis_index("dp"), lax.axis_index("mem")
    return jnp.where(core == 0, chip // strides[0], chip // strides[1]) % SIDE


def along_lines(block, strides, r):
    route = []
    for d in range(CHIPS):
        for m, stride in enumerate(strides):
            own = d // stride % SIDE
            to = d + ((own + r) % SIDE - own) * stride
            route.append((2 * d + m, 2 * to + m))
    return lax.ppermute(block, ("dp", "mem"), route)


def line_sum(part, strides):
    parts = part.reshape(SIDE, -1, part.shape[-1])
    digit = digit_of(strides)
    return parts_sum(
        [lax.dynamic_index_in_dim(parts, (digit + r) % SIDE, 0, False) for r in range(SIDE)],
        strides,
    )


def parts_sum(parts, strides):
    come = [along_lines(parts[r], strides, r) for r in range(1, SIDE)]
    total = parts[0].astype(f32)
    for block in come:
        total += block.astype(f32)
    return total


def scattered_sum(bucket, strides):
    flat = bucket.reshape(-1, bucket.shape[-1])
    groups = lines(strides[0], 0) + lines(strides[1], 1)
    return lax.psum_scatter(
        flat, ("dp", "mem"), axis_index_groups=groups, scatter_dimension=0, tiled=True
    )


def outer_kernel(items, orders, core_ref, *refs):
    inputs, out_ref, turned = refs[: 4 * len(items)], refs[4 * len(items)], refs[-len(items) :]
    step = pl.program_id(0)
    core = core_ref[0]

    def place(chip):
        at = [0, 0]
        for m in range(2):
            for stride in orders[m]:
                at[m] = at[m] * SIDE + chip // stride % SIDE
        return jnp.where(core == 0, at[0], at[1])

    def turn(lefts, to, groups):
        for start in range(0, lefts[0].shape[1], 1024):
            flat = jnp.concatenate([left[:, start : start + 1024] for left in lefts], 0).T
            if groups == 1:
                to[0, start : start + 1024] = flat
                continue
            per = ROWS * groups
            for c in range(1024 // per):
                chip = start // per + c
                for g in range(groups):
                    at = c * per + g * ROWS
                    to[g, chip * ROWS : (chip + 1) * ROWS] = flat[at : at + ROWS]

    def multiply(rights, to, begin, tiles):
        at = step - begin
        group = at // tiles
        column = pl.ds(pl.multiple_of((at - group * tiles) * TILE, TILE), TILE)
        both = jnp.concatenate([right[:, column] for right in rights], 0)
        result = dot(to[group], both).astype(bf16)
        for chip in range(CHIPS):
            out_ref[place(chip)] = result[chip * ROWS : (chip + 1) * ROWS]

    for k, (groups, tiles, begin, end) in enumerate(items):
        lefts, rights, to = inputs[4 * k : 4 * k + 2], inputs[4 * k + 2 : 4 * k + 4], turned[k]
        pl.when(step == begin)(partial(turn, lefts, to, groups))
        pl.when((step >= begin) & (step < end))(partial(multiply, rights, to, begin, tiles))


def outer_products(core, products, axes):
    items, scratch = [], []
    total = flops = 0
    for left, left_come, right, _ in products:
        groups = left.shape[1] // (ROWS * CHIPS)
        depth = left.shape[0] + left_come.shape[0]
        columns = right.shape[1]
        scratch.append(pltpu.VMEM((groups, ROWS * CHIPS, depth), bf16))
        begin = total // TILE
        total += groups * columns
        flops += 2 * groups * ROWS * CHIPS * columns * depth
        items.append((groups, columns // TILE, begin, total // TILE))
    operands = [array for product in products for array in product]
    return pl.pallas_call(
        partial(outer_kernel, tuple(items), tuple(zip(*axes))),
        out_shape=jax.ShapeDtypeStruct((CHIPS, ROWS, total), bf16),
        grid_spec=pltpu.PrefetchScalarGridSpec(
            num_scalar_prefetch=1,
            grid=(total // TILE,),
            in_specs=[pl.BlockSpec(memory_space=pltpu.VMEM) for _ in operands],
            out_specs=pl.BlockSpec((CHIPS, ROWS, TILE), lambda i, core: (0, 0, i)),
            scratch_shapes=scratch,
        ),
        compiler_params=pltpu.CompilerParams(vmem_limit_bytes=58 * MIB),
        cost_estimate=pl.CostEstimate(
            flops=flops, bytes_accessed=CHIPS * ROWS * total * 2, transcendentals=0
        ),
    )(core, *operands)


LINE = ROWS * SIDE
DEPTHS = tuple(
    2 * SIDE * (PACK[k + 1] - PACK[k]) // (2 if k == 4 else 1) for k in range(len(PACK) - 1)
)


def turn_kernel(orders, core_ref, packs_ref, out_ref):
    core = core_ref[0]
    start = 0
    for k, depth in enumerate(DEPTHS):
        numbers = range(0, 2 * SIDE, 2 if k == 4 else 1)
        blocks = [packs_ref[number, PACK[k] : PACK[k + 1]] for number in numbers]
        flat = jnp.concatenate(blocks, 0).T
        for line in range(SIDE * SIDE):
            z, y = line // SIDE, line % SIDE
            digit = {4: y, 16: z}
            at = [SIDE * digit[first] + digit[second] for first, second in orders]
            at = pl.multiple_of(jnp.where(core == 0, at[0], at[1]) * LINE, LINE)
            out_ref[pl.ds(at, LINE), start : start + depth] = flat[line * LINE : (line + 1) * LINE]
        start += depth


def turned_packs(core, packs, axes):
    width = packs.shape[2]
    return pl.pallas_call(
        partial(turn_kernel, tuple(zip(*axes))),
        in_specs=scalar_first(1),
        out_shape=jax.ShapeDtypeStruct((width, sum(DEPTHS)), bf16),
        compiler_params=pltpu.CompilerParams(vmem_limit_bytes=58 * MIB),
        cost_estimate=pl.CostEstimate(flops=0, bytes_accessed=20 * MIB, transcendentals=0),
    )(core, packs)


def line_products_kernel(
    digit_ref, turned_ref, come_ref, vectors_ref, *refs
):
    outs, (joint, plain, cross, wide) = refs[:SIDE], refs[SIDE:]
    rows = SENT[1]

    @pl.when(pl.program_id(0) == 0)
    def _():
        def part(number, k):
            return come_ref[number, SENT[k] : SENT[k + 1]]

        def added(first, second):
            return (first.astype(f32) + second.astype(f32)).astype(bf16)

        for number in range(2 * SIDE):
            at = number * rows
            here = slice(at, at + rows)
            joint[here, :PAIR] = part(number, 0)
            for k in (4, 5):
                share = added(part(number, k)[:rows], part(number ^ 1, k)[rows:])
                joint[here, (k - 3) * PAIR : (k - 2) * PAIR] = share
            plain[here, :PAIR] = part(number, 1)
            plain[here, PAIR:] = part(number, 2)
            wide[2 * at : 2 * (at + rows)] = part(number, 3)
        for chip in range(SIDE):
            here = slice(chip * rows, (chip + 1) * rows)
            for k in (6, 7):
                column = slice((k - 6) * PAIR, (k - 5) * PAIR)
                cross[here, column] = added(part(2 * chip, k), part(2 * chip + 1, k))

    ends = [sum(DEPTHS[: k + 1]) for k in range(len(DEPTHS))]
    a1, o, a2, oc, memory = (
        turned_ref[:, end - depth : end] for end, depth in zip(ends, DEPTHS)
    )
    blocks = [
        dot(a1, joint[...]),
        dot(o, plain[:, :PAIR]),
        dot(a2, plain[:, PAIR:]),
        dot(memory, cross[...]),
        dot(oc, wide[...]),
        vectors_ref[...].astype(f32),
    ]
    result = jnp.concatenate(blocks, 1).astype(bf16)
    for r, out in enumerate(outs):

        @pl.when(pl.program_id(0) == r)
        def _(out=out):
            out[...] = result


def line_products(digit, turned, come, vectors):
    width, depth = turned.shape
    block = width // SIDE
    columns = 9 * PAIR

    def part(i, digit):
        return (lax.rem(digit[0] + i, SIDE), 0)

    def fixed(*dims):
        return pl.BlockSpec(dims, lambda i, digit: (0,) * len(dims), pipeline_mode=pl.Buffered(1))

    return pl.pallas_call(
        line_products_kernel,
        grid_spec=pltpu.PrefetchScalarGridSpec(
            num_scalar_prefetch=1,
            grid=(SIDE,),
            in_specs=[
                pl.BlockSpec((block, depth), part),
                fixed(2 * SIDE, SENT[-1], PAIR),
                pl.BlockSpec((block, PAIR), part),
            ],
            out_specs=tuple(fixed(block, columns) for _ in range(SIDE)),
            scratch_shapes=[
                pltpu.VMEM((DEPTHS[0], 3 * PAIR), bf16),
                pltpu.VMEM((DEPTHS[1], 2 * PAIR), bf16),
                pltpu.VMEM((DEPTHS[4], 2 * PAIR), bf16),
                pltpu.VMEM((DEPTHS[3], PAIR), bf16),
            ],
        ),
        out_shape=(jax.ShapeDtypeStruct((block, columns), bf16),) * SIDE,
        compiler_params=pltpu.CompilerParams(vmem_limit_bytes=58 * MIB),
        cost_estimate=pl.CostEstimate(
            flops=2 * 10**9, bytes_accessed=14 * MIB, transcendentals=0
        ),
    )(digit, turned, come, vectors)


def collect_kernel(come_ref, *outs):
    qkv, out, q, kv, cross_out, gains, biases = outs
    targets = [(qkv, 0), (qkv, 1), (qkv, 2), (out, 0), (q, 0), (kv, 0), (kv, 1), (cross_out, 0)]
    for number in range(2 * SIDE):
        for k, (target, block) in enumerate(targets):
            start = (block * 2 * SIDE + number) * PAIR
            target[:, start : start + PAIR] = come_ref[number, :, k * PAIR : (k + 1) * PAIR]
    total = come_ref[0, :, 8 * PAIR :]
    for number in range(1, 2 * SIDE):
        total += come_ref[number, :, 8 * PAIR :]
    total = jnp.concatenate([total, jnp.zeros((PAIR - total.shape[0], PAIR), f32)], 0).T
    gains[...] = total[:4, : ROWS // 2]
    biases[...] = total[4:8, : ROWS // 2]


def collected(come):
    return pl.pallas_call(
        collect_kernel,
        out_shape=tuple(
            jax.ShapeDtypeStruct((ROWS // 2, columns), f32)
            for columns in (24 * PAIR, 8 * PAIR, 8 * PAIR, 16 * PAIR, 8 * PAIR)
        )
        + (jax.ShapeDtypeStruct((4, ROWS // 2), f32),) * 2,
    )(come)


def divide_kernel(grouped, core_ref, sums_ref, keep_ref, give_ref):
    core = core_ref[0]
    half = grouped // 2
    columns = sums_ref.shape[1]
    for ref, side in ((keep_ref, core), (give_ref, 1 - core)):
        if grouped:
            start = pl.ds(pl.multiple_of(side * half, 128), half)
            block = sums_ref[:, start]
            ref[:, :half] = block[: ROWS // 2]
            ref[:, half:grouped] = block[ROWS // 2 :]
        rows = pl.ds(pl.multiple_of(side * (ROWS // 2), 8), ROWS // 2)
        if columns > grouped:
            ref[:, grouped:] = sums_ref[rows, grouped:]


def divided(core, sums, grouped):
    shape = jax.ShapeDtypeStruct((ROWS // 2, sums.shape[1]), f32)
    return pl.pallas_call(
        partial(divide_kernel, grouped),
        in_specs=scalar_first(1),
        out_shape=(shape, shape),
    )(core, sums)


def assemble_kernel(layout, core_ref, keep_ref, come_ref, *outs):
    core = core_ref[0]
    for ref, side in ((keep_ref, core), (come_ref, 1 - core)):
        at = 0
        for out, (grouped, columns, span) in zip(outs, layout):
            part = span // 2
            if grouped:
                for g in range(2):
                    for h in range(2):
                        rows = slice(g * ROWS + h * ROWS // 2, g * ROWS + (h + 1) * ROWS // 2)
                        start = at + h * 2 * part + g * part
                        column = pl.ds(pl.multiple_of(side * part, 128), part)
                        out[rows, column] = ref[:, start : start + part]
                at += 4 * part
                continue
            for k in range(0, columns, span):
                column = pl.ds(pl.multiple_of(k + side * part, 128), part)
                out[:, column] = ref[:, at : at + part]
                at += part


def assembled(core, keep, come, layout):
    return pl.pallas_call(
        partial(assemble_kernel, tuple(layout)),
        in_specs=scalar_first(2),
        out_shape=tuple(
            jax.ShapeDtypeStruct((2 * ROWS if grouped else ROWS // 2, columns), f32)
            for grouped, columns, span in layout
        ),
    )(core, keep, come)


def on_device(
    tokens,
    memory,
    lengths,
    segments,
    key_mask,
    w_self_qkv,
    w_self_out,
    w_cross_q,
    w_cross_kv,
    w_cross_out,
    w_up,
    w_down,
    norm_gains,
    norm_biases,
    readout,
):
    tok_rows = tokens.shape[1]
    width = tokens.shape[2]
    half = lax.axis_index("mem")
    core = half.astype(jnp.int32).reshape(1)
    page_index = lax.axis_index("dp")
    patches = 2 * memory.shape[2]

    vocab_dev = readout.shape[1]
    readout_turned = jnp.pad(readout.T, ((0, ENTRIES - vocab_dev), (0, 0)))
    planes = [[d for d in range(CHIPS) if d % SIDE == x] for x in range(SIDE)]
    readout_part = lax.all_gather(
        readout_turned, "dp", axis=0, tiled=True, axis_index_groups=planes
    )
    is_entry = jnp.arange(readout_part.shape[0]) % ENTRIES < vocab_dev
    entry_bias = jnp.where(is_entry, 0.0, masked_score).astype(f32)[None]

    tokens_own = tokens[0]
    tokens_page = jnp.concatenate([tokens_own, swapped(tokens_own)], 0)
    memory_own = memory[:, 0]
    memory_come = swapped(memory_own)
    memory_rows = jnp.where(
        half == 0,
        jnp.concatenate([memory_own, memory_come], 1),
        jnp.concatenate([memory_come, memory_own], 1),
    ).reshape(2 * patches, width)
    mask_own = key_mask[0].astype(f32)
    mask_come = swapped(mask_own)
    mask_page = jnp.where(
        half == 0,
        jnp.concatenate([mask_own, mask_come]),
        jnp.concatenate([mask_come, mask_own]),
    )
    keep = jnp.tile(jnp.repeat(mask_page, 2), 2)[None]
    own_positions = jnp.arange(tok_rows) + half * tok_rows
    other_positions = jnp.arange(tok_rows) + (1 - half) * tok_rows
    key_positions = jnp.concatenate([own_positions, other_positions])
    cut = segments[0].reshape(2, tok_rows)
    own_segments = lax.dynamic_index_in_dim(cut, half, 0, False)
    other_segments = lax.dynamic_index_in_dim(cut, 1 - half, 0, False)
    key_segments = jnp.concatenate([own_segments, other_segments])
    allowed = (key_positions[None, :] <= own_positions[:, None]) & (
        key_segments[None, :] == own_segments[:, None]
    )
    allowed = allowed.astype(f32)
    count = jnp.sum(lengths).astype(f32)
    line = page_index // SIDE * SIDE + (page_index + jnp.arange(SIDE)) % SIDE
    valid = key_positions[None] < lengths[line][:, None]
    row_weight = (valid.astype(f32) / count)[:, :, None]
    row_weight = jnp.broadcast_to(row_weight, row_weight.shape[:2] + (128,))

    weights = (w_self_qkv, w_self_out, w_cross_q, w_cross_kv, w_cross_out)
    q, kv, h1, qc, kvc, h2, a3, pack = attention(
        tokens_page, allowed, memory_rows, keep, weights, norm_gains, norm_biases
    )
    slope, act, h3, layer_out, final = feed_forward(h2, a3, w_up, w_down, norm_gains, norm_biases)
    final = final.reshape(2, tok_rows, width)
    near = jnp.stack([final] + [along_line(final, r) for r in range(1, SIDE)])
    final_line = jnp.stack([near, swapped(near)], 1).transpose(2, 0, 1, 3, 4)
    final_line = final_line.reshape(2, 2 * SIDE * tok_rows, width)
    a3_other, act_other = swapped(a3), swapped(act)

    final_line, row_weight = lax.optimization_barrier((final_line, row_weight))

    line_groups = [
        [2 * (start + k) + m for k in range(SIDE) for m in range(2)]
        for start in range(0, CHIPS, SIDE)
    ]
    packs = lax.all_gather(pack, ("dp", "mem"), axis_index_groups=line_groups)

    def exchanged(block):
        return lax.all_to_all(
            block, ("dp", "mem"), 0, 0, axis_index_groups=line_groups, tiled=True
        )

    logits, stats = logits_and_stats(final_line, readout_part, entry_bias)
    stats = jnp.stack([stats] + [along_line(stats, r) for r in range(1, SIDE)])
    stats_come = swapped(stats)
    far_stay, give = readout_back(stats, stats_come, row_weight, logits, readout_part, True)
    come = swapped(give)
    far = (far_stay + come[: SIDE - 1].astype(f32)).astype(bf16)
    logits, far, core_late = lax.optimization_barrier((logits, far, core))
    far = [along_line(far[r - 1], -r) for r in range(1, SIDE)]
    own, terms = readout_back(stats, stats_come, row_weight, logits, readout_part, False)
    terms = terms[:, 0].reshape(2, tok_rows).sum(1)
    loss = (terms[0] + terms[1]).reshape(1)
    turned = turned_packs(core_late, packs, SECOND_AXES)
    own, turned = lax.optimization_barrier((own, turned))
    grad_parts = [part.reshape(2 * tok_rows, width) for part in [own[0], come[SIDE - 1]] + far]

    gh3_keep, gh3_give, gup_keep, gup_give, gh2, vectors_ff = feed_forward_back(
        core, grad_parts, h3, h2, slope, w_up, w_down, norm_gains
    )
    first_bucket = outer_products(
        core,
        [
            (act, act_other, gh3_keep, swapped(gh3_give)),
            (a3, a3_other, gup_keep, swapped(gup_give)),
        ],
        FIRST_AXES,
    )
    gh2, first_bucket = lax.optimization_barrier((gh2, first_bucket))
    first_part = scattered_sum(first_bucket, FIRST_AXES[0])

    gh1, gq, gkv, gkv_give, gkvc, vectors_att, sent = attention_back(
        gh2, allowed, keep, kvc, qc, h1, kv, q, w_cross_out, w_cross_q, w_self_out, norm_gains
    )
    sent = exchanged(sent)
    tokens_grad, memory_grad, vectors_in = inputs_back(
        core, tokens_own, gh1, gq, gkv, swapped(gkv_give), gkvc, swapped(gkvc), w_self_qkv,
        w_cross_kv, norm_gains,
    )
    sent, first_part, vectors_in = lax.optimization_barrier((sent, first_part, vectors_in))
    vectors = (vectors_ff + vectors_att + vectors_in).astype(bf16)
    vectors = jnp.pad(vectors.T, ((0, 0), (0, PAIR - 8))).reshape(SIDE, SIDE, LINE, PAIR)
    vectors = jnp.where(half == 0, vectors.transpose(1, 0, 2, 3), vectors).reshape(width, PAIR)
    digit = digit_of(SECOND_AXES[0]).astype(jnp.int32).reshape(1)
    second_parts = line_products(digit, turned, sent, vectors)
    second_sums = parts_sum(second_parts, SECOND_AXES[0]).astype(bf16)
    first_sums = scattered_sum(first_part, FIRST_AXES[1])
    first_sums, second_sums = lax.optimization_barrier((first_sums, second_sums))
    second_sums = line_sum(second_sums, SECOND_AXES[1])
    first_sums = line_sum(first_sums, FIRST_AXES[2])
    first_sums, second_sums = lax.optimization_barrier((first_sums, second_sums))

    first_keep, first_give = divided(core, first_sums, 2 * width)
    weight_down, weight_up = assembled(
        core,
        first_keep,
        swapped(first_give),
        [(True, width, width), (False, 4 * width, 4 * width)],
    )
    weight_qkv, weight_out, weight_q, weight_kv, weight_cross_out, grad_gains, grad_biases = (
        collected(exchanged(second_sums.reshape(2 * SIDE, ROWS // 2, -1)))
    )
    return (
        loss,
        layer_out.reshape(2, 1, tok_rows, width),
        tokens_grad[None],
        memory_grad[:, None],
        weight_qkv,
        weight_out,
        weight_q,
        weight_kv,
        weight_cross_out,
        weight_up,
        weight_down,
        grad_gains,
        grad_biases,
    )


def solution(mesh):
    in_specs = (
        P("dp", "mem", None),
        P(None, "dp", "mem", None),
        P(),
        P("dp", None),
        P("dp", "mem"),
        P(),
        P(),
        P(),
        P(),
        P(),
        P(),
        P(),
        P(),
        P(),
        P(None, ("dp", "mem")),
    )
    out_specs = (
        P("dp"),
        P(None, "dp", "mem", None),
        P("dp", "mem", None),
        P(None, "dp", "mem", None),
        P(("dp", "mem"), None),
        P(("dp", "mem"), None),
        P(("dp", "mem"), None),
        P(("dp", "mem"), None),
        P(("dp", "mem"), None),
        P(("dp", "mem"), None),
        P(("dp", "mem"), None),
        P(None, ("dp", "mem")),
        P(None, ("dp", "mem")),
    )
    return jax.shard_map(
        on_device, mesh=mesh, in_specs=in_specs, out_specs=out_specs, check_vma=False
    )
```

```python
from functools import partial

import jax
import jax.numpy as jnp
from jax import lax
from jax.experimental import pallas as pl
from jax.experimental.pallas import tpu as pltpu
from jax.sharding import PartitionSpec as P

HEAD = 64
PAIR = 2 * HEAD
SIDE = 4
CHIPS = SIDE * SIDE * SIDE
ROWS = 16
TILE = 1024
FF_TILE = 1024
BLOCK = 640
CHUNK = 16
PARTS = ((0, 1024), (1024, 2048), (2048, 3200))
ENTRIES = 200
MIB = 1024 * 1024
epsilon = 1e-05
masked_score = -1e30
bf16 = jnp.bfloat16
f32 = jnp.float32


def dot(left, right):
    return jnp.dot(left, right, preferred_element_type=f32)


def dot_nt(left, right):
    return lax.dot_general(left, right, (((1,), (1,)), ((), ())), preferred_element_type=f32)


def dot_tn(left, right):
    return lax.dot_general(left, right, (((0,), (0,)), ((), ())), preferred_element_type=f32)


def normalized(values):
    centre = values - jnp.mean(values, -1, keepdims=True)
    inverse = lax.rsqrt(jnp.mean(centre * centre, -1, keepdims=True) + epsilon)
    return centre * inverse, inverse


def norm_back(upstream, normed, inverse, gain):
    scaled = upstream * gain
    back = inverse * (
        scaled
        - jnp.mean(scaled, -1, keepdims=True)
        - normed * jnp.mean(scaled * normed, -1, keepdims=True)
    )
    return back, jnp.sum(upstream * normed, 0, keepdims=True), jnp.sum(upstream, 0, keepdims=True)


def lower_lanes(shape):
    return lax.broadcasted_iota(jnp.int32, shape, 1) < HEAD


def parted(block):
    low = lower_lanes(block.shape)
    none = jnp.zeros_like(block)
    return jnp.concatenate([jnp.where(low, block, none), jnp.where(low, none, block)], 0)


def merged(block):
    rows = block.shape[0] // 2
    return jnp.where(lower_lanes((rows, PAIR)), block[:rows], block[rows:])


def self_softmax(queries, keys, allowed):
    scores = dot_nt(queries, keys) * HEAD ** (-0.5)
    scores = jnp.where(allowed, scores, masked_score)
    weights = jnp.exp(scores - jnp.max(scores, -1, keepdims=True))
    return weights * (1.0 / jnp.sum(weights, -1, keepdims=True))


def by_view(values, is_first, combine, neutral):
    first = combine(jnp.where(is_first, values, neutral), -1, keepdims=True)
    second = combine(jnp.where(is_first, neutral, values), -1, keepdims=True)
    return jnp.where(is_first, first, second)


def cross_softmax(queries, keys, kept, is_first):
    scores = dot_nt(queries, keys) * HEAD ** (-0.5)
    scores = jnp.where(kept, scores, masked_score)
    weights = jnp.exp(scores - by_view(scores, is_first, jnp.max, masked_score))
    return weights * (1.0 / by_view(weights, is_first, jnp.sum, 0.0))


def each_view(block, is_first):
    none = jnp.zeros_like(block)
    return jnp.concatenate([jnp.where(is_first, block, none), jnp.where(is_first, none, block)], 0)


def allowed_of(allowed_ref):
    allowed = allowed_ref[...] > 0.5
    return jnp.concatenate([allowed, allowed], 0)


PACK = (0, 96, 192, 288, 480, 576)
SENT = (0, 96, 192, 288, 480, 672, 864, 960, 1056)


def attention_kernel(
    tokens_ref, allowed_ref, memory_ref, keep_ref, w_qkv, w_out, w_q, w_kv, w_cross_out, gains,
    biases, q_ref, kv_ref, h1_ref, qc_ref, kvc_ref, h2_ref, a3_ref, pack_ref, probs_ref,
    probs_cross_ref, a1,
):
    rows = q_ref.shape[0]
    width = tokens_ref.shape[1]
    a1_rows, o_rows, a2_rows, oc_rows, memory_rows = map(slice, PACK[:-1], PACK[1:])
    first_rows, second_rows = slice(PACK[3], PACK[3] + rows), slice(PACK[3] + rows, PACK[4])
    values = tokens_ref[...].astype(f32)
    normed, _ = normalized(values)
    a1[...] = (normed * gains[0:1] + biases[0:1]).astype(bf16)
    pack_ref[a1_rows] = a1[:rows]
    pack_ref[memory_rows] = memory_ref[...]
    q_ref[...] = dot(a1[:rows], w_qkv[:, :width]).astype(bf16)
    kv_ref[...] = dot(a1[...], w_qkv[:, width:]).astype(bf16)
    allowed = allowed_of(allowed_ref)
    for at in range(0, width, PAIR):
        queries = parted(q_ref[:, at : at + PAIR])
        probs = self_softmax(queries, kv_ref[:, at : at + PAIR], allowed)
        probs_ref[at // PAIR] = probs
        mixed = dot(probs.astype(bf16), kv_ref[:, width + at : width + at + PAIR])
        pack_ref[o_rows, at : at + PAIR] = merged(mixed).astype(bf16)
    h1 = values[:rows] + dot(pack_ref[o_rows], w_out[...])
    h1_ref[...] = h1
    normed, _ = normalized(h1)
    pack_ref[a2_rows] = (normed * gains[1:2] + biases[1:2]).astype(bf16)
    qc_ref[...] = dot(pack_ref[a2_rows], w_q[...]).astype(bf16)
    kvc_ref[...] = dot(memory_ref[...], w_kv[...]).astype(bf16)
    shape = (2 * rows, memory_ref.shape[0])
    kept = jnp.broadcast_to(keep_ref[...], shape) > 0.5
    is_first = lax.broadcasted_iota(jnp.int32, shape, 1) < shape[1] // 2
    for at in range(0, width, PAIR):
        queries = parted(qc_ref[:, at : at + PAIR])
        probs = cross_softmax(queries, kvc_ref[:, at : at + PAIR], kept, is_first)
        probs_cross_ref[at // PAIR] = probs
        mixed = dot(
            each_view(probs.astype(bf16), is_first), kvc_ref[:, width + at : width + at + PAIR]
        )
        pack_ref[first_rows, at : at + PAIR] = merged(mixed[: 2 * rows]).astype(bf16)
        pack_ref[second_rows, at : at + PAIR] = merged(mixed[2 * rows :]).astype(bf16)
    h2 = jnp.concatenate([h1, h1], 0) + dot(pack_ref[oc_rows], w_cross_out[...])
    h2_ref[...] = h2
    normed, _ = normalized(h2)
    a3_ref[...] = (normed * gains[2:3] + biases[2:3]).astype(bf16)


def attention(tokens_page, allowed, memory_rows, keep, weights, gains, biases):
    rows, width = allowed.shape[0], tokens_page.shape[1]
    shape = jax.ShapeDtypeStruct
    return pl.pallas_call(
        attention_kernel,
        out_shape=(
            shape((rows, width), bf16),
            shape((2 * rows, 2 * width), bf16),
            shape((rows, width), f32),
            shape((rows, width), bf16),
            shape((memory_rows.shape[0], 2 * width), bf16),
            shape((2 * rows, width), f32),
            shape((2 * rows, width), bf16),
            shape((PACK[-1], width), bf16),
            shape((width // PAIR, 2 * rows, 2 * rows), f32),
            shape((width // PAIR, 2 * rows, memory_rows.shape[0]), f32),
        ),
        scratch_shapes=[pltpu.VMEM((2 * rows, width), bf16)],
        compiler_params=pltpu.CompilerParams(vmem_limit_bytes=58 * MIB),
        cost_estimate=pl.CostEstimate(
            flops=2 * 10**9, bytes_accessed=24 * MIB, transcendentals=10**6
        ),
    )(tokens_page, allowed, memory_rows, keep, *weights, gains, biases)


def erf_parts(values):
    return 0.5 + 0.5 * lax.erf(values * (0.5**0.5))


def feed_forward_kernel(
    h2_ref, a3_ref, w_up, w_down, gains, biases, slope_ref, act_ref, h3_ref, out_ref, fin_ref, total
):
    step = pl.program_id(0)

    @pl.when(step == 0)
    def _():
        total[...] = jnp.zeros_like(total)

    up = dot(a3_ref[...], w_up[...])
    below = erf_parts(up)
    slope_ref[...] = below + up * jnp.exp(-0.5 * up * up) * (0.5 / jnp.pi) ** 0.5
    act = (up * below).astype(bf16)
    act_ref[...] = act
    total[...] += dot(act, w_down[...])

    @pl.when(step == pl.num_programs(0) - 1)
    def _():
        h3 = h2_ref[...] + total[...]
        h3_ref[...] = h3
        out_ref[...] = h3.astype(bf16)
        normed, _ = normalized(h3)
        fin_ref[...] = (normed * gains[3:4] + biases[3:4]).astype(bf16)


def whole(*shape):
    return pl.BlockSpec(shape, lambda i: (0,) * len(shape))


def feed_forward(h2, a3, w_up, w_down, gains, biases):
    rows, width = h2.shape
    hidden = w_up.shape[1]
    shape = jax.ShapeDtypeStruct
    return pl.pallas_call(
        feed_forward_kernel,
        grid=(hidden // FF_TILE,),
        in_specs=[
            whole(rows, width),
            whole(rows, width),
            pl.BlockSpec((width, FF_TILE), lambda i: (0, i)),
            pl.BlockSpec((FF_TILE, width), lambda i: (i, 0)),
            whole(4, width),
            whole(4, width),
        ],
        out_specs=(
            pl.BlockSpec((rows, FF_TILE), lambda i: (0, i)),
            pl.BlockSpec((rows, FF_TILE), lambda i: (0, i)),
            whole(rows, width),
            whole(rows, width),
            whole(rows, width),
        ),
        out_shape=(
            shape((rows, hidden), f32),
            shape((rows, hidden), bf16),
            shape((rows, width), f32),
            shape((rows, width), bf16),
            shape((rows, width), bf16),
        ),
        scratch_shapes=[pltpu.VMEM((rows, width), f32)],
        compiler_params=pltpu.CompilerParams(vmem_limit_bytes=58 * MIB),
        cost_estimate=pl.CostEstimate(
            flops=4 * rows * width * hidden, bytes_accessed=24 * MIB, transcendentals=rows * hidden
        ),
    )(h2, a3, w_up, w_down, gains, biases)


def halves(block):
    middle = block.shape[1] // 2
    return block[:, :middle], block[:, middle:]


def divide(core, block, keep_ref, give_ref):
    for side in range(2):

        @pl.when(core == side)
        def _(side=side):
            keep_ref[...] = halves(block)[side]
            give_ref[...] = halves(block)[1 - side]


def feed_forward_back_kernel(
    core_ref, own_ref, other_ref, far_a, far_b, far_c, h3_ref, h2_ref, slope_ref, w_up, w_down,
    gains, gh3_keep, gh3_give, gup_keep, gup_give, gh2_ref, vector_ref, gh3, gh3_low_ref, total,
):
    step = pl.program_id(0)
    core = core_ref[0]

    @pl.when(step == 0)
    def _():
        upstream = own_ref[...]
        for ref in (other_ref, far_a, far_b, far_c):
            upstream += ref[...].astype(f32)
        normed, inverse = normalized(h3_ref[...])
        back, gain, bias = norm_back(upstream, normed, inverse, gains[3:4])
        gh3[...] = back
        gh3_low_ref[...] = back.astype(bf16)
        divide(core, gh3_low_ref[...], gh3_keep, gh3_give)
        vector_ref[...] = jnp.zeros_like(vector_ref)
        vector_ref[3:4] = gain
        vector_ref[7:8] = bias
        total[...] = jnp.zeros_like(total)

    grad = dot_nt(gh3_low_ref[...], w_down[...])
    gup = (grad * slope_ref[...]).astype(bf16)
    side = step // (pl.num_programs(0) // 2)

    @pl.when(side == core)
    def _():
        gup_keep[...] = gup

    @pl.when(side != core)
    def _():
        gup_give[...] = gup

    total[...] += dot_nt(gup, w_up[...])

    @pl.when(step == pl.num_programs(0) - 1)
    def _():
        normed, inverse = normalized(h2_ref[...])
        back, gain, bias = norm_back(total[...], normed, inverse, gains[2:3])
        gh2 = gh3[...] + back
        gh2_ref[...] = gh2
        vector_ref[2:3] = gain
        vector_ref[6:7] = bias


def feed_forward_back(core, parts, h3, h2, slope, w_up, w_down, gains):
    rows, width = h2.shape
    hidden = w_up.shape[1]
    tiles = hidden // FF_TILE
    shape = jax.ShapeDtypeStruct

    def all_of(*dims):
        return pl.BlockSpec(dims, lambda i, core: (0,) * len(dims))

    middle = tiles // 2

    def half_tile(kept):
        def index(i, core):
            side = core[0] if kept else 1 - core[0]
            return (0, jnp.clip(i - side * middle, 0, middle - 1))

        return pl.BlockSpec((rows, FF_TILE), index)

    return pl.pallas_call(
        feed_forward_back_kernel,
        grid_spec=pltpu.PrefetchScalarGridSpec(
            num_scalar_prefetch=1,
            grid=(tiles,),
            in_specs=[
                *(all_of(rows, width) for _ in range(7)),
                pl.BlockSpec((rows, FF_TILE), lambda i, core: (0, i)),
                pl.BlockSpec((width, FF_TILE), lambda i, core: (0, i)),
                pl.BlockSpec((FF_TILE, width), lambda i, core: (i, 0)),
                all_of(4, width),
            ],
            out_specs=(
                all_of(rows, width // 2),
                all_of(rows, width // 2),
                half_tile(True),
                half_tile(False),
                all_of(rows, width),
                all_of(8, width),
            ),
            scratch_shapes=[
                pltpu.VMEM((rows, width), f32),
                pltpu.VMEM((rows, width), bf16),
                pltpu.VMEM((rows, width), f32),
            ],
        ),
        out_shape=(
            shape((rows, width // 2), bf16),
            shape((rows, width // 2), bf16),
            shape((rows, hidden // 2), bf16),
            shape((rows, hidden // 2), bf16),
            shape((rows, width), f32),
            shape((8, width), f32),
        ),
        compiler_params=pltpu.CompilerParams(vmem_limit_bytes=58 * MIB),
        cost_estimate=pl.CostEstimate(
            flops=4 * rows * width * hidden,
            bytes_accessed=24 * MIB,
            transcendentals=2 * rows * hidden,
        ),
    )(core, *parts, h3, h2, slope, w_up, w_down, gains)


def attention_back_kernel(
    gh2_ref, probs_ref, probs_cross_ref, kvc_ref, qc_ref, h1_ref, kv_ref, q_ref, w_cross_out, w_q,
    w_out, gains, gh1_ref, gq_ref, gkv_ref, give_ref, gkvc_ref, vector_ref, sent_ref, goc, go, gqc,
    gh1_low,
):
    rows, width = q_ref.shape
    scale = HEAD ** (-0.5)
    sent_rows = list(map(slice, SENT[:-1], SENT[1:]))

    def pairs_of_heads():
        for number in range(2 * SIDE):
            at = number * PAIR
            yield number, sent_ref.at[number], slice(at, at + PAIR), slice(width + at, width + at + PAIR)

    gh2_low = gh2_ref[...].astype(bf16)
    goc[...] = dot_nt(gh2_low, w_cross_out[...]).astype(bf16)
    shape = (2 * rows, kvc_ref.shape[0])
    is_first = lax.broadcasted_iota(jnp.int32, shape, 1) < shape[1] // 2
    for number, to, here, there in pairs_of_heads():
        queries = parted(qc_ref[:, here])
        probs = probs_cross_ref[number]
        upstream = jnp.concatenate([parted(goc[:rows, here]), parted(goc[rows:, here])], 0)
        grad = dot_nt(upstream, kvc_ref[:, there])
        grad = jnp.where(is_first, grad[: 2 * rows], grad[2 * rows :])
        slope = probs * (grad - by_view(probs * grad, is_first, jnp.sum, 0.0))
        slope = slope.astype(bf16)
        change = (merged(dot(slope, kvc_ref[:, here])) * scale).astype(bf16)
        gqc[:, here] = change
        to[sent_rows[2]] = change
        to[sent_rows[3]] = gh2_ref[:, here].astype(bf16)
        change = (dot_tn(slope, queries) * scale).astype(bf16)
        gkvc_ref[:, here] = change
        to[sent_rows[6]] = change
        change = dot_tn(each_view(probs.astype(bf16), is_first), upstream).astype(bf16)
        gkvc_ref[:, there] = change
        to[sent_rows[7]] = change
    normed, inverse = normalized(h1_ref[...])
    back, gain, bias = norm_back(dot_nt(gqc[...], w_q[...]), normed, inverse, gains[1:2])
    vector_ref[...] = jnp.zeros_like(vector_ref)
    vector_ref[1:2] = gain
    vector_ref[5:6] = bias
    gh1 = gh2_ref[:rows] + gh2_ref[rows:] + back
    gh1_ref[...] = gh1
    gh1_low[...] = gh1.astype(bf16)
    go[...] = dot_nt(gh1_low[...], w_out[...]).astype(bf16)
    for number, to, here, there in pairs_of_heads():
        queries = parted(q_ref[:, here])
        probs = probs_ref[number]
        upstream = parted(go[:, here])
        grad = dot_nt(upstream, kv_ref[:, there])
        slope = probs * (grad - jnp.sum(probs * grad, -1, keepdims=True))
        slope = slope.astype(bf16)
        change = (merged(dot(slope, kv_ref[:, here])) * scale).astype(bf16)
        gq_ref[:, here] = change
        to[sent_rows[0]] = change
        to[sent_rows[1]] = gh1_low[:, here]
        change = (dot_tn(slope, queries) * scale).astype(bf16)
        gkv_ref[:, here] = change[:rows]
        give_ref[:, here] = change[rows:]
        to[sent_rows[4]] = change
        change = dot_tn(probs.astype(bf16), upstream).astype(bf16)
        gkv_ref[:, there] = change[:rows]
        give_ref[:, there] = change[rows:]
        to[sent_rows[5]] = change


def scalar_first(count):
    return [pl.BlockSpec(memory_space=pltpu.SMEM)] + [
        pl.BlockSpec(memory_space=pltpu.VMEM) for _ in range(count)
    ]


def attention_back(*operands):
    kvc, kv, q = operands[3], operands[6], operands[7]
    rows, width = q.shape
    shape = jax.ShapeDtypeStruct
    return pl.pallas_call(
        attention_back_kernel,
        out_shape=(
            shape((rows, width), f32),
            shape((rows, width), bf16),
            shape((rows, 2 * width), bf16),
            shape((rows, 2 * width), bf16),
            shape(kvc.shape, bf16),
            shape((8, width), f32),
            shape((2 * SIDE, SENT[-1], PAIR), bf16),
        ),
        scratch_shapes=[
            pltpu.VMEM((2 * rows, width), bf16),
            pltpu.VMEM((rows, width), bf16),
            pltpu.VMEM((rows, width), bf16),
            pltpu.VMEM((rows, width), bf16),
        ],
        compiler_params=pltpu.CompilerParams(vmem_limit_bytes=58 * MIB),
        cost_estimate=pl.CostEstimate(
            flops=2 * 10**9, bytes_accessed=14 * MIB, transcendentals=10**6
        ),
    )(*operands)


def inputs_back_kernel(
    core_ref, tokens_ref, gh1_ref, gq_ref, gkv_ref, come_ref, gkvc_ref, come_cross_ref, w_qkv,
    w_kv, gains, tokens_grad_ref, memory_grad_ref, vector_ref, grads,
):
    core = core_ref[0]
    width = gh1_ref.shape[1]
    pairs = (gkv_ref[...].astype(f32) + come_ref[...].astype(f32)).astype(bf16)
    total = dot_nt(gq_ref[...], w_qkv[:, :width]) + dot_nt(pairs, w_qkv[:, width:])
    normed, inverse = normalized(tokens_ref[...].astype(f32))
    back, gain, bias = norm_back(total, normed, inverse, gains[0:1])
    tokens_grad_ref[...] = gh1_ref[...] + back
    vector_ref[...] = jnp.zeros_like(vector_ref)
    vector_ref[0:1] = gain
    vector_ref[4:5] = bias
    pairs = (gkvc_ref[...].astype(f32) + come_cross_ref[...].astype(f32)).astype(bf16)
    grads[...] = dot_nt(pairs, w_kv[...])
    own = memory_grad_ref.shape[1]
    for view in range(2):
        start = pl.multiple_of(view * 2 * own + core * own, 8)
        memory_grad_ref[view] = grads[pl.ds(start, own)]


def inputs_back(core, *operands):
    rows, width = operands[1].shape
    patches = operands[5].shape[0]
    shape = jax.ShapeDtypeStruct
    return pl.pallas_call(
        inputs_back_kernel,
        in_specs=scalar_first(len(operands)),
        out_shape=(
            shape((rows, width), f32),
            shape((2, patches // 4, width), f32),
            shape((8, width), f32),
        ),
        scratch_shapes=[pltpu.VMEM((patches, width), f32)],
        compiler_params=pltpu.CompilerParams(vmem_limit_bytes=58 * MIB),
        cost_estimate=pl.CostEstimate(flops=10**9, bytes_accessed=14 * MIB, transcendentals=0),
    )(core, *operands)


def logits_kernel(rows_ref, readout_ref, bias_ref, logits_ref, stats_ref, kept):
    tokens = rows_ref.shape[1]
    rows = jnp.concatenate([rows_ref[0], rows_ref[1]], 0)

    def statistics(begin, end):
        spans = range(begin, end, 128)
        for at in range(0, tokens, CHUNK):
            here = slice(at, at + CHUNK)
            first = [logits_ref[0, 0, here, c : c + 128] for c in spans]
            second = [logits_ref[0, 1, here, c : c + 128] for c in spans]
            new_first, new_second = first[0], second[0]
            for a, b in zip(first[1:], second[1:]):
                new_first = jnp.maximum(new_first, a)
                new_second = jnp.maximum(new_second, b)
            total_first = total_apart = total_second = jnp.zeros((CHUNK, 128), f32)
            if begin:
                top_first, top_second = kept[0, here], kept[3, here]
                new_first = jnp.maximum(new_first, top_first)
                new_second = jnp.maximum(new_second, top_second)
                fade_first = jnp.exp(top_first - new_first)
                total_first = kept[1, here] * fade_first
                total_apart = kept[2, here] * fade_first
                total_second = kept[4, here] * jnp.exp(top_second - new_second)
            for a, b in zip(first, second):
                weight = jnp.exp(a - new_first)
                total_first += weight
                total_apart += weight * (a - b)
                total_second += jnp.exp(b - new_second)
            kept[0, here], kept[1, here], kept[2, here] = new_first, total_first, total_apart
            kept[3, here], kept[4, here] = new_second, total_second

    before = None
    for begin, end in PARTS:
        values = dot_nt(rows, readout_ref[begin:end]) + bias_ref[:, begin:end]
        for v in range(2):
            logits_ref[0, v, :, begin:end] = values[v * tokens : (v + 1) * tokens]
        if before:
            statistics(*before)
        before = begin, end
    statistics(*before)

    top_first = jnp.max(kept[0], -1, keepdims=True)
    top_second = jnp.max(kept[3], -1, keepdims=True)
    fade_first = jnp.exp(kept[0] - top_first)
    fade_second = jnp.exp(kept[3] - top_second)
    stats = (
        top_first,
        jnp.sum(kept[1] * fade_first, -1, keepdims=True),
        jnp.sum(kept[2] * fade_first, -1, keepdims=True),
        top_second,
        jnp.sum(kept[4] * fade_second, -1, keepdims=True),
    )
    lane = lax.broadcasted_iota(jnp.int32, kept.shape[1:], 1)
    result = jnp.zeros(kept.shape[1:], f32)
    for k, stat in enumerate(stats):
        result = jnp.where(lane == k, stat, result)
    stats_ref[0] = result.T[:8]


def once(*shape):
    return pl.BlockSpec(shape, lambda i: (0,) * len(shape), pipeline_mode=pl.Buffered(1))


def logits_and_stats(rows, readout_rows, bias):
    views, tokens, width = rows.shape
    entries = readout_rows.shape[0]
    page = tokens // SIDE
    shape = jax.ShapeDtypeStruct
    return pl.pallas_call(
        logits_kernel,
        out_shape=(
            shape((SIDE, 2, page, entries), f32),
            shape((SIDE, 8, page), f32),
        ),
        grid=(SIDE,),
        in_specs=[
            pl.BlockSpec((2, page, width), lambda i: (0, i, 0)),
            once(entries, width),
            once(1, entries),
        ],
        out_specs=(
            pl.BlockSpec((1, 2, page, entries), lambda i: (i, 0, 0, 0)),
            pl.BlockSpec((1, 8, page), lambda i: (i, 0, 0)),
        ),
        scratch_shapes=[pltpu.VMEM((5, page, 128), f32)],
        compiler_params=pltpu.CompilerParams(vmem_limit_bytes=58 * MIB),
        cost_estimate=pl.CostEstimate(
            flops=4 * tokens * entries * width,
            bytes_accessed=2 * entries * width + 8 * tokens * entries,
            transcendentals=2 * tokens * entries,
        ),
    )(rows, readout_rows, bias)


def merged_stats(near_ref, come_ref, slot):
    tokens = near_ref.shape[3]
    middle = tokens // 2
    parts = []
    for ref, flipped in ((near_ref, False), (come_ref, True)):
        for r in range(SIDE):
            part = ref[r, lax.rem(slot + SIDE - r, SIDE)]
            if flipped:
                part = jnp.concatenate([part[:, middle:], part[:, :middle]], 1)
            parts.append(part)
    top_first = parts[0][0:1]
    top_second = parts[0][3:4]
    for part in parts[1:]:
        top_first = jnp.maximum(top_first, part[0:1])
        top_second = jnp.maximum(top_second, part[3:4])
    total_first = total_apart = total_second = jnp.zeros((1, tokens), f32)
    for part in parts:
        fade = jnp.exp(part[0:1] - top_first)
        total_first += part[1:2] * fade
        total_apart += part[2:3] * fade
        total_second += part[4:5] * jnp.exp(part[3:4] - top_second)
    first_lse = top_first + jnp.log(total_first)
    second_lse = top_second + jnp.log(total_second)
    return first_lse, second_lse, total_apart / total_first


def readout_back_kernel(
    far, near_ref, come_ref, weight_ref, logits_ref, readout_ref, stay_ref, other_ref, kept, slopes
):
    step = pl.program_id(0)
    tokens = weight_ref.shape[1]
    rows = tokens // 2
    slot = lax.rem(step + 1, SIDE) if far else 0
    for k, row in enumerate(merged_stats(near_ref, come_ref, slot)):
        kept[k] = jnp.broadcast_to(row, (128, row.shape[1])).T
    kept[3] = weight_ref[0]

    def gradient(start, count):
        def derivatives(begin, end):
            for at in range(start, start + count, CHUNK):
                here = slice(at, at + CHUNK)
                first_lse, second_lse, apart, weight = (kept[k, here] for k in range(4))
                for c in range(begin, end, 128):
                    first = logits_ref[0, 0, here, c : c + 128]
                    second = logits_ref[0, 1, here, c : c + 128]
                    first_prob = jnp.exp(first - first_lse) * weight
                    second_prob = jnp.exp(second - second_lse) * weight
                    change = first_prob * (first - second - apart)
                    slopes[0, here, c : c + 128] = change.astype(bf16)
                    slopes[1, here, c : c + 128] = (second_prob - first_prob).astype(bf16)

        derivatives(*PARTS[0])
        total = None
        for i, (begin, end) in enumerate(PARTS):
            block = [slopes[v, start : start + count, begin:end] for v in range(2)]
            result = dot(jnp.concatenate(block, 0), readout_ref[begin:end])
            if i + 1 < len(PARTS):
                derivatives(*PARTS[i + 1])
            total = result if total is None else total + result
        return total

    if not far:
        total = gradient(0, rows)
        for v in range(2):
            stay_ref[0, v] = total[v * rows : (v + 1) * rows]
        other_ref[...] = kept[3] * (kept[2] - kept[0] + kept[1])
        return

    @pl.when(step < SIDE - 1)
    def _():
        total = gradient(0, tokens)
        for v in range(2):
            stay_ref[0, v] = total[v * tokens : v * tokens + rows].astype(bf16)
            other_ref[0, v] = total[v * tokens + rows : (v + 1) * tokens].astype(bf16)

    @pl.when(step == SIDE - 1)
    def _():
        total = gradient(rows, rows)
        for v in range(2):
            other_ref[0, v] = total[v * rows : (v + 1) * rows].astype(bf16)


def readout_back(stats_near, stats_come, weight, logits, readout_rows, far):
    tokens, entries = logits.shape[2:]
    width = readout_rows.shape[1]
    rows = tokens // 2
    pages = SIDE if far else 1
    shape = jax.ShapeDtypeStruct
    block = (1, 2, rows, width)
    if far:
        out_shape = (
            shape((SIDE - 1, 2, rows, width), bf16),
            shape((SIDE, 2, rows, width), bf16),
        )
        out_specs = (
            pl.BlockSpec(block, lambda i: (jnp.minimum(i, SIDE - 2), 0, 0, 0)),
            pl.BlockSpec(block, lambda i: (i, 0, 0, 0)),
        )
    else:
        out_shape = (shape(block, f32), shape((tokens, 128), f32))
        out_specs = (whole(*block), whole(tokens, 128))

    def page(i):
        return lax.rem(i + 1, SIDE) if far else i

    here = tokens if far else rows
    return pl.pallas_call(
        partial(readout_back_kernel, far),
        out_shape=out_shape,
        grid=(pages,),
        in_specs=[
            once(SIDE, SIDE, 8, tokens),
            once(SIDE, SIDE, 8, tokens),
            pl.BlockSpec((1, tokens, 128), lambda i: (page(i), 0, 0)),
            pl.BlockSpec((1, 2, here, entries), lambda i: (page(i), 0, 0, 0)),
            once(entries, width),
        ],
        out_specs=out_specs,
        scratch_shapes=[
            pltpu.VMEM((4, tokens, 128), f32),
            pltpu.VMEM((2, here, entries), bf16),
        ],
        compiler_params=pltpu.CompilerParams(vmem_limit_bytes=58 * MIB),
        cost_estimate=pl.CostEstimate(
            flops=4 * pages * here * entries * width,
            bytes_accessed=2 * entries * width + 8 * pages * here * entries,
            transcendentals=2 * pages * here * entries,
        ),
    )(stats_near, stats_come, weight, logits, readout_rows)


FIRST_AXES = ((4, 16), (16, 1), (1, 4))
SECOND_AXES = ((4, 16), (16, 4))


def swapped(block):
    return lax.ppermute(block, "mem", [(0, 1), (1, 0)])


def along_line(block, distance):
    route = [(d, d // SIDE * SIDE + (d - distance) % SIDE) for d in range(CHIPS)]
    return lax.ppermute(block, "dp", route)


def lines(stride, core):
    starts = [d for d in range(CHIPS) if (d // stride) % SIDE == 0]
    return [[2 * (start + stride * k) + core for k in range(SIDE)] for start in starts]


def digit_of(strides):
    chip, core = lax.axis_index("dp"), lax.axis_index("mem")
    return jnp.where(core == 0, chip // strides[0], chip // strides[1]) % SIDE


def along_lines(block, strides, r):
    route = []
    for d in range(CHIPS):
        for m, stride in enumerate(strides):
            own = d // stride % SIDE
            to = d + ((own + r) % SIDE - own) * stride
            route.append((2 * d + m, 2 * to + m))
    return lax.ppermute(block, ("dp", "mem"), route)


def line_sum(part, strides):
    parts = part.reshape(SIDE, -1, part.shape[-1])
    digit = digit_of(strides)
    return parts_sum(
        [lax.dynamic_index_in_dim(parts, (digit + r) % SIDE, 0, False) for r in range(SIDE)],
        strides,
    )


def parts_sum(parts, strides):
    come = [along_lines(parts[r], strides, r) for r in range(1, SIDE)]
    total = parts[0].astype(f32)
    for block in come:
        total += block.astype(f32)
    return total


def scattered_sum(bucket, strides):
    flat = bucket.reshape(-1, bucket.shape[-1])
    groups = lines(strides[0], 0) + lines(strides[1], 1)
    return lax.psum_scatter(
        flat, ("dp", "mem"), axis_index_groups=groups, scatter_dimension=0, tiled=True
    )


def outer_kernel(items, orders, core_ref, *refs):
    inputs, out_ref, turned = refs[: 4 * len(items)], refs[4 * len(items)], refs[-len(items) :]
    step = pl.program_id(0)
    core = core_ref[0]

    def place(chip):
        at = [0, 0]
        for m in range(2):
            for stride in orders[m]:
                at[m] = at[m] * SIDE + chip // stride % SIDE
        return jnp.where(core == 0, at[0], at[1])

    def turn(lefts, to, groups):
        for start in range(0, lefts[0].shape[1], 1024):
            flat = jnp.concatenate([left[:, start : start + 1024] for left in lefts], 0).T
            if groups == 1:
                to[0, start : start + 1024] = flat
                continue
            per = ROWS * groups
            for c in range(1024 // per):
                chip = start // per + c
                for g in range(groups):
                    at = c * per + g * ROWS
                    to[g, chip * ROWS : (chip + 1) * ROWS] = flat[at : at + ROWS]

    def multiply(rights, to, groups, begin):
        at = step - begin
        span = min(TILE, rights[0].shape[1])
        start = at * TILE if groups == 1 else 0
        column = pl.ds(pl.multiple_of(start, span), span)
        both = jnp.concatenate([right[:, column] for right in rights], 0)
        for k in range(TILE // span):
            group = at * (TILE // span) + k if groups > 1 else 0
            result = dot(to[group], both).astype(bf16)
            for chip in range(CHIPS):
                here = result[chip * ROWS : (chip + 1) * ROWS]
                out_ref[place(chip), :, k * span : (k + 1) * span] = here

    for k, (groups, begin, end) in enumerate(items):
        lefts, rights, to = inputs[4 * k : 4 * k + 2], inputs[4 * k + 2 : 4 * k + 4], turned[k]
        pl.when(step == begin)(partial(turn, lefts, to, groups))
        pl.when((step >= begin) & (step < end))(partial(multiply, rights, to, groups, begin))


def outer_products(core, products, axes):
    items, scratch = [], []
    total = flops = 0
    for left, left_come, right, _ in products:
        groups = left.shape[1] // (ROWS * CHIPS)
        depth = left.shape[0] + left_come.shape[0]
        columns = right.shape[1]
        scratch.append(pltpu.VMEM((groups, ROWS * CHIPS, depth), bf16))
        begin = total // TILE
        total += groups * columns
        flops += 2 * groups * ROWS * CHIPS * columns * depth
        items.append((groups, begin, total // TILE))
    operands = [array for product in products for array in product]
    return pl.pallas_call(
        partial(outer_kernel, tuple(items), tuple(zip(*axes))),
        out_shape=jax.ShapeDtypeStruct((CHIPS, ROWS, total), bf16),
        grid_spec=pltpu.PrefetchScalarGridSpec(
            num_scalar_prefetch=1,
            grid=(total // TILE,),
            in_specs=[pl.BlockSpec(memory_space=pltpu.VMEM) for _ in operands],
            out_specs=pl.BlockSpec((CHIPS, ROWS, TILE), lambda i, core: (0, 0, i)),
            scratch_shapes=scratch,
        ),
        compiler_params=pltpu.CompilerParams(vmem_limit_bytes=58 * MIB),
        cost_estimate=pl.CostEstimate(
            flops=flops, bytes_accessed=CHIPS * ROWS * total * 2, transcendentals=0
        ),
    )(core, *operands)


LINE = ROWS * SIDE
DEPTHS = tuple(
    2 * SIDE * (PACK[k + 1] - PACK[k]) // (2 if k == 4 else 1) for k in range(len(PACK) - 1)
)


def turn_kernel(orders, core_ref, packs_ref, out_ref):
    core = core_ref[0]
    start = 0
    for k, depth in enumerate(DEPTHS):
        numbers = range(0, 2 * SIDE, 2 if k == 4 else 1)
        blocks = [packs_ref[number, PACK[k] : PACK[k + 1]] for number in numbers]
        flat = jnp.concatenate(blocks, 0).T
        for line in range(SIDE * SIDE):
            z, y = line // SIDE, line % SIDE
            digit = {4: y, 16: z}
            at = [SIDE * digit[first] + digit[second] for first, second in orders]
            at = pl.multiple_of(jnp.where(core == 0, at[0], at[1]) * LINE, LINE)
            out_ref[pl.ds(at, LINE), start : start + depth] = flat[line * LINE : (line + 1) * LINE]
        start += depth


def turned_packs(core, packs, axes):
    width = packs.shape[2]
    return pl.pallas_call(
        partial(turn_kernel, tuple(zip(*axes))),
        in_specs=scalar_first(1),
        out_shape=jax.ShapeDtypeStruct((width, sum(DEPTHS)), bf16),
        compiler_params=pltpu.CompilerParams(vmem_limit_bytes=58 * MIB),
        cost_estimate=pl.CostEstimate(flops=0, bytes_accessed=20 * MIB, transcendentals=0),
    )(core, packs)


def line_products_kernel(
    digit_ref, turned_ref, come_ref, vectors_ref, *refs
):
    outs, (joint, plain, cross, wide) = refs[:SIDE], refs[SIDE:]
    rows = SENT[1]

    @pl.when(pl.program_id(0) == 0)
    def _():
        def part(number, k):
            return come_ref[number, SENT[k] : SENT[k + 1]]

        def added(first, second):
            return (first.astype(f32) + second.astype(f32)).astype(bf16)

        for number in range(2 * SIDE):
            at = number * rows
            here = slice(at, at + rows)
            joint[here, :PAIR] = part(number, 0)
            for k in (4, 5):
                share = added(part(number, k)[:rows], part(number ^ 1, k)[rows:])
                joint[here, (k - 3) * PAIR : (k - 2) * PAIR] = share
            plain[here, :PAIR] = part(number, 1)
            plain[here, PAIR:] = part(number, 2)
            wide[2 * at : 2 * (at + rows)] = part(number, 3)
        for chip in range(SIDE):
            here = slice(chip * rows, (chip + 1) * rows)
            for k in (6, 7):
                column = slice((k - 6) * PAIR, (k - 5) * PAIR)
                cross[here, column] = added(part(2 * chip, k), part(2 * chip + 1, k))

    ends = [sum(DEPTHS[: k + 1]) for k in range(len(DEPTHS))]
    a1, o, a2, oc, memory = (
        turned_ref[:, end - depth : end] for end, depth in zip(ends, DEPTHS)
    )
    blocks = [
        dot(a1, joint[...]),
        dot(o, plain[:, :PAIR]),
        dot(a2, plain[:, PAIR:]),
        dot(memory, cross[...]),
        dot(oc, wide[...]),
        vectors_ref[...].astype(f32),
    ]
    result = jnp.concatenate(blocks, 1).astype(bf16)
    for r, out in enumerate(outs):

        @pl.when(pl.program_id(0) == r)
        def _(out=out):
            out[...] = result


def line_products(digit, turned, come, vectors):
    width, depth = turned.shape
    block = width // SIDE
    columns = 9 * PAIR

    def part(i, digit):
        return (lax.rem(digit[0] + i, SIDE), 0)

    def fixed(*dims):
        return pl.BlockSpec(dims, lambda i, digit: (0,) * len(dims), pipeline_mode=pl.Buffered(1))

    return pl.pallas_call(
        line_products_kernel,
        grid_spec=pltpu.PrefetchScalarGridSpec(
            num_scalar_prefetch=1,
            grid=(SIDE,),
            in_specs=[
                pl.BlockSpec((block, depth), part),
                fixed(2 * SIDE, SENT[-1], PAIR),
                pl.BlockSpec((block, PAIR), part),
            ],
            out_specs=tuple(fixed(block, columns) for _ in range(SIDE)),
            scratch_shapes=[
                pltpu.VMEM((DEPTHS[0], 3 * PAIR), bf16),
                pltpu.VMEM((DEPTHS[1], 2 * PAIR), bf16),
                pltpu.VMEM((DEPTHS[4], 2 * PAIR), bf16),
                pltpu.VMEM((DEPTHS[3], PAIR), bf16),
            ],
        ),
        out_shape=(jax.ShapeDtypeStruct((block, columns), bf16),) * SIDE,
        compiler_params=pltpu.CompilerParams(vmem_limit_bytes=58 * MIB),
        cost_estimate=pl.CostEstimate(
            flops=2 * 10**9, bytes_accessed=14 * MIB, transcendentals=0
        ),
    )(digit, turned, come, vectors)


def collect_kernel(come_ref, *outs):
    qkv, out, q, kv, cross_out, gains, biases = outs
    targets = [(qkv, 0), (qkv, 1), (qkv, 2), (out, 0), (q, 0), (kv, 0), (kv, 1), (cross_out, 0)]
    for number in range(2 * SIDE):
        for k, (target, block) in enumerate(targets):
            start = (block * 2 * SIDE + number) * PAIR
            target[:, start : start + PAIR] = come_ref[number, :, k * PAIR : (k + 1) * PAIR]
    total = come_ref[0, :, 8 * PAIR :]
    for number in range(1, 2 * SIDE):
        total += come_ref[number, :, 8 * PAIR :]
    total = jnp.concatenate([total, jnp.zeros((PAIR - total.shape[0], PAIR), f32)], 0).T
    gains[...] = total[:4, : ROWS // 2]
    biases[...] = total[4:8, : ROWS // 2]


def collected(come):
    return pl.pallas_call(
        collect_kernel,
        out_shape=tuple(
            jax.ShapeDtypeStruct((ROWS // 2, columns), f32)
            for columns in (24 * PAIR, 8 * PAIR, 8 * PAIR, 16 * PAIR, 8 * PAIR)
        )
        + (jax.ShapeDtypeStruct((4, ROWS // 2), f32),) * 2,
    )(come)


def divide_kernel(grouped, core_ref, sums_ref, keep_ref, give_ref):
    core = core_ref[0]
    half = grouped // 2
    columns = sums_ref.shape[1]
    for ref, side in ((keep_ref, core), (give_ref, 1 - core)):
        if grouped:
            start = pl.ds(pl.multiple_of(side * half, 128), half)
            block = sums_ref[:, start]
            ref[:, :half] = block[: ROWS // 2]
            ref[:, half:grouped] = block[ROWS // 2 :]
        rows = pl.ds(pl.multiple_of(side * (ROWS // 2), 8), ROWS // 2)
        if columns > grouped:
            ref[:, grouped:] = sums_ref[rows, grouped:]


def divided(core, sums, grouped):
    shape = jax.ShapeDtypeStruct((ROWS // 2, sums.shape[1]), f32)
    return pl.pallas_call(
        partial(divide_kernel, grouped),
        in_specs=scalar_first(1),
        out_shape=(shape, shape),
    )(core, sums)


def assemble_kernel(layout, core_ref, keep_ref, come_ref, *outs):
    core = core_ref[0]
    for ref, side in ((keep_ref, core), (come_ref, 1 - core)):
        at = 0
        for out, (grouped, columns, span) in zip(outs, layout):
            part = span // 2
            if grouped:
                for g in range(2):
                    for h in range(2):
                        rows = slice(g * ROWS + h * ROWS // 2, g * ROWS + (h + 1) * ROWS // 2)
                        start = at + h * 2 * part + g * part
                        column = pl.ds(pl.multiple_of(side * part, 128), part)
                        out[rows, column] = ref[:, start : start + part]
                at += 4 * part
                continue
            for k in range(0, columns, span):
                column = pl.ds(pl.multiple_of(k + side * part, 128), part)
                out[:, column] = ref[:, at : at + part]
                at += part


def assembled(core, keep, come, layout):
    return pl.pallas_call(
        partial(assemble_kernel, tuple(layout)),
        in_specs=scalar_first(2),
        out_shape=tuple(
            jax.ShapeDtypeStruct((2 * ROWS if grouped else ROWS // 2, columns), f32)
            for grouped, columns, span in layout
        ),
    )(core, keep, come)


def on_device(
    tokens,
    memory,
    lengths,
    segments,
    key_mask,
    w_self_qkv,
    w_self_out,
    w_cross_q,
    w_cross_kv,
    w_cross_out,
    w_up,
    w_down,
    norm_gains,
    norm_biases,
    readout,
):
    tok_rows = tokens.shape[1]
    width = tokens.shape[2]
    half = lax.axis_index("mem")
    core = half.astype(jnp.int32).reshape(1)
    page_index = lax.axis_index("dp")
    patches = 2 * memory.shape[2]

    vocab_dev = readout.shape[1]
    readout_turned = jnp.pad(readout.T, ((0, ENTRIES - vocab_dev), (0, 0)))
    planes = [[d for d in range(CHIPS) if d % SIDE == x] for x in range(SIDE)]
    readout_part = lax.all_gather(
        readout_turned, "dp", axis=0, tiled=True, axis_index_groups=planes
    )
    is_entry = jnp.arange(readout_part.shape[0]) % ENTRIES < vocab_dev
    entry_bias = jnp.where(is_entry, 0.0, masked_score).astype(f32)[None]

    tokens_own = tokens[0]
    tokens_page = jnp.concatenate([tokens_own, swapped(tokens_own)], 0)
    memory_own = memory[:, 0]
    memory_come = swapped(memory_own)
    memory_rows = jnp.where(
        half == 0,
        jnp.concatenate([memory_own, memory_come], 1),
        jnp.concatenate([memory_come, memory_own], 1),
    ).reshape(2 * patches, width)
    mask_own = key_mask[0].astype(f32)
    mask_come = swapped(mask_own)
    mask_page = jnp.where(
        half == 0,
        jnp.concatenate([mask_own, mask_come]),
        jnp.concatenate([mask_come, mask_own]),
    )
    keep = jnp.tile(jnp.repeat(mask_page, 2), 2)[None]
    own_positions = jnp.arange(tok_rows) + half * tok_rows
    other_positions = jnp.arange(tok_rows) + (1 - half) * tok_rows
    key_positions = jnp.concatenate([own_positions, other_positions])
    cut = segments[0].reshape(2, tok_rows)
    own_segments = lax.dynamic_index_in_dim(cut, half, 0, False)
    other_segments = lax.dynamic_index_in_dim(cut, 1 - half, 0, False)
    key_segments = jnp.concatenate([own_segments, other_segments])
    allowed = (key_positions[None, :] <= own_positions[:, None]) & (
        key_segments[None, :] == own_segments[:, None]
    )
    allowed = allowed.astype(f32)
    count = jnp.sum(lengths).astype(f32)
    line = page_index // SIDE * SIDE + (page_index + jnp.arange(SIDE)) % SIDE
    valid = key_positions[None] < lengths[line][:, None]
    row_weight = (valid.astype(f32) / count)[:, :, None]
    row_weight = jnp.broadcast_to(row_weight, row_weight.shape[:2] + (128,))

    weights = (w_self_qkv, w_self_out, w_cross_q, w_cross_kv, w_cross_out)
    q, kv, h1, qc, kvc, h2, a3, pack, probs, probs_cross = attention(
        tokens_page, allowed, memory_rows, keep, weights, norm_gains, norm_biases
    )
    slope, act, h3, layer_out, final = feed_forward(h2, a3, w_up, w_down, norm_gains, norm_biases)
    final = final.reshape(2, tok_rows, width)
    near = jnp.stack([final] + [along_line(final, r) for r in range(1, SIDE)])
    final_line = jnp.stack([near, swapped(near)], 1).transpose(2, 0, 1, 3, 4)
    final_line = final_line.reshape(2, 2 * SIDE * tok_rows, width)
    a3_other, act_other = swapped(a3), swapped(act)

    final_line, row_weight = lax.optimization_barrier((final_line, row_weight))

    line_groups = [
        [2 * (start + k) + m for k in range(SIDE) for m in range(2)]
        for start in range(0, CHIPS, SIDE)
    ]
    packs = lax.all_gather(pack, ("dp", "mem"), axis_index_groups=line_groups)

    def exchanged(block):
        return lax.all_to_all(
            block, ("dp", "mem"), 0, 0, axis_index_groups=line_groups, tiled=True
        )

    logits, stats = logits_and_stats(final_line, readout_part, entry_bias)
    stats = jnp.stack([stats] + [along_line(stats, r) for r in range(1, SIDE)])
    stats_come = swapped(stats)
    far_stay, give = readout_back(stats, stats_come, row_weight, logits, readout_part, True)
    come = swapped(give)
    far = (far_stay.astype(f32) + come[: SIDE - 1].astype(f32)).astype(bf16)
    logits, far, core_late = lax.optimization_barrier((logits, far, core))
    far = [along_line(far[r - 1], -r) for r in range(1, SIDE)]
    own, terms = readout_back(stats, stats_come, row_weight, logits, readout_part, False)
    terms = terms[:, 0].reshape(2, tok_rows).sum(1)
    loss = (terms[0] + terms[1]).reshape(1)
    turned = turned_packs(core_late, packs, SECOND_AXES)
    own, turned = lax.optimization_barrier((own, turned))
    grad_parts = [part.reshape(2 * tok_rows, width) for part in [own[0], come[SIDE - 1]] + far]

    gh3_keep, gh3_give, gup_keep, gup_give, gh2, vectors_ff = feed_forward_back(
        core, grad_parts, h3, h2, slope, w_up, w_down, norm_gains
    )
    first_bucket = outer_products(
        core,
        [
            (act, act_other, gh3_keep, swapped(gh3_give)),
            (a3, a3_other, gup_keep, swapped(gup_give)),
        ],
        FIRST_AXES,
    )
    gh2, first_bucket = lax.optimization_barrier((gh2, first_bucket))
    first_part = scattered_sum(first_bucket, FIRST_AXES[0])

    gh1, gq, gkv, gkv_give, gkvc, vectors_att, sent = attention_back(
        gh2, probs, probs_cross, kvc, qc, h1, kv, q, w_cross_out, w_cross_q, w_self_out, norm_gains
    )
    sent = exchanged(sent)
    tokens_grad, memory_grad, vectors_in = inputs_back(
        core, tokens_own, gh1, gq, gkv, swapped(gkv_give), gkvc, swapped(gkvc), w_self_qkv,
        w_cross_kv, norm_gains,
    )
    sent, first_part, vectors_in = lax.optimization_barrier((sent, first_part, vectors_in))
    vectors = (vectors_ff + vectors_att + vectors_in).astype(bf16)
    vectors = jnp.pad(vectors.T, ((0, 0), (0, PAIR - 8))).reshape(SIDE, SIDE, LINE, PAIR)
    vectors = jnp.where(half == 0, vectors.transpose(1, 0, 2, 3), vectors).reshape(width, PAIR)
    digit = digit_of(SECOND_AXES[0]).astype(jnp.int32).reshape(1)
    second_parts = line_products(digit, turned, sent, vectors)
    second_sums = parts_sum(second_parts, SECOND_AXES[0]).astype(bf16)
    first_sums = scattered_sum(first_part, FIRST_AXES[1])
    second_sums = line_sum(second_sums, SECOND_AXES[1])
    first_sums = line_sum(first_sums, FIRST_AXES[2])

    first_keep, first_give = divided(core, first_sums, 2 * width)
    weight_down, weight_up = assembled(
        core,
        first_keep,
        swapped(first_give),
        [(True, width, width), (False, 4 * width, 4 * width)],
    )
    line_sums = exchanged(second_sums.reshape(2 * SIDE, ROWS // 2, -1))
    line_sums, weight_down, weight_up = lax.optimization_barrier(
        (line_sums, weight_down, weight_up)
    )
    weight_qkv, weight_out, weight_q, weight_kv, weight_cross_out, grad_gains, grad_biases = (
        collected(line_sums)
    )
    return (
        loss,
        layer_out.reshape(2, 1, tok_rows, width),
        tokens_grad[None],
        memory_grad[:, None],
        weight_qkv,
        weight_out,
        weight_q,
        weight_kv,
        weight_cross_out,
        weight_up,
        weight_down,
        grad_gains,
        grad_biases,
    )


def solution(mesh):
    in_specs = (
        P("dp", "mem", None),
        P(None, "dp", "mem", None),
        P(),
        P("dp", None),
        P("dp", "mem"),
        P(),
        P(),
        P(),
        P(),
        P(),
        P(),
        P(),
        P(),
        P(),
        P(None, ("dp", "mem")),
    )
    out_specs = (
        P("dp"),
        P(None, "dp", "mem", None),
        P("dp", "mem", None),
        P(None, "dp", "mem", None),
        P(("dp", "mem"), None),
        P(("dp", "mem"), None),
        P(("dp", "mem"), None),
        P(("dp", "mem"), None),
        P(("dp", "mem"), None),
        P(("dp", "mem"), None),
        P(("dp", "mem"), None),
        P(None, ("dp", "mem")),
        P(None, ("dp", "mem")),
    )
    return jax.shard_map(
        on_device, mesh=mesh, in_specs=in_specs, out_specs=out_specs, check_vma=False
    )
```

```python
from functools import partial

import jax
import jax.numpy as jnp
from jax import lax
from jax.experimental import pallas as pl
from jax.experimental.pallas import tpu as pltpu
from jax.sharding import PartitionSpec as P

HEAD = 64
PAIR = 2 * HEAD
SIDE = 4
CHIPS = SIDE * SIDE * SIDE
ROWS = 16
TILE = 1024
FF_TILE = 1024
BLOCK = 640
CHUNK = 16
PARTS = ((0, 1024), (1024, 2048), (2048, 3200))
ENTRIES = 200
MIB = 1024 * 1024
epsilon = 1e-05
masked_score = -1e30
bf16 = jnp.bfloat16
f32 = jnp.float32


def dot(left, right):
    return jnp.dot(left, right, preferred_element_type=f32)


def dot_nt(left, right):
    return lax.dot_general(left, right, (((1,), (1,)), ((), ())), preferred_element_type=f32)


def dot_tn(left, right):
    return lax.dot_general(left, right, (((0,), (0,)), ((), ())), preferred_element_type=f32)


def normalized(values):
    centre = values - jnp.mean(values, -1, keepdims=True)
    inverse = lax.rsqrt(jnp.mean(centre * centre, -1, keepdims=True) + epsilon)
    return centre * inverse, inverse


def norm_back(upstream, normed, inverse, gain):
    scaled = upstream * gain
    back = inverse * (
        scaled
        - jnp.mean(scaled, -1, keepdims=True)
        - normed * jnp.mean(scaled * normed, -1, keepdims=True)
    )
    return back, jnp.sum(upstream * normed, 0, keepdims=True), jnp.sum(upstream, 0, keepdims=True)


def lower_lanes(shape):
    return lax.broadcasted_iota(jnp.int32, shape, 1) < HEAD


def parted(block):
    low = lower_lanes(block.shape)
    none = jnp.zeros_like(block)
    return jnp.concatenate([jnp.where(low, block, none), jnp.where(low, none, block)], 0)


def merged(block):
    rows = block.shape[0] // 2
    return jnp.where(lower_lanes((rows, PAIR)), block[:rows], block[rows:])


def self_softmax(queries, keys, allowed):
    scores = dot_nt(queries, keys) * HEAD ** (-0.5)
    scores = jnp.where(allowed, scores, masked_score)
    weights = jnp.exp(scores - jnp.max(scores, -1, keepdims=True))
    return weights * (1.0 / jnp.sum(weights, -1, keepdims=True))


def by_view(values, is_first, combine, neutral):
    first = combine(jnp.where(is_first, values, neutral), -1, keepdims=True)
    second = combine(jnp.where(is_first, neutral, values), -1, keepdims=True)
    return jnp.where(is_first, first, second)


def cross_softmax(queries, keys, kept, is_first):
    scores = dot_nt(queries, keys) * HEAD ** (-0.5)
    scores = jnp.where(kept, scores, masked_score)
    weights = jnp.exp(scores - by_view(scores, is_first, jnp.max, masked_score))
    return weights * (1.0 / by_view(weights, is_first, jnp.sum, 0.0))


def each_view(block, is_first):
    none = jnp.zeros_like(block)
    return jnp.concatenate([jnp.where(is_first, block, none), jnp.where(is_first, none, block)], 0)


def allowed_of(allowed_ref):
    allowed = allowed_ref[...] > 0.5
    return jnp.concatenate([allowed, allowed], 0)


PACK = (0, 96, 192, 288, 480, 576)
SENT = (0, 96, 192, 288, 480, 672, 864, 960, 1056)


def attention_kernel(
    tokens_ref, allowed_ref, memory_ref, keep_ref, w_qkv, w_out, w_q, w_kv, w_cross_out, gains,
    biases, q_ref, kv_ref, h1_ref, qc_ref, kvc_ref, h2_ref, a3_ref, pack_ref, probs_ref,
    probs_cross_ref, a1,
):
    rows = q_ref.shape[0]
    width = tokens_ref.shape[1]
    a1_rows, o_rows, a2_rows, oc_rows, memory_rows = map(slice, PACK[:-1], PACK[1:])
    first_rows, second_rows = slice(PACK[3], PACK[3] + rows), slice(PACK[3] + rows, PACK[4])
    values = tokens_ref[...].astype(f32)
    normed, _ = normalized(values)
    a1[...] = (normed * gains[0:1] + biases[0:1]).astype(bf16)
    pack_ref[a1_rows] = a1[:rows]
    pack_ref[memory_rows] = memory_ref[...]
    q_ref[...] = dot(a1[:rows], w_qkv[:, :width]).astype(bf16)
    kv_ref[...] = dot(a1[...], w_qkv[:, width:]).astype(bf16)
    allowed = allowed_of(allowed_ref)
    for at in range(0, width, PAIR):
        queries = parted(q_ref[:, at : at + PAIR])
        probs = self_softmax(queries, kv_ref[:, at : at + PAIR], allowed)
        probs_ref[at // PAIR] = probs
        mixed = dot(probs.astype(bf16), kv_ref[:, width + at : width + at + PAIR])
        pack_ref[o_rows, at : at + PAIR] = merged(mixed).astype(bf16)
    h1 = values[:rows] + dot(pack_ref[o_rows], w_out[...])
    h1_ref[...] = h1
    normed, _ = normalized(h1)
    pack_ref[a2_rows] = (normed * gains[1:2] + biases[1:2]).astype(bf16)
    qc_ref[...] = dot(pack_ref[a2_rows], w_q[...]).astype(bf16)
    kvc_ref[...] = dot(memory_ref[...], w_kv[...]).astype(bf16)
    shape = (2 * rows, memory_ref.shape[0])
    kept = jnp.broadcast_to(keep_ref[...], shape) > 0.5
    is_first = lax.broadcasted_iota(jnp.int32, shape, 1) < shape[1] // 2
    for at in range(0, width, PAIR):
        queries = parted(qc_ref[:, at : at + PAIR])
        probs = cross_softmax(queries, kvc_ref[:, at : at + PAIR], kept, is_first)
        probs_cross_ref[at // PAIR] = probs
        mixed = dot(
            each_view(probs.astype(bf16), is_first), kvc_ref[:, width + at : width + at + PAIR]
        )
        pack_ref[first_rows, at : at + PAIR] = merged(mixed[: 2 * rows]).astype(bf16)
        pack_ref[second_rows, at : at + PAIR] = merged(mixed[2 * rows :]).astype(bf16)
    h2 = jnp.concatenate([h1, h1], 0) + dot(pack_ref[oc_rows], w_cross_out[...])
    h2_ref[...] = h2
    normed, _ = normalized(h2)
    a3_ref[...] = (normed * gains[2:3] + biases[2:3]).astype(bf16)


def attention(tokens_page, allowed, memory_rows, keep, weights, gains, biases):
    rows, width = allowed.shape[0], tokens_page.shape[1]
    shape = jax.ShapeDtypeStruct
    return pl.pallas_call(
        attention_kernel,
        out_shape=(
            shape((rows, width), bf16),
            shape((2 * rows, 2 * width), bf16),
            shape((rows, width), f32),
            shape((rows, width), bf16),
            shape((memory_rows.shape[0], 2 * width), bf16),
            shape((2 * rows, width), f32),
            shape((2 * rows, width), bf16),
            shape((PACK[-1], width), bf16),
            shape((width // PAIR, 2 * rows, 2 * rows), f32),
            shape((width // PAIR, 2 * rows, memory_rows.shape[0]), f32),
        ),
        scratch_shapes=[pltpu.VMEM((2 * rows, width), bf16)],
        compiler_params=pltpu.CompilerParams(vmem_limit_bytes=58 * MIB),
        cost_estimate=pl.CostEstimate(
            flops=2 * 10**9, bytes_accessed=24 * MIB, transcendentals=10**6
        ),
    )(tokens_page, allowed, memory_rows, keep, *weights, gains, biases)


def erf_parts(values):
    return 0.5 + 0.5 * lax.erf(values * (0.5**0.5))


def feed_forward_kernel(
    h2_ref, a3_ref, w_up, w_down, gains, biases, slope_ref, act_ref, h3_ref, out_ref, fin_ref, total
):
    step = pl.program_id(0)

    @pl.when(step == 0)
    def _():
        total[...] = jnp.zeros_like(total)

    up = dot(a3_ref[...], w_up[...])
    below = erf_parts(up)
    slope = below + up * jnp.exp(-0.5 * up * up) * (0.5 / jnp.pi) ** 0.5
    slope_ref[...] = slope.astype(bf16)
    act = (up * below).astype(bf16)
    act_ref[...] = act
    total[...] += dot(act, w_down[...])

    @pl.when(step == pl.num_programs(0) - 1)
    def _():
        h3 = h2_ref[...] + total[...]
        h3_ref[...] = h3
        out_ref[...] = h3.astype(bf16)
        normed, _ = normalized(h3)
        fin_ref[...] = (normed * gains[3:4] + biases[3:4]).astype(bf16)


def whole(*shape):
    return pl.BlockSpec(shape, lambda i: (0,) * len(shape))


def feed_forward(h2, a3, w_up, w_down, gains, biases):
    rows, width = h2.shape
    hidden = w_up.shape[1]
    shape = jax.ShapeDtypeStruct
    return pl.pallas_call(
        feed_forward_kernel,
        grid=(hidden // FF_TILE,),
        in_specs=[
            whole(rows, width),
            whole(rows, width),
            pl.BlockSpec((width, FF_TILE), lambda i: (0, i)),
            pl.BlockSpec((FF_TILE, width), lambda i: (i, 0)),
            whole(4, width),
            whole(4, width),
        ],
        out_specs=(
            pl.BlockSpec((rows, FF_TILE), lambda i: (0, i)),
            pl.BlockSpec((rows, FF_TILE), lambda i: (0, i)),
            whole(rows, width),
            whole(rows, width),
            whole(rows, width),
        ),
        out_shape=(
            shape((rows, hidden), bf16),
            shape((rows, hidden), bf16),
            shape((rows, width), f32),
            shape((rows, width), bf16),
            shape((rows, width), bf16),
        ),
        scratch_shapes=[pltpu.VMEM((rows, width), f32)],
        compiler_params=pltpu.CompilerParams(vmem_limit_bytes=58 * MIB),
        cost_estimate=pl.CostEstimate(
            flops=4 * rows * width * hidden, bytes_accessed=24 * MIB, transcendentals=rows * hidden
        ),
    )(h2, a3, w_up, w_down, gains, biases)


def halves(block):
    middle = block.shape[1] // 2
    return block[:, :middle], block[:, middle:]


def divide(core, block, keep_ref, give_ref):
    for side in range(2):

        @pl.when(core == side)
        def _(side=side):
            keep_ref[...] = halves(block)[side]
            give_ref[...] = halves(block)[1 - side]


def feed_forward_back_kernel(
    core_ref, own_ref, other_ref, far_a, far_b, far_c, h3_ref, h2_ref, gains, slope_hbm, w_up_hbm,
    w_down_hbm, gh3_keep, gh3_give, gup_keep, gup_give, gh2_ref, vector_ref, gh3_low, slope, w_up,
    w_down, arrived,
):
    core = core_ref[0]
    tiles = w_up.shape[0]
    copies = []
    for t in range(tiles):
        here = slice(t * FF_TILE, (t + 1) * FF_TILE)
        pairs = (
            (w_down_hbm.at[here], w_down.at[t]),
            (slope_hbm.at[:, here], slope.at[t]),
            (w_up_hbm.at[:, here], w_up.at[t]),
        )
        copies.append(
            [pltpu.make_async_copy(*pair, arrived.at[t, k]) for k, pair in enumerate(pairs)]
        )
        for copy in copies[-1]:
            copy.start()
    upstream = own_ref[...]
    for ref in (other_ref, far_a, far_b, far_c):
        upstream += ref[...].astype(f32)
    normed, inverse = normalized(h3_ref[...])
    gh3, gain, bias = norm_back(upstream, normed, inverse, gains[3:4])
    gh3_low[...] = gh3.astype(bf16)
    divide(core, gh3_low[...], gh3_keep, gh3_give)
    vector_ref[...] = jnp.zeros_like(vector_ref)
    vector_ref[3:4] = gain
    vector_ref[7:8] = bias
    total = None
    for t in range(tiles):
        for copy in copies[t]:
            copy.wait()
        gup = (dot_nt(gh3_low[...], w_down[t]) * slope[t].astype(f32)).astype(bf16)
        side, at = t // (tiles // 2), t % (tiles // 2) * FF_TILE

        @pl.when(core == side)
        def _(gup=gup, at=at):
            gup_keep[:, at : at + FF_TILE] = gup

        @pl.when(core != side)
        def _(gup=gup, at=at):
            gup_give[:, at : at + FF_TILE] = gup

        result = dot_nt(gup, w_up[t])
        total = result if total is None else total + result
    normed, inverse = normalized(h2_ref[...])
    back, gain, bias = norm_back(total, normed, inverse, gains[2:3])
    gh2_ref[...] = gh3 + back
    vector_ref[2:3] = gain
    vector_ref[6:7] = bias


def feed_forward_back(core, parts, h3, h2, slope, w_up, w_down, gains):
    rows, width = h2.shape
    hidden = w_up.shape[1]
    tiles = hidden // FF_TILE
    shape = jax.ShapeDtypeStruct
    vmem = pl.BlockSpec(memory_space=pltpu.VMEM)
    return pl.pallas_call(
        feed_forward_back_kernel,
        in_specs=scalar_first(8) + [pl.BlockSpec(memory_space=pl.ANY) for _ in range(3)],
        out_specs=(vmem,) * 6,
        out_shape=(
            shape((rows, width // 2), bf16),
            shape((rows, width // 2), bf16),
            shape((rows, hidden // 2), bf16),
            shape((rows, hidden // 2), bf16),
            shape((rows, width), f32),
            shape((8, width), f32),
        ),
        scratch_shapes=[
            pltpu.VMEM((rows, width), bf16),
            pltpu.VMEM((tiles, rows, FF_TILE), bf16),
            pltpu.VMEM((tiles, width, FF_TILE), bf16),
            pltpu.VMEM((tiles, FF_TILE, width), bf16),
            pltpu.SemaphoreType.DMA((tiles, 3)),
        ],
        compiler_params=pltpu.CompilerParams(vmem_limit_bytes=58 * MIB),
        cost_estimate=pl.CostEstimate(
            flops=4 * rows * width * hidden,
            bytes_accessed=24 * MIB,
            transcendentals=2 * rows * hidden,
        ),
    )(core, *parts, h3, h2, gains, slope, w_up, w_down)


def attention_back_kernel(
    gh2_ref, w_cross_out, probs_cross_ref, kvc_ref, qc_ref, gains, *refs,
):
    later, refs = refs[:6], refs[6:]
    gh1_ref, gq_ref, gkv_ref, give_ref, gkvc_ref, vector_ref, sent_ref = refs[:7]
    goc, go, gqc, gh1_low, *buffers, arrived = refs[7:]
    copies = [
        pltpu.make_async_copy(ref, buffer, arrived.at[k])
        for k, (ref, buffer) in enumerate(zip(later, buffers))
    ]
    for copy in copies:
        copy.start()
    w_q, h1_ref, w_out, probs_ref, kv_ref, q_ref = buffers
    rows, width = gh1_ref.shape
    scale = HEAD ** (-0.5)
    sent_rows = list(map(slice, SENT[:-1], SENT[1:]))

    def pairs_of_heads():
        for number in range(2 * SIDE):
            at = number * PAIR
            yield number, sent_ref.at[number], slice(at, at + PAIR), slice(width + at, width + at + PAIR)

    gh2_low = gh2_ref[...].astype(bf16)
    goc[...] = dot_nt(gh2_low, w_cross_out[...]).astype(bf16)
    shape = (2 * rows, kvc_ref.shape[0])
    is_first = lax.broadcasted_iota(jnp.int32, shape, 1) < shape[1] // 2
    for number, to, here, there in pairs_of_heads():
        queries = parted(qc_ref[:, here])
        probs = probs_cross_ref[number]
        upstream = jnp.concatenate([parted(goc[:rows, here]), parted(goc[rows:, here])], 0)
        grad = dot_nt(upstream, kvc_ref[:, there])
        grad = jnp.where(is_first, grad[: 2 * rows], grad[2 * rows :])
        slope = probs * (grad - by_view(probs * grad, is_first, jnp.sum, 0.0))
        slope = slope.astype(bf16)
        change = (merged(dot(slope, kvc_ref[:, here])) * scale).astype(bf16)
        gqc[:, here] = change
        to[sent_rows[2]] = change
        to[sent_rows[3]] = gh2_ref[:, here].astype(bf16)
        change = (dot_tn(slope, queries) * scale).astype(bf16)
        gkvc_ref[:, here] = change
        to[sent_rows[6]] = change
        change = dot_tn(each_view(probs.astype(bf16), is_first), upstream).astype(bf16)
        gkvc_ref[:, there] = change
        to[sent_rows[7]] = change
    for copy in copies[:2]:
        copy.wait()
    normed, inverse = normalized(h1_ref[...])
    back, gain, bias = norm_back(dot_nt(gqc[...], w_q[...]), normed, inverse, gains[1:2])
    vector_ref[...] = jnp.zeros_like(vector_ref)
    vector_ref[1:2] = gain
    vector_ref[5:6] = bias
    gh1 = gh2_ref[:rows] + gh2_ref[rows:] + back
    gh1_ref[...] = gh1
    gh1_low[...] = gh1.astype(bf16)
    for copy in copies[2:]:
        copy.wait()
    go[...] = dot_nt(gh1_low[...], w_out[...]).astype(bf16)
    for number, to, here, there in pairs_of_heads():
        queries = parted(q_ref[:, here])
        probs = probs_ref[number]
        upstream = parted(go[:, here])
        grad = dot_nt(upstream, kv_ref[:, there])
        slope = probs * (grad - jnp.sum(probs * grad, -1, keepdims=True))
        slope = slope.astype(bf16)
        change = (merged(dot(slope, kv_ref[:, here])) * scale).astype(bf16)
        gq_ref[:, here] = change
        to[sent_rows[0]] = change
        to[sent_rows[1]] = gh1_low[:, here]
        change = (dot_tn(slope, queries) * scale).astype(bf16)
        gkv_ref[:, here] = change[:rows]
        give_ref[:, here] = change[rows:]
        to[sent_rows[4]] = change
        change = dot_tn(probs.astype(bf16), upstream).astype(bf16)
        gkv_ref[:, there] = change[:rows]
        give_ref[:, there] = change[rows:]
        to[sent_rows[5]] = change


def scalar_first(count):
    return [pl.BlockSpec(memory_space=pltpu.SMEM)] + [
        pl.BlockSpec(memory_space=pltpu.VMEM) for _ in range(count)
    ]


def attention_back(gh2, probs, probs_cross, kvc, qc, h1, kv, q, w_cross_out, w_q, w_out, gains):
    rows, width = q.shape
    shape = jax.ShapeDtypeStruct
    vmem = pl.BlockSpec(memory_space=pltpu.VMEM)
    later = (w_q, h1, w_out, probs, kv, q)
    return pl.pallas_call(
        attention_back_kernel,
        in_specs=[vmem] * 6 + [pl.BlockSpec(memory_space=pl.ANY) for _ in later],
        out_specs=(vmem,) * 7,
        out_shape=(
            shape((rows, width), f32),
            shape((rows, width), bf16),
            shape((rows, 2 * width), bf16),
            shape((rows, 2 * width), bf16),
            shape(kvc.shape, bf16),
            shape((8, width), f32),
            shape((2 * SIDE, SENT[-1], PAIR), bf16),
        ),
        scratch_shapes=[
            pltpu.VMEM((2 * rows, width), bf16),
            pltpu.VMEM((rows, width), bf16),
            pltpu.VMEM((rows, width), bf16),
            pltpu.VMEM((rows, width), bf16),
            *(pltpu.VMEM(array.shape, array.dtype) for array in later),
            pltpu.SemaphoreType.DMA((len(later),)),
        ],
        compiler_params=pltpu.CompilerParams(vmem_limit_bytes=58 * MIB),
        cost_estimate=pl.CostEstimate(
            flops=2 * 10**9, bytes_accessed=14 * MIB, transcendentals=10**6
        ),
    )(gh2, w_cross_out, probs_cross, kvc, qc, gains, *later)


def inputs_back_kernel(
    core_ref, tokens_ref, gh1_ref, gq_ref, gkv_ref, come_ref, gkvc_ref, come_cross_ref, w_qkv,
    w_kv, gains, tokens_grad_ref, memory_grad_ref, vector_ref, grads,
):
    core = core_ref[0]
    width = gh1_ref.shape[1]
    pairs = (gkv_ref[...].astype(f32) + come_ref[...].astype(f32)).astype(bf16)
    total = dot_nt(gq_ref[...], w_qkv[:, :width]) + dot_nt(pairs, w_qkv[:, width:])
    normed, inverse = normalized(tokens_ref[...].astype(f32))
    back, gain, bias = norm_back(total, normed, inverse, gains[0:1])
    tokens_grad_ref[...] = gh1_ref[...] + back
    vector_ref[...] = jnp.zeros_like(vector_ref)
    vector_ref[0:1] = gain
    vector_ref[4:5] = bias
    pairs = (gkvc_ref[...].astype(f32) + come_cross_ref[...].astype(f32)).astype(bf16)
    grads[...] = dot_nt(pairs, w_kv[...])
    own = memory_grad_ref.shape[1]
    for view in range(2):
        start = pl.multiple_of(view * 2 * own + core * own, 8)
        memory_grad_ref[view] = grads[pl.ds(start, own)]


def inputs_back(core, *operands):
    rows, width = operands[1].shape
    patches = operands[5].shape[0]
    shape = jax.ShapeDtypeStruct
    return pl.pallas_call(
        inputs_back_kernel,
        in_specs=scalar_first(len(operands)),
        out_shape=(
            shape((rows, width), f32),
            shape((2, patches // 4, width), f32),
            shape((8, width), f32),
        ),
        scratch_shapes=[pltpu.VMEM((patches, width), f32)],
        compiler_params=pltpu.CompilerParams(vmem_limit_bytes=58 * MIB),
        cost_estimate=pl.CostEstimate(flops=10**9, bytes_accessed=14 * MIB, transcendentals=0),
    )(core, *operands)


def logits_kernel(rows_ref, readout_ref, bias_ref, logits_ref, stats_ref, kept):
    tokens = rows_ref.shape[1]
    rows = jnp.concatenate([rows_ref[0], rows_ref[1]], 0)

    def statistics(begin, end):
        spans = range(begin, end, 128)
        for at in range(0, tokens, CHUNK):
            here = slice(at, at + CHUNK)
            first = [logits_ref[0, 0, here, c : c + 128] for c in spans]
            second = [logits_ref[0, 1, here, c : c + 128] for c in spans]
            new_first, new_second = first[0], second[0]
            for a, b in zip(first[1:], second[1:]):
                new_first = jnp.maximum(new_first, a)
                new_second = jnp.maximum(new_second, b)
            total_first = total_apart = total_second = jnp.zeros((CHUNK, 128), f32)
            if begin:
                top_first, top_second = kept[0, here], kept[3, here]
                new_first = jnp.maximum(new_first, top_first)
                new_second = jnp.maximum(new_second, top_second)
                fade_first = jnp.exp(top_first - new_first)
                total_first = kept[1, here] * fade_first
                total_apart = kept[2, here] * fade_first
                total_second = kept[4, here] * jnp.exp(top_second - new_second)
            for a, b in zip(first, second):
                weight = jnp.exp(a - new_first)
                total_first += weight
                total_apart += weight * (a - b)
                total_second += jnp.exp(b - new_second)
            kept[0, here], kept[1, here], kept[2, here] = new_first, total_first, total_apart
            kept[3, here], kept[4, here] = new_second, total_second

    before = None
    for begin, end in PARTS:
        values = dot_nt(rows, readout_ref[begin:end]) + bias_ref[:, begin:end]
        for v in range(2):
            logits_ref[0, v, :, begin:end] = values[v * tokens : (v + 1) * tokens]
        if before:
            statistics(*before)
        before = begin, end
    statistics(*before)

    top_first = jnp.max(kept[0], -1, keepdims=True)
    top_second = jnp.max(kept[3], -1, keepdims=True)
    fade_first = jnp.exp(kept[0] - top_first)
    fade_second = jnp.exp(kept[3] - top_second)
    stats = (
        top_first,
        jnp.sum(kept[1] * fade_first, -1, keepdims=True),
        jnp.sum(kept[2] * fade_first, -1, keepdims=True),
        top_second,
        jnp.sum(kept[4] * fade_second, -1, keepdims=True),
    )
    lane = lax.broadcasted_iota(jnp.int32, kept.shape[1:], 1)
    result = jnp.zeros(kept.shape[1:], f32)
    for k, stat in enumerate(stats):
        result = jnp.where(lane == k, stat, result)
    stats_ref[0] = result.T[:8]


def once(*shape):
    return pl.BlockSpec(shape, lambda i: (0,) * len(shape), pipeline_mode=pl.Buffered(1))


def logits_and_stats(rows, readout_rows, bias):
    views, tokens, width = rows.shape
    entries = readout_rows.shape[0]
    page = tokens // SIDE
    shape = jax.ShapeDtypeStruct
    return pl.pallas_call(
        logits_kernel,
        out_shape=(
            shape((SIDE, 2, page, entries), f32),
            shape((SIDE, 8, page), f32),
        ),
        grid=(SIDE,),
        in_specs=[
            pl.BlockSpec((2, page, width), lambda i: (0, i, 0)),
            once(entries, width),
            once(1, entries),
        ],
        out_specs=(
            pl.BlockSpec((1, 2, page, entries), lambda i: (i, 0, 0, 0)),
            pl.BlockSpec((1, 8, page), lambda i: (i, 0, 0)),
        ),
        scratch_shapes=[pltpu.VMEM((5, page, 128), f32)],
        compiler_params=pltpu.CompilerParams(vmem_limit_bytes=58 * MIB),
        cost_estimate=pl.CostEstimate(
            flops=4 * tokens * entries * width,
            bytes_accessed=2 * entries * width + 8 * tokens * entries,
            transcendentals=2 * tokens * entries,
        ),
    )(rows, readout_rows, bias)


def merged_stats(near_ref, come_ref, slot):
    tokens = near_ref.shape[3]
    middle = tokens // 2
    parts = []
    for ref, flipped in ((near_ref, False), (come_ref, True)):
        for r in range(SIDE):
            part = ref[r, lax.rem(slot + SIDE - r, SIDE)]
            if flipped:
                part = jnp.concatenate([part[:, middle:], part[:, :middle]], 1)
            parts.append(part)
    top_first = parts[0][0:1]
    top_second = parts[0][3:4]
    for part in parts[1:]:
        top_first = jnp.maximum(top_first, part[0:1])
        top_second = jnp.maximum(top_second, part[3:4])
    total_first = total_apart = total_second = jnp.zeros((1, tokens), f32)
    for part in parts:
        fade = jnp.exp(part[0:1] - top_first)
        total_first += part[1:2] * fade
        total_apart += part[2:3] * fade
        total_second += part[4:5] * jnp.exp(part[3:4] - top_second)
    first_lse = top_first + jnp.log(total_first)
    second_lse = top_second + jnp.log(total_second)
    return first_lse, second_lse, total_apart / total_first


def readout_back_kernel(
    far, near_ref, come_ref, weight_ref, logits_ref, readout_ref, stay_ref, other_ref, kept, slopes
):
    step = pl.program_id(0)
    tokens = weight_ref.shape[1]
    rows = tokens // 2
    slot = lax.rem(step + 1, SIDE) if far else 0
    for k, row in enumerate(merged_stats(near_ref, come_ref, slot)):
        kept[k] = jnp.broadcast_to(row, (128, row.shape[1])).T
    kept[3] = weight_ref[0]

    def gradient(start, count):
        def derivatives(begin, end):
            for at in range(start, start + count, CHUNK):
                here = slice(at, at + CHUNK)
                first_lse, second_lse, apart, weight = (kept[k, here] for k in range(4))
                for c in range(begin, end, 128):
                    first = logits_ref[0, 0, here, c : c + 128]
                    second = logits_ref[0, 1, here, c : c + 128]
                    first_prob = jnp.exp(first - first_lse) * weight
                    second_prob = jnp.exp(second - second_lse) * weight
                    change = first_prob * (first - second - apart)
                    slopes[0, here, c : c + 128] = change.astype(bf16)
                    slopes[1, here, c : c + 128] = (second_prob - first_prob).astype(bf16)

        derivatives(*PARTS[0])
        total = None
        for i, (begin, end) in enumerate(PARTS):
            block = [slopes[v, start : start + count, begin:end] for v in range(2)]
            result = dot(jnp.concatenate(block, 0), readout_ref[begin:end])
            if i + 1 < len(PARTS):
                derivatives(*PARTS[i + 1])
            total = result if total is None else total + result
        return total

    if not far:
        total = gradient(0, rows)
        for v in range(2):
            stay_ref[0, v] = total[v * rows : (v + 1) * rows]
        other_ref[...] = kept[3] * (kept[2] - kept[0] + kept[1])
        return

    @pl.when(step < SIDE - 1)
    def _():
        total = gradient(0, tokens)
        for v in range(2):
            stay_ref[0, v] = total[v * tokens : v * tokens + rows].astype(bf16)
            other_ref[0, v] = total[v * tokens + rows : (v + 1) * tokens].astype(bf16)

    @pl.when(step == SIDE - 1)
    def _():
        total = gradient(rows, rows)
        for v in range(2):
            other_ref[0, v] = total[v * rows : (v + 1) * rows].astype(bf16)


def readout_back(stats_near, stats_come, weight, logits, readout_rows, far):
    tokens, entries = logits.shape[2:]
    width = readout_rows.shape[1]
    rows = tokens // 2
    pages = SIDE if far else 1
    shape = jax.ShapeDtypeStruct
    block = (1, 2, rows, width)
    if far:
        out_shape = (
            shape((SIDE - 1, 2, rows, width), bf16),
            shape((SIDE, 2, rows, width), bf16),
        )
        out_specs = (
            pl.BlockSpec(block, lambda i: (jnp.minimum(i, SIDE - 2), 0, 0, 0)),
            pl.BlockSpec(block, lambda i: (i, 0, 0, 0)),
        )
    else:
        out_shape = (shape(block, f32), shape((tokens, 128), f32))
        out_specs = (whole(*block), whole(tokens, 128))

    def page(i):
        return lax.rem(i + 1, SIDE) if far else i

    here = tokens if far else rows
    return pl.pallas_call(
        partial(readout_back_kernel, far),
        out_shape=out_shape,
        grid=(pages,),
        in_specs=[
            once(SIDE, SIDE, 8, tokens),
            once(SIDE, SIDE, 8, tokens),
            pl.BlockSpec((1, tokens, 128), lambda i: (page(i), 0, 0)),
            pl.BlockSpec((1, 2, here, entries), lambda i: (page(i), 0, 0, 0)),
            once(entries, width),
        ],
        out_specs=out_specs,
        scratch_shapes=[
            pltpu.VMEM((4, tokens, 128), f32),
            pltpu.VMEM((2, here, entries), bf16),
        ],
        compiler_params=pltpu.CompilerParams(vmem_limit_bytes=58 * MIB),
        cost_estimate=pl.CostEstimate(
            flops=4 * pages * here * entries * width,
            bytes_accessed=2 * entries * width + 8 * pages * here * entries,
            transcendentals=2 * pages * here * entries,
        ),
    )(stats_near, stats_come, weight, logits, readout_rows)


FIRST_AXES = ((4, 16), (16, 1), (1, 4))
SECOND_AXES = ((4, 16), (16, 4))


def swapped(block):
    return lax.ppermute(block, "mem", [(0, 1), (1, 0)])


def along_line(block, distance):
    route = [(d, d // SIDE * SIDE + (d - distance) % SIDE) for d in range(CHIPS)]
    return lax.ppermute(block, "dp", route)


def lines(stride, core):
    starts = [d for d in range(CHIPS) if (d // stride) % SIDE == 0]
    return [[2 * (start + stride * k) + core for k in range(SIDE)] for start in starts]


def digit_of(strides):
    chip, core = lax.axis_index("dp"), lax.axis_index("mem")
    return jnp.where(core == 0, chip // strides[0], chip // strides[1]) % SIDE


def along_lines(block, strides, r):
    route = []
    for d in range(CHIPS):
        for m, stride in enumerate(strides):
            own = d // stride % SIDE
            to = d + ((own + r) % SIDE - own) * stride
            route.append((2 * d + m, 2 * to + m))
    return lax.ppermute(block, ("dp", "mem"), route)


def line_sum(part, strides):
    return parts_sum(parts_of(part, strides), strides)


def parts_of(part, strides):
    parts = part.reshape(SIDE, -1, part.shape[-1])
    digit = digit_of(strides)
    return [lax.dynamic_index_in_dim(parts, (digit + r) % SIDE, 0, False) for r in range(SIDE)]


def parts_sum(parts, strides):
    parts = parts_come(parts, strides)
    total = parts[0].astype(f32)
    for block in parts[1:]:
        total += block.astype(f32)
    return total


def parts_come(parts, strides):
    return [parts[0]] + [along_lines(parts[r], strides, r) for r in range(1, SIDE)]


def scattered_sum(bucket, strides):
    flat = bucket.reshape(-1, bucket.shape[-1])
    groups = lines(strides[0], 0) + lines(strides[1], 1)
    return lax.psum_scatter(
        flat, ("dp", "mem"), axis_index_groups=groups, scatter_dimension=0, tiled=True
    )


def outer_kernel(items, orders, core_ref, *refs):
    inputs, out_ref, turned = refs[: 4 * len(items)], refs[4 * len(items)], refs[-len(items) :]
    step = pl.program_id(0)
    core = core_ref[0]

    def place(chip):
        at = [0, 0]
        for m in range(2):
            for stride in orders[m]:
                at[m] = at[m] * SIDE + chip // stride % SIDE
        return jnp.where(core == 0, at[0], at[1])

    def turn(lefts, to, groups):
        for start in range(0, lefts[0].shape[1], 1024):
            flat = jnp.concatenate([left[:, start : start + 1024] for left in lefts], 0).T
            if groups == 1:
                to[0, start : start + 1024] = flat
                continue
            per = ROWS * groups
            for c in range(1024 // per):
                chip = start // per + c
                for g in range(groups):
                    at = c * per + g * ROWS
                    to[g, chip * ROWS : (chip + 1) * ROWS] = flat[at : at + ROWS]

    def multiply(rights, to, groups, begin):
        at = step - begin
        span = min(TILE, rights[0].shape[1])
        start = at * TILE if groups == 1 else 0
        column = pl.ds(pl.multiple_of(start, span), span)
        both = jnp.concatenate([right[:, column] for right in rights], 0)
        for k in range(TILE // span):
            group = at * (TILE // span) + k if groups > 1 else 0
            result = dot(to[group], both).astype(bf16)
            for chip in range(CHIPS):
                here = result[chip * ROWS : (chip + 1) * ROWS]
                out_ref[place(chip), :, k * span : (k + 1) * span] = here

    for k, (groups, begin, end) in enumerate(items):
        lefts, rights, to = inputs[4 * k : 4 * k + 2], inputs[4 * k + 2 : 4 * k + 4], turned[k]
        pl.when(step == begin)(partial(turn, lefts, to, groups))
        pl.when((step >= begin) & (step < end))(partial(multiply, rights, to, groups, begin))


def outer_products(core, products, axes):
    items, scratch = [], []
    total = flops = 0
    for left, left_come, right, _ in products:
        groups = left.shape[1] // (ROWS * CHIPS)
        depth = left.shape[0] + left_come.shape[0]
        columns = right.shape[1]
        scratch.append(pltpu.VMEM((groups, ROWS * CHIPS, depth), bf16))
        begin = total // TILE
        total += groups * columns
        flops += 2 * groups * ROWS * CHIPS * columns * depth
        items.append((groups, begin, total // TILE))
    operands = [array for product in products for array in product]
    return pl.pallas_call(
        partial(outer_kernel, tuple(items), tuple(zip(*axes))),
        out_shape=jax.ShapeDtypeStruct((CHIPS, ROWS, total), bf16),
        grid_spec=pltpu.PrefetchScalarGridSpec(
            num_scalar_prefetch=1,
            grid=(total // TILE,),
            in_specs=[pl.BlockSpec(memory_space=pltpu.VMEM) for _ in operands],
            out_specs=pl.BlockSpec((CHIPS, ROWS, TILE), lambda i, core: (0, 0, i)),
            scratch_shapes=scratch,
        ),
        compiler_params=pltpu.CompilerParams(vmem_limit_bytes=58 * MIB),
        cost_estimate=pl.CostEstimate(
            flops=flops, bytes_accessed=CHIPS * ROWS * total * 2, transcendentals=0
        ),
    )(core, *operands)


LINE = ROWS * SIDE
DEPTHS = tuple(
    2 * SIDE * (PACK[k + 1] - PACK[k]) // (2 if k == 4 else 1) for k in range(len(PACK) - 1)
)


def turn_kernel(orders, core_ref, packs_ref, out_ref):
    core = core_ref[0]
    start = 0
    for k, depth in enumerate(DEPTHS):
        numbers = range(0, 2 * SIDE, 2 if k == 4 else 1)
        blocks = [packs_ref[number, PACK[k] : PACK[k + 1]] for number in numbers]
        flat = jnp.concatenate(blocks, 0).T
        for line in range(SIDE * SIDE):
            z, y = line // SIDE, line % SIDE
            digit = {4: y, 16: z}
            at = [SIDE * digit[first] + digit[second] for first, second in orders]
            at = pl.multiple_of(jnp.where(core == 0, at[0], at[1]) * LINE, LINE)
            out_ref[pl.ds(at, LINE), start : start + depth] = flat[line * LINE : (line + 1) * LINE]
        start += depth


def turned_packs(core, packs, axes):
    width = packs.shape[2]
    return pl.pallas_call(
        partial(turn_kernel, tuple(zip(*axes))),
        in_specs=scalar_first(1),
        out_shape=jax.ShapeDtypeStruct((width, sum(DEPTHS)), bf16),
        compiler_params=pltpu.CompilerParams(vmem_limit_bytes=58 * MIB),
        cost_estimate=pl.CostEstimate(flops=0, bytes_accessed=20 * MIB, transcendentals=0),
    )(core, packs)


def line_products_kernel(
    digit_ref, vectors_ref, turned_hbm, come_hbm, *refs
):
    outs, (joint, plain, cross, wide, come_ref, turned_ref, results, arrived, left) = (
        refs[:SIDE],
        refs[SIDE:],
    )
    block = turned_ref.shape[1]
    fetch_come = pltpu.make_async_copy(come_hbm, come_ref, arrived.at[SIDE])
    fetch_come.start()
    starts = [
        pl.multiple_of(lax.rem(digit_ref[0] + r, SIDE) * block, block) for r in range(SIDE)
    ]
    fetches = [
        pltpu.make_async_copy(turned_hbm.at[pl.ds(start, block)], turned_ref.at[r], arrived.at[r])
        for r, start in enumerate(starts)
    ]
    for fetch in fetches:
        fetch.start()
    fetch_come.wait()
    rows = SENT[1]

    def part(number, k):
        return come_ref[number, SENT[k] : SENT[k + 1]]

    def added(first, second):
        return (first.astype(f32) + second.astype(f32)).astype(bf16)

    for number in range(2 * SIDE):
        at = number * rows
        here = slice(at, at + rows)
        joint[here, :PAIR] = part(number, 0)
        for k in (4, 5):
            share = added(part(number, k)[:rows], part(number ^ 1, k)[rows:])
            joint[here, (k - 3) * PAIR : (k - 2) * PAIR] = share
        plain[here, :PAIR] = part(number, 1)
        plain[here, PAIR:] = part(number, 2)
        wide[2 * at : 2 * (at + rows)] = part(number, 3)
    for chip in range(SIDE):
        here = slice(chip * rows, (chip + 1) * rows)
        for k in (6, 7):
            column = slice((k - 6) * PAIR, (k - 5) * PAIR)
            cross[here, column] = added(part(2 * chip, k), part(2 * chip + 1, k))

    ends = [sum(DEPTHS[: k + 1]) for k in range(len(DEPTHS))]
    stores = []
    for r in range(SIDE):
        fetches[r].wait()
        a1, o, a2, oc, memory = (
            turned_ref[r, :, end - depth : end] for end, depth in zip(ends, DEPTHS)
        )
        blocks = [
            dot(a1, joint[...]),
            dot(o, plain[:, :PAIR]),
            dot(a2, plain[:, PAIR:]),
            dot(memory, cross[...]),
            dot(oc, wide[...]),
            vectors_ref[pl.ds(starts[r], block)].astype(f32),
        ]
        results[r] = jnp.concatenate(blocks, 1).astype(bf16)
        stores.append(pltpu.make_async_copy(results.at[r], outs[r], left.at[r]))
        stores[-1].start()
    for store in stores:
        store.wait()


def line_products(digit, turned, come, vectors):
    width, depth = turned.shape
    block = width // SIDE
    columns = 9 * PAIR
    anywhere = pl.BlockSpec(memory_space=pl.ANY)
    return pl.pallas_call(
        line_products_kernel,
        in_specs=scalar_first(1) + [anywhere, anywhere],
        out_specs=(anywhere,) * SIDE,
        out_shape=(jax.ShapeDtypeStruct((block, columns), bf16),) * SIDE,
        scratch_shapes=[
            pltpu.VMEM((DEPTHS[0], 3 * PAIR), bf16),
            pltpu.VMEM((DEPTHS[1], 2 * PAIR), bf16),
            pltpu.VMEM((DEPTHS[4], 2 * PAIR), bf16),
            pltpu.VMEM((DEPTHS[3], PAIR), bf16),
            pltpu.VMEM(come.shape, bf16),
            pltpu.VMEM((SIDE, block, depth), bf16),
            pltpu.VMEM((SIDE, block, columns), bf16),
            pltpu.SemaphoreType.DMA((SIDE + 1,)),
            pltpu.SemaphoreType.DMA((SIDE,)),
        ],
        compiler_params=pltpu.CompilerParams(vmem_limit_bytes=58 * MIB),
        cost_estimate=pl.CostEstimate(
            flops=2 * 10**9, bytes_accessed=14 * MIB, transcendentals=0
        ),
    )(digit, vectors, turned, come)


def collect_kernel(come_ref, *outs):
    qkv, out, q, kv, cross_out, gains, biases = outs
    targets = [(qkv, 0), (qkv, 1), (qkv, 2), (out, 0), (q, 0), (kv, 0), (kv, 1), (cross_out, 0)]
    for number in range(2 * SIDE):
        for k, (target, block) in enumerate(targets):
            start = (block * 2 * SIDE + number) * PAIR
            target[:, start : start + PAIR] = come_ref[number, :, k * PAIR : (k + 1) * PAIR]
    total = come_ref[0, :, 8 * PAIR :]
    for number in range(1, 2 * SIDE):
        total += come_ref[number, :, 8 * PAIR :]
    total = jnp.concatenate([total, jnp.zeros((PAIR - total.shape[0], PAIR), f32)], 0).T
    gains[...] = total[:4, : ROWS // 2]
    biases[...] = total[4:8, : ROWS // 2]


def collected(come):
    return pl.pallas_call(
        collect_kernel,
        out_shape=tuple(
            jax.ShapeDtypeStruct((ROWS // 2, columns), f32)
            for columns in (24 * PAIR, 8 * PAIR, 8 * PAIR, 16 * PAIR, 8 * PAIR)
        )
        + (jax.ShapeDtypeStruct((4, ROWS // 2), f32),) * 2,
    )(come)


def divide_kernel(grouped, core_ref, *refs):
    parts, (keep_ref, give_ref, sums_ref) = refs[:SIDE], refs[SIDE:]
    sums_ref[...] = parts[0][...].astype(f32)
    for part in parts[1:]:
        sums_ref[...] += part[...].astype(f32)
    core = core_ref[0]
    half = grouped // 2
    columns = sums_ref.shape[1]
    for ref, side in ((keep_ref, core), (give_ref, 1 - core)):
        if grouped:
            start = pl.ds(pl.multiple_of(side * half, 128), half)
            block = sums_ref[:, start]
            ref[:, :half] = block[: ROWS // 2]
            ref[:, half:grouped] = block[ROWS // 2 :]
        rows = pl.ds(pl.multiple_of(side * (ROWS // 2), 8), ROWS // 2)
        if columns > grouped:
            ref[:, grouped:] = sums_ref[rows, grouped:]


def divided(core, parts, grouped):
    columns = parts[0].shape[1]
    shape = jax.ShapeDtypeStruct((ROWS // 2, columns), f32)
    return pl.pallas_call(
        partial(divide_kernel, grouped),
        in_specs=scalar_first(SIDE),
        out_shape=(shape, shape),
        scratch_shapes=[pltpu.VMEM((ROWS, columns), f32)],
    )(core, *parts)


def assemble_kernel(layout, core_ref, keep_ref, come_ref, *outs):
    core = core_ref[0]
    for ref, side in ((keep_ref, core), (come_ref, 1 - core)):
        at = 0
        for out, (grouped, columns, span) in zip(outs, layout):
            part = span // 2
            if grouped:
                for g in range(2):
                    for h in range(2):
                        rows = slice(g * ROWS + h * ROWS // 2, g * ROWS + (h + 1) * ROWS // 2)
                        start = at + h * 2 * part + g * part
                        column = pl.ds(pl.multiple_of(side * part, 128), part)
                        out[rows, column] = ref[:, start : start + part]
                at += 4 * part
                continue
            for k in range(0, columns, span):
                column = pl.ds(pl.multiple_of(k + side * part, 128), part)
                out[:, column] = ref[:, at : at + part]
                at += part


def assembled(core, keep, come, layout):
    return pl.pallas_call(
        partial(assemble_kernel, tuple(layout)),
        in_specs=scalar_first(2),
        out_shape=tuple(
            jax.ShapeDtypeStruct((2 * ROWS if grouped else ROWS // 2, columns), f32)
            for grouped, columns, span in layout
        ),
    )(core, keep, come)


def on_device(
    tokens,
    memory,
    lengths,
    segments,
    key_mask,
    w_self_qkv,
    w_self_out,
    w_cross_q,
    w_cross_kv,
    w_cross_out,
    w_up,
    w_down,
    norm_gains,
    norm_biases,
    readout,
):
    tok_rows = tokens.shape[1]
    width = tokens.shape[2]
    half = lax.axis_index("mem")
    core = half.astype(jnp.int32).reshape(1)
    page_index = lax.axis_index("dp")
    patches = 2 * memory.shape[2]

    vocab_dev = readout.shape[1]
    readout_turned = jnp.pad(readout.T, ((0, ENTRIES - vocab_dev), (0, 0)))
    planes = [[d for d in range(CHIPS) if d % SIDE == x] for x in range(SIDE)]
    readout_part = lax.all_gather(
        readout_turned, "dp", axis=0, tiled=True, axis_index_groups=planes
    )
    is_entry = jnp.arange(readout_part.shape[0]) % ENTRIES < vocab_dev
    entry_bias = jnp.where(is_entry, 0.0, masked_score).astype(f32)[None]

    tokens_own = tokens[0]
    tokens_page = jnp.concatenate([tokens_own, swapped(tokens_own)], 0)
    memory_own = memory[:, 0]
    memory_come = swapped(memory_own)
    memory_rows = jnp.where(
        half == 0,
        jnp.concatenate([memory_own, memory_come], 1),
        jnp.concatenate([memory_come, memory_own], 1),
    ).reshape(2 * patches, width)
    mask_own = key_mask[0].astype(f32)
    mask_come = swapped(mask_own)
    mask_page = jnp.where(
        half == 0,
        jnp.concatenate([mask_own, mask_come]),
        jnp.concatenate([mask_come, mask_own]),
    )
    keep = jnp.tile(jnp.repeat(mask_page, 2), 2)[None]
    own_positions = jnp.arange(tok_rows) + half * tok_rows
    other_positions = jnp.arange(tok_rows) + (1 - half) * tok_rows
    key_positions = jnp.concatenate([own_positions, other_positions])
    cut = segments[0].reshape(2, tok_rows)
    own_segments = lax.dynamic_index_in_dim(cut, half, 0, False)
    other_segments = lax.dynamic_index_in_dim(cut, 1 - half, 0, False)
    key_segments = jnp.concatenate([own_segments, other_segments])
    allowed = (key_positions[None, :] <= own_positions[:, None]) & (
        key_segments[None, :] == own_segments[:, None]
    )
    allowed = allowed.astype(f32)
    count = jnp.sum(lengths).astype(f32)
    line = page_index // SIDE * SIDE + (page_index + jnp.arange(SIDE)) % SIDE
    valid = key_positions[None] < lengths[line][:, None]
    row_weight = (valid.astype(f32) / count)[:, :, None]
    row_weight = jnp.broadcast_to(row_weight, row_weight.shape[:2] + (128,))

    weights = (w_self_qkv, w_self_out, w_cross_q, w_cross_kv, w_cross_out)
    q, kv, h1, qc, kvc, h2, a3, pack, probs, probs_cross = attention(
        tokens_page, allowed, memory_rows, keep, weights, norm_gains, norm_biases
    )
    slope, act, h3, layer_out, final = feed_forward(h2, a3, w_up, w_down, norm_gains, norm_biases)
    final = final.reshape(2, tok_rows, width)
    near = jnp.stack([final] + [along_line(final, r) for r in range(1, SIDE)])
    final_line = jnp.stack([near, swapped(near)], 1).transpose(2, 0, 1, 3, 4)
    final_line = final_line.reshape(2, 2 * SIDE * tok_rows, width)
    a3_other, act_other = swapped(a3), swapped(act)

    final_line, row_weight = lax.optimization_barrier((final_line, row_weight))

    line_groups = [
        [2 * (start + k) + m for k in range(SIDE) for m in range(2)]
        for start in range(0, CHIPS, SIDE)
    ]
    packs = lax.all_gather(pack, ("dp", "mem"), axis_index_groups=line_groups)

    def exchanged(block):
        return lax.all_to_all(
            block, ("dp", "mem"), 0, 0, axis_index_groups=line_groups, tiled=True
        )

    logits, stats = logits_and_stats(final_line, readout_part, entry_bias)
    stats = jnp.stack([stats] + [along_line(stats, r) for r in range(1, SIDE)])
    stats_come = swapped(stats)
    far_stay, give = readout_back(stats, stats_come, row_weight, logits, readout_part, True)
    come = swapped(give)
    far = (far_stay.astype(f32) + come[: SIDE - 1].astype(f32)).astype(bf16)
    logits, far, core_late = lax.optimization_barrier((logits, far, core))
    far = [along_line(far[r - 1], -r) for r in range(1, SIDE)]
    own, terms = readout_back(stats, stats_come, row_weight, logits, readout_part, False)
    terms = terms[:, 0].reshape(2, tok_rows).sum(1)
    loss = (terms[0] + terms[1]).reshape(1)
    turned = turned_packs(core_late, packs, SECOND_AXES)
    own, turned = lax.optimization_barrier((own, turned))
    grad_parts = [part.reshape(2 * tok_rows, width) for part in [own[0], come[SIDE - 1]] + far]

    gh3_keep, gh3_give, gup_keep, gup_give, gh2, vectors_ff = feed_forward_back(
        core, grad_parts, h3, h2, slope, w_up, w_down, norm_gains
    )
    first_bucket = outer_products(
        core,
        [
            (act, act_other, gh3_keep, swapped(gh3_give)),
            (a3, a3_other, gup_keep, swapped(gup_give)),
        ],
        FIRST_AXES,
    )
    gh2, first_bucket = lax.optimization_barrier((gh2, first_bucket))
    first_part = scattered_sum(first_bucket, FIRST_AXES[0])

    gh1, gq, gkv, gkv_give, gkvc, vectors_att, sent = attention_back(
        gh2, probs, probs_cross, kvc, qc, h1, kv, q, w_cross_out, w_cross_q, w_self_out, norm_gains
    )
    sent = exchanged(sent)
    tokens_grad, memory_grad, vectors_in = inputs_back(
        core, tokens_own, gh1, gq, gkv, swapped(gkv_give), gkvc, swapped(gkvc), w_self_qkv,
        w_cross_kv, norm_gains,
    )
    sent, first_part, vectors_in = lax.optimization_barrier((sent, first_part, vectors_in))
    vectors = (vectors_ff + vectors_att + vectors_in).astype(bf16)
    vectors = jnp.pad(vectors.T, ((0, 0), (0, PAIR - 8))).reshape(SIDE, SIDE, LINE, PAIR)
    vectors = jnp.where(half == 0, vectors.transpose(1, 0, 2, 3), vectors).reshape(width, PAIR)
    digit = digit_of(SECOND_AXES[0]).astype(jnp.int32).reshape(1)
    second_parts = line_products(digit, turned, sent, vectors)
    second_sums = parts_sum(second_parts, SECOND_AXES[0]).astype(bf16)
    first_sums = scattered_sum(first_part, FIRST_AXES[1])
    second_sums = line_sum(second_sums, SECOND_AXES[1])
    first_parts = parts_come(parts_of(first_sums, FIRST_AXES[2]), FIRST_AXES[2])

    first_keep, first_give = divided(core, first_parts, 2 * width)
    weight_down, weight_up = assembled(
        core,
        first_keep,
        swapped(first_give),
        [(True, width, width), (False, 4 * width, 4 * width)],
    )
    line_sums = exchanged(second_sums.reshape(2 * SIDE, ROWS // 2, -1))
    line_sums, weight_down, weight_up = lax.optimization_barrier(
        (line_sums, weight_down, weight_up)
    )
    weight_qkv, weight_out, weight_q, weight_kv, weight_cross_out, grad_gains, grad_biases = (
        collected(line_sums)
    )
    return (
        loss,
        layer_out.reshape(2, 1, tok_rows, width),
        tokens_grad[None],
        memory_grad[:, None],
        weight_qkv,
        weight_out,
        weight_q,
        weight_kv,
        weight_cross_out,
        weight_up,
        weight_down,
        grad_gains,
        grad_biases,
    )


def solution(mesh):
    in_specs = (
        P("dp", "mem", None),
        P(None, "dp", "mem", None),
        P(),
        P("dp", None),
        P("dp", "mem"),
        P(),
        P(),
        P(),
        P(),
        P(),
        P(),
        P(),
        P(),
        P(),
        P(None, ("dp", "mem")),
    )
    out_specs = (
        P("dp"),
        P(None, "dp", "mem", None),
        P("dp", "mem", None),
        P(None, "dp", "mem", None),
        P(("dp", "mem"), None),
        P(("dp", "mem"), None),
        P(("dp", "mem"), None),
        P(("dp", "mem"), None),
        P(("dp", "mem"), None),
        P(("dp", "mem"), None),
        P(("dp", "mem"), None),
        P(None, ("dp", "mem")),
        P(None, ("dp", "mem")),
    )
    return jax.shard_map(
        on_device, mesh=mesh, in_specs=in_specs, out_specs=out_specs, check_vma=False
    )
```

```python
from functools import partial

import jax
import jax.numpy as jnp
from jax import lax
from jax.experimental import pallas as pl
from jax.experimental.pallas import tpu as pltpu
from jax.sharding import PartitionSpec as P

HEAD = 64
PAIR = 2 * HEAD
SIDE = 4
CHIPS = SIDE * SIDE * SIDE
ROWS = 16
TILE = 1024
FF_TILE = 1024
BLOCK = 640
CHUNK = 16
PARTS = ((0, 1024), (1024, 2048), (2048, 3200))
ENTRIES = 200
MIB = 1024 * 1024
epsilon = 1e-05
masked_score = -1e30
bf16 = jnp.bfloat16
f32 = jnp.float32


def dot(left, right):
    return jnp.dot(left, right, preferred_element_type=f32)


def dot_nt(left, right):
    return lax.dot_general(left, right, (((1,), (1,)), ((), ())), preferred_element_type=f32)


def dot_tn(left, right):
    return lax.dot_general(left, right, (((0,), (0,)), ((), ())), preferred_element_type=f32)


def normalized(values):
    centre = values - jnp.mean(values, -1, keepdims=True)
    inverse = lax.rsqrt(jnp.mean(centre * centre, -1, keepdims=True) + epsilon)
    return centre * inverse, inverse


def norm_back(upstream, normed, inverse, gain):
    scaled = upstream * gain
    back = inverse * (
        scaled
        - jnp.mean(scaled, -1, keepdims=True)
        - normed * jnp.mean(scaled * normed, -1, keepdims=True)
    )
    return back, jnp.sum(upstream * normed, 0, keepdims=True), jnp.sum(upstream, 0, keepdims=True)


def lower_lanes(shape):
    return lax.broadcasted_iota(jnp.int32, shape, 1) < HEAD


def parted(block):
    low = lower_lanes(block.shape)
    none = jnp.zeros_like(block)
    return jnp.concatenate([jnp.where(low, block, none), jnp.where(low, none, block)], 0)


def merged(block):
    rows = block.shape[0] // 2
    return jnp.where(lower_lanes((rows, PAIR)), block[:rows], block[rows:])


def self_softmax(queries, keys, allowed):
    scores = dot_nt(queries, keys) * HEAD ** (-0.5)
    scores = jnp.where(allowed, scores, masked_score)
    weights = jnp.exp(scores - jnp.max(scores, -1, keepdims=True))
    return weights * (1.0 / jnp.sum(weights, -1, keepdims=True))


def by_view(values, is_first, combine, neutral):
    first = combine(jnp.where(is_first, values, neutral), -1, keepdims=True)
    second = combine(jnp.where(is_first, neutral, values), -1, keepdims=True)
    return jnp.where(is_first, first, second)


def cross_softmax(queries, keys, kept, is_first):
    scores = dot_nt(queries, keys) * HEAD ** (-0.5)
    scores = jnp.where(kept, scores, masked_score)
    weights = jnp.exp(scores - by_view(scores, is_first, jnp.max, masked_score))
    return weights * (1.0 / by_view(weights, is_first, jnp.sum, 0.0))


def each_view(block, is_first):
    none = jnp.zeros_like(block)
    return jnp.concatenate([jnp.where(is_first, block, none), jnp.where(is_first, none, block)], 0)


def allowed_of(allowed_ref):
    allowed = allowed_ref[...] > 0.5
    return jnp.concatenate([allowed, allowed], 0)


PACK = (0, 96, 192, 288, 480, 576)
SENT = (0, 96, 192, 288, 480, 672, 864, 960, 1056)


def attention_kernel(
    tokens_ref, allowed_ref, memory_ref, keep_ref, w_qkv, w_out, w_q, w_kv, w_cross_out, gains,
    biases, q_ref, kv_ref, h1_ref, qc_ref, kvc_ref, h2_ref, a3_ref, pack_ref, probs_ref,
    probs_cross_ref, a1,
):
    rows = q_ref.shape[0]
    width = tokens_ref.shape[1]
    a1_rows, o_rows, a2_rows, oc_rows, memory_rows = map(slice, PACK[:-1], PACK[1:])
    first_rows, second_rows = slice(PACK[3], PACK[3] + rows), slice(PACK[3] + rows, PACK[4])
    values = tokens_ref[...].astype(f32)
    normed, _ = normalized(values)
    a1[...] = (normed * gains[0:1] + biases[0:1]).astype(bf16)
    pack_ref[a1_rows] = a1[:rows]
    pack_ref[memory_rows] = memory_ref[...]
    q_ref[...] = dot(a1[:rows], w_qkv[:, :width]).astype(bf16)
    kv_ref[...] = dot(a1[...], w_qkv[:, width:]).astype(bf16)
    allowed = allowed_of(allowed_ref)
    for at in range(0, width, PAIR):
        queries = parted(q_ref[:, at : at + PAIR])
        probs = self_softmax(queries, kv_ref[:, at : at + PAIR], allowed)
        probs_ref[at // PAIR] = probs
        mixed = dot(probs.astype(bf16), kv_ref[:, width + at : width + at + PAIR])
        pack_ref[o_rows, at : at + PAIR] = merged(mixed).astype(bf16)
    h1 = values[:rows] + dot(pack_ref[o_rows], w_out[...])
    h1_ref[...] = h1
    normed, _ = normalized(h1)
    pack_ref[a2_rows] = (normed * gains[1:2] + biases[1:2]).astype(bf16)
    qc_ref[...] = dot(pack_ref[a2_rows], w_q[...]).astype(bf16)
    kvc_ref[...] = dot(memory_ref[...], w_kv[...]).astype(bf16)
    shape = (2 * rows, memory_ref.shape[0])
    kept = jnp.broadcast_to(keep_ref[...], shape) > 0.5
    is_first = lax.broadcasted_iota(jnp.int32, shape, 1) < shape[1] // 2
    for at in range(0, width, PAIR):
        queries = parted(qc_ref[:, at : at + PAIR])
        probs = cross_softmax(queries, kvc_ref[:, at : at + PAIR], kept, is_first)
        probs_cross_ref[at // PAIR] = probs
        mixed = dot(
            each_view(probs.astype(bf16), is_first), kvc_ref[:, width + at : width + at + PAIR]
        )
        pack_ref[first_rows, at : at + PAIR] = merged(mixed[: 2 * rows]).astype(bf16)
        pack_ref[second_rows, at : at + PAIR] = merged(mixed[2 * rows :]).astype(bf16)
    h2 = jnp.concatenate([h1, h1], 0) + dot(pack_ref[oc_rows], w_cross_out[...])
    h2_ref[...] = h2
    normed, _ = normalized(h2)
    a3_ref[...] = (normed * gains[2:3] + biases[2:3]).astype(bf16)


def attention(tokens_page, allowed, memory_rows, keep, weights, gains, biases):
    rows, width = allowed.shape[0], tokens_page.shape[1]
    shape = jax.ShapeDtypeStruct
    return pl.pallas_call(
        attention_kernel,
        out_shape=(
            shape((rows, width), bf16),
            shape((2 * rows, 2 * width), bf16),
            shape((rows, width), f32),
            shape((rows, width), bf16),
            shape((memory_rows.shape[0], 2 * width), bf16),
            shape((2 * rows, width), f32),
            shape((2 * rows, width), bf16),
            shape((PACK[-1], width), bf16),
            shape((width // PAIR, 2 * rows, 2 * rows), f32),
            shape((width // PAIR, 2 * rows, memory_rows.shape[0]), f32),
        ),
        scratch_shapes=[pltpu.VMEM((2 * rows, width), bf16)],
        compiler_params=pltpu.CompilerParams(vmem_limit_bytes=58 * MIB),
        cost_estimate=pl.CostEstimate(
            flops=2 * 10**9, bytes_accessed=24 * MIB, transcendentals=10**6
        ),
    )(tokens_page, allowed, memory_rows, keep, *weights, gains, biases)


def erf_parts(values):
    return 0.5 + 0.5 * lax.erf(values * (0.5**0.5))


def feed_forward_kernel(
    h2_ref, a3_ref, w_up, w_down, gains, biases, slope_ref, act_ref, h3_ref, out_ref, fin_ref, total
):
    step = pl.program_id(0)

    @pl.when(step == 0)
    def _():
        total[...] = jnp.zeros_like(total)

    up = dot(a3_ref[...], w_up[...])
    below = erf_parts(up)
    slope = below + up * jnp.exp(-0.5 * up * up) * (0.5 / jnp.pi) ** 0.5
    slope_ref[...] = slope.astype(bf16)
    act = (up * below).astype(bf16)
    act_ref[...] = act
    total[...] += dot(act, w_down[...])

    @pl.when(step == pl.num_programs(0) - 1)
    def _():
        h3 = h2_ref[...] + total[...]
        h3_ref[...] = h3
        out_ref[...] = h3.astype(bf16)
        normed, _ = normalized(h3)
        fin_ref[...] = (normed * gains[3:4] + biases[3:4]).astype(bf16)


def whole(*shape):
    return pl.BlockSpec(shape, lambda i: (0,) * len(shape))


def feed_forward(h2, a3, w_up, w_down, gains, biases):
    rows, width = h2.shape
    hidden = w_up.shape[1]
    shape = jax.ShapeDtypeStruct
    return pl.pallas_call(
        feed_forward_kernel,
        grid=(hidden // FF_TILE,),
        in_specs=[
            whole(rows, width),
            whole(rows, width),
            pl.BlockSpec((width, FF_TILE), lambda i: (0, i)),
            pl.BlockSpec((FF_TILE, width), lambda i: (i, 0)),
            whole(4, width),
            whole(4, width),
        ],
        out_specs=(
            pl.BlockSpec((rows, FF_TILE), lambda i: (0, i)),
            pl.BlockSpec((rows, FF_TILE), lambda i: (0, i)),
            whole(rows, width),
            whole(rows, width),
            whole(rows, width),
        ),
        out_shape=(
            shape((rows, hidden), bf16),
            shape((rows, hidden), bf16),
            shape((rows, width), f32),
            shape((rows, width), bf16),
            shape((rows, width), bf16),
        ),
        scratch_shapes=[pltpu.VMEM((rows, width), f32)],
        compiler_params=pltpu.CompilerParams(vmem_limit_bytes=58 * MIB),
        cost_estimate=pl.CostEstimate(
            flops=4 * rows * width * hidden, bytes_accessed=24 * MIB, transcendentals=rows * hidden
        ),
    )(h2, a3, w_up, w_down, gains, biases)


def halves(block):
    middle = block.shape[1] // 2
    return block[:, :middle], block[:, middle:]


def divide(core, block, keep_ref, give_ref):
    for side in range(2):

        @pl.when(core == side)
        def _(side=side):
            keep_ref[...] = halves(block)[side]
            give_ref[...] = halves(block)[1 - side]


def feed_forward_back_kernel(
    core_ref, own_ref, other_ref, far_a, far_b, far_c, h3_ref, h2_ref, gains, slope_hbm, w_up_hbm,
    w_down_hbm, gh3_keep, gh3_give, gup_keep, gup_give, gh2_ref, vector_ref, gh3_low, slope, w_up,
    w_down, arrived,
):
    core = core_ref[0]
    tiles = w_up.shape[0]
    copies = []
    for t in range(tiles):
        here = slice(t * FF_TILE, (t + 1) * FF_TILE)
        pairs = (
            (w_down_hbm.at[here], w_down.at[t]),
            (slope_hbm.at[:, here], slope.at[t]),
            (w_up_hbm.at[:, here], w_up.at[t]),
        )
        copies.append(
            [pltpu.make_async_copy(*pair, arrived.at[t, k]) for k, pair in enumerate(pairs)]
        )
        for copy in copies[-1]:
            copy.start()
    upstream = own_ref[...]
    for ref in (other_ref, far_a, far_b, far_c):
        upstream += ref[...].astype(f32)
    normed, inverse = normalized(h3_ref[...])
    gh3, gain, bias = norm_back(upstream, normed, inverse, gains[3:4])
    gh3_low[...] = gh3.astype(bf16)
    divide(core, gh3_low[...], gh3_keep, gh3_give)
    vector_ref[...] = jnp.zeros_like(vector_ref)
    vector_ref[3:4] = gain
    vector_ref[7:8] = bias
    total = None
    for t in range(tiles):
        for copy in copies[t]:
            copy.wait()
        gup = (dot_nt(gh3_low[...], w_down[t]) * slope[t].astype(f32)).astype(bf16)
        side, at = t // (tiles // 2), t % (tiles // 2) * FF_TILE

        @pl.when(core == side)
        def _(gup=gup, at=at):
            gup_keep[:, at : at + FF_TILE] = gup

        @pl.when(core != side)
        def _(gup=gup, at=at):
            gup_give[:, at : at + FF_TILE] = gup

        result = dot_nt(gup, w_up[t])
        total = result if total is None else total + result
    normed, inverse = normalized(h2_ref[...])
    back, gain, bias = norm_back(total, normed, inverse, gains[2:3])
    gh2_ref[...] = gh3 + back
    vector_ref[2:3] = gain
    vector_ref[6:7] = bias


def feed_forward_back(core, parts, h3, h2, slope, w_up, w_down, gains):
    rows, width = h2.shape
    hidden = w_up.shape[1]
    tiles = hidden // FF_TILE
    shape = jax.ShapeDtypeStruct
    vmem = pl.BlockSpec(memory_space=pltpu.VMEM)
    return pl.pallas_call(
        feed_forward_back_kernel,
        in_specs=scalar_first(8) + [pl.BlockSpec(memory_space=pl.ANY) for _ in range(3)],
        out_specs=(vmem,) * 6,
        out_shape=(
            shape((rows, width // 2), bf16),
            shape((rows, width // 2), bf16),
            shape((rows, hidden // 2), bf16),
            shape((rows, hidden // 2), bf16),
            shape((rows, width), f32),
            shape((8, width), f32),
        ),
        scratch_shapes=[
            pltpu.VMEM((rows, width), bf16),
            pltpu.VMEM((tiles, rows, FF_TILE), bf16),
            pltpu.VMEM((tiles, width, FF_TILE), bf16),
            pltpu.VMEM((tiles, FF_TILE, width), bf16),
            pltpu.SemaphoreType.DMA((tiles, 3)),
        ],
        compiler_params=pltpu.CompilerParams(vmem_limit_bytes=58 * MIB),
        cost_estimate=pl.CostEstimate(
            flops=4 * rows * width * hidden,
            bytes_accessed=24 * MIB,
            transcendentals=2 * rows * hidden,
        ),
    )(core, *parts, h3, h2, gains, slope, w_up, w_down)


def attention_back_kernel(
    gh2_ref, w_cross_out, probs_cross_ref, kvc_ref, qc_ref, gains, *refs,
):
    later, refs = refs[:6], refs[6:]
    gh1_ref, gq_ref, gkv_ref, give_ref, gkvc_ref, vector_ref, sent_ref = refs[:7]
    goc, go, gqc, gh1_low, *buffers, arrived = refs[7:]
    copies = [
        pltpu.make_async_copy(ref, buffer, arrived.at[k])
        for k, (ref, buffer) in enumerate(zip(later, buffers))
    ]
    for copy in copies:
        copy.start()
    w_q, h1_ref, w_out, probs_ref, kv_ref, q_ref = buffers
    rows, width = gh1_ref.shape
    scale = HEAD ** (-0.5)
    sent_rows = list(map(slice, SENT[:-1], SENT[1:]))

    def pairs_of_heads():
        for number in range(2 * SIDE):
            at = number * PAIR
            yield number, sent_ref.at[number], slice(at, at + PAIR), slice(width + at, width + at + PAIR)

    gh2_low = gh2_ref[...].astype(bf16)
    goc[...] = dot_nt(gh2_low, w_cross_out[...]).astype(bf16)
    shape = (2 * rows, kvc_ref.shape[0])
    is_first = lax.broadcasted_iota(jnp.int32, shape, 1) < shape[1] // 2
    for number, to, here, there in pairs_of_heads():
        queries = parted(qc_ref[:, here])
        probs = probs_cross_ref[number]
        upstream = jnp.concatenate([parted(goc[:rows, here]), parted(goc[rows:, here])], 0)
        grad = dot_nt(upstream, kvc_ref[:, there])
        grad = jnp.where(is_first, grad[: 2 * rows], grad[2 * rows :])
        slope = probs * (grad - by_view(probs * grad, is_first, jnp.sum, 0.0))
        slope = slope.astype(bf16)
        change = (merged(dot(slope, kvc_ref[:, here])) * scale).astype(bf16)
        gqc[:, here] = change
        to[sent_rows[2]] = change
        to[sent_rows[3]] = gh2_ref[:, here].astype(bf16)
        change = (dot_tn(slope, queries) * scale).astype(bf16)
        gkvc_ref[:, here] = change
        to[sent_rows[6]] = change
        change = dot_tn(each_view(probs.astype(bf16), is_first), upstream).astype(bf16)
        gkvc_ref[:, there] = change
        to[sent_rows[7]] = change
    for copy in copies[:2]:
        copy.wait()
    normed, inverse = normalized(h1_ref[...])
    back, gain, bias = norm_back(dot_nt(gqc[...], w_q[...]), normed, inverse, gains[1:2])
    vector_ref[...] = jnp.zeros_like(vector_ref)
    vector_ref[1:2] = gain
    vector_ref[5:6] = bias
    gh1 = gh2_ref[:rows] + gh2_ref[rows:] + back
    gh1_ref[...] = gh1
    gh1_low[...] = gh1.astype(bf16)
    for copy in copies[2:]:
        copy.wait()
    go[...] = dot_nt(gh1_low[...], w_out[...]).astype(bf16)
    for number, to, here, there in pairs_of_heads():
        queries = parted(q_ref[:, here])
        probs = probs_ref[number]
        upstream = parted(go[:, here])
        grad = dot_nt(upstream, kv_ref[:, there])
        slope = probs * (grad - jnp.sum(probs * grad, -1, keepdims=True))
        slope = slope.astype(bf16)
        change = (merged(dot(slope, kv_ref[:, here])) * scale).astype(bf16)
        gq_ref[:, here] = change
        to[sent_rows[0]] = change
        to[sent_rows[1]] = gh1_low[:, here]
        change = (dot_tn(slope, queries) * scale).astype(bf16)
        gkv_ref[:, here] = change[:rows]
        give_ref[:, here] = change[rows:]
        to[sent_rows[4]] = change
        change = dot_tn(probs.astype(bf16), upstream).astype(bf16)
        gkv_ref[:, there] = change[:rows]
        give_ref[:, there] = change[rows:]
        to[sent_rows[5]] = change


def scalar_first(count):
    return [pl.BlockSpec(memory_space=pltpu.SMEM)] + [
        pl.BlockSpec(memory_space=pltpu.VMEM) for _ in range(count)
    ]


def attention_back(gh2, probs, probs_cross, kvc, qc, h1, kv, q, w_cross_out, w_q, w_out, gains):
    rows, width = q.shape
    shape = jax.ShapeDtypeStruct
    vmem = pl.BlockSpec(memory_space=pltpu.VMEM)
    later = (w_q, h1, w_out, probs, kv, q)
    return pl.pallas_call(
        attention_back_kernel,
        in_specs=[vmem] * 6 + [pl.BlockSpec(memory_space=pl.ANY) for _ in later],
        out_specs=(vmem,) * 7,
        out_shape=(
            shape((rows, width), f32),
            shape((rows, width), bf16),
            shape((rows, 2 * width), bf16),
            shape((rows, 2 * width), bf16),
            shape(kvc.shape, bf16),
            shape((8, width), f32),
            shape((2 * SIDE, SENT[-1], PAIR), bf16),
        ),
        scratch_shapes=[
            pltpu.VMEM((2 * rows, width), bf16),
            pltpu.VMEM((rows, width), bf16),
            pltpu.VMEM((rows, width), bf16),
            pltpu.VMEM((rows, width), bf16),
            *(pltpu.VMEM(array.shape, array.dtype) for array in later),
            pltpu.SemaphoreType.DMA((len(later),)),
        ],
        compiler_params=pltpu.CompilerParams(vmem_limit_bytes=58 * MIB),
        cost_estimate=pl.CostEstimate(
            flops=2 * 10**9, bytes_accessed=14 * MIB, transcendentals=10**6
        ),
    )(gh2, w_cross_out, probs_cross, kvc, qc, gains, *later)


def inputs_back_kernel(
    core_ref, tokens_ref, gh1_ref, gq_ref, gkv_ref, come_ref, gkvc_ref, come_cross_ref, w_qkv,
    w_kv, gains, tokens_grad_ref, memory_grad_ref, vector_ref, grads,
):
    core = core_ref[0]
    width = gh1_ref.shape[1]
    pairs = (gkv_ref[...].astype(f32) + come_ref[...].astype(f32)).astype(bf16)
    total = dot_nt(gq_ref[...], w_qkv[:, :width]) + dot_nt(pairs, w_qkv[:, width:])
    normed, inverse = normalized(tokens_ref[...].astype(f32))
    back, gain, bias = norm_back(total, normed, inverse, gains[0:1])
    tokens_grad_ref[...] = gh1_ref[...] + back
    vector_ref[...] = jnp.zeros_like(vector_ref)
    vector_ref[0:1] = gain
    vector_ref[4:5] = bias
    pairs = (gkvc_ref[...].astype(f32) + come_cross_ref[...].astype(f32)).astype(bf16)
    grads[...] = dot_nt(pairs, w_kv[...])
    own = memory_grad_ref.shape[1]
    for view in range(2):
        start = pl.multiple_of(view * 2 * own + core * own, 8)
        memory_grad_ref[view] = grads[pl.ds(start, own)]


def inputs_back(core, *operands):
    rows, width = operands[1].shape
    patches = operands[5].shape[0]
    shape = jax.ShapeDtypeStruct
    return pl.pallas_call(
        inputs_back_kernel,
        in_specs=scalar_first(len(operands)),
        out_shape=(
            shape((rows, width), f32),
            shape((2, patches // 4, width), f32),
            shape((8, width), f32),
        ),
        scratch_shapes=[pltpu.VMEM((patches, width), f32)],
        compiler_params=pltpu.CompilerParams(vmem_limit_bytes=58 * MIB),
        cost_estimate=pl.CostEstimate(flops=10**9, bytes_accessed=14 * MIB, transcendentals=0),
    )(core, *operands)


def logits_kernel(rows_ref, readout_ref, bias_ref, logits_ref, stats_ref, kept):
    tokens = rows_ref.shape[1]
    rows = jnp.concatenate([rows_ref[0], rows_ref[1]], 0)

    def statistics(begin, end):
        spans = range(begin, end, 128)
        for at in range(0, tokens, CHUNK):
            here = slice(at, at + CHUNK)
            first = [logits_ref[0, 0, here, c : c + 128] for c in spans]
            second = [logits_ref[0, 1, here, c : c + 128] for c in spans]
            new_first, new_second = first[0], second[0]
            for a, b in zip(first[1:], second[1:]):
                new_first = jnp.maximum(new_first, a)
                new_second = jnp.maximum(new_second, b)
            total_first = total_apart = total_second = jnp.zeros((CHUNK, 128), f32)
            if begin:
                top_first, top_second = kept[0, here], kept[3, here]
                new_first = jnp.maximum(new_first, top_first)
                new_second = jnp.maximum(new_second, top_second)
                fade_first = jnp.exp(top_first - new_first)
                total_first = kept[1, here] * fade_first
                total_apart = kept[2, here] * fade_first
                total_second = kept[4, here] * jnp.exp(top_second - new_second)
            for a, b in zip(first, second):
                weight = jnp.exp(a - new_first)
                total_first += weight
                total_apart += weight * (a - b)
                total_second += jnp.exp(b - new_second)
            kept[0, here], kept[1, here], kept[2, here] = new_first, total_first, total_apart
            kept[3, here], kept[4, here] = new_second, total_second

    before = None
    for begin, end in PARTS:
        values = dot_nt(rows, readout_ref[begin:end]) + bias_ref[:, begin:end]
        for v in range(2):
            logits_ref[0, v, :, begin:end] = values[v * tokens : (v + 1) * tokens]
        if before:
            statistics(*before)
        before = begin, end
    statistics(*before)

    top_first = jnp.max(kept[0], -1, keepdims=True)
    top_second = jnp.max(kept[3], -1, keepdims=True)
    fade_first = jnp.exp(kept[0] - top_first)
    fade_second = jnp.exp(kept[3] - top_second)
    stats = (
        top_first,
        jnp.sum(kept[1] * fade_first, -1, keepdims=True),
        jnp.sum(kept[2] * fade_first, -1, keepdims=True),
        top_second,
        jnp.sum(kept[4] * fade_second, -1, keepdims=True),
    )
    lane = lax.broadcasted_iota(jnp.int32, kept.shape[1:], 1)
    result = jnp.zeros(kept.shape[1:], f32)
    for k, stat in enumerate(stats):
        result = jnp.where(lane == k, stat, result)
    stats_ref[0] = result.T[:8]


def once(*shape):
    return pl.BlockSpec(shape, lambda i: (0,) * len(shape), pipeline_mode=pl.Buffered(1))


def logits_and_stats(rows, readout_rows, bias):
    views, tokens, width = rows.shape
    entries = readout_rows.shape[0]
    page = tokens // SIDE
    shape = jax.ShapeDtypeStruct
    return pl.pallas_call(
        logits_kernel,
        out_shape=(
            shape((SIDE, 2, page, entries), f32),
            shape((SIDE, 8, page), f32),
        ),
        grid=(SIDE,),
        in_specs=[
            pl.BlockSpec((2, page, width), lambda i: (0, i, 0)),
            once(entries, width),
            once(1, entries),
        ],
        out_specs=(
            pl.BlockSpec((1, 2, page, entries), lambda i: (i, 0, 0, 0)),
            pl.BlockSpec((1, 8, page), lambda i: (i, 0, 0)),
        ),
        scratch_shapes=[pltpu.VMEM((5, page, 128), f32)],
        compiler_params=pltpu.CompilerParams(vmem_limit_bytes=58 * MIB),
        cost_estimate=pl.CostEstimate(
            flops=4 * tokens * entries * width,
            bytes_accessed=2 * entries * width + 8 * tokens * entries,
            transcendentals=2 * tokens * entries,
        ),
    )(rows, readout_rows, bias)


def merged_stats(near_ref, come_ref, slot):
    tokens = near_ref.shape[3]
    middle = tokens // 2
    parts = []
    for ref, flipped in ((near_ref, False), (come_ref, True)):
        for r in range(SIDE):
            part = ref[r, lax.rem(slot + SIDE - r, SIDE)]
            if flipped:
                part = jnp.concatenate([part[:, middle:], part[:, :middle]], 1)
            parts.append(part)
    top_first = parts[0][0:1]
    top_second = parts[0][3:4]
    for part in parts[1:]:
        top_first = jnp.maximum(top_first, part[0:1])
        top_second = jnp.maximum(top_second, part[3:4])
    total_first = total_apart = total_second = jnp.zeros((1, tokens), f32)
    for part in parts:
        fade = jnp.exp(part[0:1] - top_first)
        total_first += part[1:2] * fade
        total_apart += part[2:3] * fade
        total_second += part[4:5] * jnp.exp(part[3:4] - top_second)
    first_lse = top_first + jnp.log(total_first)
    second_lse = top_second + jnp.log(total_second)
    return first_lse, second_lse, total_apart / total_first


def readout_back_kernel(
    far, near_ref, come_ref, weight_ref, logits_ref, readout_ref, stay_ref, other_ref, kept, slopes
):
    step = pl.program_id(0)
    tokens = weight_ref.shape[1]
    rows = tokens // 2
    slot = lax.rem(step + 1, SIDE) if far else 0
    for k, row in enumerate(merged_stats(near_ref, come_ref, slot)):
        kept[k] = jnp.broadcast_to(row, (128, row.shape[1])).T
    kept[3] = weight_ref[0]

    def gradient(start, count):
        def derivatives(begin, end):
            for at in range(start, start + count, CHUNK):
                here = slice(at, at + CHUNK)
                first_lse, second_lse, apart, weight = (kept[k, here] for k in range(4))
                for c in range(begin, end, 128):
                    first = logits_ref[0, 0, here, c : c + 128]
                    second = logits_ref[0, 1, here, c : c + 128]
                    first_prob = jnp.exp(first - first_lse) * weight
                    second_prob = jnp.exp(second - second_lse) * weight
                    change = first_prob * (first - second - apart)
                    slopes[0, here, c : c + 128] = change.astype(bf16)
                    slopes[1, here, c : c + 128] = (second_prob - first_prob).astype(bf16)

        derivatives(*PARTS[0])
        total = None
        for i, (begin, end) in enumerate(PARTS):
            block = [slopes[v, start : start + count, begin:end] for v in range(2)]
            result = dot(jnp.concatenate(block, 0), readout_ref[begin:end])
            if i + 1 < len(PARTS):
                derivatives(*PARTS[i + 1])
            total = result if total is None else total + result
        return total

    if not far:
        total = gradient(0, rows)
        for v in range(2):
            stay_ref[0, v] = total[v * rows : (v + 1) * rows]
        other_ref[...] = kept[3] * (kept[2] - kept[0] + kept[1])
        return

    @pl.when(step < SIDE - 1)
    def _():
        total = gradient(0, tokens)
        for v in range(2):
            stay_ref[0, v] = total[v * tokens : v * tokens + rows].astype(bf16)
            other_ref[0, v] = total[v * tokens + rows : (v + 1) * tokens].astype(bf16)

    @pl.when(step == SIDE - 1)
    def _():
        total = gradient(rows, rows)
        for v in range(2):
            other_ref[0, v] = total[v * rows : (v + 1) * rows].astype(bf16)


def readout_back(stats_near, stats_come, weight, logits, readout_rows, far):
    tokens, entries = logits.shape[2:]
    width = readout_rows.shape[1]
    rows = tokens // 2
    pages = SIDE if far else 1
    shape = jax.ShapeDtypeStruct
    block = (1, 2, rows, width)
    if far:
        out_shape = (
            shape((SIDE - 1, 2, rows, width), bf16),
            shape((SIDE, 2, rows, width), bf16),
        )
        out_specs = (
            pl.BlockSpec(block, lambda i: (jnp.minimum(i, SIDE - 2), 0, 0, 0)),
            pl.BlockSpec(block, lambda i: (i, 0, 0, 0)),
        )
    else:
        out_shape = (shape(block, f32), shape((tokens, 128), f32))
        out_specs = (whole(*block), whole(tokens, 128))

    def page(i):
        return lax.rem(i + 1, SIDE) if far else i

    here = tokens if far else rows
    return pl.pallas_call(
        partial(readout_back_kernel, far),
        out_shape=out_shape,
        grid=(pages,),
        in_specs=[
            once(SIDE, SIDE, 8, tokens),
            once(SIDE, SIDE, 8, tokens),
            pl.BlockSpec((1, tokens, 128), lambda i: (page(i), 0, 0)),
            pl.BlockSpec((1, 2, here, entries), lambda i: (page(i), 0, 0, 0)),
            once(entries, width),
        ],
        out_specs=out_specs,
        scratch_shapes=[
            pltpu.VMEM((4, tokens, 128), f32),
            pltpu.VMEM((2, here, entries), bf16),
        ],
        compiler_params=pltpu.CompilerParams(vmem_limit_bytes=58 * MIB),
        cost_estimate=pl.CostEstimate(
            flops=4 * pages * here * entries * width,
            bytes_accessed=2 * entries * width + 8 * pages * here * entries,
            transcendentals=2 * pages * here * entries,
        ),
    )(stats_near, stats_come, weight, logits, readout_rows)


FIRST_AXES = ((4, 16), (16, 1), (1, 4))
SECOND_AXES = ((4, 16), (16, 4))


def swapped(block):
    return lax.ppermute(block, "mem", [(0, 1), (1, 0)])


def along_line(block, distance):
    route = [(d, d // SIDE * SIDE + (d - distance) % SIDE) for d in range(CHIPS)]
    return lax.ppermute(block, "dp", route)


def lines(stride, core):
    starts = [d for d in range(CHIPS) if (d // stride) % SIDE == 0]
    return [[2 * (start + stride * k) + core for k in range(SIDE)] for start in starts]


def digit_of(strides):
    chip, core = lax.axis_index("dp"), lax.axis_index("mem")
    return jnp.where(core == 0, chip // strides[0], chip // strides[1]) % SIDE


def along_lines(block, strides, r):
    route = []
    for d in range(CHIPS):
        for m, stride in enumerate(strides):
            own = d // stride % SIDE
            to = d + ((own + r) % SIDE - own) * stride
            route.append((2 * d + m, 2 * to + m))
    return lax.ppermute(block, ("dp", "mem"), route)


def line_sum(part, strides):
    return parts_sum(parts_of(part, strides), strides)


def parts_of(part, strides):
    parts = part.reshape(SIDE, -1, part.shape[-1])
    digit = digit_of(strides)
    return [lax.dynamic_index_in_dim(parts, (digit + r) % SIDE, 0, False) for r in range(SIDE)]


def parts_sum(parts, strides):
    parts = parts_come(parts, strides)
    total = parts[0].astype(f32)
    for block in parts[1:]:
        total += block.astype(f32)
    return total


def parts_come(parts, strides):
    return [parts[0]] + [along_lines(parts[r], strides, r) for r in range(1, SIDE)]


def scattered_sum(bucket, strides):
    flat = bucket.reshape(-1, bucket.shape[-1])
    groups = lines(strides[0], 0) + lines(strides[1], 1)
    return lax.psum_scatter(
        flat, ("dp", "mem"), axis_index_groups=groups, scatter_dimension=0, tiled=True
    )


def outer_kernel(items, orders, core_ref, *refs):
    inputs, out_ref, turned = refs[: 4 * len(items)], refs[4 * len(items)], refs[-len(items) :]
    step = pl.program_id(0)
    core = core_ref[0]

    def place(chip):
        at = [0, 0]
        for m in range(2):
            for stride in orders[m]:
                at[m] = at[m] * SIDE + chip // stride % SIDE
        return jnp.where(core == 0, at[0], at[1])

    def turn(lefts, to, groups):
        for start in range(0, lefts[0].shape[1], 1024):
            flat = jnp.concatenate([left[:, start : start + 1024] for left in lefts], 0).T
            if groups == 1:
                to[0, start : start + 1024] = flat
                continue
            per = ROWS * groups
            for c in range(1024 // per):
                chip = start // per + c
                for g in range(groups):
                    at = c * per + g * ROWS
                    to[g, chip * ROWS : (chip + 1) * ROWS] = flat[at : at + ROWS]

    def multiply(rights, to, groups, begin):
        at = step - begin
        span = min(TILE, rights[0].shape[1])
        start = at * TILE if groups == 1 else 0
        column = pl.ds(pl.multiple_of(start, span), span)
        both = jnp.concatenate([right[:, column] for right in rights], 0)
        for k in range(TILE // span):
            group = at * (TILE // span) + k if groups > 1 else 0
            result = dot(to[group], both).astype(bf16)
            for chip in range(CHIPS):
                here = result[chip * ROWS : (chip + 1) * ROWS]
                out_ref[place(chip), :, k * span : (k + 1) * span] = here

    for k, (groups, begin, end) in enumerate(items):
        lefts, rights, to = inputs[4 * k : 4 * k + 2], inputs[4 * k + 2 : 4 * k + 4], turned[k]
        pl.when(step == begin)(partial(turn, lefts, to, groups))
        pl.when((step >= begin) & (step < end))(partial(multiply, rights, to, groups, begin))


def outer_products(core, products, axes):
    items, scratch = [], []
    total = flops = 0
    for left, left_come, right, _ in products:
        groups = left.shape[1] // (ROWS * CHIPS)
        depth = left.shape[0] + left_come.shape[0]
        columns = right.shape[1]
        scratch.append(pltpu.VMEM((groups, ROWS * CHIPS, depth), bf16))
        begin = total // TILE
        total += groups * columns
        flops += 2 * groups * ROWS * CHIPS * columns * depth
        items.append((groups, begin, total // TILE))
    operands = [array for product in products for array in product]
    return pl.pallas_call(
        partial(outer_kernel, tuple(items), tuple(zip(*axes))),
        out_shape=jax.ShapeDtypeStruct((CHIPS, ROWS, total), bf16),
        grid_spec=pltpu.PrefetchScalarGridSpec(
            num_scalar_prefetch=1,
            grid=(total // TILE,),
            in_specs=[
                pl.BlockSpec(
                    array.shape, lambda i, core: (0, 0), pipeline_mode=pl.Buffered(1)
                )
                for array in operands
            ],
            out_specs=pl.BlockSpec((CHIPS, ROWS, TILE), lambda i, core: (0, 0, i)),
            scratch_shapes=scratch,
        ),
        compiler_params=pltpu.CompilerParams(vmem_limit_bytes=58 * MIB),
        cost_estimate=pl.CostEstimate(
            flops=flops, bytes_accessed=CHIPS * ROWS * total * 2, transcendentals=0
        ),
    )(core, *operands)


LINE = ROWS * SIDE
DEPTHS = tuple(
    2 * SIDE * (PACK[k + 1] - PACK[k]) // (2 if k == 4 else 1) for k in range(len(PACK) - 1)
)


def turn_kernel(orders, core_ref, packs_ref, out_ref):
    core = core_ref[0]
    start = 0
    for k, depth in enumerate(DEPTHS):
        numbers = range(0, 2 * SIDE, 2 if k == 4 else 1)
        blocks = [packs_ref[number, PACK[k] : PACK[k + 1]] for number in numbers]
        flat = jnp.concatenate(blocks, 0).T
        for line in range(SIDE * SIDE):
            z, y = line // SIDE, line % SIDE
            digit = {4: y, 16: z}
            at = [SIDE * digit[first] + digit[second] for first, second in orders]
            at = pl.multiple_of(jnp.where(core == 0, at[0], at[1]) * LINE, LINE)
            out_ref[pl.ds(at, LINE), start : start + depth] = flat[line * LINE : (line + 1) * LINE]
        start += depth


def turned_packs(core, packs, axes):
    width = packs.shape[2]
    return pl.pallas_call(
        partial(turn_kernel, tuple(zip(*axes))),
        in_specs=scalar_first(1),
        out_shape=jax.ShapeDtypeStruct((width, sum(DEPTHS)), bf16),
        compiler_params=pltpu.CompilerParams(vmem_limit_bytes=58 * MIB),
        cost_estimate=pl.CostEstimate(flops=0, bytes_accessed=20 * MIB, transcendentals=0),
    )(core, packs)


def line_products_kernel(
    digit_ref, vectors_ref, turned_hbm, come_hbm, *refs
):
    outs, (joint, plain, cross, wide, come_ref, turned_ref, results, arrived, left) = (
        refs[:SIDE],
        refs[SIDE:],
    )
    block = turned_ref.shape[1]
    fetch_come = pltpu.make_async_copy(come_hbm, come_ref, arrived.at[SIDE])
    fetch_come.start()
    starts = [
        pl.multiple_of(lax.rem(digit_ref[0] + r, SIDE) * block, block) for r in range(SIDE)
    ]
    fetches = [
        pltpu.make_async_copy(turned_hbm.at[pl.ds(start, block)], turned_ref.at[r], arrived.at[r])
        for r, start in enumerate(starts)
    ]
    for fetch in fetches:
        fetch.start()
    fetch_come.wait()
    rows = SENT[1]

    def part(number, k):
        return come_ref[number, SENT[k] : SENT[k + 1]]

    def added(first, second):
        return (first.astype(f32) + second.astype(f32)).astype(bf16)

    for number in range(2 * SIDE):
        at = number * rows
        here = slice(at, at + rows)
        joint[here, :PAIR] = part(number, 0)
        for k in (4, 5):
            share = added(part(number, k)[:rows], part(number ^ 1, k)[rows:])
            joint[here, (k - 3) * PAIR : (k - 2) * PAIR] = share
        plain[here, :PAIR] = part(number, 1)
        plain[here, PAIR:] = part(number, 2)
        wide[2 * at : 2 * (at + rows)] = part(number, 3)
    for chip in range(SIDE):
        here = slice(chip * rows, (chip + 1) * rows)
        for k in (6, 7):
            column = slice((k - 6) * PAIR, (k - 5) * PAIR)
            cross[here, column] = added(part(2 * chip, k), part(2 * chip + 1, k))

    ends = [sum(DEPTHS[: k + 1]) for k in range(len(DEPTHS))]
    stores = []
    for r in range(SIDE):
        fetches[r].wait()
        a1, o, a2, oc, memory = (
            turned_ref[r, :, end - depth : end] for end, depth in zip(ends, DEPTHS)
        )
        blocks = [
            dot(a1, joint[...]),
            dot(o, plain[:, :PAIR]),
            dot(a2, plain[:, PAIR:]),
            dot(memory, cross[...]),
            dot(oc, wide[...]),
            vectors_ref[pl.ds(starts[r], block)].astype(f32),
        ]
        results[r] = jnp.concatenate(blocks, 1).astype(bf16)
        stores.append(pltpu.make_async_copy(results.at[r], outs[r], left.at[r]))
        stores[-1].start()
    for store in stores:
        store.wait()


def line_products(digit, turned, come, vectors):
    width, depth = turned.shape
    block = width // SIDE
    columns = 9 * PAIR
    anywhere = pl.BlockSpec(memory_space=pl.ANY)
    return pl.pallas_call(
        line_products_kernel,
        in_specs=scalar_first(1) + [anywhere, anywhere],
        out_specs=(anywhere,) * SIDE,
        out_shape=(jax.ShapeDtypeStruct((block, columns), bf16),) * SIDE,
        scratch_shapes=[
            pltpu.VMEM((DEPTHS[0], 3 * PAIR), bf16),
            pltpu.VMEM((DEPTHS[1], 2 * PAIR), bf16),
            pltpu.VMEM((DEPTHS[4], 2 * PAIR), bf16),
            pltpu.VMEM((DEPTHS[3], PAIR), bf16),
            pltpu.VMEM(come.shape, bf16),
            pltpu.VMEM((SIDE, block, depth), bf16),
            pltpu.VMEM((SIDE, block, columns), bf16),
            pltpu.SemaphoreType.DMA((SIDE + 1,)),
            pltpu.SemaphoreType.DMA((SIDE,)),
        ],
        compiler_params=pltpu.CompilerParams(vmem_limit_bytes=58 * MIB),
        cost_estimate=pl.CostEstimate(
            flops=2 * 10**9, bytes_accessed=14 * MIB, transcendentals=0
        ),
    )(digit, vectors, turned, come)


def collect_kernel(come_ref, *outs):
    qkv, out, q, kv, cross_out, gains, biases = outs
    targets = [(qkv, 0), (qkv, 1), (qkv, 2), (out, 0), (q, 0), (kv, 0), (kv, 1), (cross_out, 0)]
    for number in range(2 * SIDE):
        for k, (target, block) in enumerate(targets):
            start = (block * 2 * SIDE + number) * PAIR
            target[:, start : start + PAIR] = come_ref[number, :, k * PAIR : (k + 1) * PAIR]
    total = come_ref[0, :, 8 * PAIR :]
    for number in range(1, 2 * SIDE):
        total += come_ref[number, :, 8 * PAIR :]
    total = jnp.concatenate([total, jnp.zeros((PAIR - total.shape[0], PAIR), f32)], 0).T
    gains[...] = total[:4, : ROWS // 2]
    biases[...] = total[4:8, : ROWS // 2]


def collected(come):
    return pl.pallas_call(
        collect_kernel,
        out_shape=tuple(
            jax.ShapeDtypeStruct((ROWS // 2, columns), f32)
            for columns in (24 * PAIR, 8 * PAIR, 8 * PAIR, 16 * PAIR, 8 * PAIR)
        )
        + (jax.ShapeDtypeStruct((4, ROWS // 2), f32),) * 2,
    )(come)


def divide_kernel(grouped, core_ref, *refs):
    parts, (keep_ref, give_ref, sums_ref) = refs[:SIDE], refs[SIDE:]
    sums_ref[...] = parts[0][...].astype(f32)
    for part in parts[1:]:
        sums_ref[...] += part[...].astype(f32)
    core = core_ref[0]
    half = grouped // 2
    columns = sums_ref.shape[1]
    for ref, side in ((keep_ref, core), (give_ref, 1 - core)):
        if grouped:
            start = pl.ds(pl.multiple_of(side * half, 128), half)
            block = sums_ref[:, start]
            ref[:, :half] = block[: ROWS // 2]
            ref[:, half:grouped] = block[ROWS // 2 :]
        rows = pl.ds(pl.multiple_of(side * (ROWS // 2), 8), ROWS // 2)
        if columns > grouped:
            ref[:, grouped:] = sums_ref[rows, grouped:]


def divided(core, parts, grouped):
    columns = parts[0].shape[1]
    shape = jax.ShapeDtypeStruct((ROWS // 2, columns), f32)
    return pl.pallas_call(
        partial(divide_kernel, grouped),
        in_specs=scalar_first(SIDE),
        out_shape=(shape, shape),
        scratch_shapes=[pltpu.VMEM((ROWS, columns), f32)],
    )(core, *parts)


def assemble_kernel(layout, core_ref, keep_ref, come_ref, *outs):
    core = core_ref[0]
    for ref, side in ((keep_ref, core), (come_ref, 1 - core)):
        at = 0
        for out, (grouped, columns, span) in zip(outs, layout):
            part = span // 2
            if grouped:
                for g in range(2):
                    for h in range(2):
                        rows = slice(g * ROWS + h * ROWS // 2, g * ROWS + (h + 1) * ROWS // 2)
                        start = at + h * 2 * part + g * part
                        column = pl.ds(pl.multiple_of(side * part, 128), part)
                        out[rows, column] = ref[:, start : start + part]
                at += 4 * part
                continue
            for k in range(0, columns, span):
                column = pl.ds(pl.multiple_of(k + side * part, 128), part)
                out[:, column] = ref[:, at : at + part]
                at += part


def assembled(core, keep, come, layout):
    return pl.pallas_call(
        partial(assemble_kernel, tuple(layout)),
        in_specs=scalar_first(2),
        out_shape=tuple(
            jax.ShapeDtypeStruct((2 * ROWS if grouped else ROWS // 2, columns), f32)
            for grouped, columns, span in layout
        ),
    )(core, keep, come)


def on_device(
    tokens,
    memory,
    lengths,
    segments,
    key_mask,
    w_self_qkv,
    w_self_out,
    w_cross_q,
    w_cross_kv,
    w_cross_out,
    w_up,
    w_down,
    norm_gains,
    norm_biases,
    readout,
):
    tok_rows = tokens.shape[1]
    width = tokens.shape[2]
    half = lax.axis_index("mem")
    core = half.astype(jnp.int32).reshape(1)
    page_index = lax.axis_index("dp")
    patches = 2 * memory.shape[2]

    vocab_dev = readout.shape[1]
    readout_turned = jnp.pad(readout.T, ((0, ENTRIES - vocab_dev), (0, 0)))
    planes = [[d for d in range(CHIPS) if d % SIDE == x] for x in range(SIDE)]
    readout_part = lax.all_gather(
        readout_turned, "dp", axis=0, tiled=True, axis_index_groups=planes
    )
    is_entry = jnp.arange(readout_part.shape[0]) % ENTRIES < vocab_dev
    entry_bias = jnp.where(is_entry, 0.0, masked_score).astype(f32)[None]

    tokens_own = tokens[0]
    tokens_page = jnp.concatenate([tokens_own, swapped(tokens_own)], 0)
    memory_own = memory[:, 0]
    memory_come = swapped(memory_own)
    memory_rows = jnp.where(
        half == 0,
        jnp.concatenate([memory_own, memory_come], 1),
        jnp.concatenate([memory_come, memory_own], 1),
    ).reshape(2 * patches, width)
    mask_own = key_mask[0].astype(f32)
    mask_come = swapped(mask_own)
    mask_page = jnp.where(
        half == 0,
        jnp.concatenate([mask_own, mask_come]),
        jnp.concatenate([mask_come, mask_own]),
    )
    keep = jnp.tile(jnp.repeat(mask_page, 2), 2)[None]
    own_positions = jnp.arange(tok_rows) + half * tok_rows
    other_positions = jnp.arange(tok_rows) + (1 - half) * tok_rows
    key_positions = jnp.concatenate([own_positions, other_positions])
    cut = segments[0].reshape(2, tok_rows)
    own_segments = lax.dynamic_index_in_dim(cut, half, 0, False)
    other_segments = lax.dynamic_index_in_dim(cut, 1 - half, 0, False)
    key_segments = jnp.concatenate([own_segments, other_segments])
    allowed = (key_positions[None, :] <= own_positions[:, None]) & (
        key_segments[None, :] == own_segments[:, None]
    )
    allowed = allowed.astype(f32)
    count = jnp.sum(lengths).astype(f32)
    line = page_index // SIDE * SIDE + (page_index + jnp.arange(SIDE)) % SIDE
    valid = key_positions[None] < lengths[line][:, None]
    row_weight = (valid.astype(f32) / count)[:, :, None]
    row_weight = jnp.broadcast_to(row_weight, row_weight.shape[:2] + (128,))

    weights = (w_self_qkv, w_self_out, w_cross_q, w_cross_kv, w_cross_out)
    q, kv, h1, qc, kvc, h2, a3, pack, probs, probs_cross = attention(
        tokens_page, allowed, memory_rows, keep, weights, norm_gains, norm_biases
    )
    slope, act, h3, layer_out, final = feed_forward(h2, a3, w_up, w_down, norm_gains, norm_biases)
    final = final.reshape(2, tok_rows, width)
    near = jnp.stack([final] + [along_line(final, r) for r in range(1, SIDE)])
    final_line = jnp.stack([near, swapped(near)], 1).transpose(2, 0, 1, 3, 4)
    final_line = final_line.reshape(2, 2 * SIDE * tok_rows, width)
    a3_other, act_other = swapped(a3), swapped(act)

    final_line, row_weight = lax.optimization_barrier((final_line, row_weight))

    line_groups = [
        [2 * (start + k) + m for k in range(SIDE) for m in range(2)]
        for start in range(0, CHIPS, SIDE)
    ]
    packs = lax.all_gather(pack, ("dp", "mem"), axis_index_groups=line_groups)

    def exchanged(block):
        return lax.all_to_all(
            block, ("dp", "mem"), 0, 0, axis_index_groups=line_groups, tiled=True
        )

    logits, stats = logits_and_stats(final_line, readout_part, entry_bias)
    stats = jnp.stack([stats] + [along_line(stats, r) for r in range(1, SIDE)])
    stats_come = swapped(stats)
    far_stay, give = readout_back(stats, stats_come, row_weight, logits, readout_part, True)
    come = swapped(give)
    far = [
        (far_stay[r].astype(f32) + come[r].astype(f32)).astype(bf16) for r in range(SIDE - 1)
    ]
    logits, far, core_late = lax.optimization_barrier((logits, far, core))
    far = [along_line(far[r - 1], -r) for r in range(1, SIDE)]
    own, terms = readout_back(stats, stats_come, row_weight, logits, readout_part, False)
    terms = terms[:, 0].reshape(2, tok_rows).sum(1)
    loss = (terms[0] + terms[1]).reshape(1)
    turned = turned_packs(core_late, packs, SECOND_AXES)
    own, turned = lax.optimization_barrier((own, turned))
    grad_parts = [part.reshape(2 * tok_rows, width) for part in [own[0], come[SIDE - 1]] + far]

    gh3_keep, gh3_give, gup_keep, gup_give, gh2, vectors_ff = feed_forward_back(
        core, grad_parts, h3, h2, slope, w_up, w_down, norm_gains
    )
    first_bucket = outer_products(
        core,
        [
            (act, act_other, gh3_keep, swapped(gh3_give)),
            (a3, a3_other, gup_keep, swapped(gup_give)),
        ],
        FIRST_AXES,
    )
    gh2, first_bucket = lax.optimization_barrier((gh2, first_bucket))
    first_part = scattered_sum(first_bucket, FIRST_AXES[0])

    gh1, gq, gkv, gkv_give, gkvc, vectors_att, sent = attention_back(
        gh2, probs, probs_cross, kvc, qc, h1, kv, q, w_cross_out, w_cross_q, w_self_out, norm_gains
    )
    sent = exchanged(sent)
    tokens_grad, memory_grad, vectors_in = inputs_back(
        core, tokens_own, gh1, gq, gkv, swapped(gkv_give), gkvc, swapped(gkvc), w_self_qkv,
        w_cross_kv, norm_gains,
    )
    sent, first_part, vectors_in = lax.optimization_barrier((sent, first_part, vectors_in))
    vectors = (vectors_ff + vectors_att + vectors_in).astype(bf16)
    vectors = jnp.pad(vectors.T, ((0, 0), (0, PAIR - 8))).reshape(SIDE, SIDE, LINE, PAIR)
    vectors = jnp.where(half == 0, vectors.transpose(1, 0, 2, 3), vectors).reshape(width, PAIR)
    digit = digit_of(SECOND_AXES[0]).astype(jnp.int32).reshape(1)
    second_parts = line_products(digit, turned, sent, vectors)
    second_sums = parts_sum(second_parts, SECOND_AXES[0]).astype(bf16)
    first_sums = scattered_sum(first_part, FIRST_AXES[1])
    second_sums = line_sum(second_sums, SECOND_AXES[1])
    first_parts = parts_come(parts_of(first_sums, FIRST_AXES[2]), FIRST_AXES[2])

    first_keep, first_give = divided(core, first_parts, 2 * width)
    weight_down, weight_up = assembled(
        core,
        first_keep,
        swapped(first_give),
        [(True, width, width), (False, 4 * width, 4 * width)],
    )
    line_sums = exchanged(second_sums.reshape(2 * SIDE, ROWS // 2, -1))
    line_sums, weight_down, weight_up = lax.optimization_barrier(
        (line_sums, weight_down, weight_up)
    )
    weight_qkv, weight_out, weight_q, weight_kv, weight_cross_out, grad_gains, grad_biases = (
        collected(line_sums)
    )
    return (
        loss,
        layer_out.reshape(2, 1, tok_rows, width),
        tokens_grad[None],
        memory_grad[:, None],
        weight_qkv,
        weight_out,
        weight_q,
        weight_kv,
        weight_cross_out,
        weight_up,
        weight_down,
        grad_gains,
        grad_biases,
    )


def solution(mesh):
    in_specs = (
        P("dp", "mem", None),
        P(None, "dp", "mem", None),
        P(),
        P("dp", None),
        P("dp", "mem"),
        P(),
        P(),
        P(),
        P(),
        P(),
        P(),
        P(),
        P(),
        P(),
        P(None, ("dp", "mem")),
    )
    out_specs = (
        P("dp"),
        P(None, "dp", "mem", None),
        P("dp", "mem", None),
        P(None, "dp", "mem", None),
        P(("dp", "mem"), None),
        P(("dp", "mem"), None),
        P(("dp", "mem"), None),
        P(("dp", "mem"), None),
        P(("dp", "mem"), None),
        P(("dp", "mem"), None),
        P(("dp", "mem"), None),
        P(None, ("dp", "mem")),
        P(None, ("dp", "mem")),
    )
    return jax.shard_map(
        on_device, mesh=mesh, in_specs=in_specs, out_specs=out_specs, check_vma=False
    )
```

```python
from functools import partial

import jax
import jax.numpy as jnp
from jax import lax
from jax.experimental import pallas as pl
from jax.experimental.pallas import tpu as pltpu
from jax.sharding import PartitionSpec as P

HEAD = 64
PAIR = 2 * HEAD
SIDE = 4
CHIPS = SIDE * SIDE * SIDE
ROWS = 16
TILE = 1024
FF_TILE = 1024
BACK_TILE = 512
BLOCK = 640
CHUNK = 16
PARTS = ((0, 1024), (1024, 2048), (2048, 3200))
ENTRIES = 200
MIB = 1024 * 1024
epsilon = 1e-05
masked_score = -1e30
bf16 = jnp.bfloat16
f32 = jnp.float32


def dot(left, right):
    return jnp.dot(left, right, preferred_element_type=f32)


def dot_nt(left, right):
    return lax.dot_general(left, right, (((1,), (1,)), ((), ())), preferred_element_type=f32)


def dot_tn(left, right):
    return lax.dot_general(left, right, (((0,), (0,)), ((), ())), preferred_element_type=f32)


def normalized(values):
    centre = values - jnp.mean(values, -1, keepdims=True)
    inverse = lax.rsqrt(jnp.mean(centre * centre, -1, keepdims=True) + epsilon)
    return centre * inverse, inverse


def norm_back(upstream, normed, inverse, gain):
    scaled = upstream * gain
    back = inverse * (
        scaled
        - jnp.mean(scaled, -1, keepdims=True)
        - normed * jnp.mean(scaled * normed, -1, keepdims=True)
    )
    return back, jnp.sum(upstream * normed, 0, keepdims=True), jnp.sum(upstream, 0, keepdims=True)


def lower_lanes(shape):
    return lax.broadcasted_iota(jnp.int32, shape, 1) < HEAD


def parted(block):
    low = lower_lanes(block.shape)
    none = jnp.zeros_like(block)
    return jnp.concatenate([jnp.where(low, block, none), jnp.where(low, none, block)], 0)


def merged(block):
    rows = block.shape[0] // 2
    return jnp.where(lower_lanes((rows, PAIR)), block[:rows], block[rows:])


def self_softmax(queries, keys, allowed):
    scores = dot_nt(queries, keys) * HEAD ** (-0.5)
    scores = jnp.where(allowed, scores, masked_score)
    weights = jnp.exp(scores - jnp.max(scores, -1, keepdims=True))
    return weights * (1.0 / jnp.sum(weights, -1, keepdims=True))


def by_view(values, is_first, combine, neutral):
    first = combine(jnp.where(is_first, values, neutral), -1, keepdims=True)
    second = combine(jnp.where(is_first, neutral, values), -1, keepdims=True)
    return jnp.where(is_first, first, second)


def cross_softmax(queries, keys, kept, is_first):
    scores = dot_nt(queries, keys) * HEAD ** (-0.5)
    scores = jnp.where(kept, scores, masked_score)
    weights = jnp.exp(scores - by_view(scores, is_first, jnp.max, masked_score))
    return weights * (1.0 / by_view(weights, is_first, jnp.sum, 0.0))


def each_view(block, is_first):
    none = jnp.zeros_like(block)
    return jnp.concatenate([jnp.where(is_first, block, none), jnp.where(is_first, none, block)], 0)


def allowed_of(allowed_ref):
    allowed = allowed_ref[...] > 0.5
    return jnp.concatenate([allowed, allowed], 0)


PACK = (0, 96, 192, 288, 480, 576)
SENT = (0, 96, 192, 288, 480, 672, 864, 960, 1056)


def attention_kernel(
    tokens_ref, allowed_ref, memory_ref, keep_ref, w_qkv, w_out, w_q, w_kv, w_cross_out, gains,
    biases, q_ref, kv_ref, h1_ref, qc_ref, kvc_ref, h2_ref, a3_ref, pack_ref, probs_ref,
    probs_cross_ref, a1,
):
    rows = q_ref.shape[0]
    width = tokens_ref.shape[1]
    a1_rows, o_rows, a2_rows, oc_rows, memory_rows = map(slice, PACK[:-1], PACK[1:])
    first_rows, second_rows = slice(PACK[3], PACK[3] + rows), slice(PACK[3] + rows, PACK[4])
    values = tokens_ref[...].astype(f32)
    normed, _ = normalized(values)
    a1[...] = (normed * gains[0:1] + biases[0:1]).astype(bf16)
    pack_ref[a1_rows] = a1[:rows]
    pack_ref[memory_rows] = memory_ref[...]
    q_ref[...] = dot(a1[:rows], w_qkv[:, :width]).astype(bf16)
    kv_ref[...] = dot(a1[...], w_qkv[:, width:]).astype(bf16)
    allowed = allowed_of(allowed_ref)
    for at in range(0, width, PAIR):
        queries = parted(q_ref[:, at : at + PAIR])
        probs = self_softmax(queries, kv_ref[:, at : at + PAIR], allowed)
        probs_ref[at // PAIR] = probs
        mixed = dot(probs.astype(bf16), kv_ref[:, width + at : width + at + PAIR])
        pack_ref[o_rows, at : at + PAIR] = merged(mixed).astype(bf16)
    h1 = values[:rows] + dot(pack_ref[o_rows], w_out[...])
    h1_ref[...] = h1
    normed, _ = normalized(h1)
    pack_ref[a2_rows] = (normed * gains[1:2] + biases[1:2]).astype(bf16)
    qc_ref[...] = dot(pack_ref[a2_rows], w_q[...]).astype(bf16)
    kvc_ref[...] = dot(memory_ref[...], w_kv[...]).astype(bf16)
    shape = (2 * rows, memory_ref.shape[0])
    kept = jnp.broadcast_to(keep_ref[...], shape) > 0.5
    is_first = lax.broadcasted_iota(jnp.int32, shape, 1) < shape[1] // 2
    for at in range(0, width, PAIR):
        queries = parted(qc_ref[:, at : at + PAIR])
        probs = cross_softmax(queries, kvc_ref[:, at : at + PAIR], kept, is_first)
        probs_cross_ref[at // PAIR] = probs
        mixed = dot(
            each_view(probs.astype(bf16), is_first), kvc_ref[:, width + at : width + at + PAIR]
        )
        pack_ref[first_rows, at : at + PAIR] = merged(mixed[: 2 * rows]).astype(bf16)
        pack_ref[second_rows, at : at + PAIR] = merged(mixed[2 * rows :]).astype(bf16)
    h2 = jnp.concatenate([h1, h1], 0) + dot(pack_ref[oc_rows], w_cross_out[...])
    h2_ref[...] = h2
    normed, _ = normalized(h2)
    a3_ref[...] = (normed * gains[2:3] + biases[2:3]).astype(bf16)


def attention(tokens_page, allowed, memory_rows, keep, weights, gains, biases):
    rows, width = allowed.shape[0], tokens_page.shape[1]
    shape = jax.ShapeDtypeStruct
    return pl.pallas_call(
        attention_kernel,
        out_shape=(
            shape((rows, width), bf16),
            shape((2 * rows, 2 * width), bf16),
            shape((rows, width), f32),
            shape((rows, width), bf16),
            shape((memory_rows.shape[0], 2 * width), bf16),
            shape((2 * rows, width), f32),
            shape((2 * rows, width), bf16),
            shape((PACK[-1], width), bf16),
            shape((width // PAIR, 2 * rows, 2 * rows), f32),
            shape((width // PAIR, 2 * rows, memory_rows.shape[0]), f32),
        ),
        scratch_shapes=[pltpu.VMEM((2 * rows, width), bf16)],
        compiler_params=pltpu.CompilerParams(vmem_limit_bytes=58 * MIB),
        cost_estimate=pl.CostEstimate(
            flops=2 * 10**9, bytes_accessed=24 * MIB, transcendentals=10**6
        ),
    )(tokens_page, allowed, memory_rows, keep, *weights, gains, biases)


def erf_parts(values):
    return 0.5 + 0.5 * lax.erf(values * (0.5**0.5))


def feed_forward_kernel(
    h2_ref, a3_ref, w_up, w_down, gains, biases, slope_ref, act_ref, h3_ref, out_ref, fin_ref, total
):
    step = pl.program_id(0)

    @pl.when(step == 0)
    def _():
        total[...] = jnp.zeros_like(total)

    up = dot(a3_ref[...], w_up[...])
    below = erf_parts(up)
    slope = below + up * jnp.exp(-0.5 * up * up) * (0.5 / jnp.pi) ** 0.5
    slope_ref[...] = slope.astype(bf16)
    act = (up * below).astype(bf16)
    act_ref[...] = act
    total[...] += dot(act, w_down[...])

    @pl.when(step == pl.num_programs(0) - 1)
    def _():
        h3 = h2_ref[...] + total[...]
        h3_ref[...] = h3
        out_ref[...] = h3.astype(bf16)
        normed, _ = normalized(h3)
        fin_ref[...] = (normed * gains[3:4] + biases[3:4]).astype(bf16)


def whole(*shape):
    return pl.BlockSpec(shape, lambda i: (0,) * len(shape))


def feed_forward(h2, a3, w_up, w_down, gains, biases):
    rows, width = h2.shape
    hidden = w_up.shape[1]
    shape = jax.ShapeDtypeStruct
    return pl.pallas_call(
        feed_forward_kernel,
        grid=(hidden // FF_TILE,),
        in_specs=[
            whole(rows, width),
            whole(rows, width),
            pl.BlockSpec((width, FF_TILE), lambda i: (0, i)),
            pl.BlockSpec((FF_TILE, width), lambda i: (i, 0)),
            whole(4, width),
            whole(4, width),
        ],
        out_specs=(
            pl.BlockSpec((rows, FF_TILE), lambda i: (0, i)),
            pl.BlockSpec((rows, FF_TILE), lambda i: (0, i)),
            whole(rows, width),
            whole(rows, width),
            whole(rows, width),
        ),
        out_shape=(
            shape((rows, hidden), bf16),
            shape((rows, hidden), bf16),
            shape((rows, width), f32),
            shape((rows, width), bf16),
            shape((rows, width), bf16),
        ),
        scratch_shapes=[pltpu.VMEM((rows, width), f32)],
        compiler_params=pltpu.CompilerParams(vmem_limit_bytes=58 * MIB),
        cost_estimate=pl.CostEstimate(
            flops=4 * rows * width * hidden, bytes_accessed=24 * MIB, transcendentals=rows * hidden
        ),
    )(h2, a3, w_up, w_down, gains, biases)


def halves(block):
    middle = block.shape[1] // 2
    return block[:, :middle], block[:, middle:]


def divide(core, block, keep_ref, give_ref):
    for side in range(2):

        @pl.when(core == side)
        def _(side=side):
            keep_ref[...] = halves(block)[side]
            give_ref[...] = halves(block)[1 - side]


def feed_forward_back_kernel(
    core_ref, own_ref, other_ref, far_a, far_b, far_c, h3_ref, h2_ref, gains, slope_hbm, w_up_hbm,
    w_down_hbm, gh3_keep, gh3_give, gup_keep, gup_give, gh2_ref, vector_ref, gh3_low, slope, w_up,
    w_down, arrived,
):
    core = core_ref[0]
    tiles = w_up.shape[0]
    copies = []
    for t in range(tiles):
        here = slice(t * BACK_TILE, (t + 1) * BACK_TILE)
        pairs = (
            (w_down_hbm.at[here], w_down.at[t]),
            (slope_hbm.at[:, here], slope.at[t]),
            (w_up_hbm.at[:, here], w_up.at[t]),
        )
        copies.append(
            [pltpu.make_async_copy(*pair, arrived.at[t, k]) for k, pair in enumerate(pairs)]
        )
        for copy in copies[-1]:
            copy.start()
    upstream = own_ref[...]
    for ref in (other_ref, far_a, far_b, far_c):
        upstream += ref[...].astype(f32)
    normed, inverse = normalized(h3_ref[...])
    gh3, gain, bias = norm_back(upstream, normed, inverse, gains[3:4])
    gh3_low[...] = gh3.astype(bf16)
    divide(core, gh3_low[...], gh3_keep, gh3_give)
    vector_ref[...] = jnp.zeros_like(vector_ref)
    vector_ref[3:4] = gain
    vector_ref[7:8] = bias
    total = None
    for t in range(tiles):
        for copy in copies[t]:
            copy.wait()
        gup = (dot_nt(gh3_low[...], w_down[t]) * slope[t].astype(f32)).astype(bf16)
        side, at = t // (tiles // 2), t % (tiles // 2) * BACK_TILE

        @pl.when(core == side)
        def _(gup=gup, at=at):
            gup_keep[:, at : at + BACK_TILE] = gup

        @pl.when(core != side)
        def _(gup=gup, at=at):
            gup_give[:, at : at + BACK_TILE] = gup

        result = dot_nt(gup, w_up[t])
        total = result if total is None else total + result
    normed, inverse = normalized(h2_ref[...])
    back, gain, bias = norm_back(total, normed, inverse, gains[2:3])
    gh2_ref[...] = gh3 + back
    vector_ref[2:3] = gain
    vector_ref[6:7] = bias


def feed_forward_back(core, parts, h3, h2, slope, w_up, w_down, gains):
    rows, width = h2.shape
    hidden = w_up.shape[1]
    tiles = hidden // BACK_TILE
    shape = jax.ShapeDtypeStruct
    vmem = pl.BlockSpec(memory_space=pltpu.VMEM)
    return pl.pallas_call(
        feed_forward_back_kernel,
        in_specs=scalar_first(8) + [pl.BlockSpec(memory_space=pl.ANY) for _ in range(3)],
        out_specs=(vmem,) * 6,
        out_shape=(
            shape((rows, width // 2), bf16),
            shape((rows, width // 2), bf16),
            shape((rows, hidden // 2), bf16),
            shape((rows, hidden // 2), bf16),
            shape((rows, width), f32),
            shape((8, width), f32),
        ),
        scratch_shapes=[
            pltpu.VMEM((rows, width), bf16),
            pltpu.VMEM((tiles, rows, BACK_TILE), bf16),
            pltpu.VMEM((tiles, width, BACK_TILE), bf16),
            pltpu.VMEM((tiles, BACK_TILE, width), bf16),
            pltpu.SemaphoreType.DMA((tiles, 3)),
        ],
        compiler_params=pltpu.CompilerParams(vmem_limit_bytes=58 * MIB),
        cost_estimate=pl.CostEstimate(
            flops=4 * rows * width * hidden,
            bytes_accessed=24 * MIB,
            transcendentals=2 * rows * hidden,
        ),
    )(core, *parts, h3, h2, gains, slope, w_up, w_down)


def attention_back_kernel(
    gh2_ref, w_cross_out, probs_cross_ref, kvc_ref, qc_ref, gains, *refs,
):
    later, refs = refs[:6], refs[6:]
    gh1_ref, gq_ref, gkv_ref, give_ref, gkvc_ref, vector_ref, sent_ref = refs[:7]
    goc, go, gqc, gh1_low, *buffers, arrived = refs[7:]
    copies = [
        pltpu.make_async_copy(ref, buffer, arrived.at[k])
        for k, (ref, buffer) in enumerate(zip(later, buffers))
    ]
    for copy in copies:
        copy.start()
    w_q, h1_ref, w_out, probs_ref, kv_ref, q_ref = buffers
    rows, width = gh1_ref.shape
    scale = HEAD ** (-0.5)
    sent_rows = list(map(slice, SENT[:-1], SENT[1:]))

    def pairs_of_heads():
        for number in range(2 * SIDE):
            at = number * PAIR
            yield number, sent_ref.at[number], slice(at, at + PAIR), slice(width + at, width + at + PAIR)

    gh2_low = gh2_ref[...].astype(bf16)
    goc[...] = dot_nt(gh2_low, w_cross_out[...]).astype(bf16)
    shape = (2 * rows, kvc_ref.shape[0])
    is_first = lax.broadcasted_iota(jnp.int32, shape, 1) < shape[1] // 2
    for number, to, here, there in pairs_of_heads():
        queries = parted(qc_ref[:, here])
        probs = probs_cross_ref[number]
        upstream = jnp.concatenate([parted(goc[:rows, here]), parted(goc[rows:, here])], 0)
        grad = dot_nt(upstream, kvc_ref[:, there])
        grad = jnp.where(is_first, grad[: 2 * rows], grad[2 * rows :])
        slope = probs * (grad - by_view(probs * grad, is_first, jnp.sum, 0.0))
        slope = slope.astype(bf16)
        change = (merged(dot(slope, kvc_ref[:, here])) * scale).astype(bf16)
        gqc[:, here] = change
        to[sent_rows[2]] = change
        to[sent_rows[3]] = gh2_ref[:, here].astype(bf16)
        change = (dot_tn(slope, queries) * scale).astype(bf16)
        gkvc_ref[:, here] = change
        to[sent_rows[6]] = change
        change = dot_tn(each_view(probs.astype(bf16), is_first), upstream).astype(bf16)
        gkvc_ref[:, there] = change
        to[sent_rows[7]] = change
    for copy in copies[:2]:
        copy.wait()
    normed, inverse = normalized(h1_ref[...])
    back, gain, bias = norm_back(dot_nt(gqc[...], w_q[...]), normed, inverse, gains[1:2])
    vector_ref[...] = jnp.zeros_like(vector_ref)
    vector_ref[1:2] = gain
    vector_ref[5:6] = bias
    gh1 = gh2_ref[:rows] + gh2_ref[rows:] + back
    gh1_ref[...] = gh1
    gh1_low[...] = gh1.astype(bf16)
    for copy in copies[2:]:
        copy.wait()
    go[...] = dot_nt(gh1_low[...], w_out[...]).astype(bf16)
    for number, to, here, there in pairs_of_heads():
        queries = parted(q_ref[:, here])
        probs = probs_ref[number]
        upstream = parted(go[:, here])
        grad = dot_nt(upstream, kv_ref[:, there])
        slope = probs * (grad - jnp.sum(probs * grad, -1, keepdims=True))
        slope = slope.astype(bf16)
        change = (merged(dot(slope, kv_ref[:, here])) * scale).astype(bf16)
        gq_ref[:, here] = change
        to[sent_rows[0]] = change
        to[sent_rows[1]] = gh1_low[:, here]
        change = (dot_tn(slope, queries) * scale).astype(bf16)
        gkv_ref[:, here] = change[:rows]
        give_ref[:, here] = change[rows:]
        to[sent_rows[4]] = change
        change = dot_tn(probs.astype(bf16), upstream).astype(bf16)
        gkv_ref[:, there] = change[:rows]
        give_ref[:, there] = change[rows:]
        to[sent_rows[5]] = change


def scalar_first(count):
    return [pl.BlockSpec(memory_space=pltpu.SMEM)] + [
        pl.BlockSpec(memory_space=pltpu.VMEM) for _ in range(count)
    ]


def attention_back(gh2, probs, probs_cross, kvc, qc, h1, kv, q, w_cross_out, w_q, w_out, gains):
    rows, width = q.shape
    shape = jax.ShapeDtypeStruct
    vmem = pl.BlockSpec(memory_space=pltpu.VMEM)
    later = (w_q, h1, w_out, probs, kv, q)
    return pl.pallas_call(
        attention_back_kernel,
        in_specs=[vmem] * 6 + [pl.BlockSpec(memory_space=pl.ANY) for _ in later],
        out_specs=(vmem,) * 7,
        out_shape=(
            shape((rows, width), f32),
            shape((rows, width), bf16),
            shape((rows, 2 * width), bf16),
            shape((rows, 2 * width), bf16),
            shape(kvc.shape, bf16),
            shape((8, width), f32),
            shape((2 * SIDE, SENT[-1], PAIR), bf16),
        ),
        scratch_shapes=[
            pltpu.VMEM((2 * rows, width), bf16),
            pltpu.VMEM((rows, width), bf16),
            pltpu.VMEM((rows, width), bf16),
            pltpu.VMEM((rows, width), bf16),
            *(pltpu.VMEM(array.shape, array.dtype) for array in later),
            pltpu.SemaphoreType.DMA((len(later),)),
        ],
        compiler_params=pltpu.CompilerParams(vmem_limit_bytes=58 * MIB),
        cost_estimate=pl.CostEstimate(
            flops=2 * 10**9, bytes_accessed=14 * MIB, transcendentals=10**6
        ),
    )(gh2, w_cross_out, probs_cross, kvc, qc, gains, *later)


def inputs_back_kernel(
    core_ref, tokens_ref, gh1_ref, gq_ref, gkv_ref, come_ref, gkvc_ref, come_cross_ref, w_qkv,
    w_kv, gains, tokens_grad_ref, memory_grad_ref, vector_ref, grads,
):
    core = core_ref[0]
    width = gh1_ref.shape[1]
    pairs = (gkv_ref[...].astype(f32) + come_ref[...].astype(f32)).astype(bf16)
    total = dot_nt(gq_ref[...], w_qkv[:, :width]) + dot_nt(pairs, w_qkv[:, width:])
    normed, inverse = normalized(tokens_ref[...].astype(f32))
    back, gain, bias = norm_back(total, normed, inverse, gains[0:1])
    tokens_grad_ref[...] = gh1_ref[...] + back
    vector_ref[...] = jnp.zeros_like(vector_ref)
    vector_ref[0:1] = gain
    vector_ref[4:5] = bias
    pairs = (gkvc_ref[...].astype(f32) + come_cross_ref[...].astype(f32)).astype(bf16)
    grads[...] = dot_nt(pairs, w_kv[...])
    own = memory_grad_ref.shape[1]
    for view in range(2):
        start = pl.multiple_of(view * 2 * own + core * own, 8)
        memory_grad_ref[view] = grads[pl.ds(start, own)]


def inputs_back(core, *operands):
    rows, width = operands[1].shape
    patches = operands[5].shape[0]
    shape = jax.ShapeDtypeStruct
    return pl.pallas_call(
        inputs_back_kernel,
        in_specs=scalar_first(len(operands)),
        out_shape=(
            shape((rows, width), f32),
            shape((2, patches // 4, width), f32),
            shape((8, width), f32),
        ),
        scratch_shapes=[pltpu.VMEM((patches, width), f32)],
        compiler_params=pltpu.CompilerParams(vmem_limit_bytes=58 * MIB),
        cost_estimate=pl.CostEstimate(flops=10**9, bytes_accessed=14 * MIB, transcendentals=0),
    )(core, *operands)


def logits_kernel(rows_ref, readout_ref, bias_ref, logits_ref, stats_ref, kept):
    tokens = rows_ref.shape[1]
    rows = jnp.concatenate([rows_ref[0], rows_ref[1]], 0)

    def statistics(begin, end):
        spans = range(begin, end, 128)
        for at in range(0, tokens, CHUNK):
            here = slice(at, at + CHUNK)
            first = [logits_ref[0, 0, here, c : c + 128] for c in spans]
            second = [logits_ref[0, 1, here, c : c + 128] for c in spans]
            new_first, new_second = first[0], second[0]
            for a, b in zip(first[1:], second[1:]):
                new_first = jnp.maximum(new_first, a)
                new_second = jnp.maximum(new_second, b)
            total_first = total_apart = total_second = jnp.zeros((CHUNK, 128), f32)
            if begin:
                top_first, top_second = kept[0, here], kept[3, here]
                new_first = jnp.maximum(new_first, top_first)
                new_second = jnp.maximum(new_second, top_second)
                fade_first = jnp.exp(top_first - new_first)
                total_first = kept[1, here] * fade_first
                total_apart = kept[2, here] * fade_first
                total_second = kept[4, here] * jnp.exp(top_second - new_second)
            for a, b in zip(first, second):
                weight = jnp.exp(a - new_first)
                total_first += weight
                total_apart += weight * (a - b)
                total_second += jnp.exp(b - new_second)
            kept[0, here], kept[1, here], kept[2, here] = new_first, total_first, total_apart
            kept[3, here], kept[4, here] = new_second, total_second

    before = None
    for begin, end in PARTS:
        values = dot_nt(rows, readout_ref[begin:end]) + bias_ref[:, begin:end]
        for v in range(2):
            logits_ref[0, v, :, begin:end] = values[v * tokens : (v + 1) * tokens]
        if before:
            statistics(*before)
        before = begin, end
    statistics(*before)

    top_first = jnp.max(kept[0], -1, keepdims=True)
    top_second = jnp.max(kept[3], -1, keepdims=True)
    fade_first = jnp.exp(kept[0] - top_first)
    fade_second = jnp.exp(kept[3] - top_second)
    stats = (
        top_first,
        jnp.sum(kept[1] * fade_first, -1, keepdims=True),
        jnp.sum(kept[2] * fade_first, -1, keepdims=True),
        top_second,
        jnp.sum(kept[4] * fade_second, -1, keepdims=True),
    )
    lane = lax.broadcasted_iota(jnp.int32, kept.shape[1:], 1)
    result = jnp.zeros(kept.shape[1:], f32)
    for k, stat in enumerate(stats):
        result = jnp.where(lane == k, stat, result)
    stats_ref[0] = result.T[:8]


def once(*shape):
    return pl.BlockSpec(shape, lambda i: (0,) * len(shape), pipeline_mode=pl.Buffered(1))


def logits_and_stats(rows, readout_rows, bias):
    views, tokens, width = rows.shape
    entries = readout_rows.shape[0]
    page = tokens // SIDE
    shape = jax.ShapeDtypeStruct
    return pl.pallas_call(
        logits_kernel,
        out_shape=(
            shape((SIDE, 2, page, entries), f32),
            shape((SIDE, 8, page), f32),
        ),
        grid=(SIDE,),
        in_specs=[
            pl.BlockSpec((2, page, width), lambda i: (0, i, 0)),
            once(entries, width),
            once(1, entries),
        ],
        out_specs=(
            pl.BlockSpec((1, 2, page, entries), lambda i: (i, 0, 0, 0)),
            pl.BlockSpec((1, 8, page), lambda i: (i, 0, 0)),
        ),
        scratch_shapes=[pltpu.VMEM((5, page, 128), f32)],
        compiler_params=pltpu.CompilerParams(vmem_limit_bytes=58 * MIB),
        cost_estimate=pl.CostEstimate(
            flops=4 * tokens * entries * width,
            bytes_accessed=2 * entries * width + 8 * tokens * entries,
            transcendentals=2 * tokens * entries,
        ),
    )(rows, readout_rows, bias)


def merged_stats(near_ref, come_ref, slot):
    tokens = near_ref.shape[3]
    middle = tokens // 2
    parts = []
    for ref, flipped in ((near_ref, False), (come_ref, True)):
        for r in range(SIDE):
            part = ref[r, lax.rem(slot + SIDE - r, SIDE)]
            if flipped:
                part = jnp.concatenate([part[:, middle:], part[:, :middle]], 1)
            parts.append(part)
    top_first = parts[0][0:1]
    top_second = parts[0][3:4]
    for part in parts[1:]:
        top_first = jnp.maximum(top_first, part[0:1])
        top_second = jnp.maximum(top_second, part[3:4])
    total_first = total_apart = total_second = jnp.zeros((1, tokens), f32)
    for part in parts:
        fade = jnp.exp(part[0:1] - top_first)
        total_first += part[1:2] * fade
        total_apart += part[2:3] * fade
        total_second += part[4:5] * jnp.exp(part[3:4] - top_second)
    first_lse = top_first + jnp.log(total_first)
    second_lse = top_second + jnp.log(total_second)
    return first_lse, second_lse, total_apart / total_first


def readout_back_kernel(
    far, near_ref, come_ref, weight_ref, logits_ref, readout_ref, stay_ref, other_ref, kept, slopes
):
    step = pl.program_id(0)
    tokens = weight_ref.shape[1]
    rows = tokens // 2
    slot = lax.rem(step + 1, SIDE) if far else 0
    for k, row in enumerate(merged_stats(near_ref, come_ref, slot)):
        kept[k] = jnp.broadcast_to(row, (128, row.shape[1])).T
    kept[3] = weight_ref[0]

    def gradient(start, count):
        def derivatives(begin, end):
            for at in range(start, start + count, CHUNK):
                here = slice(at, at + CHUNK)
                first_lse, second_lse, apart, weight = (kept[k, here] for k in range(4))
                for c in range(begin, end, 128):
                    first = logits_ref[0, 0, here, c : c + 128]
                    second = logits_ref[0, 1, here, c : c + 128]
                    first_prob = jnp.exp(first - first_lse) * weight
                    second_prob = jnp.exp(second - second_lse) * weight
                    change = first_prob * (first - second - apart)
                    slopes[0, here, c : c + 128] = change.astype(bf16)
                    slopes[1, here, c : c + 128] = (second_prob - first_prob).astype(bf16)

        derivatives(*PARTS[0])
        total = None
        for i, (begin, end) in enumerate(PARTS):
            block = [slopes[v, start : start + count, begin:end] for v in range(2)]
            result = dot(jnp.concatenate(block, 0), readout_ref[begin:end])
            if i + 1 < len(PARTS):
                derivatives(*PARTS[i + 1])
            total = result if total is None else total + result
        return total

    if not far:
        total = gradient(0, rows)
        for v in range(2):
            stay_ref[0, v] = total[v * rows : (v + 1) * rows]
        other_ref[...] = kept[3] * (kept[2] - kept[0] + kept[1])
        return

    @pl.when(step < SIDE - 1)
    def _():
        total = gradient(0, tokens)
        for v in range(2):
            stay_ref[0, v] = total[v * tokens : v * tokens + rows].astype(bf16)
            other_ref[0, v] = total[v * tokens + rows : (v + 1) * tokens].astype(bf16)

    @pl.when(step == SIDE - 1)
    def _():
        total = gradient(rows, rows)
        for v in range(2):
            other_ref[0, v] = total[v * rows : (v + 1) * rows].astype(bf16)


def readout_back(stats_near, stats_come, weight, logits, readout_rows, far):
    tokens, entries = logits.shape[2:]
    width = readout_rows.shape[1]
    rows = tokens // 2
    pages = SIDE if far else 1
    shape = jax.ShapeDtypeStruct
    block = (1, 2, rows, width)
    if far:
        out_shape = (
            shape((SIDE - 1, 2, rows, width), bf16),
            shape((SIDE, 2, rows, width), bf16),
        )
        out_specs = (
            pl.BlockSpec(block, lambda i: (jnp.minimum(i, SIDE - 2), 0, 0, 0)),
            pl.BlockSpec(block, lambda i: (i, 0, 0, 0)),
        )
    else:
        out_shape = (shape(block, f32), shape((tokens, 128), f32))
        out_specs = (whole(*block), whole(tokens, 128))

    def page(i):
        return lax.rem(i + 1, SIDE) if far else i

    here = tokens if far else rows
    return pl.pallas_call(
        partial(readout_back_kernel, far),
        out_shape=out_shape,
        grid=(pages,),
        in_specs=[
            once(SIDE, SIDE, 8, tokens),
            once(SIDE, SIDE, 8, tokens),
            pl.BlockSpec((1, tokens, 128), lambda i: (page(i), 0, 0)),
            pl.BlockSpec((1, 2, here, entries), lambda i: (page(i), 0, 0, 0)),
            once(entries, width),
        ],
        out_specs=out_specs,
        scratch_shapes=[
            pltpu.VMEM((4, tokens, 128), f32),
            pltpu.VMEM((2, here, entries), bf16),
        ],
        compiler_params=pltpu.CompilerParams(vmem_limit_bytes=58 * MIB),
        cost_estimate=pl.CostEstimate(
            flops=4 * pages * here * entries * width,
            bytes_accessed=2 * entries * width + 8 * pages * here * entries,
            transcendentals=2 * pages * here * entries,
        ),
    )(stats_near, stats_come, weight, logits, readout_rows)


FIRST_AXES = ((4, 16), (16, 1), (1, 4))
SECOND_AXES = ((4, 16), (16, 4))


def swapped(block):
    return lax.ppermute(block, "mem", [(0, 1), (1, 0)])


def along_line(block, distance):
    route = [(d, d // SIDE * SIDE + (d - distance) % SIDE) for d in range(CHIPS)]
    return lax.ppermute(block, "dp", route)


def lines(stride, core):
    starts = [d for d in range(CHIPS) if (d // stride) % SIDE == 0]
    return [[2 * (start + stride * k) + core for k in range(SIDE)] for start in starts]


def digit_of(strides):
    chip, core = lax.axis_index("dp"), lax.axis_index("mem")
    return jnp.where(core == 0, chip // strides[0], chip // strides[1]) % SIDE


def along_lines(block, strides, r):
    route = []
    for d in range(CHIPS):
        for m, stride in enumerate(strides):
            own = d // stride % SIDE
            to = d + ((own + r) % SIDE - own) * stride
            route.append((2 * d + m, 2 * to + m))
    return lax.ppermute(block, ("dp", "mem"), route)


def line_sum(part, strides):
    return parts_sum(parts_of(part, strides), strides)


def parts_of(part, strides):
    parts = part.reshape(SIDE, -1, part.shape[-1])
    digit = digit_of(strides)
    return [lax.dynamic_index_in_dim(parts, (digit + r) % SIDE, 0, False) for r in range(SIDE)]


def parts_sum(parts, strides):
    parts = parts_come(parts, strides)
    total = parts[0].astype(f32)
    for block in parts[1:]:
        total += block.astype(f32)
    return total


def parts_come(parts, strides):
    return [parts[0]] + [along_lines(parts[r], strides, r) for r in range(1, SIDE)]


def scattered_sum(bucket, strides):
    flat = bucket.reshape(-1, bucket.shape[-1])
    groups = lines(strides[0], 0) + lines(strides[1], 1)
    return lax.psum_scatter(
        flat, ("dp", "mem"), axis_index_groups=groups, scatter_dimension=0, tiled=True
    )


def outer_kernel(items, orders, core_ref, *refs):
    inputs, out_ref, turned = refs[: 4 * len(items)], refs[4 * len(items)], refs[-len(items) :]
    step = pl.program_id(0)
    core = core_ref[0]

    def place(chip):
        at = [0, 0]
        for m in range(2):
            for stride in orders[m]:
                at[m] = at[m] * SIDE + chip // stride % SIDE
        return jnp.where(core == 0, at[0], at[1])

    def turn(lefts, to, groups):
        for start in range(0, lefts[0].shape[1], 1024):
            flat = jnp.concatenate([left[:, start : start + 1024] for left in lefts], 0).T
            if groups == 1:
                to[0, start : start + 1024] = flat
                continue
            per = ROWS * groups
            for c in range(1024 // per):
                chip = start // per + c
                for g in range(groups):
                    at = c * per + g * ROWS
                    to[g, chip * ROWS : (chip + 1) * ROWS] = flat[at : at + ROWS]

    def multiply(rights, to, groups, begin):
        at = step - begin
        span = min(TILE, rights[0].shape[1])
        start = at * TILE if groups == 1 else 0
        column = pl.ds(pl.multiple_of(start, span), span)
        both = jnp.concatenate([right[:, column] for right in rights], 0)
        for k in range(TILE // span):
            group = at * (TILE // span) + k if groups > 1 else 0
            result = dot(to[group], both).astype(bf16)
            for chip in range(CHIPS):
                here = result[chip * ROWS : (chip + 1) * ROWS]
                out_ref[place(chip), :, k * span : (k + 1) * span] = here

    for k, (groups, begin, end) in enumerate(items):
        lefts, rights, to = inputs[4 * k : 4 * k + 2], inputs[4 * k + 2 : 4 * k + 4], turned[k]
        pl.when(step == begin)(partial(turn, lefts, to, groups))
        pl.when((step >= begin) & (step < end))(partial(multiply, rights, to, groups, begin))


def outer_products(core, products, axes):
    items, scratch = [], []
    total = flops = 0
    for left, left_come, right, _ in products:
        groups = left.shape[1] // (ROWS * CHIPS)
        depth = left.shape[0] + left_come.shape[0]
        columns = right.shape[1]
        scratch.append(pltpu.VMEM((groups, ROWS * CHIPS, depth), bf16))
        begin = total // TILE
        total += groups * columns
        flops += 2 * groups * ROWS * CHIPS * columns * depth
        items.append((groups, begin, total // TILE))
    operands = [array for product in products for array in product]
    return pl.pallas_call(
        partial(outer_kernel, tuple(items), tuple(zip(*axes))),
        out_shape=jax.ShapeDtypeStruct((CHIPS, ROWS, total), bf16),
        grid_spec=pltpu.PrefetchScalarGridSpec(
            num_scalar_prefetch=1,
            grid=(total // TILE,),
            in_specs=[
                pl.BlockSpec(
                    array.shape, lambda i, core: (0, 0), pipeline_mode=pl.Buffered(1)
                )
                for array in operands
            ],
            out_specs=pl.BlockSpec((CHIPS, ROWS, TILE), lambda i, core: (0, 0, i)),
            scratch_shapes=scratch,
        ),
        compiler_params=pltpu.CompilerParams(vmem_limit_bytes=58 * MIB),
        cost_estimate=pl.CostEstimate(
            flops=flops, bytes_accessed=CHIPS * ROWS * total * 2, transcendentals=0
        ),
    )(core, *operands)


LINE = ROWS * SIDE
DEPTHS = tuple(
    2 * SIDE * (PACK[k + 1] - PACK[k]) // (2 if k == 4 else 1) for k in range(len(PACK) - 1)
)


def turn_kernel(orders, core_ref, packs_ref, out_ref):
    core = core_ref[0]
    start = 0
    for k, depth in enumerate(DEPTHS):
        numbers = range(0, 2 * SIDE, 2 if k == 4 else 1)
        blocks = [packs_ref[number, PACK[k] : PACK[k + 1]] for number in numbers]
        flat = jnp.concatenate(blocks, 0).T
        for line in range(SIDE * SIDE):
            z, y = line // SIDE, line % SIDE
            digit = {4: y, 16: z}
            at = [SIDE * digit[first] + digit[second] for first, second in orders]
            at = pl.multiple_of(jnp.where(core == 0, at[0], at[1]) * LINE, LINE)
            out_ref[pl.ds(at, LINE), start : start + depth] = flat[line * LINE : (line + 1) * LINE]
        start += depth


def turned_packs(core, packs, axes):
    width = packs.shape[2]
    return pl.pallas_call(
        partial(turn_kernel, tuple(zip(*axes))),
        in_specs=scalar_first(1),
        out_shape=jax.ShapeDtypeStruct((width, sum(DEPTHS)), bf16),
        compiler_params=pltpu.CompilerParams(vmem_limit_bytes=58 * MIB),
        cost_estimate=pl.CostEstimate(flops=0, bytes_accessed=20 * MIB, transcendentals=0),
    )(core, packs)


def line_products_kernel(
    digit_ref, vectors_ref, turned_hbm, come_hbm, *refs
):
    outs, (joint, plain, cross, wide, come_ref, turned_ref, results, arrived, left) = (
        refs[:SIDE],
        refs[SIDE:],
    )
    block = turned_ref.shape[1]
    fetch_come = pltpu.make_async_copy(come_hbm, come_ref, arrived.at[SIDE])
    fetch_come.start()
    starts = [
        pl.multiple_of(lax.rem(digit_ref[0] + r, SIDE) * block, block) for r in range(SIDE)
    ]
    fetches = [
        pltpu.make_async_copy(turned_hbm.at[pl.ds(start, block)], turned_ref.at[r], arrived.at[r])
        for r, start in enumerate(starts)
    ]
    for fetch in fetches:
        fetch.start()
    fetch_come.wait()
    rows = SENT[1]

    def part(number, k):
        return come_ref[number, SENT[k] : SENT[k + 1]]

    def added(first, second):
        return (first.astype(f32) + second.astype(f32)).astype(bf16)

    for number in range(2 * SIDE):
        at = number * rows
        here = slice(at, at + rows)
        joint[here, :PAIR] = part(number, 0)
        for k in (4, 5):
            share = added(part(number, k)[:rows], part(number ^ 1, k)[rows:])
            joint[here, (k - 3) * PAIR : (k - 2) * PAIR] = share
        plain[here, :PAIR] = part(number, 1)
        plain[here, PAIR:] = part(number, 2)
        wide[2 * at : 2 * (at + rows)] = part(number, 3)
    for chip in range(SIDE):
        here = slice(chip * rows, (chip + 1) * rows)
        for k in (6, 7):
            column = slice((k - 6) * PAIR, (k - 5) * PAIR)
            cross[here, column] = added(part(2 * chip, k), part(2 * chip + 1, k))

    ends = [sum(DEPTHS[: k + 1]) for k in range(len(DEPTHS))]
    stores = []
    for r in range(SIDE):
        fetches[r].wait()
        a1, o, a2, oc, memory = (
            turned_ref[r, :, end - depth : end] for end, depth in zip(ends, DEPTHS)
        )
        blocks = [
            dot(a1, joint[...]),
            dot(o, plain[:, :PAIR]),
            dot(a2, plain[:, PAIR:]),
            dot(memory, cross[...]),
            dot(oc, wide[...]),
            vectors_ref[pl.ds(starts[r], block)].astype(f32),
        ]
        results[r] = jnp.concatenate(blocks, 1).astype(bf16)
        stores.append(pltpu.make_async_copy(results.at[r], outs[r], left.at[r]))
        stores[-1].start()
    for store in stores:
        store.wait()


def line_products(digit, turned, come, vectors):
    width, depth = turned.shape
    block = width // SIDE
    columns = 9 * PAIR
    anywhere = pl.BlockSpec(memory_space=pl.ANY)
    return pl.pallas_call(
        line_products_kernel,
        in_specs=scalar_first(1) + [anywhere, anywhere],
        out_specs=(anywhere,) * SIDE,
        out_shape=(jax.ShapeDtypeStruct((block, columns), bf16),) * SIDE,
        scratch_shapes=[
            pltpu.VMEM((DEPTHS[0], 3 * PAIR), bf16),
            pltpu.VMEM((DEPTHS[1], 2 * PAIR), bf16),
            pltpu.VMEM((DEPTHS[4], 2 * PAIR), bf16),
            pltpu.VMEM((DEPTHS[3], PAIR), bf16),
            pltpu.VMEM(come.shape, bf16),
            pltpu.VMEM((SIDE, block, depth), bf16),
            pltpu.VMEM((SIDE, block, columns), bf16),
            pltpu.SemaphoreType.DMA((SIDE + 1,)),
            pltpu.SemaphoreType.DMA((SIDE,)),
        ],
        compiler_params=pltpu.CompilerParams(vmem_limit_bytes=58 * MIB),
        cost_estimate=pl.CostEstimate(
            flops=2 * 10**9, bytes_accessed=14 * MIB, transcendentals=0
        ),
    )(digit, vectors, turned, come)


def collect_kernel(come_ref, *outs):
    qkv, out, q, kv, cross_out, gains, biases = outs
    targets = [(qkv, 0), (qkv, 1), (qkv, 2), (out, 0), (q, 0), (kv, 0), (kv, 1), (cross_out, 0)]
    for number in range(2 * SIDE):
        for k, (target, block) in enumerate(targets):
            start = (block * 2 * SIDE + number) * PAIR
            target[:, start : start + PAIR] = come_ref[number, :, k * PAIR : (k + 1) * PAIR]
    total = come_ref[0, :, 8 * PAIR :]
    for number in range(1, 2 * SIDE):
        total += come_ref[number, :, 8 * PAIR :]
    total = jnp.concatenate([total, jnp.zeros((PAIR - total.shape[0], PAIR), f32)], 0).T
    gains[...] = total[:4, : ROWS // 2]
    biases[...] = total[4:8, : ROWS // 2]


def collected(come):
    return pl.pallas_call(
        collect_kernel,
        out_shape=tuple(
            jax.ShapeDtypeStruct((ROWS // 2, columns), f32)
            for columns in (24 * PAIR, 8 * PAIR, 8 * PAIR, 16 * PAIR, 8 * PAIR)
        )
        + (jax.ShapeDtypeStruct((4, ROWS // 2), f32),) * 2,
    )(come)


def divide_kernel(grouped, core_ref, *refs):
    parts, (keep_ref, give_ref, sums_ref) = refs[:SIDE], refs[SIDE:]
    sums_ref[...] = parts[0][...].astype(f32)
    for part in parts[1:]:
        sums_ref[...] += part[...].astype(f32)
    core = core_ref[0]
    half = grouped // 2
    columns = sums_ref.shape[1]
    for ref, side in ((keep_ref, core), (give_ref, 1 - core)):
        if grouped:
            start = pl.ds(pl.multiple_of(side * half, 128), half)
            block = sums_ref[:, start]
            ref[:, :half] = block[: ROWS // 2]
            ref[:, half:grouped] = block[ROWS // 2 :]
        rows = pl.ds(pl.multiple_of(side * (ROWS // 2), 8), ROWS // 2)
        if columns > grouped:
            ref[:, grouped:] = sums_ref[rows, grouped:]


def divided(core, parts, grouped):
    columns = parts[0].shape[1]
    shape = jax.ShapeDtypeStruct((ROWS // 2, columns), f32)
    return pl.pallas_call(
        partial(divide_kernel, grouped),
        in_specs=scalar_first(SIDE),
        out_shape=(shape, shape),
        scratch_shapes=[pltpu.VMEM((ROWS, columns), f32)],
    )(core, *parts)


def assemble_kernel(layout, core_ref, keep_ref, come_ref, *outs):
    core = core_ref[0]
    for ref, side in ((keep_ref, core), (come_ref, 1 - core)):
        at = 0
        for out, (grouped, columns, span) in zip(outs, layout):
            part = span // 2
            if grouped:
                for g in range(2):
                    for h in range(2):
                        rows = slice(g * ROWS + h * ROWS // 2, g * ROWS + (h + 1) * ROWS // 2)
                        start = at + h * 2 * part + g * part
                        column = pl.ds(pl.multiple_of(side * part, 128), part)
                        out[rows, column] = ref[:, start : start + part]
                at += 4 * part
                continue
            for k in range(0, columns, span):
                column = pl.ds(pl.multiple_of(k + side * part, 128), part)
                out[:, column] = ref[:, at : at + part]
                at += part


def assembled(core, keep, come, layout):
    return pl.pallas_call(
        partial(assemble_kernel, tuple(layout)),
        in_specs=scalar_first(2),
        out_shape=tuple(
            jax.ShapeDtypeStruct((2 * ROWS if grouped else ROWS // 2, columns), f32)
            for grouped, columns, span in layout
        ),
    )(core, keep, come)


def on_device(
    tokens,
    memory,
    lengths,
    segments,
    key_mask,
    w_self_qkv,
    w_self_out,
    w_cross_q,
    w_cross_kv,
    w_cross_out,
    w_up,
    w_down,
    norm_gains,
    norm_biases,
    readout,
):
    tok_rows = tokens.shape[1]
    width = tokens.shape[2]
    half = lax.axis_index("mem")
    core = half.astype(jnp.int32).reshape(1)
    page_index = lax.axis_index("dp")
    patches = 2 * memory.shape[2]

    vocab_dev = readout.shape[1]
    readout_turned = jnp.pad(readout.T, ((0, ENTRIES - vocab_dev), (0, 0)))
    planes = [[d for d in range(CHIPS) if d % SIDE == x] for x in range(SIDE)]
    readout_part = lax.all_gather(
        readout_turned, "dp", axis=0, tiled=True, axis_index_groups=planes
    )
    is_entry = jnp.arange(readout_part.shape[0]) % ENTRIES < vocab_dev
    entry_bias = jnp.where(is_entry, 0.0, masked_score).astype(f32)[None]

    tokens_own = tokens[0]
    tokens_page = jnp.concatenate([tokens_own, swapped(tokens_own)], 0)
    memory_own = memory[:, 0]
    memory_come = swapped(memory_own)
    memory_rows = jnp.where(
        half == 0,
        jnp.concatenate([memory_own, memory_come], 1),
        jnp.concatenate([memory_come, memory_own], 1),
    ).reshape(2 * patches, width)
    mask_own = key_mask[0].astype(f32)
    mask_come = swapped(mask_own)
    mask_page = jnp.where(
        half == 0,
        jnp.concatenate([mask_own, mask_come]),
        jnp.concatenate([mask_come, mask_own]),
    )
    keep = jnp.tile(jnp.repeat(mask_page, 2), 2)[None]
    own_positions = jnp.arange(tok_rows) + half * tok_rows
    other_positions = jnp.arange(tok_rows) + (1 - half) * tok_rows
    key_positions = jnp.concatenate([own_positions, other_positions])
    cut = segments[0].reshape(2, tok_rows)
    own_segments = lax.dynamic_index_in_dim(cut, half, 0, False)
    other_segments = lax.dynamic_index_in_dim(cut, 1 - half, 0, False)
    key_segments = jnp.concatenate([own_segments, other_segments])
    allowed = (key_positions[None, :] <= own_positions[:, None]) & (
        key_segments[None, :] == own_segments[:, None]
    )
    allowed = allowed.astype(f32)
    count = jnp.sum(lengths).astype(f32)
    line = page_index // SIDE * SIDE + (page_index + jnp.arange(SIDE)) % SIDE
    valid = key_positions[None] < lengths[line][:, None]
    row_weight = (valid.astype(f32) / count)[:, :, None]
    row_weight = jnp.broadcast_to(row_weight, row_weight.shape[:2] + (128,))

    weights = (w_self_qkv, w_self_out, w_cross_q, w_cross_kv, w_cross_out)
    q, kv, h1, qc, kvc, h2, a3, pack, probs, probs_cross = attention(
        tokens_page, allowed, memory_rows, keep, weights, norm_gains, norm_biases
    )
    slope, act, h3, layer_out, final = feed_forward(h2, a3, w_up, w_down, norm_gains, norm_biases)
    final = final.reshape(2, tok_rows, width)
    near = jnp.stack([final] + [along_line(final, r) for r in range(1, SIDE)])
    final_line = jnp.stack([near, swapped(near)], 1).transpose(2, 0, 1, 3, 4)
    final_line = final_line.reshape(2, 2 * SIDE * tok_rows, width)
    a3_other, act_other = swapped(a3), swapped(act)

    final_line, row_weight = lax.optimization_barrier((final_line, row_weight))

    line_groups = [
        [2 * (start + k) + m for k in range(SIDE) for m in range(2)]
        for start in range(0, CHIPS, SIDE)
    ]
    packs = lax.all_gather(pack, ("dp", "mem"), axis_index_groups=line_groups)

    def exchanged(block):
        return lax.all_to_all(
            block, ("dp", "mem"), 0, 0, axis_index_groups=line_groups, tiled=True
        )

    logits, stats = logits_and_stats(final_line, readout_part, entry_bias)
    stats = jnp.stack([stats] + [along_line(stats, r) for r in range(1, SIDE)])
    stats_come = swapped(stats)
    far_stay, give = readout_back(stats, stats_come, row_weight, logits, readout_part, True)
    come = swapped(give)
    far = [
        (far_stay[r].astype(f32) + come[r].astype(f32)).astype(bf16) for r in range(SIDE - 1)
    ]
    logits, far, core_late = lax.optimization_barrier((logits, far, core))
    far = [along_line(far[r - 1], -r) for r in range(1, SIDE)]
    own, terms = readout_back(stats, stats_come, row_weight, logits, readout_part, False)
    terms = terms[:, 0].reshape(2, tok_rows).sum(1)
    loss = (terms[0] + terms[1]).reshape(1)
    turned = turned_packs(core_late, packs, SECOND_AXES)
    own, turned = lax.optimization_barrier((own, turned))
    grad_parts = [part.reshape(2 * tok_rows, width) for part in [own[0], come[SIDE - 1]] + far]

    gh3_keep, gh3_give, gup_keep, gup_give, gh2, vectors_ff = feed_forward_back(
        core, grad_parts, h3, h2, slope, w_up, w_down, norm_gains
    )
    first_bucket = outer_products(
        core,
        [
            (act, act_other, gh3_keep, swapped(gh3_give)),
            (a3, a3_other, gup_keep, swapped(gup_give)),
        ],
        FIRST_AXES,
    )
    gh2, first_bucket = lax.optimization_barrier((gh2, first_bucket))
    first_part = scattered_sum(first_bucket, FIRST_AXES[0])

    gh1, gq, gkv, gkv_give, gkvc, vectors_att, sent = attention_back(
        gh2, probs, probs_cross, kvc, qc, h1, kv, q, w_cross_out, w_cross_q, w_self_out, norm_gains
    )
    sent = exchanged(sent)
    tokens_grad, memory_grad, vectors_in = inputs_back(
        core, tokens_own, gh1, gq, gkv, swapped(gkv_give), gkvc, swapped(gkvc), w_self_qkv,
        w_cross_kv, norm_gains,
    )
    sent, first_part, vectors_in = lax.optimization_barrier((sent, first_part, vectors_in))
    vectors = (vectors_ff + vectors_att + vectors_in).astype(bf16)
    vectors = jnp.pad(vectors.T, ((0, 0), (0, PAIR - 8))).reshape(SIDE, SIDE, LINE, PAIR)
    vectors = jnp.where(half == 0, vectors.transpose(1, 0, 2, 3), vectors).reshape(width, PAIR)
    digit = digit_of(SECOND_AXES[0]).astype(jnp.int32).reshape(1)
    second_parts = line_products(digit, turned, sent, vectors)
    second_sums = parts_sum(second_parts, SECOND_AXES[0]).astype(bf16)
    first_sums = scattered_sum(first_part, FIRST_AXES[1])
    second_sums = line_sum(second_sums, SECOND_AXES[1])
    first_parts = parts_come(parts_of(first_sums, FIRST_AXES[2]), FIRST_AXES[2])

    first_keep, first_give = divided(core, first_parts, 2 * width)
    weight_down, weight_up = assembled(
        core,
        first_keep,
        swapped(first_give),
        [(True, width, width), (False, 4 * width, 4 * width)],
    )
    line_sums = exchanged(second_sums.reshape(2 * SIDE, ROWS // 2, -1))
    line_sums, weight_down, weight_up = lax.optimization_barrier(
        (line_sums, weight_down, weight_up)
    )
    weight_qkv, weight_out, weight_q, weight_kv, weight_cross_out, grad_gains, grad_biases = (
        collected(line_sums)
    )
    return (
        loss,
        layer_out.reshape(2, 1, tok_rows, width),
        tokens_grad[None],
        memory_grad[:, None],
        weight_qkv,
        weight_out,
        weight_q,
        weight_kv,
        weight_cross_out,
        weight_up,
        weight_down,
        grad_gains,
        grad_biases,
    )


def solution(mesh):
    in_specs = (
        P("dp", "mem", None),
        P(None, "dp", "mem", None),
        P(),
        P("dp", None),
        P("dp", "mem"),
        P(),
        P(),
        P(),
        P(),
        P(),
        P(),
        P(),
        P(),
        P(),
        P(None, ("dp", "mem")),
    )
    out_specs = (
        P("dp"),
        P(None, "dp", "mem", None),
        P("dp", "mem", None),
        P(None, "dp", "mem", None),
        P(("dp", "mem"), None),
        P(("dp", "mem"), None),
        P(("dp", "mem"), None),
        P(("dp", "mem"), None),
        P(("dp", "mem"), None),
        P(("dp", "mem"), None),
        P(("dp", "mem"), None),
        P(None, ("dp", "mem")),
        P(None, ("dp", "mem")),
    )
    return jax.shard_map(
        on_device, mesh=mesh, in_specs=in_specs, out_specs=out_specs, check_vma=False
    )
```
